32 devices in a mesh: seq: 8 (over z, y), fsdp: 4 (over x, core).
Axes of the slice: x: 2, y: 2, z: 4, core: 2. Of those that a mesh axis runs over, the one named last changes fastest.
Arguments:
- inputs: bfloat16 [4, 1024, 2560], P('fsdp', 'seq'), may hold values from -6 to 6
- resets: int32 [4, 1024], P('fsdp', 'seq'), may hold values from 0 to 1, as said below
- cotangent: bfloat16 [4, 1024, 2560], P('fsdp', 'seq'), may hold values from -6 to 6
- first_gain: bfloat16 [2560], P(('seq', 'fsdp')), may hold values from 0.5 to 1.5
- branch_weight: bfloat16 [2560, 2560], P(('seq', 'fsdp')), may hold values from -0.125 to 0.125
- input_weight: bfloat16 [2560, 2560], P(('seq', 'fsdp')), may hold values from -0.125 to 0.125
- conv_weight: bfloat16 [2560, 4], P(('seq', 'fsdp')), may hold values from -3 to 3
- input_gate: bfloat16 [2560, 256], P(('seq', 'fsdp')), may hold values from -0.375 to 0.375
- decay_gate: bfloat16 [2560, 256], P(('seq', 'fsdp')), may hold values from -0.375 to 0.375
- decay_param: bfloat16 [2560], P(('seq', 'fsdp')), may hold values from -14 to -4
- output_weight: bfloat16 [2560, 2560], P(('seq', 'fsdp')), may hold values from -0.25 to 0.25
- second_gain: bfloat16 [2560], P(('seq', 'fsdp')), may hold values from 0.5 to 1.5
- gate_weight: bfloat16 [2560, 7680], P(('seq', 'fsdp')), may hold values from -0.125 to 0.125
- up_weight: bfloat16 [2560, 7680], P(('seq', 'fsdp')), may hold values from -0.125 to 0.125
- down_weight: bfloat16 [2560, 7680], P(('seq', 'fsdp')), may hold values from -0.0625 to 0.0625
Outputs:
- result: bfloat16 [4, 1024, 2560], P('fsdp', 'seq')
- grad_inputs: bfloat16 [4, 1024, 2560], P('fsdp', 'seq')
- grad_first_gain: float32 [2560], P(('seq', 'fsdp'))
- grad_branch_weight: float32 [2560, 2560], P(('seq', 'fsdp'))
- grad_input_weight: float32 [2560, 2560], P(('seq', 'fsdp'))
- grad_conv_weight: float32 [2560, 4], P(('seq', 'fsdp'))
- grad_input_gate: float32 [2560, 256], P(('seq', 'fsdp'))
- grad_decay_gate: float32 [2560, 256], P(('seq', 'fsdp'))
- grad_decay_param: float32 [2560], P(('seq', 'fsdp'))
- grad_output_weight: float32 [2560, 2560], P(('seq', 'fsdp'))
- grad_second_gain: float32 [2560], P(('seq', 'fsdp'))
- grad_gate_weight: float32 [2560, 7680], P(('seq', 'fsdp'))
- grad_up_weight: float32 [2560, 7680], P(('seq', 'fsdp'))
- grad_down_weight: float32 [2560, 7680], P(('seq', 'fsdp'))
The draws below stay inside these ranges and needn't reach their ends.
Inputs may be any that keep to these rules, and one draw needn't show every extreme that they name: `resets`: each group's first token is 1. In each group one document starts within its first 64 tokens and ends within its last 64, with no other 1 in between.
All inputs are finite; a program needn't handle non-finite values.
Results may differ from the reference program's by a relative error of at most 0.012.
Values may be sent and summed in bfloat16 or wider, within the bound.
A program may use at most 1 GiB of HBM per device.

```python
import math
import jax
import jax.numpy as jnp
from jax import lax

D = 2560
HW = 256
FF = 7680
KW = 4
TOK_DEV = 128
PIECE = 16
GROUPS = 4
GROUP_TOK = 1024


def draw_resets(key, part):
    key = jax.random.fold_in(key, 11)
    first_key, second_key, third_key = jax.random.split(key, 3)
    half_dev = TOK_DEV // 2
    starts = jax.random.randint(first_key, (GROUPS, 1), 1, half_dev + 1)
    finish = jax.random.randint(second_key, (GROUPS, 1), GROUP_TOK - half_dev, GROUP_TOK)
    places = jnp.arange(GROUP_TOK)[None, :]
    coins = jax.random.randint(third_key, (GROUPS, GROUP_TOK), 0, PIECE) == 0
    outside = (places < starts) | (places > finish)
    marks = coins & outside | (places == 0) | (places == starts) | (places == finish)
    return marks.astype(jnp.int32)


def draw_decay_param(key, part):
    key = jax.random.fold_in(key, 7)
    first_key, second_key = jax.random.split(key, 2)
    head_count = D // HW
    portion = 0.5
    slow_head = jax.random.uniform(first_key, (head_count, 1)) < portion
    levels = jax.random.uniform(second_key, (head_count, HW))
    slow_low = math.log(0.02 / GROUP_TOK)
    slow_high = math.log(0.25 / GROUP_TOK)
    slow_rates = jnp.exp(slow_low + levels * (slow_high - slow_low))
    quick_rates = jnp.exp(math.log(0.003) + levels * (math.log(0.012) - math.log(0.003)))
    speeds = jnp.where(slow_head, slow_rates, quick_rates).reshape(D)
    return jnp.log(jnp.expm1(speeds)).astype(jnp.bfloat16)


def level_of(rng, extent, pieces, smallest, high):
    factor_of, own = 1.0, jax.random.fold_in(rng, 6)
    for dim, parts in pieces:
        steps = jnp.exp(jax.random.uniform(jax.random.fold_in(own, dim), (parts,), jnp.float32, smallest / len(pieces), high / len(pieces)))
        factor_of = factor_of * jnp.repeat(steps, extent[dim] // parts).reshape([-1 if axis == dim else 1 for axis in range(len(extent))])
    return factor_of


def centred(stream_key, extent, scale, reach, shards=(), kind=jnp.bfloat16):
    values = scale * jax.random.normal(stream_key, extent, jnp.float32)
    if shards:
        values = values * level_of(stream_key, extent, shards, -0.22, 0.18)
    return jnp.clip(values, -reach, reach).astype(kind)


def setup_inputs(seed: int = 0) -> dict:
    key_list = jax.random.split(jax.random.key(seed), 16)
    inputs = centred(key_list[0], (GROUPS, GROUP_TOK, D), 1.0, 6.0, ((0, 4), (1, 8)))
    resets = draw_resets(jax.random.fold_in(key_list[15], 71), 0)
    cotangent = centred(key_list[2], (GROUPS, GROUP_TOK, D), 1.0, 6.0, ((0, 4), (1, 8)))
    first_gain = jnp.clip(1.0 + 0.1 * jax.random.normal(key_list[3], (D,), jnp.float32), 0.5, 1.5).astype(jnp.bfloat16)
    branch_weight = centred(key_list[4], (D, D), D ** -0.5, 0.125, ((0, 32),))
    input_weight = centred(key_list[5], (D, D), D ** -0.5, 0.125, ((0, 32),))
    conv_weight = centred(key_list[6], (D, KW), 0.5, 3.0, ((0, 32),))
    input_gate = centred(key_list[7], (D, HW), HW ** -0.5, 0.375, ((0, 32),))
    decay_gate = centred(key_list[8], (D, HW), HW ** -0.5, 0.375, ((0, 32),))
    decay_param = draw_decay_param(jax.random.fold_in(key_list[15], 71), 0)
    output_weight = centred(key_list[10], (D, D), (D // 4) ** -0.5, 0.25, ((0, 32),))
    second_gain = jnp.clip(1.0 + 0.1 * jax.random.normal(key_list[11], (D,), jnp.float32), 0.5, 1.5).astype(jnp.bfloat16)
    gate_weight = centred(key_list[12], (D, FF), D ** -0.5, 0.125, ((0, 32),))
    up_weight = centred(key_list[13], (D, FF), D ** -0.5, 0.125, ((0, 32),))
    down_weight = centred(key_list[14], (D, FF), FF ** -0.5, 0.0625, ((0, 32),))
    return {"inputs": inputs, "resets": resets, "cotangent": cotangent, "first_gain": first_gain, "branch_weight": branch_weight, "input_weight": input_weight, "conv_weight": conv_weight, "input_gate": input_gate, "decay_gate": decay_gate, "decay_param": decay_param, "output_weight": output_weight, "second_gain": second_gain, "gate_weight": gate_weight, "up_weight": up_weight, "down_weight": down_weight}


@jax.custom_vjp
def low(v):
    return lax.optimization_barrier(v.astype(jnp.bfloat16)).astype(jnp.float32)

@jax.custom_vjp
def low_back(v):
    return v

def low_keep(v):
    return (low(v), None)

def low_pass(kept, grad):
    return (grad,)

def back_keep(v):
    return (v, None)

def back_low(kept, grad):
    return (low(grad),)
low.defvjp(low_keep, low_pass)
low_back.defvjp(back_keep, back_low)
EPSILON = 1e-06
PRECISE = lax.Precision.HIGHEST

def matmul(operand_one, operand_two):
    return jnp.dot(operand_one, operand_two, precision=PRECISE, preferred_element_type=jnp.float32)

def affine(earlier, later):
    return (earlier[0] * later[0], later[0] * earlier[1] + later[1])

def rms_norm(values, gain_vector):
    scale = lax.rsqrt(lax.optimization_barrier(jnp.mean(values * values, axis=-1, keepdims=True)) + EPSILON)
    return values * scale * gain_vector

def blockdiag(values, weight):
    head_count = D // HW
    shaped = values.reshape(values.shape[:-1] + (head_count, HW))
    blocks = weight.reshape(head_count, HW, HW)
    mixed = jnp.einsum('glhi,hij->glhj', shaped, blocks, precision=PRECISE)
    return mixed.reshape(values.shape)

def forward(inputs, first_gain, branch_weight, input_weight, conv_weight, input_gate, decay_gate, decay_param, output_weight, second_gain, gate_weight, up_weight, down_weight, resets):
    normed = low(rms_norm(inputs, first_gain))
    branch_pre = low_back(matmul(normed, branch_weight))
    branch = jax.nn.gelu(branch_pre)
    conv_in = low_back(low(matmul(normed, input_weight)))
    segment = jnp.cumsum(resets, axis=1).astype(jnp.int32)
    length = inputs.shape[1]
    conv_out = jnp.zeros_like(conv_in)
    for offset in range(KW):
        shifted = jnp.pad(conv_in, ((0, 0), (offset, 0), (0, 0)))[:, :length]
        shifted_ids = jnp.pad(segment, ((0, 0), (offset, 0)), constant_values=-1)[:, :length]
        usable = (shifted_ids == segment).astype(jnp.float32)
        conv_out = conv_out + conv_weight[:, offset] * shifted * usable[:, :, None]
    rounded = low_back(low(conv_out))
    gate_input = jax.nn.sigmoid(low_back(blockdiag(rounded, input_gate)))
    gate_decay = jax.nn.sigmoid(low_back(blockdiag(rounded, decay_gate)))
    log_decay = -jax.nn.softplus(decay_param) * (1.0 + 7.0 * gate_decay)
    decays = jnp.exp(log_decay)
    restart = resets.astype(jnp.float32)[:, :, None]
    scaling = restart + (1.0 - restart) * jnp.sqrt(-jnp.expm1(2.0 * log_decay))
    driven = rounded * gate_input * scaling
    coefficient = decays * (1.0 - restart)
    running, states = lax.associative_scan(affine, (coefficient, driven), axis=1)
    mixed = low(states * branch)
    resid = inputs + low_back(matmul(mixed, output_weight))
    hidden = low(rms_norm(resid, second_gain))
    gate_pre = low_back(matmul(hidden, gate_weight))
    up_values = low_back(matmul(hidden, up_weight))
    active = low(jax.nn.gelu(gate_pre) * up_values)
    return resid + matmul(active, down_weight.T)

def reference(inputs, resets, cotangent, first_gain, branch_weight, input_weight, conv_weight, input_gate, decay_gate, decay_param, output_weight, second_gain, gate_weight, up_weight, down_weight):
    floats = [value.astype(jnp.float32) for value in (inputs, first_gain, branch_weight, input_weight, conv_weight, input_gate, decay_gate, decay_param, output_weight, second_gain, gate_weight, up_weight, down_weight)]

    def wrapped(*values):
        return forward(*values, resets)
    result, pullback = jax.vjp(wrapped, *floats)
    gradients = pullback(cotangent.astype(jnp.float32))
    return (result.astype(jnp.bfloat16), gradients[0].astype(jnp.bfloat16), gradients[1], gradients[2], gradients[3], gradients[4], gradients[5], gradients[6], gradients[7], gradients[8], gradients[9], gradients[10], gradients[11], gradients[12])
```

```python
import jax
import jax.numpy as jnp
from jax import lax
from jax.experimental import pallas as pl
from jax.experimental.pallas import tpu as pltpu
from jax.sharding import PartitionSpec as P

EPSILON = 1e-06
CONTRACT_ROWS = (((0,), (0,)), ((), ()))
CONTRACT_LAST = (((1,), (1,)), ((), ()))


def shifted_2(value, axis, steps):
    count = lax.axis_size(axis)
    leading, last = (max(0, -steps), min(count, count - steps))
    return lax.ppermute(value, axis, [(source, source + steps) for source in range(leading, last)])


def entering(x, axis, combine, identity, reverse):
    peers, index = (lax.axis_size(axis), lax.axis_index(axis))
    everything = jax.tree.map(lambda part: lax.all_gather(part, axis), x)
    start = jax.tree.map(
        lambda part, zero: jnp.broadcast_to(jnp.asarray(zero, part.dtype), part.shape), x, identity
    )

    def lap(k, before):
        at = peers - 1 - k if reverse else k
        reached = at > index if reverse else at < index
        new = combine(before, jax.tree.map(lambda part: part[at], everything))
        return jax.tree.map(lambda a, b: jnp.where(reached, a, b), new, before)

    return lax.fori_loop(0, peers, lap, start)


def affine(earlier, later):
    return (earlier[0] * later[0], later[0] * earlier[1] + later[1])


def product(operand_one, operand_two):
    return jnp.dot(operand_one, operand_two, preferred_element_type=jnp.float32)


def rows_product(operand_one, operand_two):
    return lax.dot_general(
        operand_one, operand_two, CONTRACT_ROWS, preferred_element_type=jnp.float32
    )


def last_product(operand_one, operand_two):
    return lax.dot_general(
        operand_one, operand_two, CONTRACT_LAST, preferred_element_type=jnp.float32
    )


def heads_apply(values, weight, head_count):
    token_count = values.shape[0]
    head_width = weight.shape[1]
    shaped = values.reshape(token_count, head_count, head_width)
    blocks = weight.reshape(head_count, head_width, head_width)
    mixed = jnp.einsum("thi,hij->thj", shaped, blocks, preferred_element_type=jnp.float32)
    return mixed.reshape(token_count, head_count * head_width)


def heads_back(gradients, weight, head_count):
    token_count = gradients.shape[0]
    head_width = weight.shape[1]
    shaped = gradients.reshape(token_count, head_count, head_width)
    blocks = weight.reshape(head_count, head_width, head_width)
    mixed = jnp.einsum("thj,hij->thi", shaped, blocks, preferred_element_type=jnp.float32)
    return mixed.reshape(token_count, head_count * head_width)


def heads_grad(values, gradients, head_count):
    token_count = values.shape[0]
    head_width = values.shape[1] // head_count
    left_side = values.reshape(token_count, head_count, head_width)
    right_side = gradients.reshape(token_count, head_count, head_width)
    summed = jnp.einsum("thi,thj->hij", left_side, right_side, preferred_element_type=jnp.float32)
    return summed.reshape(head_count * head_width, head_width)


def slab_count():
    for candidate in (5, 4, 2):
        return candidate
    return 1


def local(
    inputs,
    resets,
    cotangent,
    first_gain,
    branch_weight,
    input_weight,
    conv_weight,
    input_gate,
    decay_gate,
    decay_param,
    output_weight,
    second_gain,
    gate_weight,
    up_weight,
    down_weight,
):
    sources = inputs[0].astype(jnp.float32)
    flags = resets[0]
    returned = cotangent[0]
    returned_float = returned.astype(jnp.float32)
    tokens = sources.shape[0]
    shared = (
        lax.all_gather(first_gain, ("seq", "fsdp"), axis=0, tiled=True),
        lax.all_gather(branch_weight, ("seq", "fsdp"), axis=0, tiled=True),
        lax.all_gather(input_weight, ("seq", "fsdp"), axis=0, tiled=True),
        lax.all_gather(conv_weight, ("seq", "fsdp"), axis=0, tiled=True),
        lax.all_gather(input_gate, ("seq", "fsdp"), axis=0, tiled=True),
        lax.all_gather(decay_gate, ("seq", "fsdp"), axis=0, tiled=True),
        lax.all_gather(decay_param, ("seq", "fsdp"), axis=0, tiled=True),
        lax.all_gather(output_weight, ("seq", "fsdp"), axis=0, tiled=True),
        lax.all_gather(second_gain, ("seq", "fsdp"), axis=0, tiled=True),
    )
    dense_parts = (
        lax.all_gather(gate_weight, ("seq", "fsdp"), axis=0, tiled=True),
        lax.all_gather(up_weight, ("seq", "fsdp"), axis=0, tiled=True),
        lax.all_gather(down_weight, ("seq", "fsdp"), axis=0, tiled=True),
    )
    gain_first = shared[0].astype(jnp.float32)
    w_branch = shared[1]
    w_input = shared[2]
    w_conv = shared[3].astype(jnp.float32)
    w_igate = shared[4]
    w_dgate = shared[5]
    w_decay = shared[6].astype(jnp.float32)
    w_output = shared[7]
    gain_second = shared[8].astype(jnp.float32)
    w_gate = dense_parts[0]
    w_up = dense_parts[1]
    w_down = dense_parts[2]
    model_width = w_branch.shape[0]
    head_width = w_igate.shape[1]
    head_count = model_width // head_width
    tap_count = w_conv.shape[1]
    scale_one = lax.rsqrt(jnp.mean(sources * sources, axis=1, keepdims=True) + EPSILON)
    normed = (sources * scale_one * gain_first).astype(jnp.bfloat16)
    branch_pre = product(normed, w_branch)
    branch, branch_pull = jax.vjp(jax.nn.gelu, branch_pre)
    conv_in = product(normed, w_input).astype(jnp.bfloat16)
    resets_seen = jnp.cumsum(flags)
    tail_keep = resets_seen[-1] - resets_seen[tokens - tap_count + 1 :] == 0
    tail_rows = conv_in[tokens - tap_count + 1 :] * tail_keep[:, None]
    before = shifted_2(tail_rows, "seq", 1)
    padded = jnp.concatenate([before, conv_in], axis=0)
    seen_before = jnp.concatenate([jnp.zeros((tap_count - 1,), jnp.int32), resets_seen])
    conv_out = jnp.zeros((tokens, model_width), jnp.float32)
    usable_list = []
    for offset in range(tap_count):
        first_row = tap_count - 1 - offset
        shifted = padded[first_row : first_row + tokens].astype(jnp.float32)
        usable = (resets_seen - seen_before[first_row : first_row + tokens] == 0).astype(
            jnp.float32
        )[:, None]
        usable_list.append(usable)
        conv_out = conv_out + w_conv[:, offset] * shifted * usable
    rounded = conv_out.astype(jnp.bfloat16)
    rounded_float = rounded.astype(jnp.float32)
    gate_input = jax.nn.sigmoid(heads_apply(rounded, w_igate, head_count))
    gate_decay = jax.nn.sigmoid(heads_apply(rounded, w_dgate, head_count))
    softened = jax.nn.softplus(w_decay)
    log_decay = -softened * (1.0 + 7.0 * gate_decay)
    decays = jnp.exp(log_decay)
    root_term = jnp.sqrt(-jnp.expm1(2.0 * log_decay))
    restart = flags.astype(jnp.float32)[:, None]
    carried = 1.0 - restart
    scaling = restart + carried * root_term
    driven = rounded_float * gate_input * scaling
    coefficient = decays * carried
    running, local_state = lax.associative_scan(affine, (coefficient, driven), axis=0)
    unit_ones = jnp.ones((model_width,), jnp.float32)
    unit_zeros = jnp.zeros((model_width,), jnp.float32)
    incoming = entering(
        (running[-1], local_state[-1]), "seq", affine, (unit_ones, unit_zeros), False
    )
    state_in = incoming[1]
    states = local_state + running * state_in
    mixed = (states * branch).astype(jnp.bfloat16)
    resid = sources + product(mixed, w_output)
    scale_two = lax.rsqrt(jnp.mean(resid * resid, axis=1, keepdims=True) + EPSILON)
    hidden = (resid * scale_two * gain_second).astype(jnp.bfloat16)
    gate_pre = product(hidden, w_gate)
    up_values = product(hidden, w_up)
    gate_act, gate_pull = jax.vjp(jax.nn.gelu, gate_pre)
    active = (gate_act * up_values).astype(jnp.bfloat16)
    result = (resid + last_product(active, w_down)).astype(jnp.bfloat16)
    act_grad = product(returned, w_down)
    gate_grad = gate_pull(act_grad * up_values)[0].astype(jnp.bfloat16)
    up_grad = (act_grad * gate_act).astype(jnp.bfloat16)
    hidden_grad = last_product(gate_grad, w_gate) + last_product(up_grad, w_up)
    weighted_two = hidden_grad * gain_second
    resid_grad = (
        returned_float
        + scale_two * weighted_two
        - resid * scale_two**3 * jnp.mean(weighted_two * resid, axis=1, keepdims=True)
    )
    second_term = jnp.sum(hidden_grad * resid * scale_two, axis=0)
    branch_out_grad = resid_grad.astype(jnp.bfloat16)
    mixed_grad = last_product(branch_out_grad, w_output)
    state_grad = mixed_grad * branch
    branch_grad = mixed_grad * states
    branch_pre_grad = branch_pull(branch_grad)[0].astype(jnp.bfloat16)
    next_coef = jnp.concatenate([coefficient[1:], jnp.ones((1, model_width), jnp.float32)], axis=0)
    reaches, adjoint_local = lax.associative_scan(
        affine, (next_coef, state_grad), reverse=True, axis=0
    )
    carry_back = entering(
        (coefficient[0] * reaches[0], coefficient[0] * adjoint_local[0]),
        "seq",
        affine,
        (unit_ones, unit_zeros),
        True,
    )
    adjoint = adjoint_local + reaches * carry_back[1]
    earlier_state = jnp.concatenate([state_in[None], states[:-1]], axis=0)
    log_grad = (
        adjoint * earlier_state * carried * decays
        - adjoint * rounded_float * gate_input * carried * decays * decays / root_term
    )
    decay_term = jnp.sum(-log_grad * (1.0 + 7.0 * gate_decay), axis=0) * jax.nn.sigmoid(w_decay)
    input_pre_grad = (adjoint * rounded_float * scaling * gate_input * (1.0 - gate_input)).astype(
        jnp.bfloat16
    )
    decay_pre_grad = (log_grad * (-7.0 * softened) * gate_decay * (1.0 - gate_decay)).astype(
        jnp.bfloat16
    )
    conv_out_grad = (
        adjoint * gate_input * scaling
        + heads_back(input_pre_grad, w_igate, head_count)
        + heads_back(decay_pre_grad, w_dgate, head_count)
    )
    conv_grad = conv_out_grad.astype(jnp.bfloat16)
    igate_term = heads_grad(rounded, input_pre_grad, head_count)
    dgate_term = heads_grad(rounded, decay_pre_grad, head_count)
    head_keep = resets_seen[: tap_count - 1] == 0
    head_rows = conv_grad[: tap_count - 1] * head_keep[:, None]
    following = shifted_2(head_rows, "seq", -1)
    padded_back = jnp.concatenate([conv_grad, following], axis=0)
    seen_after = jnp.concatenate(
        [resets_seen, jnp.full((tap_count - 1,), resets_seen[-1], jnp.int32)]
    )
    conv_grad_float = conv_grad.astype(jnp.float32)
    conv_in_grad = jnp.zeros((tokens, model_width), jnp.float32)
    tap_terms = []
    for offset in range(tap_count):
        first_row = tap_count - 1 - offset
        shifted = padded[first_row : first_row + tokens].astype(jnp.float32)
        tap_terms.append(jnp.sum(conv_grad_float * shifted * usable_list[offset], axis=0))
        ahead_usable = (seen_after[offset : offset + tokens] - resets_seen == 0).astype(
            jnp.float32
        )[:, None]
        conv_in_grad = (
            conv_in_grad
            + w_conv[:, offset]
            * padded_back[offset : offset + tokens].astype(jnp.float32)
            * ahead_usable
        )
    tap_grad = jnp.stack(tap_terms, axis=1)
    conv_in_low = conv_in_grad.astype(jnp.bfloat16)
    normed_grad = last_product(branch_pre_grad, w_branch) + last_product(conv_in_low, w_input)
    weighted_one = normed_grad * gain_first
    source_grad = (
        resid_grad
        + scale_one * weighted_one
        - sources * scale_one**3 * jnp.mean(weighted_one * sources, axis=1, keepdims=True)
    )
    first_term = jnp.sum(normed_grad * sources * scale_one, axis=0)
    grad_inputs = source_grad.astype(jnp.bfloat16)[None]
    vector_part = jnp.concatenate(
        [
            igate_term,
            dgate_term,
            tap_grad,
            decay_term[:, None],
            first_term[:, None],
            second_term[:, None],
        ],
        axis=1,
    )
    owned_rows = gate_weight.shape[0]
    owner_count = lax.axis_size(("seq", "fsdp"))
    slab_total = slab_count()
    slab_rows = owned_rows // slab_total
    vector_shaped = vector_part.reshape(owner_count, owned_rows, vector_part.shape[1])

    def pick_rows(values, portion):
        shaped = values.reshape(values.shape[0], owner_count, owned_rows)
        taken = shaped[:, :, portion * slab_rows : (portion + 1) * slab_rows]
        return taken.reshape(values.shape[0], owner_count * slab_rows)

    gate_pieces = []
    up_pieces = []
    down_pieces = []
    branch_pieces = []
    input_pieces = []
    output_pieces = []
    vector_pieces = []
    for portion in range(slab_total):
        hidden_rows = pick_rows(hidden, portion)
        return_rows = pick_rows(returned, portion)
        dense_sums = (
            lax.psum_scatter(
                rows_product(hidden_rows, gate_grad),
                ("seq", "fsdp"),
                scatter_dimension=0,
                tiled=True,
            ),
            lax.psum_scatter(
                rows_product(hidden_rows, up_grad), ("seq", "fsdp"), scatter_dimension=0, tiled=True
            ),
            lax.psum_scatter(
                rows_product(return_rows, active), ("seq", "fsdp"), scatter_dimension=0, tiled=True
            ),
        )
        gate_pieces.append(dense_sums[0])
        up_pieces.append(dense_sums[1])
        down_pieces.append(dense_sums[2])
        normed_rows = pick_rows(normed, portion)
        mixed_rows = pick_rows(mixed, portion)
        vector_rows = vector_shaped[:, portion * slab_rows : (portion + 1) * slab_rows].reshape(
            owner_count * slab_rows, vector_part.shape[1]
        )
        mixer_sums = (
            lax.psum_scatter(
                rows_product(normed_rows, branch_pre_grad),
                ("seq", "fsdp"),
                scatter_dimension=0,
                tiled=True,
            ),
            lax.psum_scatter(
                rows_product(normed_rows, conv_in_low),
                ("seq", "fsdp"),
                scatter_dimension=0,
                tiled=True,
            ),
            lax.psum_scatter(
                rows_product(mixed_rows, branch_out_grad),
                ("seq", "fsdp"),
                scatter_dimension=0,
                tiled=True,
            ),
            lax.psum_scatter(vector_rows, ("seq", "fsdp"), scatter_dimension=0, tiled=True),
        )
        branch_pieces.append(mixer_sums[0])
        input_pieces.append(mixer_sums[1])
        output_pieces.append(mixer_sums[2])
        vector_pieces.append(mixer_sums[3])
    grad_gate = jnp.concatenate(gate_pieces, axis=0)
    grad_up = jnp.concatenate(up_pieces, axis=0)
    grad_down = jnp.concatenate(down_pieces, axis=0)
    grad_branch = jnp.concatenate(branch_pieces, axis=0)
    grad_input = jnp.concatenate(input_pieces, axis=0)
    grad_output = jnp.concatenate(output_pieces, axis=0)
    vector_sums = jnp.concatenate(vector_pieces, axis=0)
    edge_five = 2 * head_width
    edge_six = edge_five + tap_count
    grad_igate = vector_sums[:, :head_width]
    grad_dgate = vector_sums[:, head_width:edge_five]
    grad_conv = vector_sums[:, edge_five:edge_six]
    grad_decay = vector_sums[:, edge_six]
    grad_gain_first = vector_sums[:, edge_six + 1]
    grad_gain_second = vector_sums[:, edge_six + 2]
    return (
        result[None],
        grad_inputs,
        grad_gain_first,
        grad_branch,
        grad_input,
        grad_conv,
        grad_igate,
        grad_dgate,
        grad_decay,
        grad_output,
        grad_gain_second,
        grad_gate,
        grad_up,
        grad_down,
    )


CHUNK = 128
TAPS = 4


def gelu_parts(x):
    inner = 0.7978845608028654 * (x + 0.044715 * x * x * x)
    bent = jnp.tanh(inner)
    value = 0.5 * x * (1.0 + bent)
    slope = 0.5 * (1.0 + bent) + 0.5 * x * (1.0 - bent * bent) * 0.7978845608028654 * (
        1.0 + 3.0 * 0.044715 * x * x
    )
    return value, slope


def minus_expm1(x):
    series = x / 8.0 + 1.0
    for step in (7.0, 6.0, 5.0, 4.0, 3.0, 2.0):
        series = series * x / step + 1.0
    return jnp.where(x > -0.5, -x * series, 1.0 - jnp.exp(x))


def mixer_forward_kernel(
    conv_in_ref, pre_ref, mask_ref, taps_ref, igate_ref, dgate_ref, soft_ref,
    rounded_ref, gin_ref, gdec_ref, states_ref, earlier_ref, mixed_ref,
    padded, coef, drive,
):
    tokens, width = conv_in_ref.shape
    chunk = min(CHUNK, tokens)
    padded[0:8, :] = jnp.zeros((8, width), jnp.float32)
    soft = soft_ref[0:1, :]
    igate = igate_ref[...]
    dgate = dgate_ref[...]

    def fill(c, _):
        base = pl.multiple_of(c * chunk, chunk)
        padded[pl.ds(pl.multiple_of(base + 8, 8), chunk), :] = conv_in_ref[pl.ds(base, chunk), :].astype(jnp.float32)
        return 0

    lax.fori_loop(0, tokens // chunk, fill, 0)
    row = lax.broadcasted_iota(jnp.int32, (8, width), 0)

    def body(c, carry):
        base = pl.multiple_of(c * chunk, chunk)
        mask = mask_ref[pl.ds(base, chunk), :]
        span = padded[pl.ds(base, chunk + 8), :]
        out = taps_ref[0:1, :] * span[8:]
        for k in range(1, TAPS):
            out = out + taps_ref[k : k + 1, :] * span[8 - k : 8 - k + chunk] * mask[:, k : k + 1]
        rounded = out.astype(jnp.bfloat16)
        rounded_ref[pl.ds(base, chunk), :] = rounded
        gin = jax.nn.sigmoid(jnp.dot(rounded, igate, preferred_element_type=jnp.float32))
        gdec = jax.nn.sigmoid(jnp.dot(rounded, dgate, preferred_element_type=jnp.float32))
        gin_ref[pl.ds(base, chunk), :] = gin
        gdec_ref[pl.ds(base, chunk), :] = gdec
        log_decay = -soft * (1.0 + 7.0 * gdec)
        root = jnp.sqrt(minus_expm1(2.0 * log_decay))
        restart = mask[:, 0:1]
        carried = 1.0 - restart
        coef[...] = jnp.exp(log_decay) * carried
        drive[...] = rounded.astype(jnp.float32) * gin * (restart + carried * root)

        def tile(i, state):
            at = pl.multiple_of(i * 8, 8)
            a = coef[pl.ds(at, 8), :]
            b = drive[pl.ds(at, 8), :]
            for sh in (1, 2, 4):
                keep = row >= sh
                b = b + a * jnp.where(keep, pltpu.roll(b, sh, 0), 0.0)
                a = a * jnp.where(keep, pltpu.roll(a, sh, 0), 1.0)
            new = b + a * state
            states_ref[pl.ds(pl.multiple_of(base + at, 8), 8), :] = new
            earlier_ref[pl.ds(pl.multiple_of(base + at, 8), 8), :] = jnp.where(row == 0, state, pltpu.roll(new, 1, 0))
            return jnp.broadcast_to(new[7:8, :], (8, width))

        carry = lax.fori_loop(0, chunk // 8, tile, carry, unroll=True)
        branch, _ = gelu_parts(pre_ref[pl.ds(base, chunk), :])
        mixed_ref[pl.ds(base, chunk), :] = (states_ref[pl.ds(base, chunk), :] * branch).astype(jnp.bfloat16)
        return carry

    lax.fori_loop(0, tokens // chunk, body, jnp.zeros((8, width), jnp.float32))


def mixer_forward(conv_in, pre, mask, taps, igate, dgate, soft, width):
    tokens, total = conv_in.shape
    heads = total // width
    column = lambda h: (0, h)
    row = lambda h: (h, 0)
    whole = lambda h: (0, 0)
    big = pl.BlockSpec((tokens, width), column)
    shape = lambda kind: jax.ShapeDtypeStruct((tokens, total), kind)
    return pl.pallas_call(
        mixer_forward_kernel,
        grid=(heads,),
        in_specs=[
            big, big, pl.BlockSpec(mask.shape, whole), pl.BlockSpec((8, width), column),
            pl.BlockSpec((width, width), row), pl.BlockSpec((width, width), row),
            pl.BlockSpec((8, width), column),
        ],
        out_specs=[big] * 6,
        out_shape=[shape(jnp.bfloat16), shape(jnp.float32), shape(jnp.float32), shape(jnp.float32), shape(jnp.float32), shape(jnp.bfloat16)],
        scratch_shapes=[
            pltpu.VMEM((tokens + 8, width), jnp.float32),
            pltpu.VMEM((min(CHUNK, tokens), width), jnp.float32),
            pltpu.VMEM((min(CHUNK, tokens), width), jnp.float32),
        ],
        compiler_params=pltpu.CompilerParams(vmem_limit_bytes=48 * 2**20),
        name="mixer_forward",
    )(conv_in, pre, mask, taps, igate, dgate, soft)


def mixer_backward_kernel(
    grad_ref, pre_ref, states_ref, earlier_ref, rounded_ref, gin_ref, gdec_ref, conv_in_ref, mask_ref, ahead_ref,
    taps_ref, igate_ref, dgate_ref, soft_ref, own_ref,
    bpg_ref, cig_ref, igrad_ref, dgrad_ref, tapgrad_ref,
    padded, ahead_pad, coef, drive, decay_sum, tap_sum,
):
    tokens, width = grad_ref.shape
    chunk = min(CHUNK, tokens)
    count = tokens // chunk
    padded[0:8, :] = jnp.zeros((8, width), jnp.float32)
    ahead_pad[tokens : tokens + 8, :] = jnp.zeros((8, width), jnp.float32)
    soft = soft_ref[0:1, :]
    own = own_ref[0:1, :]
    igate = igate_ref[...]
    dgate = dgate_ref[...]
    igrad_ref[...] = jnp.zeros_like(igrad_ref)
    dgrad_ref[...] = jnp.zeros_like(dgrad_ref)
    decay_sum[...] = jnp.zeros_like(decay_sum)
    tap_sum[...] = jnp.zeros_like(tap_sum)
    row = lax.broadcasted_iota(jnp.int32, (8, width), 0)
    rows_dot = lambda a, b: lax.dot_general(a, b, (((0,), (0,)), ((), ())), preferred_element_type=jnp.float32)
    last_dot = lambda a, b: lax.dot_general(a, b, (((1,), (1,)), ((), ())), preferred_element_type=jnp.float32)

    def body(step, carry):
        c = count - 1 - step
        base = pl.multiple_of(c * chunk, chunk)
        here = pl.ds(base, chunk)
        padded[pl.ds(pl.multiple_of(base + 8, 8), chunk), :] = conv_in_ref[here, :].astype(jnp.float32)
        mask = mask_ref[here, :]
        restart = mask[:, 0:1]
        carried = 1.0 - restart
        branch, slope = gelu_parts(pre_ref[here, :])
        grad = grad_ref[here, :]
        bpg_ref[here, :] = (grad * states_ref[here, :] * slope * own).astype(jnp.bfloat16)
        gdec = gdec_ref[here, :]
        gin = gin_ref[here, :]
        log_decay = -soft * (1.0 + 7.0 * gdec)
        decays = jnp.exp(log_decay)
        root = jnp.sqrt(minus_expm1(2.0 * log_decay))
        coef[...] = decays * carried
        drive[...] = grad * branch

        def tile(i, pair):
            adj_next, coef_next = pair
            at = pl.multiple_of(chunk - 8 - i * 8, 8)
            first = coef[pl.ds(at, 8), :]
            a = jnp.where(row == 7, coef_next, pltpu.roll(first, 7, 0))
            b = drive[pl.ds(at, 8), :]
            for sh in (1, 2, 4):
                keep = row < 8 - sh
                b = b + a * jnp.where(keep, pltpu.roll(b, 8 - sh, 0), 0.0)
                a = a * jnp.where(keep, pltpu.roll(a, 8 - sh, 0), 1.0)
            new = b + a * adj_next
            drive[pl.ds(at, 8), :] = new
            return jnp.broadcast_to(new[0:1, :], (8, width)), jnp.broadcast_to(first[0:1, :], (8, width))

        carry = lax.fori_loop(0, chunk // 8, tile, carry, unroll=True)
        adjoint = drive[...]
        rounded = rounded_ref[here, :]
        rounded_float = rounded.astype(jnp.float32)
        pull = adjoint * carried * decays
        log_grad = pull * (earlier_ref[here, :] - rounded_float * gin * decays / root)
        decay_sum[...] += jnp.sum((-log_grad * (1.0 + 7.0 * gdec)).reshape(chunk // 8, 8, width), axis=0)
        through = adjoint * gin * (restart + carried * root)
        ipg = (through * rounded_float * (1.0 - gin)).astype(jnp.bfloat16)
        dpg = (log_grad * (-7.0 * soft) * gdec * (1.0 - gdec)).astype(jnp.bfloat16)
        igrad_ref[...] += rows_dot(rounded, ipg)
        dgrad_ref[...] += rows_dot(rounded, dpg)
        through = through + last_dot(ipg, igate) + last_dot(dpg, dgate)
        ahead_pad[here, :] = through.astype(jnp.bfloat16).astype(jnp.float32)
        return carry

    zero = jnp.zeros((8, width), jnp.float32)
    lax.fori_loop(0, count, body, (zero, zero))

    def after(c, _):
        base = pl.multiple_of(c * chunk, chunk)
        here = pl.ds(base, chunk)
        mask = mask_ref[here, :]
        ahead = ahead_ref[here, :]
        later = ahead_pad[pl.ds(base, chunk + 8), :]
        span = padded[pl.ds(base, chunk + 8), :]
        grad = later[:chunk]
        total = taps_ref[0:1, :] * grad
        tap_sum[0:8, :] += jnp.sum((grad * span[8:]).reshape(chunk // 8, 8, width), axis=0)
        for k in range(1, TAPS):
            total = total + taps_ref[k : k + 1, :] * later[k : k + chunk] * ahead[:, k : k + 1]
            shifted = span[8 - k : 8 - k + chunk]
            tap_sum[8 * k : 8 * k + 8, :] += jnp.sum((grad * shifted * mask[:, k : k + 1]).reshape(chunk // 8, 8, width), axis=0)
        cig_ref[here, :] = (total * own).astype(jnp.bfloat16)
        return 0

    lax.fori_loop(0, count, after, 0)
    for k in range(TAPS):
        tapgrad_ref[k : k + 1, :] = jnp.sum(tap_sum[8 * k : 8 * k + 8, :], axis=0, keepdims=True)
    tapgrad_ref[4:5, :] = jnp.sum(decay_sum[...], axis=0, keepdims=True)
    tapgrad_ref[5:8, :] = jnp.zeros((3, width), jnp.float32)


def mixer_backward(grad, pre, states, earlier, rounded, gin, gdec, conv_in, mask, ahead, taps, igate, dgate, soft, own, width):
    tokens, total = grad.shape
    heads = total // width
    column = lambda h: (0, h)
    row = lambda h: (h, 0)
    whole = lambda h: (0, 0)
    big = pl.BlockSpec((tokens, width), column)
    line = pl.BlockSpec((8, width), column)
    square = pl.BlockSpec((width, width), row)
    shape = lambda kind: jax.ShapeDtypeStruct((tokens, total), kind)
    chunk = min(CHUNK, tokens)
    return pl.pallas_call(
        mixer_backward_kernel,
        grid=(heads,),
        in_specs=[big] * 8 + [pl.BlockSpec(mask.shape, whole)] * 2 + [line, square, square, line, line],
        out_specs=[big, big, square, square, line],
        out_shape=[
            shape(jnp.bfloat16), shape(jnp.bfloat16),
            jax.ShapeDtypeStruct((total, width), jnp.float32), jax.ShapeDtypeStruct((total, width), jnp.float32),
            jax.ShapeDtypeStruct((8, total), jnp.float32),
        ],
        scratch_shapes=[
            pltpu.VMEM((tokens + 8, width), jnp.float32),
            pltpu.VMEM((tokens + 8, width), jnp.float32),
            pltpu.VMEM((chunk, width), jnp.float32),
            pltpu.VMEM((chunk, width), jnp.float32),
            pltpu.VMEM((8, width), jnp.float32),
            pltpu.VMEM((8 * TAPS, width), jnp.float32),
        ],
        compiler_params=pltpu.CompilerParams(vmem_limit_bytes=56 * 2**20),
        name="mixer_backward",
    )(grad, pre, states, earlier, rounded, gin, gdec, conv_in, mask, ahead, taps, igate, dgate, soft, own)


MESH_ID = pl.DeviceIdType.MESH
PIECES = 4


class Spot:
    def __init__(self):
        self.s = lax.axis_index("seq")
        self.f = lax.axis_index("fsdp")
        self.z = self.s // 2
        self.y = self.s % 2
        self.up = (self.z < 3, (jnp.minimum(self.s + 2, 7), self.f))
        self.down = (self.z > 0, (jnp.maximum(self.s - 2, 0), self.f))
        self.beside = (None, (self.s ^ 1, self.f))
        self.across = (None, (self.s, self.f ^ 2))
        self.twin = (None, (self.s, self.f ^ 1))

    def peer(self, j):
        return (None, (self.s ^ j, self.f))

    def other(self, j):
        return (None, (self.s ^ (j // 4), self.f ^ (j % 4)))

    def meet(self, reach):
        barrier = pltpu.get_barrier_semaphore()
        if "all" in reach:
            peers = [self.other(j) for j in range(1, 32)]
        else:
            peers = [self.peer(j) for j in range(1, 8)] if "seq" in reach else []
            if "line" in reach and not peers:
                peers = [self.up, self.down, self.beside]
            if "pair" in reach:
                peers += [self.across, self.twin]
        count = 0
        for cond, where in peers:
            count = count + (1 if cond is None else cond.astype(jnp.int32))
            guarded(cond, lambda: pl.semaphore_signal(barrier, 1, device_id=where, device_id_type=MESH_ID))
        pl.semaphore_wait(barrier, count)


def guarded(cond, action):
    if cond is None:
        action()
    else:
        pl.when(cond)(action)


class Send:
    def __init__(self, src, dst, send_sem, recv_sem, target):
        self.cond, where = target
        self.copy = pltpu.make_async_remote_copy(
            src_ref=src, dst_ref=dst, send_sem=send_sem, recv_sem=recv_sem, device_id=where, device_id_type=MESH_ID
        )

    def start(self):
        guarded(self.cond, self.copy.start)

    def sent(self):
        guarded(self.cond, self.copy.wait_send)


def arrived(dst, send_sem, recv_sem, target, cond=None):
    copy = pltpu.make_async_remote_copy(
        src_ref=dst, dst_ref=dst, send_sem=send_sem, recv_sem=recv_sem, device_id=target[1], device_id_type=MESH_ID
    )
    guarded(cond, copy.wait_recv)


class Gather:
    def __init__(self, x):
        self.ins = [x]
        self.outs = [jax.ShapeDtypeStruct((8,) + x.shape, x.dtype)]
        dma = pltpu.SemaphoreType.DMA
        self.scratch = [dma((1,)), dma((8, PIECES)), dma((4, PIECES)), dma((4, PIECES)), dma((7, PIECES))]

    reach = ("line",)

    def steps(self, at, ins, outs, scratch):
        (x,), (o,) = ins, outs
        own_sem, recv, ups, downs, sides = scratch
        rows = x.shape[0] // PIECES
        cut = lambda p: pl.ds(p * rows, rows)
        sends = []

        def send(src, block, p, sem, target):
            one = Send(src, o.at[block, cut(p)], sem, recv.at[block, p], target)
            one.start()
            sends.append(one)

        own = pltpu.make_async_copy(x, o.at[at.s], own_sem.at[0])
        own.start()
        for p in range(PIECES):
            send(x.at[cut(p)], at.s, p, ups.at[0, p], at.up)
            send(x.at[cut(p)], at.s, p, downs.at[0, p], at.down)
            send(x.at[cut(p)], at.s, p, sides.at[0, p], at.beside)
        yield
        for d in range(1, 4):
            for p in range(PIECES):
                low, high = at.z >= d, at.z + d <= 3
                block = jnp.maximum(at.s - 2 * d, 0)
                arrived(o.at[block, cut(p)], ups.at[0, p], recv.at[block, p], at.down, low)
                if d < 3:
                    send(o.at[block, cut(p)], block, p, ups.at[d, p], (low & (at.z < 3), at.up[1]))
                send(o.at[block, cut(p)], block, p, sides.at[d, p], (low, at.beside[1]))
                block = jnp.minimum(at.s + 2 * d, 7)
                arrived(o.at[block, cut(p)], ups.at[0, p], recv.at[block, p], at.up, high)
                if d < 3:
                    send(o.at[block, cut(p)], block, p, downs.at[d, p], (high & (at.z > 0), at.down[1]))
                send(o.at[block, cut(p)], block, p, sides.at[3 + d, p], (high, at.beside[1]))
                yield
        for z in range(4):
            for p in range(PIECES):
                block = 2 * z + 1 - at.y
                arrived(o.at[block, cut(p)], ups.at[0, p], recv.at[block, p], at.beside)
        yield
        for one in sends:
            one.sent()
        own.wait()


class Reduce:
    def __init__(self, x):
        _, rows, width = x.shape
        self.ins = [x]
        self.outs = [jax.ShapeDtypeStruct((rows, width), jnp.float32)]
        dma = pltpu.SemaphoreType.DMA
        hold = pltpu.VMEM((4, rows, width), x.dtype)
        self.scratch = [hold, hold, hold, hold, pltpu.VMEM((rows, width), jnp.float32)]
        self.scratch += [dma((4, PIECES)) for _ in range(6)] + [dma((1,))]

    reach = ("line",)

    def steps(self, at, ins, outs, scratch):
        (x,), (o,) = ins, outs
        mine, side, below, above, total, load, ysend, yrecv, zsend, urecv, drecv, osem = scratch
        rows = x.shape[1] // PIECES
        cut = lambda p: pl.ds(p * rows, rows)
        group = 16
        sends = []
        order = []
        for k in range(3):
            order.append((3 - k, at.z < 3 - k, True))
            order.append((k, at.z > k, False))
        order.append((at.z, None, None))

        loads = []
        for t, cond, _ in order:
            for p in range(PIECES):
                one = Send(x.at[2 * t + 1 - at.y, cut(p)], side.at[t, cut(p)], ysend.at[t, p], yrecv.at[t, p], (cond, at.beside[1]))
                one.start()
                sends.append(one)
                copy = pltpu.make_async_copy(x.at[2 * t + at.y, cut(p)], mine.at[t, cut(p)], load.at[t, p])
                guarded(cond, copy.start)
        yield
        for t, cond, rising in order:
            for p in range(PIECES):
                copy = pltpu.make_async_copy(x.at[2 * t + at.y, cut(p)], mine.at[t, cut(p)], load.at[t, p])
                guarded(cond, copy.wait)
                arrived(side.at[t, cut(p)], ysend.at[t, p], yrecv.at[t, p], at.beside, cond)
                if rising is None:
                    arrived(below.at[t, cut(p)], zsend.at[t, p], urecv.at[t, p], at.down, at.z > 0)
                    arrived(above.at[t, cut(p)], zsend.at[t, p], drecv.at[t, p], at.up, at.z < 3)

                    def final(i, _):
                        here = pl.ds(pl.multiple_of(p * rows + i * group, group), group)
                        value = mine[t, here, :].astype(jnp.float32) + side[t, here, :].astype(jnp.float32)
                        total[here, :] = value

                        @pl.when(at.z > 0)
                        def _():
                            total[here, :] += below[t, here, :].astype(jnp.float32)

                        @pl.when(at.z < 3)
                        def _():
                            total[here, :] += above[t, here, :].astype(jnp.float32)

                        return 0

                    lax.fori_loop(0, rows // group, final, 0)
                else:
                    source = below if rising else above
                    inner = (cond & (at.z > 0)) if rising else (cond & (at.z < 3))
                    outer = (cond & (at.z == 0)) if rising else (cond & (at.z == 3))
                    rsem = urecv if rising else drecv
                    arrived(source.at[t, cut(p)], zsend.at[t, p], rsem.at[t, p], at.down if rising else at.up, inner)

                    def add(with_source):
                        def one(i, _):
                            here = pl.ds(pl.multiple_of(p * rows + i * group, group), group)
                            value = mine[t, here, :].astype(jnp.float32) + side[t, here, :].astype(jnp.float32)
                            if with_source:
                                value = value + source[t, here, :].astype(jnp.float32)
                            mine[t, here, :] = value.astype(mine.dtype)
                            return 0

                        lax.fori_loop(0, rows // group, one, 0)

                    pl.when(inner)(lambda: add(True))
                    pl.when(outer)(lambda: add(False))
                    one = Send(mine.at[t, cut(p)], source.at[t, cut(p)], zsend.at[t, p], rsem.at[t, p], (cond, (at.up if rising else at.down)[1]))
                    one.start()
                    sends.append(one)
                yield
        out = pltpu.make_async_copy(total, o, osem.at[0])
        out.start()
        for one in sends:
            one.sent()
        out.wait()


class Spread:
    def __init__(self, x):
        self.ins = [x]
        self.outs = [jax.ShapeDtypeStruct((8, 4) + x.shape[1:], x.dtype)]
        dma = pltpu.SemaphoreType.DMA
        self.scratch = [dma((8,)), dma((8,)), dma((8,)), dma((8,)), dma((8, 2)), dma((8, 2))]

    reach = ("seq", "pair")

    def steps(self, at, ins, outs, scratch):
        (x,), (o,) = ins, outs
        asend, arecv, xsend, xrecv, csend, crecv = scratch
        sends = []

        def send(src, dst, ss, rs, target):
            one = Send(src, dst, ss, rs, target)
            one.start()
            sends.append(one)

        for j in range(1, 8):
            send(x.at[at.s ^ j], o.at[at.s, at.f], asend.at[j], arecv.at[j], at.peer(j))
        own = pltpu.make_async_copy(x.at[at.s], o.at[at.s, at.f], asend.at[0])
        own.start()
        yield
        for j in range(8):
            block = at.s ^ j
            here = o.at[block, at.f]
            if j == 0:
                own.wait()
            else:
                arrived(here, asend.at[j], arecv.at[j], at.peer(j))
            send(here, here, xsend.at[j], xrecv.at[j], at.across)
            send(here, here, csend.at[j, 0], crecv.at[j, 0], at.twin)
            yield
        for j in range(8):
            there = o.at[at.s ^ j, at.f ^ 2]
            arrived(there, xsend.at[j], xrecv.at[j], at.across)
            send(there, there, csend.at[j, 1], crecv.at[j, 1], at.twin)
            yield
        for j in range(8):
            for k in range(2):
                arrived(o.at[at.s ^ j, (at.f ^ 1) ^ (2 * k)], csend.at[j, k], crecv.at[j, k], at.twin)
        for one in sends:
            one.sent()


def add_rows(dst, terms, rows):
    group = 16

    def one(i, _):
        here = pl.ds(pl.multiple_of(i * group, group), group)
        value = terms[0][here, :].astype(jnp.float32)
        for term in terms[1:]:
            value = value + term[here, :].astype(jnp.float32)
        dst[here, :] = value.astype(dst.dtype)
        return 0

    lax.fori_loop(0, rows // group, one, 0)


class Collect:
    def __init__(self, x):
        blocks, _, rows, width = x.shape
        self.ins = [x]
        self.blocks = blocks
        self.reach = ("seq", "pair") if blocks > 1 else ("pair",)
        self.outs = [jax.ShapeDtypeStruct((blocks, rows, width), x.dtype)]
        dma = pltpu.SemaphoreType.DMA
        hold = pltpu.VMEM((blocks, rows, width), x.dtype)
        self.scratch = [hold] * 5 + [dma((blocks, 2))] * 3 + [dma((blocks,))] * 4


    def steps(self, at, ins, outs, scratch):
        (x,), (o,) = ins, outs
        near, far, tnear, tfar, xin, lsem, csend, crecv, xsend, xrecv, asend, arecv = scratch
        rows = x.shape[2]
        many = self.blocks > 1
        spot = (lambda j: at.s ^ j) if many else (lambda j: j)
        sends = []

        def send(src, dst, ss, rs, target):
            one = Send(src, dst, ss, rs, target)
            one.start()
            sends.append(one)

        order = [j for j in range(1, 8)] + [0] if many else [0]
        loads = {}
        for j in order:
            send(x.at[spot(j), at.f ^ 3], tfar.at[j], csend.at[j, 0], crecv.at[j, 0], at.twin)
            send(x.at[spot(j), at.f ^ 1], tnear.at[j], csend.at[j, 1], crecv.at[j, 1], at.twin)
            for k, (buffer, whose) in enumerate(((far, at.f ^ 2), (near, at.f))):
                loads[j, k] = pltpu.make_async_copy(x.at[spot(j), whose], buffer.at[j], lsem.at[j, k])
                loads[j, k].start()
        yield
        for j in order:
            loads[j, 0].wait()
            arrived(tfar.at[j], csend.at[j, 0], crecv.at[j, 0], at.twin)
            add_rows(far.at[j], (far.at[j], tfar.at[j]), rows)
            send(far.at[j], xin.at[j], xsend.at[j], xrecv.at[j], at.across)
            yield
        outs_done = []
        for j in order:
            loads[j, 1].wait()
            arrived(tnear.at[j], csend.at[j, 1], crecv.at[j, 1], at.twin)
            arrived(xin.at[j], xsend.at[j], xrecv.at[j], at.across)
            add_rows(near.at[j], (near.at[j], tnear.at[j], xin.at[j]), rows)
            if j:
                send(near.at[j], o.at[at.s], asend.at[j], arecv.at[j], at.peer(j))
            else:
                outs_done.append(pltpu.make_async_copy(near.at[0], o.at[at.s if many else 0], asend.at[0]))
                outs_done[-1].start()
            yield
        for j in order:
            if j:
                arrived(o.at[at.s ^ j], asend.at[j], arecv.at[j], at.peer(j))
        for one in sends:
            one.sent()
        for one in outs_done:
            one.wait()


class Tiny:
    def __init__(self, x):
        self.ins = [x]
        self.outs = [jax.ShapeDtypeStruct(x.shape, x.dtype)]
        dma = pltpu.SemaphoreType.DMA
        self.scratch = [dma((32,)), dma((32,))]

    reach = ("all",)

    def steps(self, at, ins, outs, scratch):
        (x,), (o,) = ins, outs
        ss, rs = scratch
        me = at.s * 4 + at.f
        sends = []
        for j in range(1, 32):
            one = Send(x.at[me ^ j], o.at[me], ss.at[j], rs.at[j], at.other(j))
            one.start()
            sends.append(one)
        own = pltpu.make_async_copy(x.at[me], o.at[me], ss.at[0])
        own.start()
        yield
        yield
        for j in range(1, 32):
            arrived(o.at[me ^ j], ss.at[j], rs.at[j], at.other(j))
        for one in sends:
            one.sent()
        own.wait()


def exchange(jobs, collective, name):
    def kernel(*refs):
        at = Spot()
        refs = list(refs)
        take = lambda count: [refs.pop(0) for _ in range(count)]
        ins = [take(len(job.ins)) for job in jobs]
        outs = [take(len(job.outs)) for job in jobs]
        scratch = [take(len(job.scratch)) for job in jobs]
        at.meet({one for job in jobs for one in job.reach})
        running = [job.steps(at, i, o, s) for job, i, o, s in zip(jobs, ins, outs, scratch)]
        while running:
            running = [one for one in running if next(one, running) is not running]

    count = sum(len(job.ins) for job in jobs)
    return pl.pallas_call(
        kernel,
        out_shape=[shape for job in jobs for shape in job.outs],
        in_specs=[pl.BlockSpec(memory_space=pl.ANY)] * count,
        out_specs=[pl.BlockSpec(memory_space=pl.ANY)] * sum(len(job.outs) for job in jobs),
        scratch_shapes=[shape for job in jobs for shape in job.scratch],
        compiler_params=pltpu.CompilerParams(
            collective_id=collective, has_side_effects=True, vmem_limit_bytes=58 * 2**20
        ),
        name=name,
    )(*[x for job in jobs for x in job.ins])


class Rows:
    def __init__(self, x, near):
        self.slots = 3 if near else 1
        self.reach = ("seq", "pair") if near else ("pair",)
        self.ins = [x]
        self.outs = [jax.ShapeDtypeStruct((self.slots, 4) + x.shape, x.dtype)]
        dma = pltpu.SemaphoreType.DMA
        self.scratch = [dma((3,))] * 4 + [dma((3, 2))] * 2

    def places(self, at):
        after = (None, (lax.rem(at.s + 1, 8), at.f))
        before = (None, (lax.rem(at.s + 7, 8), at.f))
        return after, before

    def steps(self, at, ins, outs, scratch):
        (x,), (o,) = ins, outs
        asend, arecv, xsend, xrecv, csend, crecv = scratch
        after, before = self.places(at)
        sends = []

        def send(src, dst, ss, rs, target):
            one = Send(src, dst, ss, rs, target)
            one.start()
            sends.append(one)

        middle = self.slots // 2
        if self.slots == 3:
            send(x, o.at[0, at.f], asend.at[0], arecv.at[0], after)
            send(x, o.at[2, at.f], asend.at[2], arecv.at[2], before)
        own = pltpu.make_async_copy(x, o.at[middle, at.f], asend.at[1])
        own.start()
        send(x, o.at[middle, at.f], xsend.at[middle], xrecv.at[middle], at.across)
        send(x, o.at[middle, at.f], csend.at[middle, 0], crecv.at[middle, 0], at.twin)
        yield
        for j in range(self.slots):
            if j != middle:
                here = o.at[j, at.f]
                arrived(here, asend.at[j], arecv.at[j], before if j == 0 else after)
                send(here, here, xsend.at[j], xrecv.at[j], at.across)
                send(here, here, csend.at[j, 0], crecv.at[j, 0], at.twin)
        yield
        for j in range(self.slots):
            there = o.at[j, at.f ^ 2]
            arrived(there, xsend.at[j], xrecv.at[j], at.across)
            send(there, there, csend.at[j, 1], crecv.at[j, 1], at.twin)
            yield
        for j in range(self.slots):
            for k in range(2):
                arrived(o.at[j, (at.f ^ 1) ^ (2 * k)], csend.at[j, k], crecv.at[j, k], at.twin)
        for one in sends:
            one.sent()
        own.wait()


def fast(
    inputs,
    resets,
    cotangent,
    first_gain,
    branch_weight,
    input_weight,
    conv_weight,
    input_gate,
    decay_gate,
    decay_param,
    output_weight,
    second_gain,
    gate_weight,
    up_weight,
    down_weight,
):
    low = jnp.bfloat16
    peers, groups = 8, 4
    s, f = lax.axis_index("seq"), lax.axis_index("fsdp")
    sources_low = inputs[0]
    sources = sources_low.astype(jnp.float32)
    returned = cotangent[0]
    tokens, width = sources.shape
    rows = branch_weight.shape[0]
    head = input_gate.shape[1]
    own = width // peers
    hidden_own = gate_weight.shape[1] // peers
    all_tokens = peers * tokens
    firsts = [min(own * at // head, width // head - 2) for at in range(peers)]
    window = 2 * head
    offset = own * s - head * jnp.minimum(own * s // head, width // head - 2)
    owned = ((jnp.arange(window) >= offset) & (jnp.arange(window) < offset + own)).astype(jnp.float32)

    small = jnp.zeros((8, 128), jnp.float32)
    small = small.at[0, :rows].set(first_gain.astype(jnp.float32))
    small = small.at[1, :rows].set(second_gain.astype(jnp.float32))
    small = small.at[2, :tokens].set(resets[0].astype(jnp.float32))
    small = jnp.broadcast_to(small[None], (peers * groups, 8, 128))
    mixer_cut = jnp.stack(
        [
            jnp.concatenate(
                [branch_weight[:, head * at : head * at + window], input_weight[:, head * at : head * at + window]], axis=1
            )
            for at in firsts
        ]
    )
    pad = jnp.zeros((rows, 128 - 5), low)
    row_pack = jnp.concatenate([input_gate, decay_gate, conv_weight, decay_param[:, None], pad], axis=1)
    cut = lambda w: w.reshape(rows, peers, hidden_own).transpose(1, 0, 2)
    x_full, mixer_w, row_w, out_w, vectors = exchange(
        [Gather(sources_low), Spread(mixer_cut), Rows(row_pack, True), Rows(output_weight, False), Tiny(small)], 1, "first_exchange"
    )
    gate_cut, up_cut, down_cut = cut(gate_weight), cut(up_weight), cut(down_weight)
    (returned_full, w_gate, w_up, w_down) = exchange(
        [Gather(returned), Spread(gate_cut), Spread(up_cut), Spread(down_cut)], 2, "dense_exchange"
    )
    whole = lambda w: w.reshape(width, w.shape[-1])
    w_gate, w_up, w_down = whole(w_gate), whole(w_up), whole(w_down)
    returned_full = returned_full.reshape(all_tokens, width)
    x_full = x_full.reshape(all_tokens, width).astype(jnp.float32)
    mixer_w = mixer_w.reshape(width, 2 * window)
    w_output = out_w.reshape(own, width)
    before = jnp.concatenate(
        [
            lax.ppermute(w_output[own - 192 :], "seq", [(i, i + 1) for i in range(peers - 1)]),
            w_output,
            lax.ppermute(w_output[:192], "seq", [(i + 1, i) for i in range(peers - 1)]),
        ]
    )
    w_output_window = lax.dynamic_slice_in_dim(before, 192 - offset, window, 0)
    w_output_own = lax.dynamic_update_slice_in_dim(jnp.zeros((window, width), low), w_output, offset, 0)
    near = lax.dynamic_slice_in_dim(row_w.reshape(3 * own, row_pack.shape[1]), own - offset, window, 0)
    w_igate, w_dgate = near[:, :head], near[:, head : 2 * head]
    taps = jnp.zeros((8, window), jnp.float32).at[:4].set(near[:, 2 * head : 2 * head + 4].astype(jnp.float32).T)
    w_decay = near[:, 2 * head + 4].astype(jnp.float32)
    soft = jnp.broadcast_to(jax.nn.softplus(w_decay)[None], (8, window))
    gain_first = vectors[:, 0, :rows].reshape(width)
    gain_second = vectors[:, 1, :rows].reshape(width)
    flags = lax.dynamic_index_in_dim(vectors.reshape(peers, groups, 8, 128), f, 1, False)[:, 2, :tokens].reshape(all_tokens)
    segment = jnp.cumsum(flags)
    masks, aheads = [flags], [jnp.ones_like(flags)]
    for k in range(1, 4):
        same = (segment[k:] == segment[:-k]).astype(jnp.float32)
        masks.append(jnp.concatenate([jnp.zeros((k,), jnp.float32), same]))
        aheads.append(jnp.concatenate([same, jnp.zeros((k,), jnp.float32)]))
    masks = jnp.stack(masks + [jnp.zeros_like(flags)] * 4, axis=1)
    aheads = jnp.stack(aheads + [jnp.zeros_like(flags)] * 4, axis=1)
    owned_rows = jnp.broadcast_to(owned[None], (8, window))

    scale_full = lax.rsqrt(jnp.mean(x_full * x_full, axis=1, keepdims=True) + EPSILON)
    normed = (x_full * scale_full * gain_first).astype(low)
    pre = product(normed, mixer_w[:, :window])
    conv_in = product(normed, mixer_w[:, window:]).astype(low)
    rounded, gate_in, gate_dec, states, earlier, mixed = mixer_forward(conv_in, pre, masks, taps, w_igate, w_dgate, soft, head)
    out_part = product(mixed, w_output_own).astype(low)
    (mixer_out,) = exchange([Reduce(out_part.reshape(peers, tokens, width))], 3, "mixer_reduce")
    resid = sources + mixer_out
    scale_two = lax.rsqrt(jnp.mean(resid * resid, axis=1, keepdims=True) + EPSILON)
    hidden = (resid * scale_two * gain_second).astype(low)
    (hidden_full,) = exchange([Gather(hidden)], 4, "hidden_gather")
    hidden_full = hidden_full.reshape(all_tokens, width)

    gate_pre = product(hidden_full, w_gate)
    up_values = product(hidden_full, w_up)
    act_grad = product(returned_full, w_down)
    gate_act, slope = gelu_parts(gate_pre)
    active = (gate_act * up_values).astype(low)
    gate_grad = (act_grad * up_values * slope).astype(low)
    up_grad = (act_grad * gate_act).astype(low)
    hidden_part = (last_product(gate_grad, w_gate) + last_product(up_grad, w_up)).astype(low)
    result_part = last_product(active, w_down).astype(low)
    (hidden_grad,) = exchange([Reduce(hidden_part.reshape(peers, tokens, width))], 5, "hidden_reduce")
    weighted = hidden_grad * gain_second
    resid_grad = (
        returned.astype(jnp.float32)
        + scale_two * weighted
        - resid * scale_two**3 * jnp.mean(weighted * resid, axis=1, keepdims=True)
    )
    second_term = jnp.sum(hidden_grad * resid * scale_two, axis=0)
    out_grad = resid_grad.astype(low)
    split = lambda g: g.reshape(peers, groups, rows, g.shape[-1])
    grad_gate = split(rows_product(hidden_full, gate_grad).astype(low))
    grad_up = split(rows_product(hidden_full, up_grad).astype(low))
    grad_down = split(rows_product(returned_full, active).astype(low))
    (out_grad_full, ffn_out) = exchange([Gather(out_grad), Reduce(result_part.reshape(peers, tokens, width))], 6, "branch_gather")
    result = (resid + ffn_out).astype(low)
    grad_gate, grad_up, grad_down = [exchange([Collect(g)], 10 + i, "collect")[0] for i, g in enumerate((grad_gate, grad_up, grad_down))]
    out_grad_full = out_grad_full.reshape(all_tokens, width)

    mixed_grad = last_product(out_grad_full, w_output_window)
    pre_grad, conv_grad, igate_term, dgate_term, line_terms = mixer_backward(
        mixed_grad, pre, states, earlier, rounded, gate_in, gate_dec, conv_in, masks, aheads, taps, w_igate, w_dgate, soft, owned_rows, head
    )
    normed_part = (last_product(pre_grad, mixer_w[:, :window]) + last_product(conv_grad, mixer_w[:, window:])).astype(low)
    (normed_grad,) = exchange([Reduce(normed_part.reshape(peers, tokens, width))], 7, "normed_reduce")
    scale_one = lax.rsqrt(jnp.mean(sources * sources, axis=1, keepdims=True) + EPSILON)
    weighted = normed_grad * gain_first
    source_grad = (
        resid_grad
        + scale_one * weighted
        - sources * scale_one**3 * jnp.mean(weighted * sources, axis=1, keepdims=True)
    )
    first_term = jnp.sum(normed_grad * sources * scale_one, axis=0)
    take_columns = lambda g: lax.dynamic_slice_in_dim(g, offset, own, 1)
    take_rows = lambda g: lax.dynamic_slice_in_dim(g, offset, own, 0)
    grad_branch = split(take_columns(rows_product(normed, pre_grad)).astype(low))
    grad_input = split(take_columns(rows_product(normed, conv_grad)).astype(low))
    grad_output = take_rows(rows_product(mixed, out_grad_full)).astype(low)
    gates = take_rows(jnp.concatenate([igate_term, dgate_term], axis=1)).astype(low)
    lines = take_rows(jnp.concatenate([line_terms.T, jnp.zeros((window, 120), jnp.float32)], axis=1))
    vectors = jnp.zeros((peers * groups, 8, 128), jnp.float32)
    vectors = vectors.at[:, 0, :rows].set(first_term.reshape(peers * groups, rows))
    vectors = vectors.at[:, 1, :rows].set(second_term.reshape(peers * groups, rows))
    by_rows = lambda g: g.reshape(1, groups, rows, g.shape[-1])
    grad_branch, grad_input, grad_output, gates, lines, vectors = exchange(
        [Collect(grad_branch), Collect(grad_input), Collect(by_rows(grad_output)), Collect(by_rows(gates)), Collect(by_rows(lines)), Tiny(vectors)],
        8,
        "mixer_collect",
    )
    vectors = jnp.sum(vectors, axis=0)
    gates = gates[0].astype(jnp.float32)
    join = lambda g: g.transpose(1, 0, 2).reshape(rows, peers * g.shape[-1]).astype(jnp.float32)
    return (
        result[None],
        source_grad.astype(low)[None],
        vectors[0, :rows],
        join(grad_branch),
        join(grad_input),
        lines[0, :, :4],
        gates[:, :head],
        gates[:, head:],
        lines[0, :, 4] * jax.nn.sigmoid(decay_param.astype(jnp.float32)),
        grad_output[0].astype(jnp.float32),
        vectors[1, :rows],
        join(grad_gate),
        join(grad_up),
        join(grad_down),
    )


def solution(mesh):
    in_specs = (
        P("fsdp", "seq", None),
        P("fsdp", "seq"),
        P("fsdp", "seq", None),
        P(("seq", "fsdp")),
        P(("seq", "fsdp"), None),
        P(("seq", "fsdp"), None),
        P(("seq", "fsdp"), None),
        P(("seq", "fsdp"), None),
        P(("seq", "fsdp"), None),
        P(("seq", "fsdp")),
        P(("seq", "fsdp"), None),
        P(("seq", "fsdp")),
        P(("seq", "fsdp"), None),
        P(("seq", "fsdp"), None),
        P(("seq", "fsdp"), None),
    )
    out_specs = (
        P("fsdp", "seq", None),
        P("fsdp", "seq", None),
        P(("seq", "fsdp")),
        P(("seq", "fsdp"), None),
        P(("seq", "fsdp"), None),
        P(("seq", "fsdp"), None),
        P(("seq", "fsdp"), None),
        P(("seq", "fsdp"), None),
        P(("seq", "fsdp")),
        P(("seq", "fsdp"), None),
        P(("seq", "fsdp")),
        P(("seq", "fsdp"), None),
        P(("seq", "fsdp"), None),
        P(("seq", "fsdp"), None),
    )
    program = fast if dict(mesh.shape) == {"seq": 8, "fsdp": 4} else local
    return jax.shard_map(program, mesh=mesh, in_specs=in_specs, out_specs=out_specs, check_vma=False)
```

```python
import jax
import jax.numpy as jnp
from jax import lax
from jax.experimental import pallas as pl
from jax.experimental.pallas import tpu as pltpu
from jax.sharding import PartitionSpec as P

EPSILON = 1e-06
CONTRACT_ROWS = (((0,), (0,)), ((), ()))
CONTRACT_LAST = (((1,), (1,)), ((), ()))


def shifted_2(value, axis, steps):
    count = lax.axis_size(axis)
    leading, last = (max(0, -steps), min(count, count - steps))
    return lax.ppermute(value, axis, [(source, source + steps) for source in range(leading, last)])


def entering(x, axis, combine, identity, reverse):
    peers, index = (lax.axis_size(axis), lax.axis_index(axis))
    everything = jax.tree.map(lambda part: lax.all_gather(part, axis), x)
    start = jax.tree.map(
        lambda part, zero: jnp.broadcast_to(jnp.asarray(zero, part.dtype), part.shape), x, identity
    )

    def lap(k, before):
        at = peers - 1 - k if reverse else k
        reached = at > index if reverse else at < index
        new = combine(before, jax.tree.map(lambda part: part[at], everything))
        return jax.tree.map(lambda a, b: jnp.where(reached, a, b), new, before)

    return lax.fori_loop(0, peers, lap, start)


def affine(earlier, later):
    return (earlier[0] * later[0], later[0] * earlier[1] + later[1])


def product(operand_one, operand_two):
    return jnp.dot(operand_one, operand_two, preferred_element_type=jnp.float32)


def rows_product(operand_one, operand_two):
    return lax.dot_general(
        operand_one, operand_two, CONTRACT_ROWS, preferred_element_type=jnp.float32
    )


def last_product(operand_one, operand_two):
    return lax.dot_general(
        operand_one, operand_two, CONTRACT_LAST, preferred_element_type=jnp.float32
    )


def heads_apply(values, weight, head_count):
    token_count = values.shape[0]
    head_width = weight.shape[1]
    shaped = values.reshape(token_count, head_count, head_width)
    blocks = weight.reshape(head_count, head_width, head_width)
    mixed = jnp.einsum("thi,hij->thj", shaped, blocks, preferred_element_type=jnp.float32)
    return mixed.reshape(token_count, head_count * head_width)


def heads_back(gradients, weight, head_count):
    token_count = gradients.shape[0]
    head_width = weight.shape[1]
    shaped = gradients.reshape(token_count, head_count, head_width)
    blocks = weight.reshape(head_count, head_width, head_width)
    mixed = jnp.einsum("thj,hij->thi", shaped, blocks, preferred_element_type=jnp.float32)
    return mixed.reshape(token_count, head_count * head_width)


def heads_grad(values, gradients, head_count):
    token_count = values.shape[0]
    head_width = values.shape[1] // head_count
    left_side = values.reshape(token_count, head_count, head_width)
    right_side = gradients.reshape(token_count, head_count, head_width)
    summed = jnp.einsum("thi,thj->hij", left_side, right_side, preferred_element_type=jnp.float32)
    return summed.reshape(head_count * head_width, head_width)


def slab_count():
    for candidate in (5, 4, 2):
        return candidate
    return 1


def local(
    inputs,
    resets,
    cotangent,
    first_gain,
    branch_weight,
    input_weight,
    conv_weight,
    input_gate,
    decay_gate,
    decay_param,
    output_weight,
    second_gain,
    gate_weight,
    up_weight,
    down_weight,
):
    sources = inputs[0].astype(jnp.float32)
    flags = resets[0]
    returned = cotangent[0]
    returned_float = returned.astype(jnp.float32)
    tokens = sources.shape[0]
    shared = (
        lax.all_gather(first_gain, ("seq", "fsdp"), axis=0, tiled=True),
        lax.all_gather(branch_weight, ("seq", "fsdp"), axis=0, tiled=True),
        lax.all_gather(input_weight, ("seq", "fsdp"), axis=0, tiled=True),
        lax.all_gather(conv_weight, ("seq", "fsdp"), axis=0, tiled=True),
        lax.all_gather(input_gate, ("seq", "fsdp"), axis=0, tiled=True),
        lax.all_gather(decay_gate, ("seq", "fsdp"), axis=0, tiled=True),
        lax.all_gather(decay_param, ("seq", "fsdp"), axis=0, tiled=True),
        lax.all_gather(output_weight, ("seq", "fsdp"), axis=0, tiled=True),
        lax.all_gather(second_gain, ("seq", "fsdp"), axis=0, tiled=True),
    )
    dense_parts = (
        lax.all_gather(gate_weight, ("seq", "fsdp"), axis=0, tiled=True),
        lax.all_gather(up_weight, ("seq", "fsdp"), axis=0, tiled=True),
        lax.all_gather(down_weight, ("seq", "fsdp"), axis=0, tiled=True),
    )
    gain_first = shared[0].astype(jnp.float32)
    w_branch = shared[1]
    w_input = shared[2]
    w_conv = shared[3].astype(jnp.float32)
    w_igate = shared[4]
    w_dgate = shared[5]
    w_decay = shared[6].astype(jnp.float32)
    w_output = shared[7]
    gain_second = shared[8].astype(jnp.float32)
    w_gate = dense_parts[0]
    w_up = dense_parts[1]
    w_down = dense_parts[2]
    model_width = w_branch.shape[0]
    head_width = w_igate.shape[1]
    head_count = model_width // head_width
    tap_count = w_conv.shape[1]
    scale_one = lax.rsqrt(jnp.mean(sources * sources, axis=1, keepdims=True) + EPSILON)
    normed = (sources * scale_one * gain_first).astype(jnp.bfloat16)
    branch_pre = product(normed, w_branch)
    branch, branch_pull = jax.vjp(jax.nn.gelu, branch_pre)
    conv_in = product(normed, w_input).astype(jnp.bfloat16)
    resets_seen = jnp.cumsum(flags)
    tail_keep = resets_seen[-1] - resets_seen[tokens - tap_count + 1 :] == 0
    tail_rows = conv_in[tokens - tap_count + 1 :] * tail_keep[:, None]
    before = shifted_2(tail_rows, "seq", 1)
    padded = jnp.concatenate([before, conv_in], axis=0)
    seen_before = jnp.concatenate([jnp.zeros((tap_count - 1,), jnp.int32), resets_seen])
    conv_out = jnp.zeros((tokens, model_width), jnp.float32)
    usable_list = []
    for offset in range(tap_count):
        first_row = tap_count - 1 - offset
        shifted = padded[first_row : first_row + tokens].astype(jnp.float32)
        usable = (resets_seen - seen_before[first_row : first_row + tokens] == 0).astype(
            jnp.float32
        )[:, None]
        usable_list.append(usable)
        conv_out = conv_out + w_conv[:, offset] * shifted * usable
    rounded = conv_out.astype(jnp.bfloat16)
    rounded_float = rounded.astype(jnp.float32)
    gate_input = jax.nn.sigmoid(heads_apply(rounded, w_igate, head_count))
    gate_decay = jax.nn.sigmoid(heads_apply(rounded, w_dgate, head_count))
    softened = jax.nn.softplus(w_decay)
    log_decay = -softened * (1.0 + 7.0 * gate_decay)
    decays = jnp.exp(log_decay)
    root_term = jnp.sqrt(-jnp.expm1(2.0 * log_decay))
    restart = flags.astype(jnp.float32)[:, None]
    carried = 1.0 - restart
    scaling = restart + carried * root_term
    driven = rounded_float * gate_input * scaling
    coefficient = decays * carried
    running, local_state = lax.associative_scan(affine, (coefficient, driven), axis=0)
    unit_ones = jnp.ones((model_width,), jnp.float32)
    unit_zeros = jnp.zeros((model_width,), jnp.float32)
    incoming = entering(
        (running[-1], local_state[-1]), "seq", affine, (unit_ones, unit_zeros), False
    )
    state_in = incoming[1]
    states = local_state + running * state_in
    mixed = (states * branch).astype(jnp.bfloat16)
    resid = sources + product(mixed, w_output)
    scale_two = lax.rsqrt(jnp.mean(resid * resid, axis=1, keepdims=True) + EPSILON)
    hidden = (resid * scale_two * gain_second).astype(jnp.bfloat16)
    gate_pre = product(hidden, w_gate)
    up_values = product(hidden, w_up)
    gate_act, gate_pull = jax.vjp(jax.nn.gelu, gate_pre)
    active = (gate_act * up_values).astype(jnp.bfloat16)
    result = (resid + last_product(active, w_down)).astype(jnp.bfloat16)
    act_grad = product(returned, w_down)
    gate_grad = gate_pull(act_grad * up_values)[0].astype(jnp.bfloat16)
    up_grad = (act_grad * gate_act).astype(jnp.bfloat16)
    hidden_grad = last_product(gate_grad, w_gate) + last_product(up_grad, w_up)
    weighted_two = hidden_grad * gain_second
    resid_grad = (
        returned_float
        + scale_two * weighted_two
        - resid * scale_two**3 * jnp.mean(weighted_two * resid, axis=1, keepdims=True)
    )
    second_term = jnp.sum(hidden_grad * resid * scale_two, axis=0)
    branch_out_grad = resid_grad.astype(jnp.bfloat16)
    mixed_grad = last_product(branch_out_grad, w_output)
    state_grad = mixed_grad * branch
    branch_grad = mixed_grad * states
    branch_pre_grad = branch_pull(branch_grad)[0].astype(jnp.bfloat16)
    next_coef = jnp.concatenate([coefficient[1:], jnp.ones((1, model_width), jnp.float32)], axis=0)
    reaches, adjoint_local = lax.associative_scan(
        affine, (next_coef, state_grad), reverse=True, axis=0
    )
    carry_back = entering(
        (coefficient[0] * reaches[0], coefficient[0] * adjoint_local[0]),
        "seq",
        affine,
        (unit_ones, unit_zeros),
        True,
    )
    adjoint = adjoint_local + reaches * carry_back[1]
    earlier_state = jnp.concatenate([state_in[None], states[:-1]], axis=0)
    log_grad = (
        adjoint * earlier_state * carried * decays
        - adjoint * rounded_float * gate_input * carried * decays * decays / root_term
    )
    decay_term = jnp.sum(-log_grad * (1.0 + 7.0 * gate_decay), axis=0) * jax.nn.sigmoid(w_decay)
    input_pre_grad = (adjoint * rounded_float * scaling * gate_input * (1.0 - gate_input)).astype(
        jnp.bfloat16
    )
    decay_pre_grad = (log_grad * (-7.0 * softened) * gate_decay * (1.0 - gate_decay)).astype(
        jnp.bfloat16
    )
    conv_out_grad = (
        adjoint * gate_input * scaling
        + heads_back(input_pre_grad, w_igate, head_count)
        + heads_back(decay_pre_grad, w_dgate, head_count)
    )
    conv_grad = conv_out_grad.astype(jnp.bfloat16)
    igate_term = heads_grad(rounded, input_pre_grad, head_count)
    dgate_term = heads_grad(rounded, decay_pre_grad, head_count)
    head_keep = resets_seen[: tap_count - 1] == 0
    head_rows = conv_grad[: tap_count - 1] * head_keep[:, None]
    following = shifted_2(head_rows, "seq", -1)
    padded_back = jnp.concatenate([conv_grad, following], axis=0)
    seen_after = jnp.concatenate(
        [resets_seen, jnp.full((tap_count - 1,), resets_seen[-1], jnp.int32)]
    )
    conv_grad_float = conv_grad.astype(jnp.float32)
    conv_in_grad = jnp.zeros((tokens, model_width), jnp.float32)
    tap_terms = []
    for offset in range(tap_count):
        first_row = tap_count - 1 - offset
        shifted = padded[first_row : first_row + tokens].astype(jnp.float32)
        tap_terms.append(jnp.sum(conv_grad_float * shifted * usable_list[offset], axis=0))
        ahead_usable = (seen_after[offset : offset + tokens] - resets_seen == 0).astype(
            jnp.float32
        )[:, None]
        conv_in_grad = (
            conv_in_grad
            + w_conv[:, offset]
            * padded_back[offset : offset + tokens].astype(jnp.float32)
            * ahead_usable
        )
    tap_grad = jnp.stack(tap_terms, axis=1)
    conv_in_low = conv_in_grad.astype(jnp.bfloat16)
    normed_grad = last_product(branch_pre_grad, w_branch) + last_product(conv_in_low, w_input)
    weighted_one = normed_grad * gain_first
    source_grad = (
        resid_grad
        + scale_one * weighted_one
        - sources * scale_one**3 * jnp.mean(weighted_one * sources, axis=1, keepdims=True)
    )
    first_term = jnp.sum(normed_grad * sources * scale_one, axis=0)
    grad_inputs = source_grad.astype(jnp.bfloat16)[None]
    vector_part = jnp.concatenate(
        [
            igate_term,
            dgate_term,
            tap_grad,
            decay_term[:, None],
            first_term[:, None],
            second_term[:, None],
        ],
        axis=1,
    )
    owned_rows = gate_weight.shape[0]
    owner_count = lax.axis_size(("seq", "fsdp"))
    slab_total = slab_count()
    slab_rows = owned_rows // slab_total
    vector_shaped = vector_part.reshape(owner_count, owned_rows, vector_part.shape[1])

    def pick_rows(values, portion):
        shaped = values.reshape(values.shape[0], owner_count, owned_rows)
        taken = shaped[:, :, portion * slab_rows : (portion + 1) * slab_rows]
        return taken.reshape(values.shape[0], owner_count * slab_rows)

    gate_pieces = []
    up_pieces = []
    down_pieces = []
    branch_pieces = []
    input_pieces = []
    output_pieces = []
    vector_pieces = []
    for portion in range(slab_total):
        hidden_rows = pick_rows(hidden, portion)
        return_rows = pick_rows(returned, portion)
        dense_sums = (
            lax.psum_scatter(
                rows_product(hidden_rows, gate_grad),
                ("seq", "fsdp"),
                scatter_dimension=0,
                tiled=True,
            ),
            lax.psum_scatter(
                rows_product(hidden_rows, up_grad), ("seq", "fsdp"), scatter_dimension=0, tiled=True
            ),
            lax.psum_scatter(
                rows_product(return_rows, active), ("seq", "fsdp"), scatter_dimension=0, tiled=True
            ),
        )
        gate_pieces.append(dense_sums[0])
        up_pieces.append(dense_sums[1])
        down_pieces.append(dense_sums[2])
        normed_rows = pick_rows(normed, portion)
        mixed_rows = pick_rows(mixed, portion)
        vector_rows = vector_shaped[:, portion * slab_rows : (portion + 1) * slab_rows].reshape(
            owner_count * slab_rows, vector_part.shape[1]
        )
        mixer_sums = (
            lax.psum_scatter(
                rows_product(normed_rows, branch_pre_grad),
                ("seq", "fsdp"),
                scatter_dimension=0,
                tiled=True,
            ),
            lax.psum_scatter(
                rows_product(normed_rows, conv_in_low),
                ("seq", "fsdp"),
                scatter_dimension=0,
                tiled=True,
            ),
            lax.psum_scatter(
                rows_product(mixed_rows, branch_out_grad),
                ("seq", "fsdp"),
                scatter_dimension=0,
                tiled=True,
            ),
            lax.psum_scatter(vector_rows, ("seq", "fsdp"), scatter_dimension=0, tiled=True),
        )
        branch_pieces.append(mixer_sums[0])
        input_pieces.append(mixer_sums[1])
        output_pieces.append(mixer_sums[2])
        vector_pieces.append(mixer_sums[3])
    grad_gate = jnp.concatenate(gate_pieces, axis=0)
    grad_up = jnp.concatenate(up_pieces, axis=0)
    grad_down = jnp.concatenate(down_pieces, axis=0)
    grad_branch = jnp.concatenate(branch_pieces, axis=0)
    grad_input = jnp.concatenate(input_pieces, axis=0)
    grad_output = jnp.concatenate(output_pieces, axis=0)
    vector_sums = jnp.concatenate(vector_pieces, axis=0)
    edge_five = 2 * head_width
    edge_six = edge_five + tap_count
    grad_igate = vector_sums[:, :head_width]
    grad_dgate = vector_sums[:, head_width:edge_five]
    grad_conv = vector_sums[:, edge_five:edge_six]
    grad_decay = vector_sums[:, edge_six]
    grad_gain_first = vector_sums[:, edge_six + 1]
    grad_gain_second = vector_sums[:, edge_six + 2]
    return (
        result[None],
        grad_inputs,
        grad_gain_first,
        grad_branch,
        grad_input,
        grad_conv,
        grad_igate,
        grad_dgate,
        grad_decay,
        grad_output,
        grad_gain_second,
        grad_gate,
        grad_up,
        grad_down,
    )


CHUNK = 128
TAPS = 4


def gelu_parts(x):
    inner = 0.7978845608028654 * (x + 0.044715 * x * x * x)
    bent = jnp.tanh(inner)
    value = 0.5 * x * (1.0 + bent)
    slope = 0.5 * (1.0 + bent) + 0.5 * x * (1.0 - bent * bent) * 0.7978845608028654 * (
        1.0 + 3.0 * 0.044715 * x * x
    )
    return value, slope


def minus_expm1(x):
    series = x / 8.0 + 1.0
    for step in (7.0, 6.0, 5.0, 4.0, 3.0, 2.0):
        series = series * x / step + 1.0
    return jnp.where(x > -0.5, -x * series, 1.0 - jnp.exp(x))


def mixer_forward_kernel(
    conv_in_ref, pre_ref, mask_ref, taps_ref, igate_ref, dgate_ref, soft_ref,
    rounded_ref, gin_ref, gdec_ref, states_ref, earlier_ref, mixed_ref,
    padded, coef, drive,
):
    tokens, width = conv_in_ref.shape
    chunk = min(CHUNK, tokens)
    padded[0:8, :] = jnp.zeros((8, width), jnp.float32)
    soft = soft_ref[0:1, :]
    igate = igate_ref[...]
    dgate = dgate_ref[...]

    def fill(c, _):
        base = pl.multiple_of(c * chunk, chunk)
        padded[pl.ds(pl.multiple_of(base + 8, 8), chunk), :] = conv_in_ref[pl.ds(base, chunk), :].astype(jnp.float32)
        return 0

    lax.fori_loop(0, tokens // chunk, fill, 0)
    row = lax.broadcasted_iota(jnp.int32, (8, width), 0)

    def body(c, carry):
        base = pl.multiple_of(c * chunk, chunk)
        mask = mask_ref[pl.ds(base, chunk), :]
        span = padded[pl.ds(base, chunk + 8), :]
        out = taps_ref[0:1, :] * span[8:]
        for k in range(1, TAPS):
            out = out + taps_ref[k : k + 1, :] * span[8 - k : 8 - k + chunk] * mask[:, k : k + 1]
        rounded = out.astype(jnp.bfloat16)
        rounded_ref[pl.ds(base, chunk), :] = rounded
        gin = jax.nn.sigmoid(jnp.dot(rounded, igate, preferred_element_type=jnp.float32))
        gdec = jax.nn.sigmoid(jnp.dot(rounded, dgate, preferred_element_type=jnp.float32))
        gin_ref[pl.ds(base, chunk), :] = gin
        gdec_ref[pl.ds(base, chunk), :] = gdec
        log_decay = -soft * (1.0 + 7.0 * gdec)
        root = jnp.sqrt(minus_expm1(2.0 * log_decay))
        restart = mask[:, 0:1]
        carried = 1.0 - restart
        coef[...] = jnp.exp(log_decay) * carried
        drive[...] = rounded.astype(jnp.float32) * gin * (restart + carried * root)

        def tile(i, state):
            at = pl.multiple_of(i * 8, 8)
            a = coef[pl.ds(at, 8), :]
            b = drive[pl.ds(at, 8), :]
            for sh in (1, 2, 4):
                keep = row >= sh
                b = b + a * jnp.where(keep, pltpu.roll(b, sh, 0), 0.0)
                a = a * jnp.where(keep, pltpu.roll(a, sh, 0), 1.0)
            new = b + a * state
            states_ref[pl.ds(pl.multiple_of(base + at, 8), 8), :] = new
            earlier_ref[pl.ds(pl.multiple_of(base + at, 8), 8), :] = jnp.where(row == 0, state, pltpu.roll(new, 1, 0))
            return jnp.broadcast_to(new[7:8, :], (8, width))

        carry = lax.fori_loop(0, chunk // 8, tile, carry, unroll=True)
        branch, _ = gelu_parts(pre_ref[pl.ds(base, chunk), :])
        mixed_ref[pl.ds(base, chunk), :] = (states_ref[pl.ds(base, chunk), :] * branch).astype(jnp.bfloat16)
        return carry

    lax.fori_loop(0, tokens // chunk, body, jnp.zeros((8, width), jnp.float32))


def mixer_forward(conv_in, pre, mask, taps, igate, dgate, soft, width):
    tokens, total = conv_in.shape
    heads = total // width
    column = lambda h: (0, h)
    row = lambda h: (h, 0)
    whole = lambda h: (0, 0)
    big = pl.BlockSpec((tokens, width), column)
    shape = lambda kind: jax.ShapeDtypeStruct((tokens, total), kind)
    return pl.pallas_call(
        mixer_forward_kernel,
        grid=(heads,),
        in_specs=[
            big, big, pl.BlockSpec(mask.shape, whole), pl.BlockSpec((8, width), column),
            pl.BlockSpec((width, width), row), pl.BlockSpec((width, width), row),
            pl.BlockSpec((8, width), column),
        ],
        out_specs=[big] * 6,
        out_shape=[shape(jnp.bfloat16), shape(jnp.float32), shape(jnp.float32), shape(jnp.float32), shape(jnp.float32), shape(jnp.bfloat16)],
        scratch_shapes=[
            pltpu.VMEM((tokens + 8, width), jnp.float32),
            pltpu.VMEM((min(CHUNK, tokens), width), jnp.float32),
            pltpu.VMEM((min(CHUNK, tokens), width), jnp.float32),
        ],
        compiler_params=pltpu.CompilerParams(vmem_limit_bytes=48 * 2**20),
        name="mixer_forward",
    )(conv_in, pre, mask, taps, igate, dgate, soft)


def mixer_backward_kernel(
    grad_ref, pre_ref, states_ref, earlier_ref, rounded_ref, gin_ref, gdec_ref, conv_in_ref, mask_ref, ahead_ref,
    taps_ref, igate_ref, dgate_ref, soft_ref, own_ref,
    bpg_ref, cig_ref, igrad_ref, dgrad_ref, tapgrad_ref,
    padded, ahead_pad, coef, drive, decay_sum, tap_sum,
):
    tokens, width = grad_ref.shape
    chunk = min(CHUNK, tokens)
    count = tokens // chunk
    padded[0:8, :] = jnp.zeros((8, width), jnp.float32)
    ahead_pad[tokens : tokens + 8, :] = jnp.zeros((8, width), jnp.float32)
    soft = soft_ref[0:1, :]
    own = own_ref[0:1, :]
    igate = igate_ref[...]
    dgate = dgate_ref[...]
    igrad_ref[...] = jnp.zeros_like(igrad_ref)
    dgrad_ref[...] = jnp.zeros_like(dgrad_ref)
    decay_sum[...] = jnp.zeros_like(decay_sum)
    tap_sum[...] = jnp.zeros_like(tap_sum)
    row = lax.broadcasted_iota(jnp.int32, (8, width), 0)
    rows_dot = lambda a, b: lax.dot_general(a, b, (((0,), (0,)), ((), ())), preferred_element_type=jnp.float32)
    last_dot = lambda a, b: lax.dot_general(a, b, (((1,), (1,)), ((), ())), preferred_element_type=jnp.float32)

    def body(step, carry):
        c = count - 1 - step
        base = pl.multiple_of(c * chunk, chunk)
        here = pl.ds(base, chunk)
        padded[pl.ds(pl.multiple_of(base + 8, 8), chunk), :] = conv_in_ref[here, :].astype(jnp.float32)
        mask = mask_ref[here, :]
        restart = mask[:, 0:1]
        carried = 1.0 - restart
        branch, slope = gelu_parts(pre_ref[here, :])
        grad = grad_ref[here, :]
        bpg_ref[here, :] = (grad * states_ref[here, :] * slope * own).astype(jnp.bfloat16)
        gdec = gdec_ref[here, :]
        gin = gin_ref[here, :]
        log_decay = -soft * (1.0 + 7.0 * gdec)
        decays = jnp.exp(log_decay)
        root = jnp.sqrt(minus_expm1(2.0 * log_decay))
        coef[...] = decays * carried
        drive[...] = grad * branch

        def tile(i, pair):
            adj_next, coef_next = pair
            at = pl.multiple_of(chunk - 8 - i * 8, 8)
            first = coef[pl.ds(at, 8), :]
            a = jnp.where(row == 7, coef_next, pltpu.roll(first, 7, 0))
            b = drive[pl.ds(at, 8), :]
            for sh in (1, 2, 4):
                keep = row < 8 - sh
                b = b + a * jnp.where(keep, pltpu.roll(b, 8 - sh, 0), 0.0)
                a = a * jnp.where(keep, pltpu.roll(a, 8 - sh, 0), 1.0)
            new = b + a * adj_next
            drive[pl.ds(at, 8), :] = new
            return jnp.broadcast_to(new[0:1, :], (8, width)), jnp.broadcast_to(first[0:1, :], (8, width))

        carry = lax.fori_loop(0, chunk // 8, tile, carry, unroll=True)
        adjoint = drive[...]
        rounded = rounded_ref[here, :]
        rounded_float = rounded.astype(jnp.float32)
        pull = adjoint * carried * decays
        log_grad = pull * (earlier_ref[here, :] - rounded_float * gin * decays / root)
        decay_sum[...] += jnp.sum((-log_grad * (1.0 + 7.0 * gdec)).reshape(chunk // 8, 8, width), axis=0)
        through = adjoint * gin * (restart + carried * root)
        ipg = (through * rounded_float * (1.0 - gin)).astype(jnp.bfloat16)
        dpg = (log_grad * (-7.0 * soft) * gdec * (1.0 - gdec)).astype(jnp.bfloat16)
        igrad_ref[...] += rows_dot(rounded, ipg)
        dgrad_ref[...] += rows_dot(rounded, dpg)
        through = through + last_dot(ipg, igate) + last_dot(dpg, dgate)
        ahead_pad[here, :] = through.astype(jnp.bfloat16).astype(jnp.float32)
        return carry

    zero = jnp.zeros((8, width), jnp.float32)
    lax.fori_loop(0, count, body, (zero, zero))

    def after(c, _):
        base = pl.multiple_of(c * chunk, chunk)
        here = pl.ds(base, chunk)
        mask = mask_ref[here, :]
        ahead = ahead_ref[here, :]
        later = ahead_pad[pl.ds(base, chunk + 8), :]
        span = padded[pl.ds(base, chunk + 8), :]
        grad = later[:chunk]
        total = taps_ref[0:1, :] * grad
        tap_sum[0:8, :] += jnp.sum((grad * span[8:]).reshape(chunk // 8, 8, width), axis=0)
        for k in range(1, TAPS):
            total = total + taps_ref[k : k + 1, :] * later[k : k + chunk] * ahead[:, k : k + 1]
            shifted = span[8 - k : 8 - k + chunk]
            tap_sum[8 * k : 8 * k + 8, :] += jnp.sum((grad * shifted * mask[:, k : k + 1]).reshape(chunk // 8, 8, width), axis=0)
        cig_ref[here, :] = (total * own).astype(jnp.bfloat16)
        return 0

    lax.fori_loop(0, count, after, 0)
    for k in range(TAPS):
        tapgrad_ref[k : k + 1, :] = jnp.sum(tap_sum[8 * k : 8 * k + 8, :], axis=0, keepdims=True)
    tapgrad_ref[4:5, :] = jnp.sum(decay_sum[...], axis=0, keepdims=True)
    tapgrad_ref[5:8, :] = jnp.zeros((3, width), jnp.float32)


def mixer_backward(grad, pre, states, earlier, rounded, gin, gdec, conv_in, mask, ahead, taps, igate, dgate, soft, own, width):
    tokens, total = grad.shape
    heads = total // width
    column = lambda h: (0, h)
    row = lambda h: (h, 0)
    whole = lambda h: (0, 0)
    big = pl.BlockSpec((tokens, width), column)
    line = pl.BlockSpec((8, width), column)
    square = pl.BlockSpec((width, width), row)
    shape = lambda kind: jax.ShapeDtypeStruct((tokens, total), kind)
    chunk = min(CHUNK, tokens)
    return pl.pallas_call(
        mixer_backward_kernel,
        grid=(heads,),
        in_specs=[big] * 8 + [pl.BlockSpec(mask.shape, whole)] * 2 + [line, square, square, line, line],
        out_specs=[big, big, square, square, line],
        out_shape=[
            shape(jnp.bfloat16), shape(jnp.bfloat16),
            jax.ShapeDtypeStruct((total, width), jnp.float32), jax.ShapeDtypeStruct((total, width), jnp.float32),
            jax.ShapeDtypeStruct((8, total), jnp.float32),
        ],
        scratch_shapes=[
            pltpu.VMEM((tokens + 8, width), jnp.float32),
            pltpu.VMEM((tokens + 8, width), jnp.float32),
            pltpu.VMEM((chunk, width), jnp.float32),
            pltpu.VMEM((chunk, width), jnp.float32),
            pltpu.VMEM((8, width), jnp.float32),
            pltpu.VMEM((8 * TAPS, width), jnp.float32),
        ],
        compiler_params=pltpu.CompilerParams(vmem_limit_bytes=56 * 2**20),
        name="mixer_backward",
    )(grad, pre, states, earlier, rounded, gin, gdec, conv_in, mask, ahead, taps, igate, dgate, soft, own)


MESH_ID = pl.DeviceIdType.MESH
PIECES = 4


class Spot:
    def __init__(self):
        self.s = lax.axis_index("seq")
        self.f = lax.axis_index("fsdp")
        self.z = self.s // 2
        self.y = self.s % 2
        self.up = (self.z < 3, (jnp.minimum(self.s + 2, 7), self.f))
        self.down = (self.z > 0, (jnp.maximum(self.s - 2, 0), self.f))
        self.beside = (None, (self.s ^ 1, self.f))
        self.across = (None, (self.s, self.f ^ 2))
        self.twin = (None, (self.s, self.f ^ 1))

    def peer(self, j):
        return (None, (self.s ^ j, self.f))

    def other(self, j):
        return (None, (self.s ^ (j // 4), self.f ^ (j % 4)))

    def meet(self, reach):
        barrier = pltpu.get_barrier_semaphore()
        if "all" in reach:
            peers = [self.other(j) for j in range(1, 32)]
        else:
            peers = [self.peer(j) for j in range(1, 8)] if "seq" in reach else []
            if "line" in reach and not peers:
                peers = [self.up, self.down, self.beside]
            if "pair" in reach:
                peers += [self.across, self.twin]
        count = 0
        for cond, where in peers:
            count = count + (1 if cond is None else cond.astype(jnp.int32))
            guarded(cond, lambda: pl.semaphore_signal(barrier, 1, device_id=where, device_id_type=MESH_ID))
        pl.semaphore_wait(barrier, count)


def guarded(cond, action):
    if cond is None:
        action()
    else:
        pl.when(cond)(action)


class Send:
    def __init__(self, src, dst, send_sem, recv_sem, target):
        self.cond, where = target
        self.copy = pltpu.make_async_remote_copy(
            src_ref=src, dst_ref=dst, send_sem=send_sem, recv_sem=recv_sem, device_id=where, device_id_type=MESH_ID
        )

    def start(self):
        guarded(self.cond, self.copy.start)

    def sent(self):
        guarded(self.cond, self.copy.wait_send)


def arrived(dst, send_sem, recv_sem, target, cond=None):
    copy = pltpu.make_async_remote_copy(
        src_ref=dst, dst_ref=dst, send_sem=send_sem, recv_sem=recv_sem, device_id=target[1], device_id_type=MESH_ID
    )
    guarded(cond, copy.wait_recv)


class Gather:
    letter = "g"
    def __init__(self, x):
        self.ins = [x]
        self.outs = [jax.ShapeDtypeStruct((8,) + x.shape, x.dtype)]
        dma = pltpu.SemaphoreType.DMA
        self.scratch = [dma((1,)), dma((8, PIECES)), dma((4, PIECES)), dma((4, PIECES)), dma((7, PIECES))]

    reach = ("line",)

    def steps(self, at, ins, outs, scratch):
        (x,), (o,) = ins, outs
        own_sem, recv, ups, downs, sides = scratch
        rows = x.shape[0] // PIECES
        cut = lambda p: pl.ds(p * rows, rows)
        sends = []

        def send(src, block, p, sem, target):
            one = Send(src, o.at[block, cut(p)], sem, recv.at[block, p], target)
            one.start()
            sends.append(one)

        own = pltpu.make_async_copy(x, o.at[at.s], own_sem.at[0])
        own.start()
        for p in range(PIECES):
            send(x.at[cut(p)], at.s, p, ups.at[0, p], at.up)
            send(x.at[cut(p)], at.s, p, downs.at[0, p], at.down)
            send(x.at[cut(p)], at.s, p, sides.at[0, p], at.beside)
        yield
        for d in range(1, 4):
            for p in range(PIECES):
                low, high = at.z >= d, at.z + d <= 3
                block = jnp.maximum(at.s - 2 * d, 0)
                arrived(o.at[block, cut(p)], ups.at[0, p], recv.at[block, p], at.down, low)
                if d < 3:
                    send(o.at[block, cut(p)], block, p, ups.at[d, p], (low & (at.z < 3), at.up[1]))
                send(o.at[block, cut(p)], block, p, sides.at[d, p], (low, at.beside[1]))
                block = jnp.minimum(at.s + 2 * d, 7)
                arrived(o.at[block, cut(p)], ups.at[0, p], recv.at[block, p], at.up, high)
                if d < 3:
                    send(o.at[block, cut(p)], block, p, downs.at[d, p], (high & (at.z > 0), at.down[1]))
                send(o.at[block, cut(p)], block, p, sides.at[3 + d, p], (high, at.beside[1]))
                yield
        for z in range(4):
            for p in range(PIECES):
                block = 2 * z + 1 - at.y
                arrived(o.at[block, cut(p)], ups.at[0, p], recv.at[block, p], at.beside)
        yield
        for one in sends:
            one.sent()
        own.wait()


class Reduce:
    letter = "r"
    def __init__(self, x):
        _, rows, width = x.shape
        self.ins = [x]
        self.outs = [jax.ShapeDtypeStruct((rows, width), jnp.float32)]
        dma = pltpu.SemaphoreType.DMA
        hold = pltpu.VMEM((4, rows, width), x.dtype)
        self.scratch = [hold, hold, hold, hold, pltpu.VMEM((rows, width), jnp.float32)]
        self.scratch += [dma((4, PIECES)) for _ in range(6)] + [dma((1,))]

    reach = ("line",)

    def steps(self, at, ins, outs, scratch):
        (x,), (o,) = ins, outs
        mine, side, below, above, total, load, ysend, yrecv, zsend, urecv, drecv, osem = scratch
        rows = x.shape[1] // PIECES
        cut = lambda p: pl.ds(p * rows, rows)
        group = 16
        sends = []
        order = []
        for k in range(3):
            order.append((3 - k, at.z < 3 - k, True))
            order.append((k, at.z > k, False))
        order.append((at.z, None, None))

        loads = []
        for t, cond, _ in order:
            for p in range(PIECES):
                one = Send(x.at[2 * t + 1 - at.y, cut(p)], side.at[t, cut(p)], ysend.at[t, p], yrecv.at[t, p], (cond, at.beside[1]))
                one.start()
                sends.append(one)
                copy = pltpu.make_async_copy(x.at[2 * t + at.y, cut(p)], mine.at[t, cut(p)], load.at[t, p])
                guarded(cond, copy.start)
        yield
        for t, cond, rising in order:
            for p in range(PIECES):
                copy = pltpu.make_async_copy(x.at[2 * t + at.y, cut(p)], mine.at[t, cut(p)], load.at[t, p])
                guarded(cond, copy.wait)
                arrived(side.at[t, cut(p)], ysend.at[t, p], yrecv.at[t, p], at.beside, cond)
                if rising is None:
                    arrived(below.at[t, cut(p)], zsend.at[t, p], urecv.at[t, p], at.down, at.z > 0)
                    arrived(above.at[t, cut(p)], zsend.at[t, p], drecv.at[t, p], at.up, at.z < 3)

                    def final(i, _):
                        here = pl.ds(pl.multiple_of(p * rows + i * group, group), group)
                        value = mine[t, here, :].astype(jnp.float32) + side[t, here, :].astype(jnp.float32)
                        total[here, :] = value

                        @pl.when(at.z > 0)
                        def _():
                            total[here, :] += below[t, here, :].astype(jnp.float32)

                        @pl.when(at.z < 3)
                        def _():
                            total[here, :] += above[t, here, :].astype(jnp.float32)

                        return 0

                    lax.fori_loop(0, rows // group, final, 0)
                else:
                    source = below if rising else above
                    inner = (cond & (at.z > 0)) if rising else (cond & (at.z < 3))
                    outer = (cond & (at.z == 0)) if rising else (cond & (at.z == 3))
                    rsem = urecv if rising else drecv
                    arrived(source.at[t, cut(p)], zsend.at[t, p], rsem.at[t, p], at.down if rising else at.up, inner)

                    def add(with_source):
                        def one(i, _):
                            here = pl.ds(pl.multiple_of(p * rows + i * group, group), group)
                            value = mine[t, here, :].astype(jnp.float32) + side[t, here, :].astype(jnp.float32)
                            if with_source:
                                value = value + source[t, here, :].astype(jnp.float32)
                            mine[t, here, :] = value.astype(mine.dtype)
                            return 0

                        lax.fori_loop(0, rows // group, one, 0)

                    pl.when(inner)(lambda: add(True))
                    pl.when(outer)(lambda: add(False))
                    one = Send(mine.at[t, cut(p)], source.at[t, cut(p)], zsend.at[t, p], rsem.at[t, p], (cond, (at.up if rising else at.down)[1]))
                    one.start()
                    sends.append(one)
                yield
        out = pltpu.make_async_copy(total, o, osem.at[0])
        out.start()
        for one in sends:
            one.sent()
        out.wait()


class Spread:
    letter = "s"
    reach = ("seq", "pair")

    def __init__(self, x, starts, wide):
        self.ins = [x]
        self.starts, self.wide = starts, wide
        self.outs = [jax.ShapeDtypeStruct((8, 4, x.shape[0], wide), x.dtype)]
        dma = pltpu.SemaphoreType.DMA
        self.scratch = [dma((8,)), dma((8,)), dma((8,)), dma((8,)), dma((8, 2)), dma((8, 2))]

    def steps(self, at, ins, outs, scratch):
        (x,), (o,) = ins, outs
        asend, arecv, xsend, xrecv, csend, crecv = scratch
        sends = []
        part = lambda to: x.at[:, pl.ds(pl.multiple_of(self.starts(to), 128), self.wide)]

        def send(src, dst, ss, rs, target):
            one = Send(src, dst, ss, rs, target)
            one.start()
            sends.append(one)

        for j in range(1, 8):
            send(part(at.s ^ j), o.at[at.s, at.f], asend.at[j], arecv.at[j], at.peer(j))
        own = pltpu.make_async_copy(part(at.s), o.at[at.s, at.f], asend.at[0])
        own.start()
        yield
        for j in range(8):
            block = at.s ^ j
            here = o.at[block, at.f]
            if j == 0:
                own.wait()
            else:
                arrived(here, asend.at[j], arecv.at[j], at.peer(j))
            send(here, here, xsend.at[j], xrecv.at[j], at.across)
            send(here, here, csend.at[j, 0], crecv.at[j, 0], at.twin)
            yield
        for j in range(8):
            there = o.at[at.s ^ j, at.f ^ 2]
            arrived(there, xsend.at[j], xrecv.at[j], at.across)
            send(there, there, csend.at[j, 1], crecv.at[j, 1], at.twin)
            yield
        for j in range(8):
            for k in range(2):
                arrived(o.at[at.s ^ j, (at.f ^ 1) ^ (2 * k)], csend.at[j, k], crecv.at[j, k], at.twin)
        for one in sends:
            one.sent()


def add_rows(dst, terms, rows):
    group = 16

    def one(i, _):
        here = pl.ds(pl.multiple_of(i * group, group), group)
        value = terms[0][here, :].astype(jnp.float32)
        for term in terms[1:]:
            value = value + term[here, :].astype(jnp.float32)
        dst[here, :] = value.astype(dst.dtype)
        return 0

    lax.fori_loop(0, rows // group, one, 0)


class Collect:
    letter = "c"
    def __init__(self, x):
        blocks, _, rows, width = x.shape
        self.ins = [x]
        self.blocks = blocks
        self.reach = ("seq", "pair") if blocks > 1 else ("pair",)
        self.outs = [jax.ShapeDtypeStruct((blocks, rows, width), x.dtype)]
        dma = pltpu.SemaphoreType.DMA
        hold = pltpu.VMEM((blocks, rows, width), x.dtype)
        self.scratch = [pltpu.VMEM((2, rows, width), x.dtype)] + [hold] * 3 + [dma((2,))] + [dma((blocks, 2))] * 2 + [dma((blocks,))] * 4

    def steps(self, at, ins, outs, scratch):
        (x,), (o,) = ins, outs
        stage, tnear, tfar, xin, lsem, csend, crecv, xsend, xrecv, asend, arecv = scratch
        rows = x.shape[2]
        many = self.blocks > 1
        spot = (lambda j: at.s ^ j) if many else (lambda j: j)
        sends = []

        def send(src, dst, ss, rs, target):
            one = Send(src, dst, ss, rs, target)
            one.start()
            sends.append(one)

        order = [j for j in range(1, 8)] + [0] if many else [0]
        pieces = [(j, at.f ^ 2) for j in order] + [(j, at.f) for j in order]

        def load(i):
            j, whose = pieces[i]
            return pltpu.make_async_copy(x.at[spot(j), whose], stage.at[i % 2], lsem.at[i % 2])

        for j in order:
            send(x.at[spot(j), at.f ^ 3], tfar.at[j], csend.at[j, 0], crecv.at[j, 0], at.twin)
            send(x.at[spot(j), at.f ^ 1], tnear.at[j], csend.at[j, 1], crecv.at[j, 1], at.twin)
        load(0).start()
        yield
        outs_done = []
        for i, (j, _) in enumerate(pieces):
            far = i < len(order)
            if i + 1 < len(pieces):
                load(i + 1).start()
            load(i).wait()
            if far:
                arrived(tfar.at[j], csend.at[j, 0], crecv.at[j, 0], at.twin)
                add_rows(tfar.at[j], (tfar.at[j], stage.at[i % 2]), rows)
                send(tfar.at[j], xin.at[j], xsend.at[j], xrecv.at[j], at.across)
            else:
                arrived(tnear.at[j], csend.at[j, 1], crecv.at[j, 1], at.twin)
                arrived(xin.at[j], xsend.at[j], xrecv.at[j], at.across)
                add_rows(tnear.at[j], (tnear.at[j], stage.at[i % 2], xin.at[j]), rows)
                if j:
                    send(tnear.at[j], o.at[at.s], asend.at[j], arecv.at[j], at.peer(j))
                else:
                    outs_done.append(pltpu.make_async_copy(tnear.at[0], o.at[at.s if many else 0], asend.at[0]))
                    outs_done[-1].start()
            yield
        for j in order:
            if j:
                arrived(o.at[at.s ^ j], asend.at[j], arecv.at[j], at.peer(j))
        for one in sends:
            one.sent()
        for one in outs_done:
            one.wait()


class Tiny:
    letter = "t"
    def __init__(self, x):
        self.ins = [x]
        self.outs = [jax.ShapeDtypeStruct(x.shape, x.dtype)]
        dma = pltpu.SemaphoreType.DMA
        self.scratch = [dma((32,)), dma((32,))]

    reach = ("all",)

    def steps(self, at, ins, outs, scratch):
        (x,), (o,) = ins, outs
        ss, rs = scratch
        me = at.s * 4 + at.f
        sends = []
        for j in range(1, 32):
            one = Send(x.at[me ^ j], o.at[me], ss.at[j], rs.at[j], at.other(j))
            one.start()
            sends.append(one)
        own = pltpu.make_async_copy(x.at[me], o.at[me], ss.at[0])
        own.start()
        for _ in range(40):
            yield
        for j in range(1, 32):
            arrived(o.at[me ^ j], ss.at[j], rs.at[j], at.other(j))
        for one in sends:
            one.sent()
        own.wait()


class Chain:
    @staticmethod
    def scratch(rows, width, kind):
        dma = pltpu.SemaphoreType.DMA
        return [
            pltpu.VMEM((4, rows, width), kind),
            pltpu.VMEM((5, rows, width), kind),
            pltpu.VMEM((rows, width), jnp.float32),
            dma((4, PIECES)),
            dma((4, PIECES)),
            dma((4, PIECES)),
            dma((5, PIECES)),
            dma((1,)),
        ]

    def __init__(self, at, parts, out, scratch, order):
        self.at, self.parts, self.out, self.order = at, parts, out, order
        self.side, self.inflow, self.total, self.ysend, self.yrecv, self.zsend, self.zrecv, self.osem = scratch
        self.rows = parts.shape[1] // PIECES

    def cut(self, p):
        return pl.ds(pl.multiple_of(p * self.rows, self.rows), self.rows)

    def side_copy(self, t, p):
        at = self.at
        return Send(
            self.parts.at[2 * t + 1 - at.y, self.cut(p)], self.side.at[t, self.cut(p)], self.ysend.at[t, p], self.yrecv.at[t, p], at.beside
        )

    def send_side(self, t):
        for p in range(PIECES):
            self.side_copy(t, p).start()

    def z_copy(self, t, p, rising):
        at = self.at
        slot = t if rising else jnp.where(t == at.z - 1, 4, t)
        mine = self.parts.at[2 * t + at.y, self.cut(p)]
        target = (None, (at.up if rising else at.down)[1])
        return Send(mine, self.inflow.at[slot, self.cut(p)], self.zsend.at[t, p], self.zrecv.at[slot, p], target)

    def wait_side(self, t, p):
        arrived(self.side.at[t, self.cut(p)], self.ysend.at[t, p], self.yrecv.at[t, p], self.at.beside)

    def wait_inflow(self, slot, p):
        arrived(self.inflow.at[slot, self.cut(p)], self.zsend.at[0, p], self.zrecv.at[slot, p], self.at.down)

    def step(self, k, p):
        at = self.at
        group = 16
        rises, falls = self.order(k)
        for t, cond, rising in ((rises, at.z < rises, True), (falls, at.z > falls, False)):

            @pl.when(cond)
            def _():
                self.wait_side(t, p)
                first = at.z == (0 if rising else 3)

                def add(inner):
                    def one(i, _):
                        here = pl.ds(pl.multiple_of(p * self.rows + i * group, group), group)
                        value = self.parts[2 * t + at.y, here, :].astype(jnp.float32) + self.side[t, here, :].astype(jnp.float32)
                        if inner:
                            value = value + self.inflow[t, here, :].astype(jnp.float32)
                        self.parts[2 * t + at.y, here, :] = value.astype(self.parts.dtype)
                        return 0

                    lax.fori_loop(0, self.rows // group, one, 0)

                pl.when(first)(lambda: add(False))

                @pl.when(jnp.logical_not(first))
                def _():
                    self.wait_inflow(t, p)
                    add(True)

                self.z_copy(t, p, rising).start()

    def last(self, p):
        at = self.at
        group = 16
        self.wait_side(at.z, p)
        pl.when(at.z > 0)(lambda: self.wait_inflow(at.z, p))
        pl.when(at.z < 3)(lambda: self.wait_inflow(4, p))

        def one(i, _):
            here = pl.ds(pl.multiple_of(p * self.rows + i * group, group), group)
            self.total[here, :] = self.parts[at.s, here, :].astype(jnp.float32) + self.side[at.z, here, :].astype(jnp.float32)

            @pl.when(at.z > 0)
            def _():
                self.total[here, :] += self.inflow[at.z, here, :].astype(jnp.float32)

            @pl.when(at.z < 3)
            def _():
                self.total[here, :] += self.inflow[4, here, :].astype(jnp.float32)

            return 0

        lax.fori_loop(0, self.rows // group, one, 0)

    def finish(self):
        def one(p, _):
            self.last(p)
            return 0

        lax.fori_loop(0, PIECES, one, 0)
        self.out_copy().start()

    def out_copy(self):
        return pltpu.make_async_copy(self.total, self.out, self.osem.at[0])

    def sent(self):
        def one(i, _):
            t, p = i // PIECES, lax.rem(i, PIECES)
            self.side_copy(t, p).sent()

            @pl.when(t != self.at.z)
            def _():
                self.z_copy(t, p, True).sent()

            return 0

        lax.fori_loop(0, 4 * PIECES, one, 0)
        self.out_copy().wait()


def outward(k):
    return k + 1, 2 - k


def ascending(k):
    return k + 1, k


def descending(k):
    return 3 - k, 2 - k


class Dense:
    letter = "d"
    reach = ("line",)

    def __init__(self, hidden, returned, w_gate, w_up, w_down, held):
        rows, width = hidden.shape
        wide = w_gate.shape[1]
        low = hidden.dtype
        dma = pltpu.SemaphoreType.DMA
        self.ins = [hidden, returned, w_gate, w_up, w_down, held]
        sums = jax.ShapeDtypeStruct((rows, width), jnp.float32)
        grad = jax.ShapeDtypeStruct((width, wide), low)
        self.outs = [sums, jax.ShapeDtypeStruct((8, rows, width), low), grad, grad, grad]
        tokens = pltpu.VMEM((8, rows, width), low)
        weight = pltpu.VMEM((width, wide), low)
        inner = pltpu.VMEM((8, rows, wide), low)
        self.own = [tokens, tokens, weight, weight, weight, inner, inner, inner, tokens, tokens, pltpu.VMEM(held.shape, held.dtype), dma((8,))]
        self.gather = Gather(hidden)
        self.chain = Chain.scratch(rows, width, low)
        self.scratch = self.own + self.gather.scratch + self.chain

    def steps(self, at, ins, outs, scratch):
        hidden, returned, w_gate, w_up, w_down, held = ins
        count = len(self.own)
        toks, cots, wg, wu, wd, act, ggrad, ugrad, hpart, rpart, mask, sems = scratch[:count]
        scratch = scratch[count:]
        gsems, scratch = scratch[: len(self.gather.scratch)], scratch[len(self.gather.scratch) :]
        hchain = Chain(at, hpart, outs[0], scratch, outward)
        rows, width = hidden.shape
        wide = w_gate.shape[1]
        tile = 256
        loads = [
            pltpu.make_async_copy(src, dst, sems.at[i])
            for i, (src, dst) in enumerate(((w_gate, wg), (w_up, wu), (w_down, wd), (returned, cots), (held, mask)))
        ]
        relay = Relay(at, hidden, toks, gsems)
        relay.begin()
        for load in loads:
            load.start()
        yield
        for p in range(PIECES):
            relay.step(1, p)
        for load in loads:
            load.wait()
        relay.own_copy().wait()
        last_dot = lambda a, b: lax.dot_general(a, b, CONTRACT_LAST, preferred_element_type=jnp.float32)
        rows_dot = lambda a, b: lax.dot_general(a, b, CONTRACT_ROWS, preferred_element_type=jnp.float32)

        def pair(i, _):
            far = at.z < 2
            t = jnp.where(
                i == 0, at.z, jnp.where(i == 1, at.z ^ 1, jnp.where(i == 2, jnp.where(far, 2, 1), jnp.where(far, 3, 0)))
            )
            relay.wait_beside(t)
            both = pl.ds(2 * t, 2)

            def first(n, _):
                lanes = pl.ds(pl.multiple_of(n * tile, tile), tile)
                h = toks[both].reshape(2 * rows, width)
                c = cots[both].reshape(2 * rows, width)
                pre = jnp.dot(h, wg[:, lanes], preferred_element_type=jnp.float32)
                up = jnp.dot(h, wu[:, lanes], preferred_element_type=jnp.float32)
                grad = jnp.dot(c, wd[:, lanes], preferred_element_type=jnp.float32)
                value, slope = gelu_parts(pre)
                keep = mask[0:1, lanes]
                put = lambda ref, v: ref.__setitem__((both, slice(None), lanes), v.astype(ref.dtype).reshape(2, rows, tile))
                put(act, value * up * keep)
                put(ggrad, grad * up * slope * keep)
                put(ugrad, grad * value * keep)
                pl.when(n == 1)(lambda: relay.step(i + 2, 0))
                pl.when(n == 3)(lambda: relay.step(i + 2, 1))
                return 0

            lax.fori_loop(0, wide // tile, first, 0)

            def second(n, _):
                lanes = pl.ds(pl.multiple_of(n * tile, tile), tile)
                a = act[both].reshape(2 * rows, wide)
                g = ggrad[both].reshape(2 * rows, wide)
                u = ugrad[both].reshape(2 * rows, wide)
                put = lambda ref, v: ref.__setitem__((both, slice(None), lanes), v.astype(ref.dtype).reshape(2, rows, tile))
                put(hpart, last_dot(g, wg[lanes, :]) + last_dot(u, wu[lanes, :]))
                put(rpart, last_dot(a, wd[lanes, :]))
                pl.when(n == 2)(lambda: relay.step(i + 2, 2))
                pl.when(n == 6)(lambda: relay.step(i + 2, 3))
                return 0

            lax.fori_loop(0, width // tile, second, 0)
            hchain.send_side(t)
            return 0

        lax.fori_loop(0, 4, pair, 0)
        out = pltpu.make_async_copy(rpart, outs[1], sems.at[7])
        out.start()

        def grads(r):
            lanes = pl.ds(pl.multiple_of(r * tile, tile), tile)
            h = toks[:, :, lanes].reshape(8 * rows, tile)
            c = cots[:, :, lanes].reshape(8 * rows, tile)
            wg[lanes, :] = rows_dot(h, ggrad[...].reshape(8 * rows, wide)).astype(wg.dtype)
            wu[lanes, :] = rows_dot(h, ugrad[...].reshape(8 * rows, wide)).astype(wu.dtype)
            wd[lanes, :] = rows_dot(c, act[...].reshape(8 * rows, wide)).astype(wd.dtype)

        def hstep(i, _):
            hchain.step(i // PIECES, lax.rem(i, PIECES))
            pl.when(i < width // tile)(lambda: grads(i))
            return 0

        lax.fori_loop(0, 3 * PIECES, hstep, 0)
        hchain.finish()
        stores = [pltpu.make_async_copy(src, dst, sems.at[i]) for i, (src, dst) in enumerate(((wg, outs[2]), (wu, outs[3]), (wd, outs[4])))]
        for store in stores:
            store.start()
        hchain.sent()
        relay.sent()
        for store in stores + [out]:
            store.wait()
        yield


class Relay:
    def __init__(self, at, x, o, sems):
        self.at, self.x, self.o = at, x, o
        self.own_sem, self.recv, self.ups, self.downs, self.sides = sems
        self.rows = x.shape[0] // PIECES

    def cut(self, p):
        return pl.ds(p * self.rows, self.rows)

    def copy(self, src, block, p, sem, target):
        return Send(src, self.o.at[block, self.cut(p)], sem, self.recv.at[block, p], target)

    def own_copy(self):
        return pltpu.make_async_copy(self.x, self.o.at[self.at.s], self.own_sem.at[0])

    def begin(self):
        at = self.at
        self.own_copy().start()
        for p in range(PIECES):
            src = self.x.at[self.cut(p)]
            self.copy(src, at.s, p, self.ups.at[0, p], at.up).start()
            self.copy(src, at.s, p, self.downs.at[0, p], at.down).start()
            self.copy(src, at.s, p, self.sides.at[0, p], at.beside).start()

    def halves(self, d):
        at = self.at
        low = (at.z >= d, jnp.maximum(at.s - 2 * d, 0), self.ups, at.up, d, at.down)
        high = (at.z + d <= 3, jnp.minimum(at.s + 2 * d, 7), self.downs, at.down, 3 + d, at.up)
        return low, high

    def step(self, d, p):
        for cond, block, along, ahead, slot, source in self.halves(d):

            @pl.when(cond)
            def _():
                here = self.o.at[block, self.cut(p)]
                arrived(here, self.ups.at[0, p], self.recv.at[block, p], source)
                self.copy(here, block, p, along.at[d, p], ahead).start()
                self.copy(here, block, p, self.sides.at[slot, p], self.at.beside).start()

    def wait_beside(self, t):
        block = 2 * t + 1 - self.at.y
        for p in range(PIECES):
            arrived(self.o.at[block, self.cut(p)], self.ups.at[0, p], self.recv.at[block, p], self.at.beside)

    def sent(self):
        at = self.at
        for p in range(PIECES):
            src = self.x.at[self.cut(p)]
            self.copy(src, at.s, p, self.ups.at[0, p], at.up).sent()
            self.copy(src, at.s, p, self.downs.at[0, p], at.down).sent()
            self.copy(src, at.s, p, self.sides.at[0, p], at.beside).sent()
            for d in range(1, 4):
                for cond, block, along, ahead, slot, source in self.halves(d):

                    @pl.when(cond)
                    def _():
                        here = self.o.at[block, self.cut(p)]
                        self.copy(here, block, p, along.at[d, p], ahead).sent()
                        self.copy(here, block, p, self.sides.at[slot, p], at.beside).sent()


def exchange(jobs, collective, name, plan=()):
    def kernel(*refs):
        at = Spot()
        refs = list(refs)
        take = lambda count: [refs.pop(0) for _ in range(count)]
        ins = [take(len(job.ins)) for job in jobs]
        outs = [take(len(job.outs)) for job in jobs]
        scratch = [take(len(job.scratch)) for job in jobs]
        at.meet({one for job in jobs for one in job.reach})
        running = [job.steps(at, i, o, s) for job, i, o, s in zip(jobs, ins, outs, scratch)]
        turns = iter(plan)
        while running:
            if plan and running[0] is not None:
                if next(running[0], plan) is plan:
                    running[0] = None
                for letter in next(turns, ""):
                    for job, one in zip(jobs, running):
                        if one is not None and job.letter == letter:
                            next(one, None)
            else:
                running = [one for one in running if one is not None and next(one, running) is not running]

    count = sum(len(job.ins) for job in jobs)
    return pl.pallas_call(
        kernel,
        out_shape=[shape for job in jobs for shape in job.outs],
        in_specs=[pl.BlockSpec(memory_space=pl.ANY)] * count,
        out_specs=[pl.BlockSpec(memory_space=pl.ANY)] * sum(len(job.outs) for job in jobs),
        scratch_shapes=[shape for job in jobs for shape in job.scratch],
        compiler_params=pltpu.CompilerParams(
            collective_id=collective, has_side_effects=True, vmem_limit_bytes=62 * 2**20
        ),
        name=name,
    )(*[x for job in jobs for x in job.ins])


class Rows:
    letter = "o"

    def __init__(self, x, near):
        self.slots = 3 if near else 1
        self.reach = ("seq", "pair") if near else ("pair",)
        self.ins = [x]
        self.outs = [jax.ShapeDtypeStruct((self.slots, 4) + x.shape, x.dtype)]
        dma = pltpu.SemaphoreType.DMA
        self.scratch = [dma((3,))] * 4 + [dma((3, 2))] * 2

    def places(self, at):
        after = (None, (lax.rem(at.s + 1, 8), at.f))
        before = (None, (lax.rem(at.s + 7, 8), at.f))
        return after, before

    def steps(self, at, ins, outs, scratch):
        (x,), (o,) = ins, outs
        asend, arecv, xsend, xrecv, csend, crecv = scratch
        after, before = self.places(at)
        sends = []

        def send(src, dst, ss, rs, target):
            one = Send(src, dst, ss, rs, target)
            one.start()
            sends.append(one)

        middle = self.slots // 2
        if self.slots == 3:
            send(x, o.at[0, at.f], asend.at[0], arecv.at[0], after)
            send(x, o.at[2, at.f], asend.at[2], arecv.at[2], before)
        own = pltpu.make_async_copy(x, o.at[middle, at.f], asend.at[1])
        own.start()
        send(x, o.at[middle, at.f], xsend.at[middle], xrecv.at[middle], at.across)
        send(x, o.at[middle, at.f], csend.at[middle, 0], crecv.at[middle, 0], at.twin)
        yield
        for j in range(self.slots):
            if j != middle:
                here = o.at[j, at.f]
                arrived(here, asend.at[j], arecv.at[j], before if j == 0 else after)
                send(here, here, xsend.at[j], xrecv.at[j], at.across)
                send(here, here, csend.at[j, 0], crecv.at[j, 0], at.twin)
        yield
        for j in range(self.slots):
            there = o.at[j, at.f ^ 2]
            arrived(there, xsend.at[j], xrecv.at[j], at.across)
            send(there, there, csend.at[j, 1], crecv.at[j, 1], at.twin)
            yield
        for j in range(self.slots):
            for k in range(2):
                arrived(o.at[j, (at.f ^ 1) ^ (2 * k)], csend.at[j, k], crecv.at[j, k], at.twin)
        for one in sends:
            one.sent()
        own.wait()


def rms_rows(values):
    mean = jnp.mean(values * values, axis=1, keepdims=True) + EPSILON
    guess = lax.rsqrt(mean)
    return guess * (1.5 - 0.5 * mean * guess * guess)


class MixerForward:
    letter = "m"
    reach = ("line",)

    def __init__(self, x_full, w_branch, w_input, w_out, igate, dgate, gain, mask, taps, soft):
        _, rows, width = x_full.shape
        window, head = igate.shape
        tokens = 8 * rows
        low, full = x_full.dtype, jnp.float32
        dma = pltpu.SemaphoreType.DMA
        self.ins = [x_full, w_branch, w_input, w_out, igate, dgate, gain, mask, taps, soft]
        kinds = [low, full, low, low, full, full, full, low]
        shapes = [(8, rows, width)] + [(tokens, window)] * 7
        self.outs = [jax.ShapeDtypeStruct((rows, width), full)]
        self.outs += [jax.ShapeDtypeStruct(shape, kind) for shape, kind in zip(shapes, kinds)]
        self.kept = [pltpu.VMEM(shape, kind) for shape, kind in zip(shapes, kinds)]
        self.held = [pltpu.VMEM(x.shape, x.dtype) for x in self.ins[1:]]
        self.local = [
            pltpu.VMEM((8, rows, width), low),
            pltpu.VMEM((8 + 2 * rows, window), full),
            pltpu.VMEM((CHUNK, head), full),
            pltpu.VMEM((CHUNK, head), full),
            pltpu.VMEM((8, window), full),
            dma((len(self.ins),)),
            dma((len(kinds),)),
        ]
        self.chain = Chain.scratch(rows, width, low)
        self.scratch = self.kept + self.held + self.local + self.chain

    def steps(self, at, ins, outs, scratch):
        take = lambda count: [scratch.pop(0) for _ in range(count)]
        scratch = list(scratch)
        kept = take(len(self.kept))
        held = take(len(self.held))
        parts, padded, coef, drive, carry, lsem, ssem = take(len(self.local))
        normed, pre, conv_in, rounded, gin, gdec, states, mixed = kept
        w_branch, w_input, w_out, igate, dgate, gain, mask, taps, soft = held
        chain = Chain(at, parts, outs[0], scratch, ascending)
        _, rows, width = normed.shape
        window, head = igate.shape
        span = 2 * rows
        loads = [pltpu.make_async_copy(src, dst, lsem.at[i]) for i, (src, dst) in enumerate(zip(ins, [normed] + held))]
        for load in loads:
            load.start()
        yield
        for load in loads:
            load.wait()
        padded[0:8, :] = jnp.zeros((8, window), jnp.float32)
        carry[...] = jnp.zeros_like(carry)
        line = lax.broadcasted_iota(jnp.int32, (8, head), 0)

        def scale(i, _):
            block, here = i // (rows // 16), pl.ds(pl.multiple_of(lax.rem(i, rows // 16) * 16, 16), 16)
            value = normed[block, here, :].astype(jnp.float32)
            normed[block, here, :] = (value * rms_rows(value) * gain[0:1, :]).astype(normed.dtype)
            return 0

        def work(t):
            lax.fori_loop(2 * t * (rows // 16), 2 * (t + 1) * (rows // 16), scale, 0)
            tokens = pl.ds(span * t, span)
            source = normed[2 * t : 2 * t + 2].reshape(span, width)
            if t:
                padded[0:8, :] = padded[span : span + 8, :]
            for h in range(window // head):
                lanes = slice(h * head, (h + 1) * head)
                pre[tokens, lanes] = jnp.dot(source, w_branch[:, lanes], preferred_element_type=jnp.float32)
                value = jnp.dot(source, w_input[:, lanes], preferred_element_type=jnp.float32).astype(conv_in.dtype)
                conv_in[tokens, lanes] = value
                padded[8:, lanes] = value.astype(jnp.float32)
            if t:
                yield

            def piece(c, _):
                for h in range(window // head):
                    lanes = slice(h * head, (h + 1) * head)
                    base = pl.multiple_of(c * CHUNK, CHUNK)
                    here = pl.ds(pl.multiple_of(t * span + base, CHUNK), CHUNK)
                    marks = mask[here, :]
                    rolls = padded[pl.ds(base, CHUNK + 8), lanes]
                    out = taps[0:1, lanes] * rolls[8:]
                    for k in range(1, TAPS):
                        out = out + taps[k : k + 1, lanes] * rolls[8 - k : 8 - k + CHUNK] * marks[:, k : k + 1]
                    small = out.astype(rounded.dtype)
                    rounded[here, lanes] = small
                    g_in = jax.nn.sigmoid(jnp.dot(small, igate[lanes, :], preferred_element_type=jnp.float32))
                    g_dec = jax.nn.sigmoid(jnp.dot(small, dgate[lanes, :], preferred_element_type=jnp.float32))
                    gin[here, lanes] = g_in
                    gdec[here, lanes] = g_dec
                    log_decay = -soft[0:1, lanes] * (1.0 + 7.0 * g_dec)
                    root = jnp.sqrt(minus_expm1(2.0 * log_decay))
                    restart = marks[:, 0:1]
                    carried = 1.0 - restart
                    coef[...] = jnp.exp(log_decay) * carried
                    drive[...] = small.astype(jnp.float32) * g_in * (restart + carried * root)

                    def tile(i, state):
                        now = pl.multiple_of(i * 8, 8)
                        a = coef[pl.ds(now, 8), :]
                        b = drive[pl.ds(now, 8), :]
                        for sh in (1, 2, 4):
                            keep = line >= sh
                            b = b + a * jnp.where(keep, pltpu.roll(b, sh, 0), 0.0)
                            a = a * jnp.where(keep, pltpu.roll(a, sh, 0), 1.0)
                        new = b + a * state
                        there = pl.ds(pl.multiple_of(t * span + base + now, 8), 8)
                        states[there, lanes] = new
                        return jnp.broadcast_to(new[7:8, :], (8, head))

                    carry[:, lanes] = lax.fori_loop(0, CHUNK // 8, tile, carry[:, lanes], unroll=True)
                    branch, _ = gelu_parts(pre[here, lanes])
                    mixed[here, lanes] = (states[here, lanes] * branch).astype(mixed.dtype)
                return 0

            lax.fori_loop(0, span // CHUNK, piece, 0)
            if t:
                yield
            values = mixed[tokens, :]

            def product(n, _):
                columns = pl.ds(pl.multiple_of(n * 256, 256), 256)
                out = jnp.dot(values, w_out[:, columns], preferred_element_type=jnp.float32)
                parts[2 * t : 2 * t + 2, :, columns] = out.astype(parts.dtype).reshape(2, rows, 256)
                return 0

            lax.fori_loop(0, width // 256, product, 0)
            chain.send_side(t)

        for t in range(4):
            yield from work(t)
            yield
        stores = [pltpu.make_async_copy(src, dst, ssem.at[i]) for i, (src, dst) in enumerate(zip(kept, outs[1:]))]
        for store in stores:
            store.start()
        for k in range(3):
            for p in range(PIECES):
                chain.step(k, p)
                yield
        chain.finish()
        yield
        chain.sent()
        for store in stores:
            store.wait()


class MixerBackward:
    letter = "b"
    reach = ("line",)

    def __init__(self, out_grad, w_out, w_branch, w_input, normed, pre, conv_in, rounded, gin, gdec, states, mixed, igate, dgate, mask, ahead, taps, soft, owned):
        rows, width = out_grad.shape
        tokens, window = pre.shape
        head = igate.shape[1]
        low, full = out_grad.dtype, jnp.float32
        dma = pltpu.SemaphoreType.DMA
        self.ins = [out_grad, w_out, w_branch, w_input, normed, pre, conv_in, rounded, gin, gdec, states, mixed, igate, dgate, mask, ahead, taps, soft, owned]
        shape = jax.ShapeDtypeStruct
        self.outs = [
            shape((rows, width), full), shape((width, window), low), shape((width, window), low), shape((window, width), low),
            shape((window, head), full), shape((window, head), full), shape((8, window), full),
        ]
        self.held = [pltpu.VMEM(x.shape, x.dtype) for x in self.ins[1:]]
        self.held[9] = pltpu.VMEM((8 + tokens, window), full)
        self.local = [
            pltpu.VMEM((8, rows, width), low),
            pltpu.VMEM((8, rows, width), low),
            pltpu.VMEM((2 * rows, window), full),
            pltpu.VMEM((tokens, window), low),
            pltpu.VMEM((tokens, window), low),
            pltpu.VMEM((2 * rows + 8, window), full),
            pltpu.VMEM((2 * rows + 8, window), full),
            pltpu.VMEM((CHUNK, head), full),
            pltpu.VMEM((CHUNK, head), full),
            pltpu.VMEM((16, window), full),
            pltpu.VMEM((window, head), full),
            pltpu.VMEM((window, head), full),
            pltpu.VMEM((8 * 5, window), full),
            pltpu.VMEM((8, window), full),
            dma((len(self.ins),)),
            dma((8,)),
        ]
        self.gather = Gather(out_grad)
        self.chain = Chain.scratch(rows, width, low)
        self.scratch = self.held + self.local + self.gather.scratch + self.chain

    def steps(self, at, ins, outs, scratch):
        scratch = list(scratch)
        take = lambda count: [scratch.pop(0) for _ in range(count)]
        held = take(len(self.held))
        toks, parts, mgrad, pgrad, cgrad, padded, later, coef, drive, carry, igrad, dgrad, sums, lines, lsem, ssem = take(len(self.local))
        gsems = take(len(self.gather.scratch))
        w_out, w_branch, w_input, normed, pre, conv_in, rounded, gin, gdec, states, mixed, igate, dgate, mask, ahead, taps, soft, owned = held
        chain = Chain(at, parts, outs[0], scratch, descending)
        relay = Relay(at, ins[0], toks, gsems)
        _, rows, width = toks.shape
        tokens, window = pre.shape
        head = igate.shape[1]
        span = 2 * rows
        heads = [slice(h * head, (h + 1) * head) for h in range(window // head)]
        relay.begin()
        loads = []
        for i, (src, dst) in enumerate(zip(ins[1:], held)):
            loads.append(pltpu.make_async_copy(src, dst.at[8:] if dst is states else dst, lsem.at[i]))
            loads[-1].start()
        states[0:8, :] = jnp.zeros((8, window), jnp.float32)
        for ref in (later, carry, igrad, dgrad, sums):
            ref[...] = jnp.zeros_like(ref)
        yield
        for d in range(1, 4):
            for p in range(PIECES):
                relay.step(d, p)
                yield
        for load in loads:
            load.wait()
        relay.own_copy().wait()
        for t in range(4):
            relay.wait_beside(t)
        line = lax.broadcasted_iota(jnp.int32, (8, head), 0)
        rows_dot = lambda a, b: lax.dot_general(a, b, CONTRACT_ROWS, preferred_element_type=jnp.float32)
        last_dot = lambda a, b: lax.dot_general(a, b, CONTRACT_LAST, preferred_element_type=jnp.float32)
        fold = lambda v: jnp.sum(v.reshape(v.shape[0] // 8, 8, v.shape[1]), axis=0)

        def work(t):
            source = toks[2 * t : 2 * t + 2].reshape(span, width)
            for lanes in heads:
                mgrad[:, lanes] = last_dot(source, w_out[lanes, :])
            later[span : span + 8, :] = later[0:8, :]
            if t:
                padded[0:8, :] = conv_in[span * t - 16 : span * t, :].astype(jnp.float32)[8:]
            else:
                padded[0:8, :] = jnp.zeros((8, window), jnp.float32)
            padded[8:, :] = conv_in[span * t : span * (t + 1), :].astype(jnp.float32)

            def piece(step, _):
                base = pl.multiple_of((span // CHUNK - 1 - step) * CHUNK, CHUNK)
                here = pl.ds(pl.multiple_of(t * span + base, CHUNK), CHUNK)
                inside = pl.ds(base, CHUNK)
                marks = mask[here, :]
                restart = marks[:, 0:1]
                carried = 1.0 - restart
                for lanes in heads:
                    branch, slope = gelu_parts(pre[here, lanes])
                    grad = mgrad[inside, lanes]
                    state = states[pl.ds(pl.multiple_of(t * span + base, CHUNK), CHUNK + 8), lanes]
                    pgrad[here, lanes] = (grad * state[8:] * slope * owned[0:1, lanes]).astype(pgrad.dtype)
                    g_dec = gdec[here, lanes]
                    g_in = gin[here, lanes]
                    log_decay = -soft[0:1, lanes] * (1.0 + 7.0 * g_dec)
                    decays = jnp.exp(log_decay)
                    root = jnp.sqrt(minus_expm1(2.0 * log_decay))
                    coef[...] = decays * carried
                    drive[...] = grad * branch

                    def tile(i, pair):
                        adj_next, coef_next = pair
                        now = pl.multiple_of(CHUNK - 8 - i * 8, 8)
                        first = coef[pl.ds(now, 8), :]
                        a = jnp.where(line == 7, coef_next, pltpu.roll(first, 7, 0))
                        b = drive[pl.ds(now, 8), :]
                        for sh in (1, 2, 4):
                            keep = line < 8 - sh
                            b = b + a * jnp.where(keep, pltpu.roll(b, 8 - sh, 0), 0.0)
                            a = a * jnp.where(keep, pltpu.roll(a, 8 - sh, 0), 1.0)
                        new = b + a * adj_next
                        drive[pl.ds(now, 8), :] = new
                        return jnp.broadcast_to(new[0:1, :], (8, head)), jnp.broadcast_to(first[0:1, :], (8, head))

                    adj_next, coef_next = lax.fori_loop(0, CHUNK // 8, tile, (carry[0:8, lanes], carry[8:16, lanes]), unroll=True)
                    carry[0:8, lanes] = adj_next
                    carry[8:16, lanes] = coef_next
                    adjoint = drive[...]
                    small = rounded[here, lanes]
                    value = small.astype(jnp.float32)
                    log_grad = adjoint * carried * decays * (state[7 : 7 + CHUNK] - value * g_in * decays / root)
                    sums[32:40, lanes] += fold(-log_grad * (1.0 + 7.0 * g_dec))
                    through = adjoint * g_in * (restart + carried * root)
                    ipg = (through * value * (1.0 - g_in)).astype(jnp.bfloat16)
                    dpg = (log_grad * (-7.0 * soft[0:1, lanes]) * g_dec * (1.0 - g_dec)).astype(jnp.bfloat16)
                    igrad[lanes, :] += rows_dot(small, ipg)
                    dgrad[lanes, :] += rows_dot(small, dpg)
                    through = through + last_dot(ipg, igate[lanes, :]) + last_dot(dpg, dgate[lanes, :])
                    later[inside, lanes] = through.astype(jnp.bfloat16).astype(jnp.float32)
                return 0

            lax.fori_loop(0, span // CHUNK, piece, 0)
            yield

            def after(c, _):
                base = pl.multiple_of(c * CHUNK, CHUNK)
                here = pl.ds(pl.multiple_of(t * span + base, CHUNK), CHUNK)
                marks = mask[here, :]
                ahead_marks = ahead[here, :]
                for lanes in heads:
                    follow = later[pl.ds(base, CHUNK + 8), lanes]
                    before = padded[pl.ds(base, CHUNK + 8), lanes]
                    grad = follow[:CHUNK]
                    total = taps[0:1, lanes] * grad
                    sums[0:8, lanes] += fold(grad * before[8:])
                    for k in range(1, TAPS):
                        total = total + taps[k : k + 1, lanes] * follow[k : k + CHUNK] * ahead_marks[:, k : k + 1]
                        sums[8 * k : 8 * k + 8, lanes] += fold(grad * before[8 - k : 8 - k + CHUNK] * marks[:, k : k + 1])
                    cgrad[here, lanes] = (total * owned[0:1, lanes]).astype(cgrad.dtype)
                return 0

            lax.fori_loop(0, span // CHUNK, after, 0)
            mine = slice(span * t, span * (t + 1))

            def product(n, _):
                columns = pl.ds(pl.multiple_of(n * 256, 256), 256)
                out = last_dot(pgrad[mine, :], w_branch[columns, :]) + last_dot(cgrad[mine, :], w_input[columns, :])
                parts[2 * t : 2 * t + 2, :, columns] = out.astype(parts.dtype).reshape(2, rows, 256)
                return 0

            lax.fori_loop(0, width // 256, product, 0)
            chain.send_side(t)

        for t in (3, 2, 1, 0):
            yield from work(t)
            yield
        for k in range(5):
            lines[k : k + 1, :] = jnp.sum(sums[8 * k : 8 * k + 8, :], axis=0, keepdims=True)
        lines[5:8, :] = jnp.zeros((3, window), jnp.float32)

        def grads(r):
            lanes = pl.ds(pl.multiple_of(r * 256, 256), 256)
            value = normed[:, :, lanes].reshape(tokens, 256)
            w_branch[lanes, :] = rows_dot(value, pgrad[...]).astype(w_branch.dtype)
            w_input[lanes, :] = rows_dot(value, cgrad[...]).astype(w_input.dtype)
            w_out[:, lanes] = rows_dot(mixed[...], toks[:, :, lanes].reshape(tokens, 256)).astype(w_out.dtype)

        done = 0
        for k in range(3):

            def chain_step(p, _):
                chain.step(k, p)
                pl.when(k * PIECES + p < width // 256)(lambda: grads(k * PIECES + p))
                return 0

            lax.fori_loop(0, PIECES, chain_step, 0)
            yield
        chain.finish()
        stores = [
            pltpu.make_async_copy(src, dst, ssem.at[i])
            for i, (src, dst) in enumerate(zip((w_branch, w_input, w_out, igrad, dgrad, lines), outs[1:]))
        ]
        for store in stores:
            store.start()
        yield
        chain.sent()
        relay.sent()
        for store in stores:
            store.wait()


def fast(
    inputs,
    resets,
    cotangent,
    first_gain,
    branch_weight,
    input_weight,
    conv_weight,
    input_gate,
    decay_gate,
    decay_param,
    output_weight,
    second_gain,
    gate_weight,
    up_weight,
    down_weight,
):
    low = jnp.bfloat16
    peers, groups = 8, 4
    s, f = lax.axis_index("seq"), lax.axis_index("fsdp")
    sources_low = inputs[0]
    sources = sources_low.astype(jnp.float32)
    returned = cotangent[0]
    tokens, width = sources.shape
    rows = branch_weight.shape[0]
    head = input_gate.shape[1]
    own = width // peers
    hidden_own = gate_weight.shape[1] // peers
    all_tokens = peers * tokens
    firsts = [min(own * at // head, width // head - 2) for at in range(peers)]
    window = 2 * head
    offset = own * s - head * jnp.minimum(own * s // head, width // head - 2)
    owned = ((jnp.arange(window) >= offset) & (jnp.arange(window) < offset + own)).astype(jnp.float32)

    small = jnp.zeros((8, 128), jnp.float32)
    small = small.at[0, :rows].set(first_gain.astype(jnp.float32))
    small = small.at[1, :rows].set(second_gain.astype(jnp.float32))
    small = small.at[2, :tokens].set(resets[0].astype(jnp.float32))
    small = jnp.broadcast_to(small[None], (peers * groups, 8, 128))
    mixer_start = lambda to: head * jnp.minimum(own * to // head, width // head - 2)
    dense_start = lambda to: 128 * (hidden_own * to // 128)
    wide = 128 * -(-hidden_own // 128)
    lanes = jnp.arange(wide) + dense_start(s) - hidden_own * s
    held = jnp.broadcast_to(((lanes >= 0) & (lanes < hidden_own)).astype(jnp.float32)[None], (8, wide))
    pad = jnp.zeros((rows, 128 - 5), low)
    row_pack = jnp.concatenate([input_gate, decay_gate, conv_weight, decay_param[:, None], pad], axis=1)
    x_full, w_branch, w_input, row_w, out_w, vectors = exchange(
        [
            Gather(sources_low),
            Spread(branch_weight, mixer_start, window),
            Spread(input_weight, mixer_start, window),
            Rows(row_pack, True),
            Rows(output_weight, False),
            Tiny(small),
        ],
        1,
        "first_exchange",
    )
    whole = lambda w: w.reshape(width, w.shape[-1])
    w_branch, w_input = whole(w_branch), whole(w_input)
    w_output = out_w.reshape(own, width)
    before = jnp.concatenate(
        [
            lax.ppermute(w_output[own - 192 :], "seq", [(i, i + 1) for i in range(peers - 1)]),
            w_output,
            lax.ppermute(w_output[:192], "seq", [(i + 1, i) for i in range(peers - 1)]),
        ]
    )
    w_output_window = lax.dynamic_slice_in_dim(before, 192 - offset, window, 0)
    w_output_own = lax.dynamic_update_slice_in_dim(jnp.zeros((window, width), low), w_output, offset, 0)
    near = lax.dynamic_slice_in_dim(row_w.reshape(3 * own, row_pack.shape[1]), own - offset, window, 0)
    w_igate, w_dgate = near[:, :head], near[:, head : 2 * head]
    taps = jnp.zeros((8, window), jnp.float32).at[:4].set(near[:, 2 * head : 2 * head + 4].astype(jnp.float32).T)
    w_decay = near[:, 2 * head + 4].astype(jnp.float32)
    soft = jnp.broadcast_to(jax.nn.softplus(w_decay)[None], (8, window))
    gain_first = vectors[:, 0, :rows].reshape(width)
    gain_second = vectors[:, 1, :rows].reshape(width)
    flags = lax.dynamic_index_in_dim(vectors.reshape(peers, groups, 8, 128), f, 1, False)[:, 2, :tokens].reshape(all_tokens)
    segment = jnp.cumsum(flags)
    masks, aheads = [flags], [jnp.ones_like(flags)]
    for k in range(1, 4):
        same = (segment[k:] == segment[:-k]).astype(jnp.float32)
        masks.append(jnp.concatenate([jnp.zeros((k,), jnp.float32), same]))
        aheads.append(jnp.concatenate([same, jnp.zeros((k,), jnp.float32)]))
    masks = jnp.stack(masks + [jnp.zeros_like(flags)] * 4, axis=1)
    aheads = jnp.stack(aheads + [jnp.zeros_like(flags)] * 4, axis=1)
    owned_rows = jnp.broadcast_to(owned[None], (8, window))

    gain_rows = jnp.broadcast_to(gain_first[None], (8, width))
    (
        mixer_out, normed, pre, conv_in, rounded, gate_in, gate_dec, states, mixed,
        returned_full, w_gate, w_up, w_down,
    ) = exchange(
        [
            MixerForward(x_full, w_branch, w_input, w_output_own, w_igate, w_dgate, gain_rows, masks, taps, soft),
            Gather(returned),
        ]
        + [Spread(w, dense_start, wide) for w in (gate_weight, up_weight, down_weight)],
        2,
        "mixer_forward",
        ["gs"] + [""] * 9 + ["ggggsssggggssggggsss"] + [""] * 12,
    )
    resid = sources + mixer_out
    scale_two = lax.rsqrt(jnp.mean(resid * resid, axis=1, keepdims=True) + EPSILON)
    hidden = (resid * scale_two * gain_second).astype(low)
    hidden_grad, result_part, grad_gate, grad_up, grad_down = exchange(
        [Dense(hidden, returned_full, whole(w_gate), whole(w_up), whole(w_down), held)], 3, "dense"
    )
    weighted = hidden_grad * gain_second
    resid_grad = (
        returned.astype(jnp.float32)
        + scale_two * weighted
        - resid * scale_two**3 * jnp.mean(weighted * resid, axis=1, keepdims=True)
    )
    second_term = jnp.sum(hidden_grad * resid * scale_two, axis=0)
    out_grad = resid_grad.astype(low)
    split = lambda g: g.reshape(peers, groups, rows, g.shape[-1])
    (
        normed_grad, grad_branch, grad_input, grad_output, igate_term, dgate_term, line_terms,
        grad_gate, grad_up, grad_down,
    ) = exchange(
        [
            MixerBackward(
                out_grad, w_output_window, w_branch, w_input, normed, pre, conv_in, rounded, gate_in, gate_dec, states, mixed,
                w_igate, w_dgate, masks, aheads, taps, soft, owned_rows,
            )
        ]
        + [Collect(split(g)) for g in (grad_gate, grad_up, grad_down)],
        4,
        "mixer_backward",
    )
    scale_one = lax.rsqrt(jnp.mean(sources * sources, axis=1, keepdims=True) + EPSILON)
    weighted = normed_grad * gain_first
    source_grad = (
        resid_grad
        + scale_one * weighted
        - sources * scale_one**3 * jnp.mean(weighted * sources, axis=1, keepdims=True)
    )
    first_term = jnp.sum(normed_grad * sources * scale_one, axis=0)
    take_rows = lambda g: lax.dynamic_slice_in_dim(g, offset, own, 0)
    grad_branch, grad_input, grad_output = split(grad_branch), split(grad_input), take_rows(grad_output)
    gates = take_rows(jnp.concatenate([igate_term, dgate_term], axis=1)).astype(low)
    lines = take_rows(jnp.concatenate([line_terms.T, jnp.zeros((window, 120), jnp.float32)], axis=1))
    vectors = jnp.zeros((peers * groups, 8, 128), jnp.float32)
    vectors = vectors.at[:, 0, :rows].set(first_term.reshape(peers * groups, rows))
    vectors = vectors.at[:, 1, :rows].set(second_term.reshape(peers * groups, rows))
    by_rows = lambda g: g.reshape(1, groups, rows, g.shape[-1])
    ffn_out, grad_branch, grad_input, grad_output, gates, lines, vectors = exchange(
        [Reduce(result_part), Collect(grad_branch), Collect(grad_input), Collect(by_rows(grad_output)), Collect(by_rows(gates)), Collect(by_rows(lines)), Tiny(vectors)],
        6,
        "mixer_collect",
    )
    result = (resid + ffn_out).astype(low)
    vectors = jnp.sum(vectors, axis=0)
    gates = gates[0].astype(jnp.float32)

    def join(g, starts):
        size = g.shape[-1]
        marks = sorted({edge for start in starts for edge in (start, start + size)})
        pieces = []
        for low_mark, high_mark in zip(marks[:-1], marks[1:]):
            terms = [
                g[at, :, low_mark - start : high_mark - start].astype(jnp.float32)
                for at, start in enumerate(starts)
                if start <= low_mark and high_mark <= start + size
            ]
            pieces.append(sum(terms[1:], terms[0]))
        return jnp.concatenate(pieces, axis=1)

    firsts = [head * first for first in firsts]
    dense_firsts = [128 * (hidden_own * at // 128) for at in range(peers)]
    return (
        result[None],
        source_grad.astype(low)[None],
        vectors[0, :rows],
        join(grad_branch, firsts),
        join(grad_input, firsts),
        lines[0, :, :4],
        gates[:, :head],
        gates[:, head:],
        lines[0, :, 4] * jax.nn.sigmoid(decay_param.astype(jnp.float32)),
        grad_output[0].astype(jnp.float32),
        vectors[1, :rows],
        join(grad_gate, dense_firsts),
        join(grad_up, dense_firsts),
        join(grad_down, dense_firsts),
    )


def solution(mesh):
    in_specs = (
        P("fsdp", "seq", None),
        P("fsdp", "seq"),
        P("fsdp", "seq", None),
        P(("seq", "fsdp")),
        P(("seq", "fsdp"), None),
        P(("seq", "fsdp"), None),
        P(("seq", "fsdp"), None),
        P(("seq", "fsdp"), None),
        P(("seq", "fsdp"), None),
        P(("seq", "fsdp")),
        P(("seq", "fsdp"), None),
        P(("seq", "fsdp")),
        P(("seq", "fsdp"), None),
        P(("seq", "fsdp"), None),
        P(("seq", "fsdp"), None),
    )
    out_specs = (
        P("fsdp", "seq", None),
        P("fsdp", "seq", None),
        P(("seq", "fsdp")),
        P(("seq", "fsdp"), None),
        P(("seq", "fsdp"), None),
        P(("seq", "fsdp"), None),
        P(("seq", "fsdp"), None),
        P(("seq", "fsdp"), None),
        P(("seq", "fsdp")),
        P(("seq", "fsdp"), None),
        P(("seq", "fsdp")),
        P(("seq", "fsdp"), None),
        P(("seq", "fsdp"), None),
        P(("seq", "fsdp"), None),
    )
    program = fast if dict(mesh.shape) == {"seq": 8, "fsdp": 4} else local
    return jax.shard_map(program, mesh=mesh, in_specs=in_specs, out_specs=out_specs, check_vma=False)
```

```python
import functools

import jax
import jax.numpy as jnp
from jax import lax
from jax.experimental import pallas as pl
from jax.experimental.pallas import tpu as pltpu
from jax.sharding import PartitionSpec as P

EPSILON = 1e-06
CONTRACT_ROWS = (((0,), (0,)), ((), ()))
CONTRACT_LAST = (((1,), (1,)), ((), ()))


def shifted_2(value, axis, steps):
    count = lax.axis_size(axis)
    leading, last = (max(0, -steps), min(count, count - steps))
    return lax.ppermute(value, axis, [(source, source + steps) for source in range(leading, last)])


def entering(x, axis, combine, identity, reverse):
    peers, index = (lax.axis_size(axis), lax.axis_index(axis))
    everything = jax.tree.map(lambda part: lax.all_gather(part, axis), x)
    start = jax.tree.map(
        lambda part, zero: jnp.broadcast_to(jnp.asarray(zero, part.dtype), part.shape), x, identity
    )

    def lap(k, before):
        at = peers - 1 - k if reverse else k
        reached = at > index if reverse else at < index
        new = combine(before, jax.tree.map(lambda part: part[at], everything))
        return jax.tree.map(lambda a, b: jnp.where(reached, a, b), new, before)

    return lax.fori_loop(0, peers, lap, start)


def affine(earlier, later):
    return (earlier[0] * later[0], later[0] * earlier[1] + later[1])


def product(operand_one, operand_two):
    return jnp.dot(operand_one, operand_two, preferred_element_type=jnp.float32)


def rows_product(operand_one, operand_two):
    return lax.dot_general(
        operand_one, operand_two, CONTRACT_ROWS, preferred_element_type=jnp.float32
    )


def last_product(operand_one, operand_two):
    return lax.dot_general(
        operand_one, operand_two, CONTRACT_LAST, preferred_element_type=jnp.float32
    )


def heads_apply(values, weight, head_count):
    token_count = values.shape[0]
    head_width = weight.shape[1]
    shaped = values.reshape(token_count, head_count, head_width)
    blocks = weight.reshape(head_count, head_width, head_width)
    mixed = jnp.einsum("thi,hij->thj", shaped, blocks, preferred_element_type=jnp.float32)
    return mixed.reshape(token_count, head_count * head_width)


def heads_back(gradients, weight, head_count):
    token_count = gradients.shape[0]
    head_width = weight.shape[1]
    shaped = gradients.reshape(token_count, head_count, head_width)
    blocks = weight.reshape(head_count, head_width, head_width)
    mixed = jnp.einsum("thj,hij->thi", shaped, blocks, preferred_element_type=jnp.float32)
    return mixed.reshape(token_count, head_count * head_width)


def heads_grad(values, gradients, head_count):
    token_count = values.shape[0]
    head_width = values.shape[1] // head_count
    left_side = values.reshape(token_count, head_count, head_width)
    right_side = gradients.reshape(token_count, head_count, head_width)
    summed = jnp.einsum("thi,thj->hij", left_side, right_side, preferred_element_type=jnp.float32)
    return summed.reshape(head_count * head_width, head_width)


def slab_count():
    for candidate in (5, 4, 2):
        return candidate
    return 1


def local(
    inputs,
    resets,
    cotangent,
    first_gain,
    branch_weight,
    input_weight,
    conv_weight,
    input_gate,
    decay_gate,
    decay_param,
    output_weight,
    second_gain,
    gate_weight,
    up_weight,
    down_weight,
):
    sources = inputs[0].astype(jnp.float32)
    flags = resets[0]
    returned = cotangent[0]
    returned_float = returned.astype(jnp.float32)
    tokens = sources.shape[0]
    shared = (
        lax.all_gather(first_gain, ("seq", "fsdp"), axis=0, tiled=True),
        lax.all_gather(branch_weight, ("seq", "fsdp"), axis=0, tiled=True),
        lax.all_gather(input_weight, ("seq", "fsdp"), axis=0, tiled=True),
        lax.all_gather(conv_weight, ("seq", "fsdp"), axis=0, tiled=True),
        lax.all_gather(input_gate, ("seq", "fsdp"), axis=0, tiled=True),
        lax.all_gather(decay_gate, ("seq", "fsdp"), axis=0, tiled=True),
        lax.all_gather(decay_param, ("seq", "fsdp"), axis=0, tiled=True),
        lax.all_gather(output_weight, ("seq", "fsdp"), axis=0, tiled=True),
        lax.all_gather(second_gain, ("seq", "fsdp"), axis=0, tiled=True),
    )
    dense_parts = (
        lax.all_gather(gate_weight, ("seq", "fsdp"), axis=0, tiled=True),
        lax.all_gather(up_weight, ("seq", "fsdp"), axis=0, tiled=True),
        lax.all_gather(down_weight, ("seq", "fsdp"), axis=0, tiled=True),
    )
    gain_first = shared[0].astype(jnp.float32)
    w_branch = shared[1]
    w_input = shared[2]
    w_conv = shared[3].astype(jnp.float32)
    w_igate = shared[4]
    w_dgate = shared[5]
    w_decay = shared[6].astype(jnp.float32)
    w_output = shared[7]
    gain_second = shared[8].astype(jnp.float32)
    w_gate = dense_parts[0]
    w_up = dense_parts[1]
    w_down = dense_parts[2]
    model_width = w_branch.shape[0]
    head_width = w_igate.shape[1]
    head_count = model_width // head_width
    tap_count = w_conv.shape[1]
    scale_one = lax.rsqrt(jnp.mean(sources * sources, axis=1, keepdims=True) + EPSILON)
    normed = (sources * scale_one * gain_first).astype(jnp.bfloat16)
    branch_pre = product(normed, w_branch)
    branch, branch_pull = jax.vjp(jax.nn.gelu, branch_pre)
    conv_in = product(normed, w_input).astype(jnp.bfloat16)
    resets_seen = jnp.cumsum(flags)
    tail_keep = resets_seen[-1] - resets_seen[tokens - tap_count + 1 :] == 0
    tail_rows = conv_in[tokens - tap_count + 1 :] * tail_keep[:, None]
    before = shifted_2(tail_rows, "seq", 1)
    padded = jnp.concatenate([before, conv_in], axis=0)
    seen_before = jnp.concatenate([jnp.zeros((tap_count - 1,), jnp.int32), resets_seen])
    conv_out = jnp.zeros((tokens, model_width), jnp.float32)
    usable_list = []
    for offset in range(tap_count):
        first_row = tap_count - 1 - offset
        shifted = padded[first_row : first_row + tokens].astype(jnp.float32)
        usable = (resets_seen - seen_before[first_row : first_row + tokens] == 0).astype(
            jnp.float32
        )[:, None]
        usable_list.append(usable)
        conv_out = conv_out + w_conv[:, offset] * shifted * usable
    rounded = conv_out.astype(jnp.bfloat16)
    rounded_float = rounded.astype(jnp.float32)
    gate_input = jax.nn.sigmoid(heads_apply(rounded, w_igate, head_count))
    gate_decay = jax.nn.sigmoid(heads_apply(rounded, w_dgate, head_count))
    softened = jax.nn.softplus(w_decay)
    log_decay = -softened * (1.0 + 7.0 * gate_decay)
    decays = jnp.exp(log_decay)
    root_term = jnp.sqrt(-jnp.expm1(2.0 * log_decay))
    restart = flags.astype(jnp.float32)[:, None]
    carried = 1.0 - restart
    scaling = restart + carried * root_term
    driven = rounded_float * gate_input * scaling
    coefficient = decays * carried
    running, local_state = lax.associative_scan(affine, (coefficient, driven), axis=0)
    unit_ones = jnp.ones((model_width,), jnp.float32)
    unit_zeros = jnp.zeros((model_width,), jnp.float32)
    incoming = entering(
        (running[-1], local_state[-1]), "seq", affine, (unit_ones, unit_zeros), False
    )
    state_in = incoming[1]
    states = local_state + running * state_in
    mixed = (states * branch).astype(jnp.bfloat16)
    resid = sources + product(mixed, w_output)
    scale_two = lax.rsqrt(jnp.mean(resid * resid, axis=1, keepdims=True) + EPSILON)
    hidden = (resid * scale_two * gain_second).astype(jnp.bfloat16)
    gate_pre = product(hidden, w_gate)
    up_values = product(hidden, w_up)
    gate_act, gate_pull = jax.vjp(jax.nn.gelu, gate_pre)
    active = (gate_act * up_values).astype(jnp.bfloat16)
    result = (resid + last_product(active, w_down)).astype(jnp.bfloat16)
    act_grad = product(returned, w_down)
    gate_grad = gate_pull(act_grad * up_values)[0].astype(jnp.bfloat16)
    up_grad = (act_grad * gate_act).astype(jnp.bfloat16)
    hidden_grad = last_product(gate_grad, w_gate) + last_product(up_grad, w_up)
    weighted_two = hidden_grad * gain_second
    resid_grad = (
        returned_float
        + scale_two * weighted_two
        - resid * scale_two**3 * jnp.mean(weighted_two * resid, axis=1, keepdims=True)
    )
    second_term = jnp.sum(hidden_grad * resid * scale_two, axis=0)
    branch_out_grad = resid_grad.astype(jnp.bfloat16)
    mixed_grad = last_product(branch_out_grad, w_output)
    state_grad = mixed_grad * branch
    branch_grad = mixed_grad * states
    branch_pre_grad = branch_pull(branch_grad)[0].astype(jnp.bfloat16)
    next_coef = jnp.concatenate([coefficient[1:], jnp.ones((1, model_width), jnp.float32)], axis=0)
    reaches, adjoint_local = lax.associative_scan(
        affine, (next_coef, state_grad), reverse=True, axis=0
    )
    carry_back = entering(
        (coefficient[0] * reaches[0], coefficient[0] * adjoint_local[0]),
        "seq",
        affine,
        (unit_ones, unit_zeros),
        True,
    )
    adjoint = adjoint_local + reaches * carry_back[1]
    earlier_state = jnp.concatenate([state_in[None], states[:-1]], axis=0)
    log_grad = (
        adjoint * earlier_state * carried * decays
        - adjoint * rounded_float * gate_input * carried * decays * decays / root_term
    )
    decay_term = jnp.sum(-log_grad * (1.0 + 7.0 * gate_decay), axis=0) * jax.nn.sigmoid(w_decay)
    input_pre_grad = (adjoint * rounded_float * scaling * gate_input * (1.0 - gate_input)).astype(
        jnp.bfloat16
    )
    decay_pre_grad = (log_grad * (-7.0 * softened) * gate_decay * (1.0 - gate_decay)).astype(
        jnp.bfloat16
    )
    conv_out_grad = (
        adjoint * gate_input * scaling
        + heads_back(input_pre_grad, w_igate, head_count)
        + heads_back(decay_pre_grad, w_dgate, head_count)
    )
    conv_grad = conv_out_grad.astype(jnp.bfloat16)
    igate_term = heads_grad(rounded, input_pre_grad, head_count)
    dgate_term = heads_grad(rounded, decay_pre_grad, head_count)
    head_keep = resets_seen[: tap_count - 1] == 0
    head_rows = conv_grad[: tap_count - 1] * head_keep[:, None]
    following = shifted_2(head_rows, "seq", -1)
    padded_back = jnp.concatenate([conv_grad, following], axis=0)
    seen_after = jnp.concatenate(
        [resets_seen, jnp.full((tap_count - 1,), resets_seen[-1], jnp.int32)]
    )
    conv_grad_float = conv_grad.astype(jnp.float32)
    conv_in_grad = jnp.zeros((tokens, model_width), jnp.float32)
    tap_terms = []
    for offset in range(tap_count):
        first_row = tap_count - 1 - offset
        shifted = padded[first_row : first_row + tokens].astype(jnp.float32)
        tap_terms.append(jnp.sum(conv_grad_float * shifted * usable_list[offset], axis=0))
        ahead_usable = (seen_after[offset : offset + tokens] - resets_seen == 0).astype(
            jnp.float32
        )[:, None]
        conv_in_grad = (
            conv_in_grad
            + w_conv[:, offset]
            * padded_back[offset : offset + tokens].astype(jnp.float32)
            * ahead_usable
        )
    tap_grad = jnp.stack(tap_terms, axis=1)
    conv_in_low = conv_in_grad.astype(jnp.bfloat16)
    normed_grad = last_product(branch_pre_grad, w_branch) + last_product(conv_in_low, w_input)
    weighted_one = normed_grad * gain_first
    source_grad = (
        resid_grad
        + scale_one * weighted_one
        - sources * scale_one**3 * jnp.mean(weighted_one * sources, axis=1, keepdims=True)
    )
    first_term = jnp.sum(normed_grad * sources * scale_one, axis=0)
    grad_inputs = source_grad.astype(jnp.bfloat16)[None]
    vector_part = jnp.concatenate(
        [
            igate_term,
            dgate_term,
            tap_grad,
            decay_term[:, None],
            first_term[:, None],
            second_term[:, None],
        ],
        axis=1,
    )
    owned_rows = gate_weight.shape[0]
    owner_count = lax.axis_size(("seq", "fsdp"))
    slab_total = slab_count()
    slab_rows = owned_rows // slab_total
    vector_shaped = vector_part.reshape(owner_count, owned_rows, vector_part.shape[1])

    def pick_rows(values, portion):
        shaped = values.reshape(values.shape[0], owner_count, owned_rows)
        taken = shaped[:, :, portion * slab_rows : (portion + 1) * slab_rows]
        return taken.reshape(values.shape[0], owner_count * slab_rows)

    gate_pieces = []
    up_pieces = []
    down_pieces = []
    branch_pieces = []
    input_pieces = []
    output_pieces = []
    vector_pieces = []
    for portion in range(slab_total):
        hidden_rows = pick_rows(hidden, portion)
        return_rows = pick_rows(returned, portion)
        dense_sums = (
            lax.psum_scatter(
                rows_product(hidden_rows, gate_grad),
                ("seq", "fsdp"),
                scatter_dimension=0,
                tiled=True,
            ),
            lax.psum_scatter(
                rows_product(hidden_rows, up_grad), ("seq", "fsdp"), scatter_dimension=0, tiled=True
            ),
            lax.psum_scatter(
                rows_product(return_rows, active), ("seq", "fsdp"), scatter_dimension=0, tiled=True
            ),
        )
        gate_pieces.append(dense_sums[0])
        up_pieces.append(dense_sums[1])
        down_pieces.append(dense_sums[2])
        normed_rows = pick_rows(normed, portion)
        mixed_rows = pick_rows(mixed, portion)
        vector_rows = vector_shaped[:, portion * slab_rows : (portion + 1) * slab_rows].reshape(
            owner_count * slab_rows, vector_part.shape[1]
        )
        mixer_sums = (
            lax.psum_scatter(
                rows_product(normed_rows, branch_pre_grad),
                ("seq", "fsdp"),
                scatter_dimension=0,
                tiled=True,
            ),
            lax.psum_scatter(
                rows_product(normed_rows, conv_in_low),
                ("seq", "fsdp"),
                scatter_dimension=0,
                tiled=True,
            ),
            lax.psum_scatter(
                rows_product(mixed_rows, branch_out_grad),
                ("seq", "fsdp"),
                scatter_dimension=0,
                tiled=True,
            ),
            lax.psum_scatter(vector_rows, ("seq", "fsdp"), scatter_dimension=0, tiled=True),
        )
        branch_pieces.append(mixer_sums[0])
        input_pieces.append(mixer_sums[1])
        output_pieces.append(mixer_sums[2])
        vector_pieces.append(mixer_sums[3])
    grad_gate = jnp.concatenate(gate_pieces, axis=0)
    grad_up = jnp.concatenate(up_pieces, axis=0)
    grad_down = jnp.concatenate(down_pieces, axis=0)
    grad_branch = jnp.concatenate(branch_pieces, axis=0)
    grad_input = jnp.concatenate(input_pieces, axis=0)
    grad_output = jnp.concatenate(output_pieces, axis=0)
    vector_sums = jnp.concatenate(vector_pieces, axis=0)
    edge_five = 2 * head_width
    edge_six = edge_five + tap_count
    grad_igate = vector_sums[:, :head_width]
    grad_dgate = vector_sums[:, head_width:edge_five]
    grad_conv = vector_sums[:, edge_five:edge_six]
    grad_decay = vector_sums[:, edge_six]
    grad_gain_first = vector_sums[:, edge_six + 1]
    grad_gain_second = vector_sums[:, edge_six + 2]
    return (
        result[None],
        grad_inputs,
        grad_gain_first,
        grad_branch,
        grad_input,
        grad_conv,
        grad_igate,
        grad_dgate,
        grad_decay,
        grad_output,
        grad_gain_second,
        grad_gate,
        grad_up,
        grad_down,
    )


CHUNK = 128
TAPS = 4


def gelu_parts(x):
    inner = 0.7978845608028654 * (x + 0.044715 * x * x * x)
    bent = jnp.tanh(inner)
    value = 0.5 * x * (1.0 + bent)
    slope = 0.5 * (1.0 + bent) + 0.5 * x * (1.0 - bent * bent) * 0.7978845608028654 * (
        1.0 + 3.0 * 0.044715 * x * x
    )
    return value, slope


def minus_expm1(x):
    series = x / 8.0 + 1.0
    for step in (7.0, 6.0, 5.0, 4.0, 3.0, 2.0):
        series = series * x / step + 1.0
    return jnp.where(x > -0.5, -x * series, 1.0 - jnp.exp(x))


def mixer_forward_kernel(
    conv_in_ref, pre_ref, mask_ref, taps_ref, igate_ref, dgate_ref, soft_ref,
    rounded_ref, gin_ref, gdec_ref, states_ref, earlier_ref, mixed_ref,
    padded, coef, drive,
):
    tokens, width = conv_in_ref.shape
    chunk = min(CHUNK, tokens)
    padded[0:8, :] = jnp.zeros((8, width), jnp.float32)
    soft = soft_ref[0:1, :]
    igate = igate_ref[...]
    dgate = dgate_ref[...]

    def fill(c, _):
        base = pl.multiple_of(c * chunk, chunk)
        padded[pl.ds(pl.multiple_of(base + 8, 8), chunk), :] = conv_in_ref[pl.ds(base, chunk), :].astype(jnp.float32)
        return 0

    lax.fori_loop(0, tokens // chunk, fill, 0)
    row = lax.broadcasted_iota(jnp.int32, (8, width), 0)

    def body(c, carry):
        base = pl.multiple_of(c * chunk, chunk)
        mask = mask_ref[pl.ds(base, chunk), :]
        span = padded[pl.ds(base, chunk + 8), :]
        out = taps_ref[0:1, :] * span[8:]
        for k in range(1, TAPS):
            out = out + taps_ref[k : k + 1, :] * span[8 - k : 8 - k + chunk] * mask[:, k : k + 1]
        rounded = out.astype(jnp.bfloat16)
        rounded_ref[pl.ds(base, chunk), :] = rounded
        gin = jax.nn.sigmoid(jnp.dot(rounded, igate, preferred_element_type=jnp.float32))
        gdec = jax.nn.sigmoid(jnp.dot(rounded, dgate, preferred_element_type=jnp.float32))
        gin_ref[pl.ds(base, chunk), :] = gin
        gdec_ref[pl.ds(base, chunk), :] = gdec
        log_decay = -soft * (1.0 + 7.0 * gdec)
        root = jnp.sqrt(minus_expm1(2.0 * log_decay))
        restart = mask[:, 0:1]
        carried = 1.0 - restart
        coef[...] = jnp.exp(log_decay) * carried
        drive[...] = rounded.astype(jnp.float32) * gin * (restart + carried * root)

        def tile(i, state):
            at = pl.multiple_of(i * 8, 8)
            a = coef[pl.ds(at, 8), :]
            b = drive[pl.ds(at, 8), :]
            for sh in (1, 2, 4):
                keep = row >= sh
                b = b + a * jnp.where(keep, pltpu.roll(b, sh, 0), 0.0)
                a = a * jnp.where(keep, pltpu.roll(a, sh, 0), 1.0)
            new = b + a * state
            states_ref[pl.ds(pl.multiple_of(base + at, 8), 8), :] = new
            earlier_ref[pl.ds(pl.multiple_of(base + at, 8), 8), :] = jnp.where(row == 0, state, pltpu.roll(new, 1, 0))
            return jnp.broadcast_to(new[7:8, :], (8, width))

        carry = lax.fori_loop(0, chunk // 8, tile, carry, unroll=True)
        branch, _ = gelu_parts(pre_ref[pl.ds(base, chunk), :])
        mixed_ref[pl.ds(base, chunk), :] = (states_ref[pl.ds(base, chunk), :] * branch).astype(jnp.bfloat16)
        return carry

    lax.fori_loop(0, tokens // chunk, body, jnp.zeros((8, width), jnp.float32))


def mixer_forward(conv_in, pre, mask, taps, igate, dgate, soft, width):
    tokens, total = conv_in.shape
    heads = total // width
    column = lambda h: (0, h)
    row = lambda h: (h, 0)
    whole = lambda h: (0, 0)
    big = pl.BlockSpec((tokens, width), column)
    shape = lambda kind: jax.ShapeDtypeStruct((tokens, total), kind)
    return pl.pallas_call(
        mixer_forward_kernel,
        grid=(heads,),
        in_specs=[
            big, big, pl.BlockSpec(mask.shape, whole), pl.BlockSpec((8, width), column),
            pl.BlockSpec((width, width), row), pl.BlockSpec((width, width), row),
            pl.BlockSpec((8, width), column),
        ],
        out_specs=[big] * 6,
        out_shape=[shape(jnp.bfloat16), shape(jnp.float32), shape(jnp.float32), shape(jnp.float32), shape(jnp.float32), shape(jnp.bfloat16)],
        scratch_shapes=[
            pltpu.VMEM((tokens + 8, width), jnp.float32),
            pltpu.VMEM((min(CHUNK, tokens), width), jnp.float32),
            pltpu.VMEM((min(CHUNK, tokens), width), jnp.float32),
        ],
        compiler_params=pltpu.CompilerParams(vmem_limit_bytes=48 * 2**20),
        name="mixer_forward",
    )(conv_in, pre, mask, taps, igate, dgate, soft)


def mixer_backward_kernel(
    grad_ref, pre_ref, states_ref, earlier_ref, rounded_ref, gin_ref, gdec_ref, conv_in_ref, mask_ref, ahead_ref,
    taps_ref, igate_ref, dgate_ref, soft_ref, own_ref,
    bpg_ref, cig_ref, igrad_ref, dgrad_ref, tapgrad_ref,
    padded, ahead_pad, coef, drive, decay_sum, tap_sum,
):
    tokens, width = grad_ref.shape
    chunk = min(CHUNK, tokens)
    count = tokens // chunk
    padded[0:8, :] = jnp.zeros((8, width), jnp.float32)
    ahead_pad[tokens : tokens + 8, :] = jnp.zeros((8, width), jnp.float32)
    soft = soft_ref[0:1, :]
    own = own_ref[0:1, :]
    igate = igate_ref[...]
    dgate = dgate_ref[...]
    igrad_ref[...] = jnp.zeros_like(igrad_ref)
    dgrad_ref[...] = jnp.zeros_like(dgrad_ref)
    decay_sum[...] = jnp.zeros_like(decay_sum)
    tap_sum[...] = jnp.zeros_like(tap_sum)
    row = lax.broadcasted_iota(jnp.int32, (8, width), 0)
    rows_dot = lambda a, b: lax.dot_general(a, b, (((0,), (0,)), ((), ())), preferred_element_type=jnp.float32)
    last_dot = lambda a, b: lax.dot_general(a, b, (((1,), (1,)), ((), ())), preferred_element_type=jnp.float32)

    def body(step, carry):
        c = count - 1 - step
        base = pl.multiple_of(c * chunk, chunk)
        here = pl.ds(base, chunk)
        padded[pl.ds(pl.multiple_of(base + 8, 8), chunk), :] = conv_in_ref[here, :].astype(jnp.float32)
        mask = mask_ref[here, :]
        restart = mask[:, 0:1]
        carried = 1.0 - restart
        branch, slope = gelu_parts(pre_ref[here, :])
        grad = grad_ref[here, :]
        bpg_ref[here, :] = (grad * states_ref[here, :] * slope * own).astype(jnp.bfloat16)
        gdec = gdec_ref[here, :]
        gin = gin_ref[here, :]
        log_decay = -soft * (1.0 + 7.0 * gdec)
        decays = jnp.exp(log_decay)
        root = jnp.sqrt(minus_expm1(2.0 * log_decay))
        coef[...] = decays * carried
        drive[...] = grad * branch

        def tile(i, pair):
            adj_next, coef_next = pair
            at = pl.multiple_of(chunk - 8 - i * 8, 8)
            first = coef[pl.ds(at, 8), :]
            a = jnp.where(row == 7, coef_next, pltpu.roll(first, 7, 0))
            b = drive[pl.ds(at, 8), :]
            for sh in (1, 2, 4):
                keep = row < 8 - sh
                b = b + a * jnp.where(keep, pltpu.roll(b, 8 - sh, 0), 0.0)
                a = a * jnp.where(keep, pltpu.roll(a, 8 - sh, 0), 1.0)
            new = b + a * adj_next
            drive[pl.ds(at, 8), :] = new
            return jnp.broadcast_to(new[0:1, :], (8, width)), jnp.broadcast_to(first[0:1, :], (8, width))

        carry = lax.fori_loop(0, chunk // 8, tile, carry, unroll=True)
        adjoint = drive[...]
        rounded = rounded_ref[here, :]
        rounded_float = rounded.astype(jnp.float32)
        pull = adjoint * carried * decays
        log_grad = pull * (earlier_ref[here, :] - rounded_float * gin * decays / root)
        decay_sum[...] += jnp.sum((-log_grad * (1.0 + 7.0 * gdec)).reshape(chunk // 8, 8, width), axis=0)
        through = adjoint * gin * (restart + carried * root)
        ipg = (through * rounded_float * (1.0 - gin)).astype(jnp.bfloat16)
        dpg = (log_grad * (-7.0 * soft) * gdec * (1.0 - gdec)).astype(jnp.bfloat16)
        igrad_ref[...] += rows_dot(rounded, ipg)
        dgrad_ref[...] += rows_dot(rounded, dpg)
        through = through + last_dot(ipg, igate) + last_dot(dpg, dgate)
        ahead_pad[here, :] = through.astype(jnp.bfloat16).astype(jnp.float32)
        return carry

    zero = jnp.zeros((8, width), jnp.float32)
    lax.fori_loop(0, count, body, (zero, zero))

    def after(c, _):
        base = pl.multiple_of(c * chunk, chunk)
        here = pl.ds(base, chunk)
        mask = mask_ref[here, :]
        ahead = ahead_ref[here, :]
        later = ahead_pad[pl.ds(base, chunk + 8), :]
        span = padded[pl.ds(base, chunk + 8), :]
        grad = later[:chunk]
        total = taps_ref[0:1, :] * grad
        tap_sum[0:8, :] += jnp.sum((grad * span[8:]).reshape(chunk // 8, 8, width), axis=0)
        for k in range(1, TAPS):
            total = total + taps_ref[k : k + 1, :] * later[k : k + chunk] * ahead[:, k : k + 1]
            shifted = span[8 - k : 8 - k + chunk]
            tap_sum[8 * k : 8 * k + 8, :] += jnp.sum((grad * shifted * mask[:, k : k + 1]).reshape(chunk // 8, 8, width), axis=0)
        cig_ref[here, :] = (total * own).astype(jnp.bfloat16)
        return 0

    lax.fori_loop(0, count, after, 0)
    for k in range(TAPS):
        tapgrad_ref[k : k + 1, :] = jnp.sum(tap_sum[8 * k : 8 * k + 8, :], axis=0, keepdims=True)
    tapgrad_ref[4:5, :] = jnp.sum(decay_sum[...], axis=0, keepdims=True)
    tapgrad_ref[5:8, :] = jnp.zeros((3, width), jnp.float32)


def mixer_backward(grad, pre, states, earlier, rounded, gin, gdec, conv_in, mask, ahead, taps, igate, dgate, soft, own, width):
    tokens, total = grad.shape
    heads = total // width
    column = lambda h: (0, h)
    row = lambda h: (h, 0)
    whole = lambda h: (0, 0)
    big = pl.BlockSpec((tokens, width), column)
    line = pl.BlockSpec((8, width), column)
    square = pl.BlockSpec((width, width), row)
    shape = lambda kind: jax.ShapeDtypeStruct((tokens, total), kind)
    chunk = min(CHUNK, tokens)
    return pl.pallas_call(
        mixer_backward_kernel,
        grid=(heads,),
        in_specs=[big] * 8 + [pl.BlockSpec(mask.shape, whole)] * 2 + [line, square, square, line, line],
        out_specs=[big, big, square, square, line],
        out_shape=[
            shape(jnp.bfloat16), shape(jnp.bfloat16),
            jax.ShapeDtypeStruct((total, width), jnp.float32), jax.ShapeDtypeStruct((total, width), jnp.float32),
            jax.ShapeDtypeStruct((8, total), jnp.float32),
        ],
        scratch_shapes=[
            pltpu.VMEM((tokens + 8, width), jnp.float32),
            pltpu.VMEM((tokens + 8, width), jnp.float32),
            pltpu.VMEM((chunk, width), jnp.float32),
            pltpu.VMEM((chunk, width), jnp.float32),
            pltpu.VMEM((8, width), jnp.float32),
            pltpu.VMEM((8 * TAPS, width), jnp.float32),
        ],
        compiler_params=pltpu.CompilerParams(vmem_limit_bytes=56 * 2**20),
        name="mixer_backward",
    )(grad, pre, states, earlier, rounded, gin, gdec, conv_in, mask, ahead, taps, igate, dgate, soft, own)


MESH_ID = pl.DeviceIdType.MESH
PIECES = 4


class Spot:
    def __init__(self):
        self.s = lax.axis_index("seq")
        self.f = lax.axis_index("fsdp")
        self.z = self.s // 2
        self.y = self.s % 2
        self.up = (self.z < 3, (jnp.minimum(self.s + 2, 7), self.f))
        self.down = (self.z > 0, (jnp.maximum(self.s - 2, 0), self.f))
        self.beside = (None, (self.s ^ 1, self.f))
        self.across = (None, (self.s, self.f ^ 2))
        self.twin = (None, (self.s, self.f ^ 1))

    def peer(self, j):
        return (None, (self.s ^ j, self.f))

    def other(self, j):
        return (None, (self.s ^ (j // 4), self.f ^ (j % 4)))

    def meet(self, reach):
        barrier = pltpu.get_barrier_semaphore()
        if "all" in reach:
            peers = [self.other(j) for j in range(1, 32)]
        else:
            peers = [self.peer(j) for j in range(1, 8)] if "seq" in reach else []
            if "line" in reach and not peers:
                peers = [self.up, self.down, self.beside]
            if "pair" in reach:
                peers += [self.across, self.twin]
        count = 0
        for cond, where in peers:
            count = count + (1 if cond is None else cond.astype(jnp.int32))
            guarded(cond, lambda: pl.semaphore_signal(barrier, 1, device_id=where, device_id_type=MESH_ID))
        pl.semaphore_wait(barrier, count)


def guarded(cond, action):
    if cond is None:
        action()
    else:
        pl.when(cond)(action)


class Send:
    def __init__(self, src, dst, send_sem, recv_sem, target):
        self.cond, where = target
        self.copy = pltpu.make_async_remote_copy(
            src_ref=src, dst_ref=dst, send_sem=send_sem, recv_sem=recv_sem, device_id=where, device_id_type=MESH_ID
        )

    def start(self):
        guarded(self.cond, self.copy.start)

    def sent(self):
        guarded(self.cond, self.copy.wait_send)


def arrived(dst, send_sem, recv_sem, target, cond=None):
    copy = pltpu.make_async_remote_copy(
        src_ref=dst, dst_ref=dst, send_sem=send_sem, recv_sem=recv_sem, device_id=target[1], device_id_type=MESH_ID
    )
    guarded(cond, copy.wait_recv)


class Gather:
    letter = "g"
    def __init__(self, x):
        self.ins = [x]
        self.outs = [jax.ShapeDtypeStruct((8,) + x.shape, x.dtype)]
        dma = pltpu.SemaphoreType.DMA
        self.scratch = [dma((1,)), dma((8, PIECES)), dma((4, PIECES)), dma((4, PIECES)), dma((7, PIECES))]

    reach = ("line",)

    def steps(self, at, ins, outs, scratch):
        (x,), (o,) = ins, outs
        own_sem, recv, ups, downs, sides = scratch
        rows = x.shape[0] // PIECES
        cut = lambda p: pl.ds(p * rows, rows)
        sends = []

        def send(src, block, p, sem, target):
            one = Send(src, o.at[block, cut(p)], sem, recv.at[block, p], target)
            one.start()
            sends.append(one)

        own = pltpu.make_async_copy(x, o.at[at.s], own_sem.at[0])
        own.start()
        for p in range(PIECES):
            send(x.at[cut(p)], at.s, p, ups.at[0, p], at.up)
            send(x.at[cut(p)], at.s, p, downs.at[0, p], at.down)
            send(x.at[cut(p)], at.s, p, sides.at[0, p], at.beside)
        yield
        for d in range(1, 4):
            for p in range(PIECES):
                low, high = at.z >= d, at.z + d <= 3
                block = jnp.maximum(at.s - 2 * d, 0)
                arrived(o.at[block, cut(p)], ups.at[0, p], recv.at[block, p], at.down, low)
                if d < 3:
                    send(o.at[block, cut(p)], block, p, ups.at[d, p], (low & (at.z < 3), at.up[1]))
                send(o.at[block, cut(p)], block, p, sides.at[d, p], (low, at.beside[1]))
                block = jnp.minimum(at.s + 2 * d, 7)
                arrived(o.at[block, cut(p)], ups.at[0, p], recv.at[block, p], at.up, high)
                if d < 3:
                    send(o.at[block, cut(p)], block, p, downs.at[d, p], (high & (at.z > 0), at.down[1]))
                send(o.at[block, cut(p)], block, p, sides.at[3 + d, p], (high, at.beside[1]))
                yield
        for z in range(4):
            for p in range(PIECES):
                block = 2 * z + 1 - at.y
                arrived(o.at[block, cut(p)], ups.at[0, p], recv.at[block, p], at.beside)
        yield
        for one in sends:
            one.sent()
        own.wait()


class Reduce:
    letter = "r"
    def __init__(self, x):
        _, rows, width = x.shape
        self.ins = [x]
        self.outs = [jax.ShapeDtypeStruct((rows, width), jnp.float32)]
        dma = pltpu.SemaphoreType.DMA
        hold = pltpu.VMEM((4, rows, width), x.dtype)
        self.scratch = [hold, hold, hold, hold, pltpu.VMEM((rows, width), jnp.float32)]
        self.scratch += [dma((4, PIECES)) for _ in range(6)] + [dma((1,))]

    reach = ("line",)

    def steps(self, at, ins, outs, scratch):
        (x,), (o,) = ins, outs
        mine, side, below, above, total, load, ysend, yrecv, zsend, urecv, drecv, osem = scratch
        rows = x.shape[1] // PIECES
        cut = lambda p: pl.ds(p * rows, rows)
        group = 16
        sends = []
        order = []
        for k in range(3):
            order.append((3 - k, at.z < 3 - k, True))
            order.append((k, at.z > k, False))
        order.append((at.z, None, None))

        loads = []
        for t, cond, _ in order:
            for p in range(PIECES):
                one = Send(x.at[2 * t + 1 - at.y, cut(p)], side.at[t, cut(p)], ysend.at[t, p], yrecv.at[t, p], (cond, at.beside[1]))
                one.start()
                sends.append(one)
                copy = pltpu.make_async_copy(x.at[2 * t + at.y, cut(p)], mine.at[t, cut(p)], load.at[t, p])
                guarded(cond, copy.start)
        yield
        for t, cond, rising in order:
            for p in range(PIECES):
                copy = pltpu.make_async_copy(x.at[2 * t + at.y, cut(p)], mine.at[t, cut(p)], load.at[t, p])
                guarded(cond, copy.wait)
                arrived(side.at[t, cut(p)], ysend.at[t, p], yrecv.at[t, p], at.beside, cond)
                if rising is None:
                    arrived(below.at[t, cut(p)], zsend.at[t, p], urecv.at[t, p], at.down, at.z > 0)
                    arrived(above.at[t, cut(p)], zsend.at[t, p], drecv.at[t, p], at.up, at.z < 3)

                    def final(i, _):
                        here = pl.ds(pl.multiple_of(p * rows + i * group, group), group)
                        value = mine[t, here, :].astype(jnp.float32) + side[t, here, :].astype(jnp.float32)
                        total[here, :] = value

                        @pl.when(at.z > 0)
                        def _():
                            total[here, :] += below[t, here, :].astype(jnp.float32)

                        @pl.when(at.z < 3)
                        def _():
                            total[here, :] += above[t, here, :].astype(jnp.float32)

                        return 0

                    lax.fori_loop(0, rows // group, final, 0)
                else:
                    source = below if rising else above
                    inner = (cond & (at.z > 0)) if rising else (cond & (at.z < 3))
                    outer = (cond & (at.z == 0)) if rising else (cond & (at.z == 3))
                    rsem = urecv if rising else drecv
                    arrived(source.at[t, cut(p)], zsend.at[t, p], rsem.at[t, p], at.down if rising else at.up, inner)

                    def add(with_source):
                        def one(i, _):
                            here = pl.ds(pl.multiple_of(p * rows + i * group, group), group)
                            value = mine[t, here, :].astype(jnp.float32) + side[t, here, :].astype(jnp.float32)
                            if with_source:
                                value = value + source[t, here, :].astype(jnp.float32)
                            mine[t, here, :] = value.astype(mine.dtype)
                            return 0

                        lax.fori_loop(0, rows // group, one, 0)

                    pl.when(inner)(lambda: add(True))
                    pl.when(outer)(lambda: add(False))
                    one = Send(mine.at[t, cut(p)], source.at[t, cut(p)], zsend.at[t, p], rsem.at[t, p], (cond, (at.up if rising else at.down)[1]))
                    one.start()
                    sends.append(one)
                yield
        out = pltpu.make_async_copy(total, o, osem.at[0])
        out.start()
        for one in sends:
            one.sent()
        out.wait()


class Spread:
    letter = "s"
    reach = ("seq", "pair")

    def __init__(self, x, starts, wide, letter="s"):
        self.ins = [x]
        self.starts, self.wide, self.letter = starts, wide, letter
        self.outs = [jax.ShapeDtypeStruct((8, 4, x.shape[0], wide), x.dtype)]
        dma = pltpu.SemaphoreType.DMA
        self.scratch = [dma((8,)), dma((8,)), dma((8,)), dma((8,)), dma((8, 2)), dma((8, 2))]

    def steps(self, at, ins, outs, scratch):
        (x,), (o,) = ins, outs
        asend, arecv, xsend, xrecv, csend, crecv = scratch
        sends = []
        part = lambda to: x.at[:, pl.ds(pl.multiple_of(self.starts(to), 128), self.wide)]

        def send(src, dst, ss, rs, target):
            one = Send(src, dst, ss, rs, target)
            one.start()
            sends.append(one)

        for j in range(1, 8):
            send(part(at.s ^ j), o.at[at.s, at.f], asend.at[j], arecv.at[j], at.peer(j))
        own = pltpu.make_async_copy(part(at.s), o.at[at.s, at.f], asend.at[0])
        own.start()
        yield
        for j in range(8):
            block = at.s ^ j
            here = o.at[block, at.f]
            if j == 0:
                own.wait()
            else:
                arrived(here, asend.at[j], arecv.at[j], at.peer(j))
            send(here, here, xsend.at[j], xrecv.at[j], at.across)
            send(here, here, csend.at[j, 0], crecv.at[j, 0], at.twin)
            yield
        for j in range(8):
            there = o.at[at.s ^ j, at.f ^ 2]
            arrived(there, xsend.at[j], xrecv.at[j], at.across)
            send(there, there, csend.at[j, 1], crecv.at[j, 1], at.twin)
            yield
        for j in range(8):
            for k in range(2):
                arrived(o.at[at.s ^ j, (at.f ^ 1) ^ (2 * k)], csend.at[j, k], crecv.at[j, k], at.twin)
        for one in sends:
            one.sent()


def add_rows(dst, terms, rows):
    group = 16

    def one(i, _):
        here = pl.ds(pl.multiple_of(i * group, group), group)
        value = terms[0][here, :].astype(jnp.float32)
        for term in terms[1:]:
            value = value + term[here, :].astype(jnp.float32)
        dst[here, :] = value.astype(dst.dtype)
        return 0

    lax.fori_loop(0, rows // group, one, 0)


class Collect:
    letter = "c"
    def __init__(self, x, window=None):
        self.window = window
        blocks, rows, width = (1, window.rows, x.shape[1]) if window else (x.shape[0],) + x.shape[2:]
        self.shape = (blocks, rows, width)
        self.ins = [x]
        self.blocks = blocks
        self.reach = ("seq", "pair") if blocks > 1 else ("pair",)
        self.outs = [jax.ShapeDtypeStruct((blocks, rows, width), x.dtype)]
        dma = pltpu.SemaphoreType.DMA
        hold = pltpu.VMEM((blocks, rows, width), x.dtype)
        self.scratch = [pltpu.VMEM((2, rows, width), x.dtype)] + [hold] * 3 + [dma((2,))] + [dma((blocks, 2))] * 2 + [dma((blocks,))] * 4

    def steps(self, at, ins, outs, scratch):
        (x,), (o,) = ins, outs
        stage, tnear, tfar, xin, lsem, csend, crecv, xsend, xrecv, asend, arecv = scratch
        rows = self.shape[1]
        many = self.blocks > 1
        spot = (lambda j: at.s ^ j) if many else (lambda j: j)
        sends = []

        def part(j, whose):
            if self.window is None:
                return x.at[spot(j), whose]
            return x.at[pl.ds(pl.multiple_of(self.window.offset(at.s) + rows * whose, 16), rows)]

        def send(src, dst, ss, rs, target):
            one = Send(src, dst, ss, rs, target)
            one.start()
            sends.append(one)

        order = [j for j in range(1, 8)] + [0] if many else [0]
        pieces = [(j, at.f ^ 2) for j in order] + [(j, at.f) for j in order]

        def load(i):
            j, whose = pieces[i]
            return pltpu.make_async_copy(part(j, whose), stage.at[i % 2], lsem.at[i % 2])

        for j in order:
            send(part(j, at.f ^ 3), tfar.at[j], csend.at[j, 0], crecv.at[j, 0], at.twin)
            send(part(j, at.f ^ 1), tnear.at[j], csend.at[j, 1], crecv.at[j, 1], at.twin)
        load(0).start()
        yield
        outs_done = []
        for i, (j, _) in enumerate(pieces):
            far = i < len(order)
            if i + 1 < len(pieces):
                load(i + 1).start()
            load(i).wait()
            if far:
                arrived(tfar.at[j], csend.at[j, 0], crecv.at[j, 0], at.twin)
                add_rows(tfar.at[j], (tfar.at[j], stage.at[i % 2]), rows)
                send(tfar.at[j], xin.at[j], xsend.at[j], xrecv.at[j], at.across)
            else:
                arrived(tnear.at[j], csend.at[j, 1], crecv.at[j, 1], at.twin)
                arrived(xin.at[j], xsend.at[j], xrecv.at[j], at.across)
                add_rows(tnear.at[j], (tnear.at[j], stage.at[i % 2], xin.at[j]), rows)
                if j:
                    send(tnear.at[j], o.at[at.s], asend.at[j], arecv.at[j], at.peer(j))
                else:
                    outs_done.append(pltpu.make_async_copy(tnear.at[0], o.at[at.s if many else 0], asend.at[0]))
                    outs_done[-1].start()
            yield
        for j in order:
            if j:
                arrived(o.at[at.s ^ j], asend.at[j], arecv.at[j], at.peer(j))
        for one in sends:
            one.sent()
        for one in outs_done:
            one.wait()


class Tiny:
    letter = "t"
    def __init__(self, x):
        self.ins = [x]
        self.outs = [jax.ShapeDtypeStruct((32,) + x.shape[1:], x.dtype)]
        self.same = x.shape[0] == 1
        dma = pltpu.SemaphoreType.DMA
        self.scratch = [dma((32,)), dma((32,))]

    reach = ("all",)

    def steps(self, at, ins, outs, scratch):
        (x,), (o,) = ins, outs
        ss, rs = scratch
        me = at.s * 4 + at.f
        part = lambda to: x.at[0] if self.same else x.at[to]
        sends = []
        for j in range(1, 32):
            one = Send(part(me ^ j), o.at[me], ss.at[j], rs.at[j], at.other(j))
            one.start()
            sends.append(one)
        own = pltpu.make_async_copy(part(me), o.at[me], ss.at[0])
        own.start()
        for _ in range(40):
            yield
        for j in range(1, 32):
            arrived(o.at[me ^ j], ss.at[j], rs.at[j], at.other(j))
        for one in sends:
            one.sent()
        own.wait()


class Chain:
    @staticmethod
    def scratch(rows, width, kind):
        dma = pltpu.SemaphoreType.DMA
        return [
            pltpu.VMEM((4, rows, width), kind),
            pltpu.VMEM((5, rows, width), kind),
            pltpu.VMEM((rows, width), jnp.float32),
            dma((4, PIECES)),
            dma((4, PIECES)),
            dma((4, PIECES)),
            dma((5, PIECES)),
            dma((1,)),
        ]

    def __init__(self, at, parts, out, scratch, order):
        self.at, self.parts, self.out, self.order = at, parts, out, order
        self.side, self.inflow, self.total, self.ysend, self.yrecv, self.zsend, self.zrecv, self.osem = scratch
        self.rows = parts.shape[1] // PIECES

    def cut(self, p):
        return pl.ds(pl.multiple_of(p * self.rows, self.rows), self.rows)

    def side_copy(self, t, p):
        at = self.at
        return Send(
            self.parts.at[2 * t + 1 - at.y, self.cut(p)], self.side.at[t, self.cut(p)], self.ysend.at[t, p], self.yrecv.at[t, p], at.beside
        )

    def send_side(self, t):
        for p in range(PIECES):
            self.side_copy(t, p).start()

    def z_copy(self, t, p, rising):
        at = self.at
        slot = t if rising else jnp.where(t == at.z - 1, 4, t)
        mine = self.parts.at[2 * t + at.y, self.cut(p)]
        target = (None, (at.up if rising else at.down)[1])
        return Send(mine, self.inflow.at[slot, self.cut(p)], self.zsend.at[t, p], self.zrecv.at[slot, p], target)

    def wait_side(self, t, p):
        arrived(self.side.at[t, self.cut(p)], self.ysend.at[t, p], self.yrecv.at[t, p], self.at.beside)

    def wait_inflow(self, slot, p):
        arrived(self.inflow.at[slot, self.cut(p)], self.zsend.at[0, p], self.zrecv.at[slot, p], self.at.down)

    def step(self, k, p):
        at = self.at
        group = 16
        rises, falls = self.order(k)
        for t, cond, rising in ((rises, at.z < rises, True), (falls, at.z > falls, False)):

            @pl.when(cond)
            def _():
                self.wait_side(t, p)
                first = at.z == (0 if rising else 3)

                def add(inner):
                    def one(i, _):
                        here = pl.ds(pl.multiple_of(p * self.rows + i * group, group), group)
                        value = self.parts[2 * t + at.y, here, :].astype(jnp.float32) + self.side[t, here, :].astype(jnp.float32)
                        if inner:
                            value = value + self.inflow[t, here, :].astype(jnp.float32)
                        self.parts[2 * t + at.y, here, :] = value.astype(self.parts.dtype)
                        return 0

                    lax.fori_loop(0, self.rows // group, one, 0)

                pl.when(first)(lambda: add(False))

                @pl.when(jnp.logical_not(first))
                def _():
                    self.wait_inflow(t, p)
                    add(True)

                self.z_copy(t, p, rising).start()

    def last(self, p):
        at = self.at
        group = 16
        self.wait_side(at.z, p)
        pl.when(at.z > 0)(lambda: self.wait_inflow(at.z, p))
        pl.when(at.z < 3)(lambda: self.wait_inflow(4, p))

        def one(i, _):
            here = pl.ds(pl.multiple_of(p * self.rows + i * group, group), group)
            self.total[here, :] = self.parts[at.s, here, :].astype(jnp.float32) + self.side[at.z, here, :].astype(jnp.float32)

            @pl.when(at.z > 0)
            def _():
                self.total[here, :] += self.inflow[at.z, here, :].astype(jnp.float32)

            @pl.when(at.z < 3)
            def _():
                self.total[here, :] += self.inflow[4, here, :].astype(jnp.float32)

            return 0

        lax.fori_loop(0, self.rows // group, one, 0)

    def finish(self):
        def one(p, _):
            self.last(p)
            return 0

        lax.fori_loop(0, PIECES, one, 0)
        self.out_copy().start()

    def out_copy(self):
        return pltpu.make_async_copy(self.total, self.out, self.osem.at[0])

    def sent(self):
        def one(i, _):
            t, p = i // PIECES, lax.rem(i, PIECES)
            self.side_copy(t, p).sent()

            @pl.when(t != self.at.z)
            def _():
                self.z_copy(t, p, True).sent()

            return 0

        lax.fori_loop(0, 4 * PIECES, one, 0)
        self.out_copy().wait()


def outward(k):
    rises = jnp.where(k == 0, 1, jnp.where(k == 1, 3, 2))
    return rises, 3 - rises


def farthest(k):
    return 3 - k, k


def descending(k):
    return 3 - k, (2, 0, 1)[k]


class Dense:
    letter = "d"
    reach = ("line",)

    def __init__(self, hidden, returned, w_gate, w_up, w_down, held):
        rows, width = hidden.shape
        wide = w_gate.shape[1]
        low = hidden.dtype
        dma = pltpu.SemaphoreType.DMA
        self.ins = [hidden, returned, w_gate, w_up, w_down, held]
        sums = jax.ShapeDtypeStruct((rows, width), jnp.float32)
        grad = jax.ShapeDtypeStruct((width, wide), low)
        self.outs = [sums, jax.ShapeDtypeStruct((8, rows, width), low), grad, grad, grad]
        tokens = pltpu.VMEM((8, rows, width), low)
        weight = pltpu.VMEM((width, wide), low)
        inner = pltpu.VMEM((8, rows, wide), low)
        self.own = [tokens, tokens, weight, weight, weight, inner, inner, inner, tokens, tokens, pltpu.VMEM(held.shape, held.dtype), dma((8,))]
        self.gather = Gather(hidden)
        self.chain = Chain.scratch(rows, width, low)
        self.scratch = self.own + self.gather.scratch + self.chain

    def steps(self, at, ins, outs, scratch):
        hidden, returned, w_gate, w_up, w_down, held = ins
        count = len(self.own)
        toks, cots, wg, wu, wd, act, ggrad, ugrad, hpart, rpart, mask, sems = scratch[:count]
        scratch = scratch[count:]
        gsems, scratch = scratch[: len(self.gather.scratch)], scratch[len(self.gather.scratch) :]
        hchain = Chain(at, hpart, outs[0], scratch, outward)
        rows, width = hidden.shape
        wide = w_gate.shape[1]
        tile = 256
        loads = [
            pltpu.make_async_copy(src, dst, sems.at[i])
            for i, (src, dst) in enumerate(((w_gate, wg), (w_up, wu), (w_down, wd), (returned, cots), (held, mask)))
        ]
        relay = Relay(at, hidden, toks, gsems)
        relay.begin()
        for load in loads:
            load.start()
        yield
        for p in range(PIECES):
            relay.step(1, p)
        for load in loads:
            load.wait()
        relay.own_copy().wait()
        last_dot = lambda a, b: lax.dot_general(a, b, CONTRACT_LAST, preferred_element_type=jnp.float32)
        rows_dot = lambda a, b: lax.dot_general(a, b, CONTRACT_ROWS, preferred_element_type=jnp.float32)

        def pair(i, _):
            far = at.z < 2
            t = jnp.where(
                i == 0, at.z, jnp.where(i == 1, at.z ^ 1, jnp.where(i == 2, jnp.where(far, 2, 1), jnp.where(far, 3, 0)))
            )
            relay.wait_beside(t)

            @pl.when(i == 3)
            def _():
                hchain.send_side(at.z ^ 1)

            both = pl.ds(2 * t, 2)

            def first(n, _):
                lanes = pl.ds(pl.multiple_of(n * tile, tile), tile)
                h = toks[both].reshape(2 * rows, width)
                c = cots[both].reshape(2 * rows, width)
                pre = jnp.dot(h, wg[:, lanes], preferred_element_type=jnp.float32)
                up = jnp.dot(h, wu[:, lanes], preferred_element_type=jnp.float32)
                grad = jnp.dot(c, wd[:, lanes], preferred_element_type=jnp.float32)
                value, slope = gelu_parts(pre)
                keep = mask[0:1, lanes]
                put = lambda ref, v: ref.__setitem__((both, slice(None), lanes), v.astype(ref.dtype).reshape(2, rows, tile))
                put(act, value * up * keep)
                put(ggrad, grad * up * slope * keep)
                put(ugrad, grad * value * keep)
                pl.when(n == 1)(lambda: relay.step(i + 2, 0))
                pl.when(n == 3)(lambda: relay.step(i + 2, 1))
                return 0

            lax.fori_loop(0, wide // tile, first, 0)

            def second(n, _):
                lanes = pl.ds(pl.multiple_of(n * tile, tile), tile)
                a = act[both].reshape(2 * rows, wide)
                g = ggrad[both].reshape(2 * rows, wide)
                u = ugrad[both].reshape(2 * rows, wide)
                put = lambda ref, v: ref.__setitem__((both, slice(None), lanes), v.astype(ref.dtype).reshape(2, rows, tile))
                put(hpart, last_dot(g, wg[lanes, :]) + last_dot(u, wu[lanes, :]))
                put(rpart, last_dot(a, wd[lanes, :]))
                pl.when(n == 2)(lambda: relay.step(i + 2, 2))
                pl.when(n == 6)(lambda: relay.step(i + 2, 3))
                return 0

            lax.fori_loop(0, width // tile, second, 0)
            return 0

        lax.fori_loop(0, 4, pair, 0)
        hchain.send_side(jnp.where(at.z < 2, 3, 0))
        hchain.send_side(jnp.where(at.z < 2, 2, 1))
        hchain.send_side(at.z)
        out = pltpu.make_async_copy(rpart, outs[1], sems.at[7])
        out.start()

        def grads(r):
            lanes = pl.ds(pl.multiple_of(r * tile, tile), tile)
            h = toks[:, :, lanes].reshape(8 * rows, tile)
            c = cots[:, :, lanes].reshape(8 * rows, tile)
            wg[lanes, :] = rows_dot(h, ggrad[...].reshape(8 * rows, wide)).astype(wg.dtype)
            wu[lanes, :] = rows_dot(h, ugrad[...].reshape(8 * rows, wide)).astype(wu.dtype)
            wd[lanes, :] = rows_dot(c, act[...].reshape(8 * rows, wide)).astype(wd.dtype)

        def hstep(i, _):
            hchain.step(i // PIECES, lax.rem(i, PIECES))
            pl.when(i < width // tile)(lambda: grads(i))
            return 0

        lax.fori_loop(0, 3 * PIECES, hstep, 0)
        hchain.finish()
        stores = [pltpu.make_async_copy(src, dst, sems.at[i]) for i, (src, dst) in enumerate(((wg, outs[2]), (wu, outs[3]), (wd, outs[4])))]
        for store in stores:
            store.start()
        hchain.sent()
        relay.sent()
        for store in stores + [out]:
            store.wait()
        yield


class Relay:
    def __init__(self, at, x, o, sems):
        self.at, self.x, self.o = at, x, o
        self.own_sem, self.recv, self.ups, self.downs, self.sides = sems
        self.rows = x.shape[0] // PIECES

    def cut(self, p):
        return pl.ds(p * self.rows, self.rows)

    def copy(self, src, block, p, sem, target):
        return Send(src, self.o.at[block, self.cut(p)], sem, self.recv.at[block, p], target)

    def own_copy(self):
        return pltpu.make_async_copy(self.x, self.o.at[self.at.s], self.own_sem.at[0])

    def begin(self):
        at = self.at
        self.own_copy().start()
        for p in range(PIECES):
            src = self.x.at[self.cut(p)]
            self.copy(src, at.s, p, self.ups.at[0, p], at.up).start()
            self.copy(src, at.s, p, self.downs.at[0, p], at.down).start()
            self.copy(src, at.s, p, self.sides.at[0, p], at.beside).start()

    def halves(self, d):
        at = self.at
        low = (at.z >= d, jnp.maximum(at.s - 2 * d, 0), self.ups, at.up, d, at.down)
        high = (at.z + d <= 3, jnp.minimum(at.s + 2 * d, 7), self.downs, at.down, 3 + d, at.up)
        return low, high

    def step(self, d, p):
        for cond, block, along, ahead, slot, source in self.halves(d):

            @pl.when(cond)
            def _():
                here = self.o.at[block, self.cut(p)]
                arrived(here, self.ups.at[0, p], self.recv.at[block, p], source)
                self.copy(here, block, p, along.at[d, p], ahead).start()
                self.copy(here, block, p, self.sides.at[slot, p], self.at.beside).start()

    def begin_rising(self):
        at = self.at
        self.own_copy().start()
        for p in range(PIECES):
            src = self.x.at[self.cut(p)]
            self.copy(src, at.s, p, self.ups.at[0, p], at.up).start()
            self.copy(src, at.s, p, self.sides.at[0, p], at.beside).start()

    def take(self, half, d, p):
        cond, block, along, ahead, slot, source = half

        @pl.when(cond)
        def _():
            here = self.o.at[block, self.cut(p)]
            arrived(here, self.ups.at[0, p], self.recv.at[block, p], source)
            self.copy(here, block, p, along.at[d, p], ahead).start()
            self.copy(here, block, p, self.sides.at[slot, p], self.at.beside).start()

    def step_up(self, d, p):
        self.take(self.halves(d)[0], d, p)

    def step_down(self, k, p):
        at = self.at
        d = jnp.maximum(3 - k - at.z, 0)
        high = self.halves(d)[1]
        self.take((at.z < 3 - k,) + high[1:], d, p)

    def own_down(self, top):
        at = self.at
        for p in range(PIECES):

            @pl.when(at.z == 3 if top else at.z < 3)
            def _():
                self.copy(self.x.at[self.cut(p)], at.s, p, self.downs.at[0, p], at.down).start()

    def wait_beside(self, t):
        block = 2 * t + 1 - self.at.y
        for p in range(PIECES):
            arrived(self.o.at[block, self.cut(p)], self.ups.at[0, p], self.recv.at[block, p], self.at.beside)

    def sent(self):
        at = self.at
        for p in range(PIECES):
            src = self.x.at[self.cut(p)]
            self.copy(src, at.s, p, self.ups.at[0, p], at.up).sent()
            self.copy(src, at.s, p, self.downs.at[0, p], at.down).sent()
            self.copy(src, at.s, p, self.sides.at[0, p], at.beside).sent()
            for d in range(1, 4):
                for cond, block, along, ahead, slot, source in self.halves(d):

                    @pl.when(cond)
                    def _():
                        here = self.o.at[block, self.cut(p)]
                        self.copy(here, block, p, along.at[d, p], ahead).sent()
                        self.copy(here, block, p, self.sides.at[slot, p], at.beside).sent()


def exchange(jobs, collective, name, plan=()):
    def kernel(*refs):
        at = Spot()
        refs = list(refs)
        take = lambda count: [refs.pop(0) for _ in range(count)]
        ins = [take(len(job.ins)) for job in jobs]
        outs = [take(len(job.outs)) for job in jobs]
        scratch = [take(len(job.scratch)) for job in jobs]
        at.meet({one for job in jobs for one in job.reach})
        running = [job.steps(at, i, o, s) for job, i, o, s in zip(jobs, ins, outs, scratch)]
        turns = iter(plan)
        while running:
            if plan and running[0] is not None:
                if next(running[0], plan) is plan:
                    running[0] = None
                for letter in next(turns, ""):
                    for job, one in zip(jobs, running):
                        if one is not None and job.letter == letter:
                            next(one, None)
            else:
                running = [one for one in running if one is not None and next(one, running) is not running]

    count = sum(len(job.ins) for job in jobs)
    return pl.pallas_call(
        kernel,
        out_shape=[shape for job in jobs for shape in job.outs],
        in_specs=[pl.BlockSpec(memory_space=pl.ANY)] * count,
        out_specs=[pl.BlockSpec(memory_space=pl.ANY)] * sum(len(job.outs) for job in jobs),
        scratch_shapes=[shape for job in jobs for shape in job.scratch],
        compiler_params=pltpu.CompilerParams(
            collective_id=collective, has_side_effects=True, vmem_limit_bytes=62 * 2**20
        ),
        name=name,
    )(*[x for job in jobs for x in job.ins])


class Window:
    def __init__(self, own, head, width, rows):
        self.own, self.head, self.heads, self.rows = own, head, width // head, rows
        self.size = 2 * head

    def first(self, s):
        return self.head * jnp.minimum(self.own * s // self.head, self.heads - 2)

    def offset(self, s):
        return self.own * s - self.first(s)

    def takes(self, s, slot, f):
        before = self.offset(s)
        if slot == 0:
            return self.own - before < (f + 1) * self.rows
        return f * self.rows < self.size - self.own - before


class Rows:
    letter = "o"

    def __init__(self, x, window=None):
        self.window = window
        self.slots = 1 if window is None else 3
        self.reach = ("pair",) if window is None else ("seq", "pair")
        self.ins = [x]
        self.outs = [jax.ShapeDtypeStruct((self.slots, 4) + x.shape, x.dtype)]
        dma = pltpu.SemaphoreType.DMA
        self.scratch = [dma((3,))] * 4 + [dma((3, 2))] * 2

    def steps(self, at, ins, outs, scratch):
        (x,), (o,) = ins, outs
        asend, arecv, xsend, xrecv, csend, crecv = scratch
        after = lax.rem(at.s + 1, 8)
        before = lax.rem(at.s + 7, 8)
        sends = []

        def send(src, dst, ss, rs, target, cond=None):
            one = Send(src, dst, ss, rs, (cond, target[1]))
            one.start()
            sends.append(one)

        middle = self.slots // 2
        takes = (lambda j, f: self.window.takes(at.s, j, f)) if self.window else None
        holds = lambda j, f: None if j == middle else takes(j, f)
        if self.slots == 3:
            send(x, o.at[0, at.f], asend.at[0], arecv.at[0], (None, (after, at.f)), (at.s < 7) & self.window.takes(after, 0, at.f))
            send(x, o.at[2, at.f], asend.at[2], arecv.at[2], (None, (before, at.f)), (at.s > 0) & self.window.takes(before, 2, at.f))
        own = pltpu.make_async_copy(x, o.at[middle, at.f], asend.at[1])
        own.start()
        send(x, o.at[middle, at.f], xsend.at[middle], xrecv.at[middle], at.across)
        send(x, o.at[middle, at.f], csend.at[middle, 0], crecv.at[middle, 0], at.twin)
        yield
        for j in range(self.slots):
            if j != middle:
                here = o.at[j, at.f]
                cond = holds(j, at.f)
                arrived(here, asend.at[j], arecv.at[j], at.twin, cond)
                send(here, here, xsend.at[j], xrecv.at[j], at.across, cond)
                send(here, here, csend.at[j, 0], crecv.at[j, 0], at.twin, cond)
        yield
        for j in range(self.slots):
            there = o.at[j, at.f ^ 2]
            cond = holds(j, at.f ^ 2)
            arrived(there, xsend.at[j], xrecv.at[j], at.across, cond)
            send(there, there, csend.at[j, 1], crecv.at[j, 1], at.twin, cond)
            yield
        for j in range(self.slots):
            for k in range(2):
                other = (at.f ^ 1) ^ (2 * k)
                arrived(o.at[j, other], csend.at[j, k], crecv.at[j, k], at.twin, holds(j, other))
        for one in sends:
            one.sent()
        own.wait()


def runs(starts, size):
    marks = sorted({edge for start in starts for edge in (start, start + size)})
    found = []
    for begin, end in zip(marks[:-1], marks[1:]):
        found.append((begin, end, [(at, begin - start) for at, start in enumerate(starts) if start <= begin and end <= start + size]))
    return found


def join_kernel(terms, *refs):
    half = len(refs) // 2
    for term, parts_ref, out_ref in zip(terms, refs[:half], refs[half:]):
        for begin, end, sources in term:
            value = None
            for at, first in sources:
                part = parts_ref[at, :, first : first + end - begin].astype(jnp.float32)
                value = part if value is None else value + part
            out_ref[:, begin:end] = value
    refs[-1][...] = refs[half - 1][0].astype(jnp.float32)


def join(dense, dense_starts, mixer, mixer_starts, plain):
    steps = 4
    terms, ins, outs, shapes = [], [], [], []
    for arrays, starts, period, every in ((dense, dense_starts, 2, 1), (mixer, mixer_starts, 4, 2)):
        for x in arrays:
            _, rows, size = x.shape
            term = runs(starts[:period], size)
            columns = term[-1][1]
            terms.append(term)
            ins.append(pl.BlockSpec((period, rows, size), lambda i, every=every: (i // every, 0, 0)))
            outs.append(pl.BlockSpec((rows, columns), lambda i, every=every: (0, i // every)))
            shapes.append(jax.ShapeDtypeStruct((rows, columns * steps // every), jnp.float32))
    _, rows, columns = plain.shape
    ins.append(pl.BlockSpec((1, rows, columns // steps), lambda i: (0, 0, i)))
    outs.append(pl.BlockSpec((rows, columns // steps), lambda i: (0, i)))
    shapes.append(jax.ShapeDtypeStruct((rows, columns), jnp.float32))
    return pl.pallas_call(
        functools.partial(join_kernel, terms), grid=(steps,), in_specs=ins, out_specs=outs, out_shape=shapes, name="join"
    )(*dense, *mixer, plain)


def rms_rows(values):
    mean = jnp.mean(values * values, axis=1, keepdims=True) + EPSILON
    guess = lax.rsqrt(mean)
    return guess * (1.5 - 0.5 * mean * guess * guess)


class MixerForward:
    letter = "m"
    reach = ("line",)

    def __init__(self, window_of, x_full, w_branch, w_input, w_out, igate, dgate, gain, mask, taps, soft):
        self.window_of = window_of
        _, rows, width = x_full.shape
        window, head = igate.shape
        tokens = 8 * rows
        low, full = x_full.dtype, jnp.float32
        dma = pltpu.SemaphoreType.DMA
        self.ins = [x_full, w_branch, w_input, w_out, igate, dgate, gain, mask, taps, soft]
        kinds = [low, full, low, low, full, full, full, low]
        shapes = [(8, rows, width)] + [(tokens, window)] * 7
        self.outs = [jax.ShapeDtypeStruct((rows, width), full)]
        self.outs += [jax.ShapeDtypeStruct(shape, kind) for shape, kind in zip(shapes, kinds)]
        self.kept = [pltpu.VMEM(shape, kind) for shape, kind in zip(shapes, kinds)]
        self.held = [pltpu.VMEM(x.shape, x.dtype) for x in self.ins[1:]]
        self.held[2] = pltpu.VMEM((window, width), low)
        self.local = [
            pltpu.VMEM((8, rows, width), low),
            pltpu.VMEM((8 + 2 * rows, window), full),
            pltpu.VMEM((CHUNK, head), full),
            pltpu.VMEM((CHUNK, head), full),
            pltpu.VMEM((8, window), full),
            dma((len(self.ins),)),
            dma((len(kinds),)),
        ]
        self.chain = Chain.scratch(rows, width, low)
        self.scratch = self.kept + self.held + self.local + self.chain

    def steps(self, at, ins, outs, scratch):
        take = lambda count: [scratch.pop(0) for _ in range(count)]
        scratch = list(scratch)
        kept = take(len(self.kept))
        held = take(len(self.held))
        parts, padded, coef, drive, carry, lsem, ssem = take(len(self.local))
        normed, pre, conv_in, rounded, gin, gdec, states, mixed = kept
        w_branch, w_input, w_out, igate, dgate, gain, mask, taps, soft = held
        chain = Chain(at, parts, outs[0], scratch, farthest)
        _, rows, width = normed.shape
        window, head = igate.shape
        span = 2 * rows
        w_out[...] = jnp.zeros_like(w_out)
        offset = pl.multiple_of(self.window_of.offset(at.s), 16)
        place = lambda dst: dst.at[pl.ds(offset, ins[3].shape[0])] if dst is w_out else dst
        loads = [pltpu.make_async_copy(src, place(dst), lsem.at[i]) for i, (src, dst) in enumerate(zip(ins, [normed] + held))]
        for load in loads:
            load.start()
        yield
        for load in loads:
            load.wait()
        padded[0:8, :] = jnp.zeros((8, window), jnp.float32)
        carry[...] = jnp.zeros_like(carry)
        line = lax.broadcasted_iota(jnp.int32, (8, head), 0)

        def scale(i, _):
            block, here = i // (rows // 16), pl.ds(pl.multiple_of(lax.rem(i, rows // 16) * 16, 16), 16)
            value = normed[block, here, :].astype(jnp.float32)
            normed[block, here, :] = (value * rms_rows(value) * gain[0:1, :]).astype(normed.dtype)
            return 0

        def work(t):
            lax.fori_loop(2 * t * (rows // 16), 2 * (t + 1) * (rows // 16), scale, 0)
            tokens = pl.ds(span * t, span)
            source = normed[2 * t : 2 * t + 2].reshape(span, width)
            if t:
                padded[0:8, :] = padded[span : span + 8, :]
            for h in range(window // head):
                lanes = slice(h * head, (h + 1) * head)
                pre[tokens, lanes] = jnp.dot(source, w_branch[:, lanes], preferred_element_type=jnp.float32)
                value = jnp.dot(source, w_input[:, lanes], preferred_element_type=jnp.float32).astype(conv_in.dtype)
                conv_in[tokens, lanes] = value
                padded[8:, lanes] = value.astype(jnp.float32)
            if t:
                yield
            def piece(c, _):
                for h in range(window // head):
                    lanes = slice(h * head, (h + 1) * head)
                    base = pl.multiple_of(c * CHUNK, CHUNK)
                    here = pl.ds(pl.multiple_of(t * span + base, CHUNK), CHUNK)
                    marks = mask[here, :]
                    rolls = padded[pl.ds(base, CHUNK + 8), lanes]
                    out = taps[0:1, lanes] * rolls[8:]
                    for k in range(1, TAPS):
                        out = out + taps[k : k + 1, lanes] * rolls[8 - k : 8 - k + CHUNK] * marks[:, k : k + 1]
                    small = out.astype(rounded.dtype)
                    rounded[here, lanes] = small
                    g_in = jax.nn.sigmoid(jnp.dot(small, igate[lanes, :], preferred_element_type=jnp.float32))
                    g_dec = jax.nn.sigmoid(jnp.dot(small, dgate[lanes, :], preferred_element_type=jnp.float32))
                    gin[here, lanes] = g_in
                    gdec[here, lanes] = g_dec
                    log_decay = -soft[0:1, lanes] * (1.0 + 7.0 * g_dec)
                    root = jnp.sqrt(minus_expm1(2.0 * log_decay))
                    restart = marks[:, 0:1]
                    carried = 1.0 - restart
                    coef[...] = jnp.exp(log_decay) * carried
                    drive[...] = small.astype(jnp.float32) * g_in * (restart + carried * root)

                    def tile(i, state):
                        now = pl.multiple_of(i * 8, 8)
                        a = coef[pl.ds(now, 8), :]
                        b = drive[pl.ds(now, 8), :]
                        for sh in (1, 2, 4):
                            keep = line >= sh
                            b = b + a * jnp.where(keep, pltpu.roll(b, sh, 0), 0.0)
                            a = a * jnp.where(keep, pltpu.roll(a, sh, 0), 1.0)
                        new = b + a * state
                        there = pl.ds(pl.multiple_of(t * span + base + now, 8), 8)
                        states[there, lanes] = new
                        return jnp.broadcast_to(new[7:8, :], (8, head))

                    carry[:, lanes] = lax.fori_loop(0, CHUNK // 8, tile, carry[:, lanes], unroll=True)
                    branch, _ = gelu_parts(pre[here, lanes])
                    mixed[here, lanes] = (states[here, lanes] * branch).astype(mixed.dtype)
                return 0

            lax.fori_loop(0, span // CHUNK, piece, 0)
            if t:
                yield
            values = mixed[tokens, :]

            def product(n, _):
                columns = pl.ds(pl.multiple_of(n * 256, 256), 256)
                out = jnp.dot(values, w_out[:, columns], preferred_element_type=jnp.float32)
                parts[2 * t : 2 * t + 2, :, columns] = out.astype(parts.dtype).reshape(2, rows, 256)
                return 0

            lax.fori_loop(0, width // 256, product, 0)
            if t == 0:
                chain.send_side(0)

        for t in range(4):
            yield from work(t)
            if t == 3:
                chain.send_side(jnp.where(at.z == 3, 1, 3))
                chain.send_side(jnp.where(at.z == 2, 1, 2))
                chain.send_side(jnp.where(at.z == 3, 3, jnp.where(at.z == 2, 2, 1)))
            yield
        stores = [pltpu.make_async_copy(src, dst, ssem.at[i]) for i, (src, dst) in enumerate(zip(kept, outs[1:]))]
        for store in stores:
            store.start()
        for k in range(3):
            for p in range(PIECES):
                chain.step(k, p)
                yield
        chain.finish()
        yield
        chain.sent()
        for store in stores:
            store.wait()


class MixerBackward:
    letter = "b"
    reach = ("line",)

    def __init__(self, window_of, out_grad, w_out, w_branch, w_input, normed, pre, conv_in, rounded, gin, gdec, states, mixed, igate, dgate, mask, ahead, taps, soft, owned):
        self.window_of = window_of
        rows, width = out_grad.shape
        tokens, window = pre.shape
        head = igate.shape[1]
        low, full = out_grad.dtype, jnp.float32
        dma = pltpu.SemaphoreType.DMA
        self.ins = [out_grad, w_out, w_branch, w_input, normed, pre, conv_in, rounded, gin, gdec, states, mixed, igate, dgate, mask, ahead, taps, soft, owned]
        shape = jax.ShapeDtypeStruct
        self.outs = [
            shape((rows, width), full), shape((width, window), low), shape((width, window), low), shape((window, width), low),
            shape((window, 2 * head), low), shape((window, 128), full),
        ]
        self.held = [pltpu.VMEM(x.shape, x.dtype) for x in self.ins[1:]]
        self.held[0] = pltpu.VMEM((window, width), low)
        self.held[9] = pltpu.VMEM((8 + tokens, window), full)
        self.local = [
            pltpu.VMEM((8, rows, width), low),
            pltpu.VMEM((8, rows, width), low),
            pltpu.VMEM((2 * rows, window), full),
            pltpu.VMEM((tokens, window), low),
            pltpu.VMEM((tokens, window), low),
            pltpu.VMEM((2 * rows + 8, window), full),
            pltpu.VMEM((2 * rows + 8, window), full),
            pltpu.VMEM((CHUNK, head), full),
            pltpu.VMEM((CHUNK, head), full),
            pltpu.VMEM((16, window), full),
            pltpu.VMEM((window, head), full),
            pltpu.VMEM((window, head), full),
            pltpu.VMEM((8 * 5, window), full),
            pltpu.VMEM((window, 2 * head), low),
            pltpu.VMEM((window, 128), full),
            dma((len(self.ins),)),
            dma((8,)),
        ]
        self.gather = Gather(out_grad)
        self.chain = Chain.scratch(rows, width, low)
        self.scratch = self.held + self.local + self.gather.scratch + self.chain

    def steps(self, at, ins, outs, scratch):
        scratch = list(scratch)
        take = lambda count: [scratch.pop(0) for _ in range(count)]
        held = take(len(self.held))
        toks, parts, mgrad, pgrad, cgrad, padded, later, coef, drive, carry, igrad, dgrad, sums, gates, lines, lsem, ssem = take(len(self.local))
        gsems = take(len(self.gather.scratch))
        w_out, w_branch, w_input, normed, pre, conv_in, rounded, gin, gdec, states, mixed, igate, dgate, mask, ahead, taps, soft, owned = held
        chain = Chain(at, parts, outs[0], scratch, descending)
        relay = Relay(at, ins[0], toks, gsems)
        _, rows, width = toks.shape
        tokens, window = pre.shape
        head = igate.shape[1]
        span = 2 * rows
        heads = [slice(h * head, (h + 1) * head) for h in range(window // head)]
        relay.begin()
        loads = []
        for i, (src, dst) in enumerate(zip(ins[1:], held)):
            if dst is w_out:
                first = pl.multiple_of(self.window_of.own - self.window_of.offset(at.s), 16)
                src = src.at[pl.ds(first, window)]
            loads.append(pltpu.make_async_copy(src, dst.at[8:] if dst is states else dst, lsem.at[i]))
            loads[-1].start()
        states[0:8, :] = jnp.zeros((8, window), jnp.float32)
        for ref in (later, carry, igrad, dgrad, sums):
            ref[...] = jnp.zeros_like(ref)
        yield
        for d in range(1, 4):
            for p in range(PIECES):
                relay.step(d, p)
                yield
        for load in loads:
            load.wait()
        relay.own_copy().wait()
        for t in range(4):
            relay.wait_beside(t)
        line = lax.broadcasted_iota(jnp.int32, (8, head), 0)
        rows_dot = lambda a, b: lax.dot_general(a, b, CONTRACT_ROWS, preferred_element_type=jnp.float32)
        last_dot = lambda a, b: lax.dot_general(a, b, CONTRACT_LAST, preferred_element_type=jnp.float32)
        fold = lambda v: jnp.sum(v.reshape(v.shape[0] // 8, 8, v.shape[1]), axis=0)

        def work(t):
            source = toks[2 * t : 2 * t + 2].reshape(span, width)
            for lanes in heads:
                mgrad[:, lanes] = last_dot(source, w_out[lanes, :])
            later[span : span + 8, :] = later[0:8, :]
            if t:
                padded[0:8, :] = conv_in[span * t - 16 : span * t, :].astype(jnp.float32)[8:]
            else:
                padded[0:8, :] = jnp.zeros((8, window), jnp.float32)
            padded[8:, :] = conv_in[span * t : span * (t + 1), :].astype(jnp.float32)

            def piece(step, _):
                base = pl.multiple_of((span // CHUNK - 1 - step) * CHUNK, CHUNK)
                here = pl.ds(pl.multiple_of(t * span + base, CHUNK), CHUNK)
                inside = pl.ds(base, CHUNK)
                marks = mask[here, :]
                restart = marks[:, 0:1]
                carried = 1.0 - restart
                for lanes in heads:
                    branch, slope = gelu_parts(pre[here, lanes])
                    grad = mgrad[inside, lanes]
                    state = states[pl.ds(pl.multiple_of(t * span + base, CHUNK), CHUNK + 8), lanes]
                    pgrad[here, lanes] = (grad * state[8:] * slope * owned[0:1, lanes]).astype(pgrad.dtype)
                    g_dec = gdec[here, lanes]
                    g_in = gin[here, lanes]
                    log_decay = -soft[0:1, lanes] * (1.0 + 7.0 * g_dec)
                    decays = jnp.exp(log_decay)
                    root = jnp.sqrt(minus_expm1(2.0 * log_decay))
                    coef[...] = decays * carried
                    drive[...] = grad * branch

                    def tile(i, pair):
                        adj_next, coef_next = pair
                        now = pl.multiple_of(CHUNK - 8 - i * 8, 8)
                        first = coef[pl.ds(now, 8), :]
                        a = jnp.where(line == 7, coef_next, pltpu.roll(first, 7, 0))
                        b = drive[pl.ds(now, 8), :]
                        for sh in (1, 2, 4):
                            keep = line < 8 - sh
                            b = b + a * jnp.where(keep, pltpu.roll(b, 8 - sh, 0), 0.0)
                            a = a * jnp.where(keep, pltpu.roll(a, 8 - sh, 0), 1.0)
                        new = b + a * adj_next
                        drive[pl.ds(now, 8), :] = new
                        return jnp.broadcast_to(new[0:1, :], (8, head)), jnp.broadcast_to(first[0:1, :], (8, head))

                    adj_next, coef_next = lax.fori_loop(0, CHUNK // 8, tile, (carry[0:8, lanes], carry[8:16, lanes]), unroll=True)
                    carry[0:8, lanes] = adj_next
                    carry[8:16, lanes] = coef_next
                    adjoint = drive[...]
                    small = rounded[here, lanes]
                    value = small.astype(jnp.float32)
                    log_grad = adjoint * carried * decays * (state[7 : 7 + CHUNK] - value * g_in * decays / root)
                    sums[32:40, lanes] += fold(-log_grad * (1.0 + 7.0 * g_dec))
                    through = adjoint * g_in * (restart + carried * root)
                    ipg = (through * value * (1.0 - g_in)).astype(jnp.bfloat16)
                    dpg = (log_grad * (-7.0 * soft[0:1, lanes]) * g_dec * (1.0 - g_dec)).astype(jnp.bfloat16)
                    igrad[lanes, :] += rows_dot(small, ipg)
                    dgrad[lanes, :] += rows_dot(small, dpg)
                    through = through + last_dot(ipg, igate[lanes, :]) + last_dot(dpg, dgate[lanes, :])
                    later[inside, lanes] = through.astype(jnp.bfloat16).astype(jnp.float32)
                return 0

            lax.fori_loop(0, span // CHUNK, piece, 0)
            yield

            def after(c, _):
                base = pl.multiple_of(c * CHUNK, CHUNK)
                here = pl.ds(pl.multiple_of(t * span + base, CHUNK), CHUNK)
                marks = mask[here, :]
                ahead_marks = ahead[here, :]
                for lanes in heads:
                    follow = later[pl.ds(base, CHUNK + 8), lanes]
                    before = padded[pl.ds(base, CHUNK + 8), lanes]
                    grad = follow[:CHUNK]
                    total = taps[0:1, lanes] * grad
                    sums[0:8, lanes] += fold(grad * before[8:])
                    for k in range(1, TAPS):
                        total = total + taps[k : k + 1, lanes] * follow[k : k + CHUNK] * ahead_marks[:, k : k + 1]
                        sums[8 * k : 8 * k + 8, lanes] += fold(grad * before[8 - k : 8 - k + CHUNK] * marks[:, k : k + 1])
                    cgrad[here, lanes] = (total * owned[0:1, lanes]).astype(cgrad.dtype)
                return 0

            lax.fori_loop(0, span // CHUNK, after, 0)
            mine = slice(span * t, span * (t + 1))

            def product(n, _):
                columns = pl.ds(pl.multiple_of(n * 256, 256), 256)
                out = last_dot(pgrad[mine, :], w_branch[columns, :]) + last_dot(cgrad[mine, :], w_input[columns, :])
                parts[2 * t : 2 * t + 2, :, columns] = out.astype(parts.dtype).reshape(2, rows, 256)
                return 0

            lax.fori_loop(0, width // 256, product, 0)
            if t > 1:
                chain.send_side(t)

        for t in (3, 2, 1, 0):
            yield from work(t)
            if t == 0:
                chain.send_side(jnp.where(at.z == 0, 1, 0))
                chain.send_side(jnp.where(at.z == 0, 0, 1))
            yield
        gates[:, :head] = igrad[...].astype(gates.dtype)
        gates[:, head:] = dgrad[...].astype(gates.dtype)
        totals = [jnp.sum(sums[8 * k : 8 * k + 8, :], axis=0, keepdims=True) for k in range(5)]
        lines[...] = jnp.concatenate(totals + [jnp.zeros((123, window), jnp.float32)], axis=0).T

        def grads(r):
            lanes = pl.ds(pl.multiple_of(r * 256, 256), 256)
            value = normed[:, :, lanes].reshape(tokens, 256)
            w_branch[lanes, :] = rows_dot(value, pgrad[...]).astype(w_branch.dtype)
            w_input[lanes, :] = rows_dot(value, cgrad[...]).astype(w_input.dtype)
            w_out[:, lanes] = rows_dot(mixed[...], toks[:, :, lanes].reshape(tokens, 256)).astype(w_out.dtype)

        done = 0
        for k in range(3):

            def chain_step(p, _):
                chain.step(k, p)
                pl.when(k * PIECES + p < width // 256)(lambda: grads(k * PIECES + p))
                return 0

            lax.fori_loop(0, PIECES, chain_step, 0)
            yield
        chain.finish()
        stores = [
            pltpu.make_async_copy(src, dst, ssem.at[i])
            for i, (src, dst) in enumerate(zip((w_branch, w_input, w_out, gates, lines), outs[1:]))
        ]
        for store in stores:
            store.start()
        yield
        chain.sent()
        relay.sent()
        for store in stores:
            store.wait()


def fast(
    inputs,
    resets,
    cotangent,
    first_gain,
    branch_weight,
    input_weight,
    conv_weight,
    input_gate,
    decay_gate,
    decay_param,
    output_weight,
    second_gain,
    gate_weight,
    up_weight,
    down_weight,
):
    low = jnp.bfloat16
    peers, groups = 8, 4
    s, f = lax.axis_index("seq"), lax.axis_index("fsdp")
    sources_low = inputs[0]
    sources = sources_low.astype(jnp.float32)
    returned = cotangent[0]
    tokens, width = sources.shape
    rows = branch_weight.shape[0]
    head = input_gate.shape[1]
    own = width // peers
    hidden_own = gate_weight.shape[1] // peers
    all_tokens = peers * tokens
    window = 2 * head
    channels = Window(own, head, width, rows)
    offset = channels.offset(s)
    owned = ((jnp.arange(window) >= offset) & (jnp.arange(window) < offset + own)).astype(jnp.float32)

    wide_row = lambda v: jnp.pad(v.astype(jnp.float32), (0, 128 - v.shape[0]))
    small = jnp.pad(jnp.stack([wide_row(first_gain), wide_row(second_gain), wide_row(resets[0])]), ((0, 5), (0, 0)))[None]
    dense_start = lambda to: 128 * (hidden_own * to // 128)
    wide = 128 * -(-hidden_own // 128)
    lanes = jnp.arange(wide) + dense_start(s) - hidden_own * s
    held = jnp.broadcast_to(((lanes >= 0) & (lanes < hidden_own)).astype(jnp.float32)[None], (8, wide))
    pad = jnp.zeros((rows, 128 - 5), low)
    row_pack = jnp.concatenate([input_gate, decay_gate, conv_weight, decay_param[:, None], pad], axis=1)
    x_full, w_branch, w_input, row_w, out_w, vectors = exchange(
        [
            Gather(sources_low),
            Spread(branch_weight, channels.first, window),
            Spread(input_weight, channels.first, window),
            Rows(row_pack, channels),
            Rows(output_weight),
            Tiny(small),
        ],
        1,
        "first_exchange",
    )
    whole = lambda w: w.reshape(width, w.shape[-1])
    w_branch, w_input = whole(w_branch), whole(w_input)
    w_output = out_w.reshape(own, width)
    near = lax.dynamic_slice_in_dim(row_w.reshape(3 * own, row_pack.shape[1]), own - offset, window, 0)
    w_igate, w_dgate = near[:, :head], near[:, head : 2 * head]
    taps = jnp.zeros((8, window), jnp.float32).at[:4].set(near[:, 2 * head : 2 * head + 4].astype(jnp.float32).T)
    w_decay = near[:, 2 * head + 4].astype(jnp.float32)
    soft = jnp.broadcast_to(jax.nn.softplus(w_decay)[None], (8, window))
    gain_first = vectors[:, 0, :rows].reshape(width)
    gain_second = vectors[:, 1, :rows].reshape(width)
    flags = lax.dynamic_index_in_dim(vectors.reshape(peers, groups, 8, 128), f, 1, False)[:, 2, :tokens].reshape(all_tokens)
    segment = jnp.cumsum(flags)
    masks, aheads = [flags], [jnp.ones_like(flags)]
    for k in range(1, 4):
        same = (segment[k:] == segment[:-k]).astype(jnp.float32)
        masks.append(jnp.concatenate([jnp.zeros((k,), jnp.float32), same]))
        aheads.append(jnp.concatenate([same, jnp.zeros((k,), jnp.float32)]))
    masks = jnp.stack(masks + [jnp.zeros_like(flags)] * 4, axis=1)
    aheads = jnp.stack(aheads + [jnp.zeros_like(flags)] * 4, axis=1)
    owned_rows = jnp.broadcast_to(owned[None], (8, window))

    gain_rows = jnp.broadcast_to(gain_first[None], (8, width))
    (
        mixer_out, normed, pre, conv_in, rounded, gate_in, gate_dec, states, mixed,
        returned_full, w_gate, w_up, w_down, w_output_near,
    ) = exchange(
        [
            MixerForward(channels, x_full, w_branch, w_input, w_output, w_igate, w_dgate, gain_rows, masks, taps, soft),
            Gather(returned),
        ]
        + [Spread(w, dense_start, wide) for w in (gate_weight, up_weight, down_weight)]
        + [Rows(output_weight, channels)],
        2,
        "mixer_forward",
        ["gso", "s", "", "", "s", "", "", "s", "", "", "ggggssggggssggggs"],
    )
    resid = sources + mixer_out
    scale_two = lax.rsqrt(jnp.mean(resid * resid, axis=1, keepdims=True) + EPSILON)
    hidden = (resid * scale_two * gain_second).astype(low)
    hidden_grad, result_part, grad_gate, grad_up, grad_down = exchange(
        [Dense(hidden, returned_full, whole(w_gate), whole(w_up), whole(w_down), held)], 3, "dense"
    )
    weighted = hidden_grad * gain_second
    resid_grad = (
        returned.astype(jnp.float32)
        + scale_two * weighted
        - resid * scale_two**3 * jnp.mean(weighted * resid, axis=1, keepdims=True)
    )
    second_term = jnp.sum(hidden_grad * resid * scale_two, axis=0)
    out_grad = resid_grad.astype(low)
    split = lambda g: g.reshape(peers, groups, rows, g.shape[-1])
    (
        normed_grad, grad_branch, grad_input, grad_output, gates, lines,
        grad_gate, grad_up, grad_down,
    ) = exchange(
        [
            MixerBackward(
                channels, out_grad, w_output_near.reshape(3 * own, width), w_branch, w_input, normed, pre, conv_in, rounded, gate_in, gate_dec, states, mixed,
                w_igate, w_dgate, masks, aheads, taps, soft, owned_rows,
            )
        ]
        + [Collect(split(g)) for g in (grad_gate, grad_up, grad_down)],
        4,
        "mixer_backward",
        ["c"] * 13 + ["", "c"] * 4,
    )
    scale_one = lax.rsqrt(jnp.mean(sources * sources, axis=1, keepdims=True) + EPSILON)
    weighted = normed_grad * gain_first
    source_grad = (
        resid_grad
        + scale_one * weighted
        - sources * scale_one**3 * jnp.mean(weighted * sources, axis=1, keepdims=True)
    )
    first_term = jnp.sum(normed_grad * sources * scale_one, axis=0)
    grad_branch, grad_input = split(grad_branch), split(grad_input)
    terms = jnp.stack([first_term.reshape(peers * groups, rows), second_term.reshape(peers * groups, rows)], axis=1)
    vectors = jnp.pad(terms, ((0, 0), (0, 6), (0, 128 - rows)))
    ffn_out, grad_branch, grad_input, grad_output, gates, lines, vectors = exchange(
        [
            Reduce(result_part),
            Collect(grad_branch),
            Collect(grad_input),
            Collect(grad_output, channels),
            Collect(gates, channels),
            Collect(lines, channels),
            Tiny(vectors),
        ],
        6,
        "mixer_collect",
    )
    result = (resid + ffn_out).astype(low)
    vectors = jnp.sum(vectors, axis=0)
    gates = gates[0].astype(jnp.float32)

    dense_grads, dense_starts = (grad_gate, grad_up, grad_down), [128 * (hidden_own * at // 128) for at in range(peers)]
    mixer_starts = [head * min(own * at // head, width // head - 2) for at in range(peers)]
    grad_gate, grad_up, grad_down, grad_branch, grad_input, grad_output = join(
        dense_grads, dense_starts, (grad_branch, grad_input), mixer_starts, grad_output
    )
    return (
        result[None],
        source_grad.astype(low)[None],
        vectors[0, :rows],
        grad_branch,
        grad_input,
        lines[0, :, :4],
        gates[:, :head],
        gates[:, head:],
        lines[0, :, 4] * jax.nn.sigmoid(decay_param.astype(jnp.float32)),
        grad_output,
        vectors[1, :rows],
        grad_gate,
        grad_up,
        grad_down,
    )


def solution(mesh):
    in_specs = (
        P("fsdp", "seq", None),
        P("fsdp", "seq"),
        P("fsdp", "seq", None),
        P(("seq", "fsdp")),
        P(("seq", "fsdp"), None),
        P(("seq", "fsdp"), None),
        P(("seq", "fsdp"), None),
        P(("seq", "fsdp"), None),
        P(("seq", "fsdp"), None),
        P(("seq", "fsdp")),
        P(("seq", "fsdp"), None),
        P(("seq", "fsdp")),
        P(("seq", "fsdp"), None),
        P(("seq", "fsdp"), None),
        P(("seq", "fsdp"), None),
    )
    out_specs = (
        P("fsdp", "seq", None),
        P("fsdp", "seq", None),
        P(("seq", "fsdp")),
        P(("seq", "fsdp"), None),
        P(("seq", "fsdp"), None),
        P(("seq", "fsdp"), None),
        P(("seq", "fsdp"), None),
        P(("seq", "fsdp"), None),
        P(("seq", "fsdp")),
        P(("seq", "fsdp"), None),
        P(("seq", "fsdp")),
        P(("seq", "fsdp"), None),
        P(("seq", "fsdp"), None),
        P(("seq", "fsdp"), None),
    )
    program = fast if dict(mesh.shape) == {"seq": 8, "fsdp": 4} else local
    return jax.shard_map(program, mesh=mesh, in_specs=in_specs, out_specs=out_specs, check_vma=False)
```

```python
import functools

import jax
import jax.numpy as jnp
from jax import lax
from jax.experimental import pallas as pl
from jax.experimental.pallas import tpu as pltpu
from jax.sharding import PartitionSpec as P

EPSILON = 1e-06
CONTRACT_ROWS = (((0,), (0,)), ((), ()))
CONTRACT_LAST = (((1,), (1,)), ((), ()))


def shifted_2(value, axis, steps):
    count = lax.axis_size(axis)
    leading, last = (max(0, -steps), min(count, count - steps))
    return lax.ppermute(value, axis, [(source, source + steps) for source in range(leading, last)])


def entering(x, axis, combine, identity, reverse):
    peers, index = (lax.axis_size(axis), lax.axis_index(axis))
    everything = jax.tree.map(lambda part: lax.all_gather(part, axis), x)
    start = jax.tree.map(
        lambda part, zero: jnp.broadcast_to(jnp.asarray(zero, part.dtype), part.shape), x, identity
    )

    def lap(k, before):
        at = peers - 1 - k if reverse else k
        reached = at > index if reverse else at < index
        new = combine(before, jax.tree.map(lambda part: part[at], everything))
        return jax.tree.map(lambda a, b: jnp.where(reached, a, b), new, before)

    return lax.fori_loop(0, peers, lap, start)


def affine(earlier, later):
    return (earlier[0] * later[0], later[0] * earlier[1] + later[1])


def product(operand_one, operand_two):
    return jnp.dot(operand_one, operand_two, preferred_element_type=jnp.float32)


def rows_product(operand_one, operand_two):
    return lax.dot_general(
        operand_one, operand_two, CONTRACT_ROWS, preferred_element_type=jnp.float32
    )


def last_product(operand_one, operand_two):
    return lax.dot_general(
        operand_one, operand_two, CONTRACT_LAST, preferred_element_type=jnp.float32
    )


def heads_apply(values, weight, head_count):
    token_count = values.shape[0]
    head_width = weight.shape[1]
    shaped = values.reshape(token_count, head_count, head_width)
    blocks = weight.reshape(head_count, head_width, head_width)
    mixed = jnp.einsum("thi,hij->thj", shaped, blocks, preferred_element_type=jnp.float32)
    return mixed.reshape(token_count, head_count * head_width)


def heads_back(gradients, weight, head_count):
    token_count = gradients.shape[0]
    head_width = weight.shape[1]
    shaped = gradients.reshape(token_count, head_count, head_width)
    blocks = weight.reshape(head_count, head_width, head_width)
    mixed = jnp.einsum("thj,hij->thi", shaped, blocks, preferred_element_type=jnp.float32)
    return mixed.reshape(token_count, head_count * head_width)


def heads_grad(values, gradients, head_count):
    token_count = values.shape[0]
    head_width = values.shape[1] // head_count
    left_side = values.reshape(token_count, head_count, head_width)
    right_side = gradients.reshape(token_count, head_count, head_width)
    summed = jnp.einsum("thi,thj->hij", left_side, right_side, preferred_element_type=jnp.float32)
    return summed.reshape(head_count * head_width, head_width)


def slab_count():
    for candidate in (5, 4, 2):
        return candidate
    return 1


def local(
    inputs,
    resets,
    cotangent,
    first_gain,
    branch_weight,
    input_weight,
    conv_weight,
    input_gate,
    decay_gate,
    decay_param,
    output_weight,
    second_gain,
    gate_weight,
    up_weight,
    down_weight,
):
    sources = inputs[0].astype(jnp.float32)
    flags = resets[0]
    returned = cotangent[0]
    returned_float = returned.astype(jnp.float32)
    tokens = sources.shape[0]
    shared = (
        lax.all_gather(first_gain, ("seq", "fsdp"), axis=0, tiled=True),
        lax.all_gather(branch_weight, ("seq", "fsdp"), axis=0, tiled=True),
        lax.all_gather(input_weight, ("seq", "fsdp"), axis=0, tiled=True),
        lax.all_gather(conv_weight, ("seq", "fsdp"), axis=0, tiled=True),
        lax.all_gather(input_gate, ("seq", "fsdp"), axis=0, tiled=True),
        lax.all_gather(decay_gate, ("seq", "fsdp"), axis=0, tiled=True),
        lax.all_gather(decay_param, ("seq", "fsdp"), axis=0, tiled=True),
        lax.all_gather(output_weight, ("seq", "fsdp"), axis=0, tiled=True),
        lax.all_gather(second_gain, ("seq", "fsdp"), axis=0, tiled=True),
    )
    dense_parts = (
        lax.all_gather(gate_weight, ("seq", "fsdp"), axis=0, tiled=True),
        lax.all_gather(up_weight, ("seq", "fsdp"), axis=0, tiled=True),
        lax.all_gather(down_weight, ("seq", "fsdp"), axis=0, tiled=True),
    )
    gain_first = shared[0].astype(jnp.float32)
    w_branch = shared[1]
    w_input = shared[2]
    w_conv = shared[3].astype(jnp.float32)
    w_igate = shared[4]
    w_dgate = shared[5]
    w_decay = shared[6].astype(jnp.float32)
    w_output = shared[7]
    gain_second = shared[8].astype(jnp.float32)
    w_gate = dense_parts[0]
    w_up = dense_parts[1]
    w_down = dense_parts[2]
    model_width = w_branch.shape[0]
    head_width = w_igate.shape[1]
    head_count = model_width // head_width
    tap_count = w_conv.shape[1]
    scale_one = lax.rsqrt(jnp.mean(sources * sources, axis=1, keepdims=True) + EPSILON)
    normed = (sources * scale_one * gain_first).astype(jnp.bfloat16)
    branch_pre = product(normed, w_branch)
    branch, branch_pull = jax.vjp(jax.nn.gelu, branch_pre)
    conv_in = product(normed, w_input).astype(jnp.bfloat16)
    resets_seen = jnp.cumsum(flags)
    tail_keep = resets_seen[-1] - resets_seen[tokens - tap_count + 1 :] == 0
    tail_rows = conv_in[tokens - tap_count + 1 :] * tail_keep[:, None]
    before = shifted_2(tail_rows, "seq", 1)
    padded = jnp.concatenate([before, conv_in], axis=0)
    seen_before = jnp.concatenate([jnp.zeros((tap_count - 1,), jnp.int32), resets_seen])
    conv_out = jnp.zeros((tokens, model_width), jnp.float32)
    usable_list = []
    for offset in range(tap_count):
        first_row = tap_count - 1 - offset
        shifted = padded[first_row : first_row + tokens].astype(jnp.float32)
        usable = (resets_seen - seen_before[first_row : first_row + tokens] == 0).astype(
            jnp.float32
        )[:, None]
        usable_list.append(usable)
        conv_out = conv_out + w_conv[:, offset] * shifted * usable
    rounded = conv_out.astype(jnp.bfloat16)
    rounded_float = rounded.astype(jnp.float32)
    gate_input = jax.nn.sigmoid(heads_apply(rounded, w_igate, head_count))
    gate_decay = jax.nn.sigmoid(heads_apply(rounded, w_dgate, head_count))
    softened = jax.nn.softplus(w_decay)
    log_decay = -softened * (1.0 + 7.0 * gate_decay)
    decays = jnp.exp(log_decay)
    root_term = jnp.sqrt(-jnp.expm1(2.0 * log_decay))
    restart = flags.astype(jnp.float32)[:, None]
    carried = 1.0 - restart
    scaling = restart + carried * root_term
    driven = rounded_float * gate_input * scaling
    coefficient = decays * carried
    running, local_state = lax.associative_scan(affine, (coefficient, driven), axis=0)
    unit_ones = jnp.ones((model_width,), jnp.float32)
    unit_zeros = jnp.zeros((model_width,), jnp.float32)
    incoming = entering(
        (running[-1], local_state[-1]), "seq", affine, (unit_ones, unit_zeros), False
    )
    state_in = incoming[1]
    states = local_state + running * state_in
    mixed = (states * branch).astype(jnp.bfloat16)
    resid = sources + product(mixed, w_output)
    scale_two = lax.rsqrt(jnp.mean(resid * resid, axis=1, keepdims=True) + EPSILON)
    hidden = (resid * scale_two * gain_second).astype(jnp.bfloat16)
    gate_pre = product(hidden, w_gate)
    up_values = product(hidden, w_up)
    gate_act, gate_pull = jax.vjp(jax.nn.gelu, gate_pre)
    active = (gate_act * up_values).astype(jnp.bfloat16)
    result = (resid + last_product(active, w_down)).astype(jnp.bfloat16)
    act_grad = product(returned, w_down)
    gate_grad = gate_pull(act_grad * up_values)[0].astype(jnp.bfloat16)
    up_grad = (act_grad * gate_act).astype(jnp.bfloat16)
    hidden_grad = last_product(gate_grad, w_gate) + last_product(up_grad, w_up)
    weighted_two = hidden_grad * gain_second
    resid_grad = (
        returned_float
        + scale_two * weighted_two
        - resid * scale_two**3 * jnp.mean(weighted_two * resid, axis=1, keepdims=True)
    )
    second_term = jnp.sum(hidden_grad * resid * scale_two, axis=0)
    branch_out_grad = resid_grad.astype(jnp.bfloat16)
    mixed_grad = last_product(branch_out_grad, w_output)
    state_grad = mixed_grad * branch
    branch_grad = mixed_grad * states
    branch_pre_grad = branch_pull(branch_grad)[0].astype(jnp.bfloat16)
    next_coef = jnp.concatenate([coefficient[1:], jnp.ones((1, model_width), jnp.float32)], axis=0)
    reaches, adjoint_local = lax.associative_scan(
        affine, (next_coef, state_grad), reverse=True, axis=0
    )
    carry_back = entering(
        (coefficient[0] * reaches[0], coefficient[0] * adjoint_local[0]),
        "seq",
        affine,
        (unit_ones, unit_zeros),
        True,
    )
    adjoint = adjoint_local + reaches * carry_back[1]
    earlier_state = jnp.concatenate([state_in[None], states[:-1]], axis=0)
    log_grad = (
        adjoint * earlier_state * carried * decays
        - adjoint * rounded_float * gate_input * carried * decays * decays / root_term
    )
    decay_term = jnp.sum(-log_grad * (1.0 + 7.0 * gate_decay), axis=0) * jax.nn.sigmoid(w_decay)
    input_pre_grad = (adjoint * rounded_float * scaling * gate_input * (1.0 - gate_input)).astype(
        jnp.bfloat16
    )
    decay_pre_grad = (log_grad * (-7.0 * softened) * gate_decay * (1.0 - gate_decay)).astype(
        jnp.bfloat16
    )
    conv_out_grad = (
        adjoint * gate_input * scaling
        + heads_back(input_pre_grad, w_igate, head_count)
        + heads_back(decay_pre_grad, w_dgate, head_count)
    )
    conv_grad = conv_out_grad.astype(jnp.bfloat16)
    igate_term = heads_grad(rounded, input_pre_grad, head_count)
    dgate_term = heads_grad(rounded, decay_pre_grad, head_count)
    head_keep = resets_seen[: tap_count - 1] == 0
    head_rows = conv_grad[: tap_count - 1] * head_keep[:, None]
    following = shifted_2(head_rows, "seq", -1)
    padded_back = jnp.concatenate([conv_grad, following], axis=0)
    seen_after = jnp.concatenate(
        [resets_seen, jnp.full((tap_count - 1,), resets_seen[-1], jnp.int32)]
    )
    conv_grad_float = conv_grad.astype(jnp.float32)
    conv_in_grad = jnp.zeros((tokens, model_width), jnp.float32)
    tap_terms = []
    for offset in range(tap_count):
        first_row = tap_count - 1 - offset
        shifted = padded[first_row : first_row + tokens].astype(jnp.float32)
        tap_terms.append(jnp.sum(conv_grad_float * shifted * usable_list[offset], axis=0))
        ahead_usable = (seen_after[offset : offset + tokens] - resets_seen == 0).astype(
            jnp.float32
        )[:, None]
        conv_in_grad = (
            conv_in_grad
            + w_conv[:, offset]
            * padded_back[offset : offset + tokens].astype(jnp.float32)
            * ahead_usable
        )
    tap_grad = jnp.stack(tap_terms, axis=1)
    conv_in_low = conv_in_grad.astype(jnp.bfloat16)
    normed_grad = last_product(branch_pre_grad, w_branch) + last_product(conv_in_low, w_input)
    weighted_one = normed_grad * gain_first
    source_grad = (
        resid_grad
        + scale_one * weighted_one
        - sources * scale_one**3 * jnp.mean(weighted_one * sources, axis=1, keepdims=True)
    )
    first_term = jnp.sum(normed_grad * sources * scale_one, axis=0)
    grad_inputs = source_grad.astype(jnp.bfloat16)[None]
    vector_part = jnp.concatenate(
        [
            igate_term,
            dgate_term,
            tap_grad,
            decay_term[:, None],
            first_term[:, None],
            second_term[:, None],
        ],
        axis=1,
    )
    owned_rows = gate_weight.shape[0]
    owner_count = lax.axis_size(("seq", "fsdp"))
    slab_total = slab_count()
    slab_rows = owned_rows // slab_total
    vector_shaped = vector_part.reshape(owner_count, owned_rows, vector_part.shape[1])

    def pick_rows(values, portion):
        shaped = values.reshape(values.shape[0], owner_count, owned_rows)
        taken = shaped[:, :, portion * slab_rows : (portion + 1) * slab_rows]
        return taken.reshape(values.shape[0], owner_count * slab_rows)

    gate_pieces = []
    up_pieces = []
    down_pieces = []
    branch_pieces = []
    input_pieces = []
    output_pieces = []
    vector_pieces = []
    for portion in range(slab_total):
        hidden_rows = pick_rows(hidden, portion)
        return_rows = pick_rows(returned, portion)
        dense_sums = (
            lax.psum_scatter(
                rows_product(hidden_rows, gate_grad),
                ("seq", "fsdp"),
                scatter_dimension=0,
                tiled=True,
            ),
            lax.psum_scatter(
                rows_product(hidden_rows, up_grad), ("seq", "fsdp"), scatter_dimension=0, tiled=True
            ),
            lax.psum_scatter(
                rows_product(return_rows, active), ("seq", "fsdp"), scatter_dimension=0, tiled=True
            ),
        )
        gate_pieces.append(dense_sums[0])
        up_pieces.append(dense_sums[1])
        down_pieces.append(dense_sums[2])
        normed_rows = pick_rows(normed, portion)
        mixed_rows = pick_rows(mixed, portion)
        vector_rows = vector_shaped[:, portion * slab_rows : (portion + 1) * slab_rows].reshape(
            owner_count * slab_rows, vector_part.shape[1]
        )
        mixer_sums = (
            lax.psum_scatter(
                rows_product(normed_rows, branch_pre_grad),
                ("seq", "fsdp"),
                scatter_dimension=0,
                tiled=True,
            ),
            lax.psum_scatter(
                rows_product(normed_rows, conv_in_low),
                ("seq", "fsdp"),
                scatter_dimension=0,
                tiled=True,
            ),
            lax.psum_scatter(
                rows_product(mixed_rows, branch_out_grad),
                ("seq", "fsdp"),
                scatter_dimension=0,
                tiled=True,
            ),
            lax.psum_scatter(vector_rows, ("seq", "fsdp"), scatter_dimension=0, tiled=True),
        )
        branch_pieces.append(mixer_sums[0])
        input_pieces.append(mixer_sums[1])
        output_pieces.append(mixer_sums[2])
        vector_pieces.append(mixer_sums[3])
    grad_gate = jnp.concatenate(gate_pieces, axis=0)
    grad_up = jnp.concatenate(up_pieces, axis=0)
    grad_down = jnp.concatenate(down_pieces, axis=0)
    grad_branch = jnp.concatenate(branch_pieces, axis=0)
    grad_input = jnp.concatenate(input_pieces, axis=0)
    grad_output = jnp.concatenate(output_pieces, axis=0)
    vector_sums = jnp.concatenate(vector_pieces, axis=0)
    edge_five = 2 * head_width
    edge_six = edge_five + tap_count
    grad_igate = vector_sums[:, :head_width]
    grad_dgate = vector_sums[:, head_width:edge_five]
    grad_conv = vector_sums[:, edge_five:edge_six]
    grad_decay = vector_sums[:, edge_six]
    grad_gain_first = vector_sums[:, edge_six + 1]
    grad_gain_second = vector_sums[:, edge_six + 2]
    return (
        result[None],
        grad_inputs,
        grad_gain_first,
        grad_branch,
        grad_input,
        grad_conv,
        grad_igate,
        grad_dgate,
        grad_decay,
        grad_output,
        grad_gain_second,
        grad_gate,
        grad_up,
        grad_down,
    )


CHUNK = 128
TAPS = 4


def gelu_parts(x):
    inner = 0.7978845608028654 * (x + 0.044715 * x * x * x)
    bent = jnp.tanh(inner)
    value = 0.5 * x * (1.0 + bent)
    slope = 0.5 * (1.0 + bent) + 0.5 * x * (1.0 - bent * bent) * 0.7978845608028654 * (
        1.0 + 3.0 * 0.044715 * x * x
    )
    return value, slope


def minus_expm1(x):
    series = x / 8.0 + 1.0
    for step in (7.0, 6.0, 5.0, 4.0, 3.0, 2.0):
        series = series * x / step + 1.0
    return jnp.where(x > -0.5, -x * series, 1.0 - jnp.exp(x))


def mixer_forward_kernel(
    conv_in_ref, pre_ref, mask_ref, taps_ref, igate_ref, dgate_ref, soft_ref,
    rounded_ref, gin_ref, gdec_ref, states_ref, earlier_ref, mixed_ref,
    padded, coef, drive,
):
    tokens, width = conv_in_ref.shape
    chunk = min(CHUNK, tokens)
    padded[0:8, :] = jnp.zeros((8, width), jnp.float32)
    soft = soft_ref[0:1, :]
    igate = igate_ref[...]
    dgate = dgate_ref[...]

    def fill(c, _):
        base = pl.multiple_of(c * chunk, chunk)
        padded[pl.ds(pl.multiple_of(base + 8, 8), chunk), :] = conv_in_ref[pl.ds(base, chunk), :].astype(jnp.float32)
        return 0

    lax.fori_loop(0, tokens // chunk, fill, 0)
    row = lax.broadcasted_iota(jnp.int32, (8, width), 0)

    def body(c, carry):
        base = pl.multiple_of(c * chunk, chunk)
        mask = mask_ref[pl.ds(base, chunk), :]
        span = padded[pl.ds(base, chunk + 8), :]
        out = taps_ref[0:1, :] * span[8:]
        for k in range(1, TAPS):
            out = out + taps_ref[k : k + 1, :] * span[8 - k : 8 - k + chunk] * mask[:, k : k + 1]
        rounded = out.astype(jnp.bfloat16)
        rounded_ref[pl.ds(base, chunk), :] = rounded
        gin = jax.nn.sigmoid(jnp.dot(rounded, igate, preferred_element_type=jnp.float32))
        gdec = jax.nn.sigmoid(jnp.dot(rounded, dgate, preferred_element_type=jnp.float32))
        gin_ref[pl.ds(base, chunk), :] = gin
        gdec_ref[pl.ds(base, chunk), :] = gdec
        log_decay = -soft * (1.0 + 7.0 * gdec)
        root = jnp.sqrt(minus_expm1(2.0 * log_decay))
        restart = mask[:, 0:1]
        carried = 1.0 - restart
        coef[...] = jnp.exp(log_decay) * carried
        drive[...] = rounded.astype(jnp.float32) * gin * (restart + carried * root)

        def tile(i, state):
            at = pl.multiple_of(i * 8, 8)
            a = coef[pl.ds(at, 8), :]
            b = drive[pl.ds(at, 8), :]
            for sh in (1, 2, 4):
                keep = row >= sh
                b = b + a * jnp.where(keep, pltpu.roll(b, sh, 0), 0.0)
                a = a * jnp.where(keep, pltpu.roll(a, sh, 0), 1.0)
            new = b + a * state
            states_ref[pl.ds(pl.multiple_of(base + at, 8), 8), :] = new
            earlier_ref[pl.ds(pl.multiple_of(base + at, 8), 8), :] = jnp.where(row == 0, state, pltpu.roll(new, 1, 0))
            return jnp.broadcast_to(new[7:8, :], (8, width))

        carry = lax.fori_loop(0, chunk // 8, tile, carry, unroll=True)
        branch, _ = gelu_parts(pre_ref[pl.ds(base, chunk), :])
        mixed_ref[pl.ds(base, chunk), :] = (states_ref[pl.ds(base, chunk), :] * branch).astype(jnp.bfloat16)
        return carry

    lax.fori_loop(0, tokens // chunk, body, jnp.zeros((8, width), jnp.float32))


def mixer_forward(conv_in, pre, mask, taps, igate, dgate, soft, width):
    tokens, total = conv_in.shape
    heads = total // width
    column = lambda h: (0, h)
    row = lambda h: (h, 0)
    whole = lambda h: (0, 0)
    big = pl.BlockSpec((tokens, width), column)
    shape = lambda kind: jax.ShapeDtypeStruct((tokens, total), kind)
    return pl.pallas_call(
        mixer_forward_kernel,
        grid=(heads,),
        in_specs=[
            big, big, pl.BlockSpec(mask.shape, whole), pl.BlockSpec((8, width), column),
            pl.BlockSpec((width, width), row), pl.BlockSpec((width, width), row),
            pl.BlockSpec((8, width), column),
        ],
        out_specs=[big] * 6,
        out_shape=[shape(jnp.bfloat16), shape(jnp.float32), shape(jnp.float32), shape(jnp.float32), shape(jnp.float32), shape(jnp.bfloat16)],
        scratch_shapes=[
            pltpu.VMEM((tokens + 8, width), jnp.float32),
            pltpu.VMEM((min(CHUNK, tokens), width), jnp.float32),
            pltpu.VMEM((min(CHUNK, tokens), width), jnp.float32),
        ],
        compiler_params=pltpu.CompilerParams(vmem_limit_bytes=48 * 2**20),
        name="mixer_forward",
    )(conv_in, pre, mask, taps, igate, dgate, soft)


def mixer_backward_kernel(
    grad_ref, pre_ref, states_ref, earlier_ref, rounded_ref, gin_ref, gdec_ref, conv_in_ref, mask_ref, ahead_ref,
    taps_ref, igate_ref, dgate_ref, soft_ref, own_ref,
    bpg_ref, cig_ref, igrad_ref, dgrad_ref, tapgrad_ref,
    padded, ahead_pad, coef, drive, decay_sum, tap_sum,
):
    tokens, width = grad_ref.shape
    chunk = min(CHUNK, tokens)
    count = tokens // chunk
    padded[0:8, :] = jnp.zeros((8, width), jnp.float32)
    ahead_pad[tokens : tokens + 8, :] = jnp.zeros((8, width), jnp.float32)
    soft = soft_ref[0:1, :]
    own = own_ref[0:1, :]
    igate = igate_ref[...]
    dgate = dgate_ref[...]
    igrad_ref[...] = jnp.zeros_like(igrad_ref)
    dgrad_ref[...] = jnp.zeros_like(dgrad_ref)
    decay_sum[...] = jnp.zeros_like(decay_sum)
    tap_sum[...] = jnp.zeros_like(tap_sum)
    row = lax.broadcasted_iota(jnp.int32, (8, width), 0)
    rows_dot = lambda a, b: lax.dot_general(a, b, (((0,), (0,)), ((), ())), preferred_element_type=jnp.float32)
    last_dot = lambda a, b: lax.dot_general(a, b, (((1,), (1,)), ((), ())), preferred_element_type=jnp.float32)

    def body(step, carry):
        c = count - 1 - step
        base = pl.multiple_of(c * chunk, chunk)
        here = pl.ds(base, chunk)
        padded[pl.ds(pl.multiple_of(base + 8, 8), chunk), :] = conv_in_ref[here, :].astype(jnp.float32)
        mask = mask_ref[here, :]
        restart = mask[:, 0:1]
        carried = 1.0 - restart
        branch, slope = gelu_parts(pre_ref[here, :])
        grad = grad_ref[here, :]
        bpg_ref[here, :] = (grad * states_ref[here, :] * slope * own).astype(jnp.bfloat16)
        gdec = gdec_ref[here, :]
        gin = gin_ref[here, :]
        log_decay = -soft * (1.0 + 7.0 * gdec)
        decays = jnp.exp(log_decay)
        root = jnp.sqrt(minus_expm1(2.0 * log_decay))
        coef[...] = decays * carried
        drive[...] = grad * branch

        def tile(i, pair):
            adj_next, coef_next = pair
            at = pl.multiple_of(chunk - 8 - i * 8, 8)
            first = coef[pl.ds(at, 8), :]
            a = jnp.where(row == 7, coef_next, pltpu.roll(first, 7, 0))
            b = drive[pl.ds(at, 8), :]
            for sh in (1, 2, 4):
                keep = row < 8 - sh
                b = b + a * jnp.where(keep, pltpu.roll(b, 8 - sh, 0), 0.0)
                a = a * jnp.where(keep, pltpu.roll(a, 8 - sh, 0), 1.0)
            new = b + a * adj_next
            drive[pl.ds(at, 8), :] = new
            return jnp.broadcast_to(new[0:1, :], (8, width)), jnp.broadcast_to(first[0:1, :], (8, width))

        carry = lax.fori_loop(0, chunk // 8, tile, carry, unroll=True)
        adjoint = drive[...]
        rounded = rounded_ref[here, :]
        rounded_float = rounded.astype(jnp.float32)
        pull = adjoint * carried * decays
        log_grad = pull * (earlier_ref[here, :] - rounded_float * gin * decays / root)
        decay_sum[...] += jnp.sum((-log_grad * (1.0 + 7.0 * gdec)).reshape(chunk // 8, 8, width), axis=0)
        through = adjoint * gin * (restart + carried * root)
        ipg = (through * rounded_float * (1.0 - gin)).astype(jnp.bfloat16)
        dpg = (log_grad * (-7.0 * soft) * gdec * (1.0 - gdec)).astype(jnp.bfloat16)
        igrad_ref[...] += rows_dot(rounded, ipg)
        dgrad_ref[...] += rows_dot(rounded, dpg)
        through = through + last_dot(ipg, igate) + last_dot(dpg, dgate)
        ahead_pad[here, :] = through.astype(jnp.bfloat16).astype(jnp.float32)
        return carry

    zero = jnp.zeros((8, width), jnp.float32)
    lax.fori_loop(0, count, body, (zero, zero))

    def after(c, _):
        base = pl.multiple_of(c * chunk, chunk)
        here = pl.ds(base, chunk)
        mask = mask_ref[here, :]
        ahead = ahead_ref[here, :]
        later = ahead_pad[pl.ds(base, chunk + 8), :]
        span = padded[pl.ds(base, chunk + 8), :]
        grad = later[:chunk]
        total = taps_ref[0:1, :] * grad
        tap_sum[0:8, :] += jnp.sum((grad * span[8:]).reshape(chunk // 8, 8, width), axis=0)
        for k in range(1, TAPS):
            total = total + taps_ref[k : k + 1, :] * later[k : k + chunk] * ahead[:, k : k + 1]
            shifted = span[8 - k : 8 - k + chunk]
            tap_sum[8 * k : 8 * k + 8, :] += jnp.sum((grad * shifted * mask[:, k : k + 1]).reshape(chunk // 8, 8, width), axis=0)
        cig_ref[here, :] = (total * own).astype(jnp.bfloat16)
        return 0

    lax.fori_loop(0, count, after, 0)
    for k in range(TAPS):
        tapgrad_ref[k : k + 1, :] = jnp.sum(tap_sum[8 * k : 8 * k + 8, :], axis=0, keepdims=True)
    tapgrad_ref[4:5, :] = jnp.sum(decay_sum[...], axis=0, keepdims=True)
    tapgrad_ref[5:8, :] = jnp.zeros((3, width), jnp.float32)


def mixer_backward(grad, pre, states, earlier, rounded, gin, gdec, conv_in, mask, ahead, taps, igate, dgate, soft, own, width):
    tokens, total = grad.shape
    heads = total // width
    column = lambda h: (0, h)
    row = lambda h: (h, 0)
    whole = lambda h: (0, 0)
    big = pl.BlockSpec((tokens, width), column)
    line = pl.BlockSpec((8, width), column)
    square = pl.BlockSpec((width, width), row)
    shape = lambda kind: jax.ShapeDtypeStruct((tokens, total), kind)
    chunk = min(CHUNK, tokens)
    return pl.pallas_call(
        mixer_backward_kernel,
        grid=(heads,),
        in_specs=[big] * 8 + [pl.BlockSpec(mask.shape, whole)] * 2 + [line, square, square, line, line],
        out_specs=[big, big, square, square, line],
        out_shape=[
            shape(jnp.bfloat16), shape(jnp.bfloat16),
            jax.ShapeDtypeStruct((total, width), jnp.float32), jax.ShapeDtypeStruct((total, width), jnp.float32),
            jax.ShapeDtypeStruct((8, total), jnp.float32),
        ],
        scratch_shapes=[
            pltpu.VMEM((tokens + 8, width), jnp.float32),
            pltpu.VMEM((tokens + 8, width), jnp.float32),
            pltpu.VMEM((chunk, width), jnp.float32),
            pltpu.VMEM((chunk, width), jnp.float32),
            pltpu.VMEM((8, width), jnp.float32),
            pltpu.VMEM((8 * TAPS, width), jnp.float32),
        ],
        compiler_params=pltpu.CompilerParams(vmem_limit_bytes=56 * 2**20),
        name="mixer_backward",
    )(grad, pre, states, earlier, rounded, gin, gdec, conv_in, mask, ahead, taps, igate, dgate, soft, own)


MESH_ID = pl.DeviceIdType.MESH
PIECES = 4


class Spot:
    def __init__(self):
        self.s = lax.axis_index("seq")
        self.f = lax.axis_index("fsdp")
        self.z = self.s // 2
        self.y = self.s % 2
        self.up = (self.z < 3, (jnp.minimum(self.s + 2, 7), self.f))
        self.down = (self.z > 0, (jnp.maximum(self.s - 2, 0), self.f))
        self.beside = (None, (self.s ^ 1, self.f))
        self.across = (None, (self.s, self.f ^ 2))
        self.twin = (None, (self.s, self.f ^ 1))

    def peer(self, j):
        return (None, (self.s ^ j, self.f))

    def other(self, j):
        return (None, (self.s ^ (j // 4), self.f ^ (j % 4)))

    def meet(self, reach):
        barrier = pltpu.get_barrier_semaphore()
        if "all" in reach:
            peers = [self.other(j) for j in range(1, 32)]
        else:
            peers = [self.peer(j) for j in range(1, 8)] if "seq" in reach else []
            if "line" in reach and not peers:
                peers = [self.up, self.down, self.beside]
            if "pair" in reach:
                peers += [self.across, self.twin]
        count = 0
        for cond, where in peers:
            count = count + (1 if cond is None else cond.astype(jnp.int32))
            guarded(cond, lambda: pl.semaphore_signal(barrier, 1, device_id=where, device_id_type=MESH_ID))
        pl.semaphore_wait(barrier, count)


def guarded(cond, action):
    if cond is None:
        action()
    else:
        pl.when(cond)(action)


class Send:
    def __init__(self, src, dst, send_sem, recv_sem, target):
        self.cond, where = target
        self.copy = pltpu.make_async_remote_copy(
            src_ref=src, dst_ref=dst, send_sem=send_sem, recv_sem=recv_sem, device_id=where, device_id_type=MESH_ID
        )

    def start(self):
        guarded(self.cond, self.copy.start)

    def sent(self):
        guarded(self.cond, self.copy.wait_send)


def arrived(dst, send_sem, recv_sem, target, cond=None):
    copy = pltpu.make_async_remote_copy(
        src_ref=dst, dst_ref=dst, send_sem=send_sem, recv_sem=recv_sem, device_id=target[1], device_id_type=MESH_ID
    )
    guarded(cond, copy.wait_recv)


class Gather:
    letter = "g"
    def __init__(self, x):
        self.ins = [x]
        self.outs = [jax.ShapeDtypeStruct((8,) + x.shape, x.dtype)]
        dma = pltpu.SemaphoreType.DMA
        self.scratch = [dma((1,)), dma((8, PIECES)), dma((4, PIECES)), dma((4, PIECES)), dma((7, PIECES))]

    reach = ("line",)

    def steps(self, at, ins, outs, scratch):
        (x,), (o,) = ins, outs
        own_sem, recv, ups, downs, sides = scratch
        rows = x.shape[0] // PIECES
        cut = lambda p: pl.ds(p * rows, rows)
        sends = []

        def send(src, block, p, sem, target):
            one = Send(src, o.at[block, cut(p)], sem, recv.at[block, p], target)
            one.start()
            sends.append(one)

        own = pltpu.make_async_copy(x, o.at[at.s], own_sem.at[0])
        own.start()
        for p in range(PIECES):
            send(x.at[cut(p)], at.s, p, ups.at[0, p], at.up)
            send(x.at[cut(p)], at.s, p, downs.at[0, p], at.down)
            send(x.at[cut(p)], at.s, p, sides.at[0, p], at.beside)
        yield
        for d in range(1, 4):
            for p in range(PIECES):
                low, high = at.z >= d, at.z + d <= 3
                block = jnp.maximum(at.s - 2 * d, 0)
                arrived(o.at[block, cut(p)], ups.at[0, p], recv.at[block, p], at.down, low)
                if d < 3:
                    send(o.at[block, cut(p)], block, p, ups.at[d, p], (low & (at.z < 3), at.up[1]))
                send(o.at[block, cut(p)], block, p, sides.at[d, p], (low, at.beside[1]))
                block = jnp.minimum(at.s + 2 * d, 7)
                arrived(o.at[block, cut(p)], ups.at[0, p], recv.at[block, p], at.up, high)
                if d < 3:
                    send(o.at[block, cut(p)], block, p, downs.at[d, p], (high & (at.z > 0), at.down[1]))
                send(o.at[block, cut(p)], block, p, sides.at[3 + d, p], (high, at.beside[1]))
                yield
        for z in range(4):
            for p in range(PIECES):
                block = 2 * z + 1 - at.y
                arrived(o.at[block, cut(p)], ups.at[0, p], recv.at[block, p], at.beside)
        yield
        for one in sends:
            one.sent()
        own.wait()


class Reduce:
    letter = "r"
    def __init__(self, x):
        _, rows, width = x.shape
        self.ins = [x]
        self.outs = [jax.ShapeDtypeStruct((rows, width), jnp.float32)]
        dma = pltpu.SemaphoreType.DMA
        hold = pltpu.VMEM((4, rows, width), x.dtype)
        self.scratch = [hold, hold, hold, hold, pltpu.VMEM((rows, width), jnp.float32)]
        self.scratch += [dma((4, PIECES)) for _ in range(6)] + [dma((1,))]

    reach = ("line",)

    def steps(self, at, ins, outs, scratch):
        (x,), (o,) = ins, outs
        mine, side, below, above, total, load, ysend, yrecv, zsend, urecv, drecv, osem = scratch
        rows = x.shape[1] // PIECES
        cut = lambda p: pl.ds(p * rows, rows)
        group = 16
        sends = []
        order = []
        for k in range(3):
            order.append((3 - k, at.z < 3 - k, True))
            order.append((k, at.z > k, False))
        order.append((at.z, None, None))

        loads = []
        for t, cond, _ in order:
            for p in range(PIECES):
                one = Send(x.at[2 * t + 1 - at.y, cut(p)], side.at[t, cut(p)], ysend.at[t, p], yrecv.at[t, p], (cond, at.beside[1]))
                one.start()
                sends.append(one)
                copy = pltpu.make_async_copy(x.at[2 * t + at.y, cut(p)], mine.at[t, cut(p)], load.at[t, p])
                guarded(cond, copy.start)
        yield
        for t, cond, rising in order:
            for p in range(PIECES):
                copy = pltpu.make_async_copy(x.at[2 * t + at.y, cut(p)], mine.at[t, cut(p)], load.at[t, p])
                guarded(cond, copy.wait)
                arrived(side.at[t, cut(p)], ysend.at[t, p], yrecv.at[t, p], at.beside, cond)
                if rising is None:
                    arrived(below.at[t, cut(p)], zsend.at[t, p], urecv.at[t, p], at.down, at.z > 0)
                    arrived(above.at[t, cut(p)], zsend.at[t, p], drecv.at[t, p], at.up, at.z < 3)

                    def final(i, _):
                        here = pl.ds(pl.multiple_of(p * rows + i * group, group), group)
                        value = mine[t, here, :].astype(jnp.float32) + side[t, here, :].astype(jnp.float32)
                        total[here, :] = value

                        @pl.when(at.z > 0)
                        def _():
                            total[here, :] += below[t, here, :].astype(jnp.float32)

                        @pl.when(at.z < 3)
                        def _():
                            total[here, :] += above[t, here, :].astype(jnp.float32)

                        return 0

                    lax.fori_loop(0, rows // group, final, 0)
                else:
                    source = below if rising else above
                    inner = (cond & (at.z > 0)) if rising else (cond & (at.z < 3))
                    outer = (cond & (at.z == 0)) if rising else (cond & (at.z == 3))
                    rsem = urecv if rising else drecv
                    arrived(source.at[t, cut(p)], zsend.at[t, p], rsem.at[t, p], at.down if rising else at.up, inner)

                    def add(with_source):
                        def one(i, _):
                            here = pl.ds(pl.multiple_of(p * rows + i * group, group), group)
                            value = mine[t, here, :].astype(jnp.float32) + side[t, here, :].astype(jnp.float32)
                            if with_source:
                                value = value + source[t, here, :].astype(jnp.float32)
                            mine[t, here, :] = value.astype(mine.dtype)
                            return 0

                        lax.fori_loop(0, rows // group, one, 0)

                    pl.when(inner)(lambda: add(True))
                    pl.when(outer)(lambda: add(False))
                    one = Send(mine.at[t, cut(p)], source.at[t, cut(p)], zsend.at[t, p], rsem.at[t, p], (cond, (at.up if rising else at.down)[1]))
                    one.start()
                    sends.append(one)
                yield
        out = pltpu.make_async_copy(total, o, osem.at[0])
        out.start()
        for one in sends:
            one.sent()
        out.wait()


class Spread:
    letter = "s"
    reach = ("seq", "pair")

    def __init__(self, x, starts, wide, letter="s"):
        self.ins = [x]
        self.starts, self.wide, self.letter = starts, wide, letter
        self.outs = [jax.ShapeDtypeStruct((8, 4, x.shape[0], wide), x.dtype)]
        dma = pltpu.SemaphoreType.DMA
        self.scratch = [dma((8,)), dma((8,)), dma((8,)), dma((8,)), dma((8, 2)), dma((8, 2))]

    def steps(self, at, ins, outs, scratch):
        (x,), (o,) = ins, outs
        asend, arecv, xsend, xrecv, csend, crecv = scratch
        sends = []
        part = lambda to: x.at[:, pl.ds(pl.multiple_of(self.starts(to), 128), self.wide)]

        def send(src, dst, ss, rs, target):
            one = Send(src, dst, ss, rs, target)
            one.start()
            sends.append(one)

        for j in range(1, 8):
            send(part(at.s ^ j), o.at[at.s, at.f], asend.at[j], arecv.at[j], at.peer(j))
        own = pltpu.make_async_copy(part(at.s), o.at[at.s, at.f], asend.at[0])
        own.start()
        yield
        for j in range(8):
            block = at.s ^ j
            here = o.at[block, at.f]
            if j == 0:
                own.wait()
            else:
                arrived(here, asend.at[j], arecv.at[j], at.peer(j))
            send(here, here, xsend.at[j], xrecv.at[j], at.across)
            send(here, here, csend.at[j, 0], crecv.at[j, 0], at.twin)
            yield
        for j in range(8):
            there = o.at[at.s ^ j, at.f ^ 2]
            arrived(there, xsend.at[j], xrecv.at[j], at.across)
            send(there, there, csend.at[j, 1], crecv.at[j, 1], at.twin)
            yield
        for j in range(8):
            for k in range(2):
                arrived(o.at[at.s ^ j, (at.f ^ 1) ^ (2 * k)], csend.at[j, k], crecv.at[j, k], at.twin)
        for one in sends:
            one.sent()


def add_rows(dst, terms, rows):
    group = 16

    def one(i, _):
        here = pl.ds(pl.multiple_of(i * group, group), group)
        value = terms[0][here, :].astype(jnp.float32)
        for term in terms[1:]:
            value = value + term[here, :].astype(jnp.float32)
        dst[here, :] = value.astype(dst.dtype)
        return 0

    lax.fori_loop(0, rows // group, one, 0)


class Collect:
    letter = "c"
    def __init__(self, x, window=None):
        self.window = window
        blocks, rows, width = (1, window.rows, x.shape[1]) if window else (x.shape[0],) + x.shape[2:]
        self.shape = (blocks, rows, width)
        self.ins = [x]
        self.blocks = blocks
        self.reach = ("seq", "pair") if blocks > 1 else ("pair",)
        self.outs = [jax.ShapeDtypeStruct((blocks, rows, width), x.dtype)]
        dma = pltpu.SemaphoreType.DMA
        hold = pltpu.VMEM((blocks, rows, width), x.dtype)
        self.scratch = [pltpu.VMEM((2, rows, width), x.dtype)] + [hold] * 3 + [dma((2,))] + [dma((blocks, 2))] * 2 + [dma((blocks,))] * 4

    def steps(self, at, ins, outs, scratch):
        (x,), (o,) = ins, outs
        stage, tnear, tfar, xin, lsem, csend, crecv, xsend, xrecv, asend, arecv = scratch
        rows = self.shape[1]
        many = self.blocks > 1
        spot = (lambda j: at.s ^ j) if many else (lambda j: j)
        sends = []

        def part(j, whose):
            if self.window is None:
                return x.at[spot(j), whose]
            return x.at[pl.ds(pl.multiple_of(self.window.offset(at.s) + rows * whose, 16), rows)]

        def send(src, dst, ss, rs, target):
            one = Send(src, dst, ss, rs, target)
            one.start()
            sends.append(one)

        order = [j for j in range(1, 8)] + [0] if many else [0]
        pieces = [(j, at.f ^ 2) for j in order] + [(j, at.f) for j in order]

        def load(i):
            j, whose = pieces[i]
            return pltpu.make_async_copy(part(j, whose), stage.at[i % 2], lsem.at[i % 2])

        for j in order:
            send(part(j, at.f ^ 3), tfar.at[j], csend.at[j, 0], crecv.at[j, 0], at.twin)
            send(part(j, at.f ^ 1), tnear.at[j], csend.at[j, 1], crecv.at[j, 1], at.twin)
        load(0).start()
        yield
        outs_done = []
        for i, (j, _) in enumerate(pieces):
            far = i < len(order)
            if i + 1 < len(pieces):
                load(i + 1).start()
            load(i).wait()
            if far:
                arrived(tfar.at[j], csend.at[j, 0], crecv.at[j, 0], at.twin)
                add_rows(tfar.at[j], (tfar.at[j], stage.at[i % 2]), rows)
                send(tfar.at[j], xin.at[j], xsend.at[j], xrecv.at[j], at.across)
            else:
                arrived(tnear.at[j], csend.at[j, 1], crecv.at[j, 1], at.twin)
                arrived(xin.at[j], xsend.at[j], xrecv.at[j], at.across)
                add_rows(tnear.at[j], (tnear.at[j], stage.at[i % 2], xin.at[j]), rows)
                if j:
                    send(tnear.at[j], o.at[at.s], asend.at[j], arecv.at[j], at.peer(j))
                else:
                    outs_done.append(pltpu.make_async_copy(tnear.at[0], o.at[at.s if many else 0], asend.at[0]))
                    outs_done[-1].start()
            yield
        for j in order:
            if j:
                arrived(o.at[at.s ^ j], asend.at[j], arecv.at[j], at.peer(j))
        for one in sends:
            one.sent()
        for one in outs_done:
            one.wait()


class Tiny:
    letter = "t"
    def __init__(self, x):
        self.ins = [x]
        self.outs = [jax.ShapeDtypeStruct((32,) + x.shape[1:], x.dtype)]
        self.same = x.shape[0] == 1
        dma = pltpu.SemaphoreType.DMA
        self.scratch = [dma((32,)), dma((32,))]

    reach = ("all",)

    def steps(self, at, ins, outs, scratch):
        (x,), (o,) = ins, outs
        ss, rs = scratch
        me = at.s * 4 + at.f
        part = lambda to: x.at[0] if self.same else x.at[to]
        sends = []
        for j in range(1, 32):
            one = Send(part(me ^ j), o.at[me], ss.at[j], rs.at[j], at.other(j))
            one.start()
            sends.append(one)
        own = pltpu.make_async_copy(part(me), o.at[me], ss.at[0])
        own.start()
        for _ in range(40):
            yield
        for j in range(1, 32):
            arrived(o.at[me ^ j], ss.at[j], rs.at[j], at.other(j))
        for one in sends:
            one.sent()
        own.wait()


class Chain:
    @staticmethod
    def scratch(rows, width, kind):
        dma = pltpu.SemaphoreType.DMA
        return [
            pltpu.VMEM((4, rows, width), kind),
            pltpu.VMEM((5, rows, width), kind),
            pltpu.VMEM((rows, width), jnp.float32),
            dma((4, PIECES)),
            dma((4, PIECES)),
            dma((4, PIECES)),
            dma((5, PIECES)),
            dma((1,)),
        ]

    def __init__(self, at, parts, out, scratch, order):
        self.at, self.parts, self.out, self.order = at, parts, out, order
        self.side, self.inflow, self.total, self.ysend, self.yrecv, self.zsend, self.zrecv, self.osem = scratch
        self.rows = parts.shape[1] // PIECES

    def cut(self, p):
        return pl.ds(pl.multiple_of(p * self.rows, self.rows), self.rows)

    def side_copy(self, t, p):
        at = self.at
        return Send(
            self.parts.at[2 * t + 1 - at.y, self.cut(p)], self.side.at[t, self.cut(p)], self.ysend.at[t, p], self.yrecv.at[t, p], at.beside
        )

    def send_side(self, t):
        for p in range(PIECES):
            self.side_copy(t, p).start()

    def z_copy(self, t, p, rising):
        at = self.at
        slot = t if rising else jnp.where(t == at.z - 1, 4, t)
        mine = self.parts.at[2 * t + at.y, self.cut(p)]
        target = (None, (at.up if rising else at.down)[1])
        return Send(mine, self.inflow.at[slot, self.cut(p)], self.zsend.at[t, p], self.zrecv.at[slot, p], target)

    def wait_side(self, t, p):
        arrived(self.side.at[t, self.cut(p)], self.ysend.at[t, p], self.yrecv.at[t, p], self.at.beside)

    def wait_inflow(self, slot, p):
        arrived(self.inflow.at[slot, self.cut(p)], self.zsend.at[0, p], self.zrecv.at[slot, p], self.at.down)

    def step(self, k, p):
        at = self.at
        group = 16
        rises, falls = self.order(k)
        for t, cond, rising in ((rises, at.z < rises, True), (falls, at.z > falls, False)):

            @pl.when(cond)
            def _():
                self.wait_side(t, p)
                first = at.z == (0 if rising else 3)

                def add(inner):
                    def one(i, _):
                        here = pl.ds(pl.multiple_of(p * self.rows + i * group, group), group)
                        value = self.parts[2 * t + at.y, here, :].astype(jnp.float32) + self.side[t, here, :].astype(jnp.float32)
                        if inner:
                            value = value + self.inflow[t, here, :].astype(jnp.float32)
                        self.parts[2 * t + at.y, here, :] = value.astype(self.parts.dtype)
                        return 0

                    lax.fori_loop(0, self.rows // group, one, 0)

                pl.when(first)(lambda: add(False))

                @pl.when(jnp.logical_not(first))
                def _():
                    self.wait_inflow(t, p)
                    add(True)

                self.z_copy(t, p, rising).start()

    def last(self, p):
        at = self.at
        group = 16
        self.wait_side(at.z, p)
        pl.when(at.z > 0)(lambda: self.wait_inflow(at.z, p))
        pl.when(at.z < 3)(lambda: self.wait_inflow(4, p))

        def one(i, _):
            here = pl.ds(pl.multiple_of(p * self.rows + i * group, group), group)
            self.total[here, :] = self.parts[at.s, here, :].astype(jnp.float32) + self.side[at.z, here, :].astype(jnp.float32)

            @pl.when(at.z > 0)
            def _():
                self.total[here, :] += self.inflow[at.z, here, :].astype(jnp.float32)

            @pl.when(at.z < 3)
            def _():
                self.total[here, :] += self.inflow[4, here, :].astype(jnp.float32)

            return 0

        lax.fori_loop(0, self.rows // group, one, 0)

    def finish(self):
        def one(p, _):
            self.last(p)
            return 0

        lax.fori_loop(0, PIECES, one, 0)
        self.out_copy().start()

    def out_copy(self):
        return pltpu.make_async_copy(self.total, self.out, self.osem.at[0])

    def sent(self):
        def one(i, _):
            t, p = i // PIECES, lax.rem(i, PIECES)
            self.side_copy(t, p).sent()

            @pl.when(t != self.at.z)
            def _():
                self.z_copy(t, p, True).sent()

            return 0

        lax.fori_loop(0, 4 * PIECES, one, 0)
        self.out_copy().wait()


def outward(k):
    rises = jnp.where(k == 0, 1, jnp.where(k == 1, 3, 2))
    return rises, 3 - rises


def farthest(k):
    return 3 - k, k


def descending(k):
    return 3 - k, (2, 0, 1)[k]


class Dense:
    letter = "d"
    reach = ("line",)

    def __init__(self, hidden, returned, w_gate, w_up, w_down, held):
        rows, width = hidden.shape
        wide = w_gate.shape[1]
        low = hidden.dtype
        dma = pltpu.SemaphoreType.DMA
        self.ins = [hidden, returned, w_gate, w_up, w_down, held]
        sums = jax.ShapeDtypeStruct((rows, width), jnp.float32)
        grad = jax.ShapeDtypeStruct((width, wide), low)
        self.outs = [sums, jax.ShapeDtypeStruct((8, rows, width), low), grad, grad, grad]
        tokens = pltpu.VMEM((8, rows, width), low)
        weight = pltpu.VMEM((width, wide), low)
        inner = pltpu.VMEM((8, rows, wide), low)
        self.own = [tokens, tokens, weight, weight, weight, inner, inner, inner, tokens, tokens, pltpu.VMEM(held.shape, held.dtype), dma((8,))]
        self.gather = Gather(hidden)
        self.chain = Chain.scratch(rows, width, low)
        self.scratch = self.own + self.gather.scratch + self.chain

    def steps(self, at, ins, outs, scratch):
        hidden, returned, w_gate, w_up, w_down, held = ins
        count = len(self.own)
        toks, cots, wg, wu, wd, act, ggrad, ugrad, hpart, rpart, mask, sems = scratch[:count]
        scratch = scratch[count:]
        gsems, scratch = scratch[: len(self.gather.scratch)], scratch[len(self.gather.scratch) :]
        hchain = Chain(at, hpart, outs[0], scratch, outward)
        rows, width = hidden.shape
        wide = w_gate.shape[1]
        tile = 256
        loads = [
            pltpu.make_async_copy(src, dst, sems.at[i])
            for i, (src, dst) in enumerate(((w_gate, wg), (w_up, wu), (w_down, wd), (returned, cots), (held, mask)))
        ]
        relay = Relay(at, hidden, toks, gsems)
        relay.begin()
        for load in loads:
            load.start()
        yield
        for p in range(PIECES):
            relay.step(1, p)
        for load in loads:
            load.wait()
        relay.own_copy().wait()
        last_dot = lambda a, b: lax.dot_general(a, b, CONTRACT_LAST, preferred_element_type=jnp.float32)
        rows_dot = lambda a, b: lax.dot_general(a, b, CONTRACT_ROWS, preferred_element_type=jnp.float32)

        def pair(i, _):
            far = at.z < 2
            t = jnp.where(
                i == 0, at.z, jnp.where(i == 1, at.z ^ 1, jnp.where(i == 2, jnp.where(far, 2, 1), jnp.where(far, 3, 0)))
            )
            relay.wait_beside(t)

            @pl.when(i == 3)
            def _():
                hchain.send_side(at.z ^ 1)

            both = pl.ds(2 * t, 2)

            def first(n, _):
                lanes = pl.ds(pl.multiple_of(n * tile, tile), tile)
                h = toks[both].reshape(2 * rows, width)
                c = cots[both].reshape(2 * rows, width)
                pre = jnp.dot(h, wg[:, lanes], preferred_element_type=jnp.float32)
                up = jnp.dot(h, wu[:, lanes], preferred_element_type=jnp.float32)
                grad = jnp.dot(c, wd[:, lanes], preferred_element_type=jnp.float32)
                value, slope = gelu_parts(pre)
                keep = mask[0:1, lanes]
                put = lambda ref, v: ref.__setitem__((both, slice(None), lanes), v.astype(ref.dtype).reshape(2, rows, tile))
                put(act, value * up * keep)
                put(ggrad, grad * up * slope * keep)
                put(ugrad, grad * value * keep)
                for p in range(PIECES // 2):
                    pl.when(n == (p + 1) * wide // tile // (PIECES // 2) - 1)(lambda: relay.step(i + 2, p))
                return 0

            lax.fori_loop(0, wide // tile, first, 0)

            def second(n, _):
                lanes = pl.ds(pl.multiple_of(n * tile, tile), tile)
                a = act[both].reshape(2 * rows, wide)
                g = ggrad[both].reshape(2 * rows, wide)
                u = ugrad[both].reshape(2 * rows, wide)
                put = lambda ref, v: ref.__setitem__((both, slice(None), lanes), v.astype(ref.dtype).reshape(2, rows, tile))
                put(hpart, last_dot(g, wg[lanes, :]) + last_dot(u, wu[lanes, :]))
                put(rpart, last_dot(a, wd[lanes, :]))
                for p in range(PIECES // 2):
                    pl.when(n == 2 + p * (8 // PIECES + 1 if PIECES > 4 else 4))(lambda: relay.step(i + 2, PIECES // 2 + p))
                return 0

            lax.fori_loop(0, width // tile, second, 0)
            return 0

        lax.fori_loop(0, 4, pair, 0)
        hchain.send_side(jnp.where(at.z < 2, 3, 0))
        hchain.send_side(jnp.where(at.z < 2, 2, 1))
        hchain.send_side(at.z)
        out = pltpu.make_async_copy(rpart, outs[1], sems.at[7])
        out.start()

        def grads(r):
            lanes = pl.ds(pl.multiple_of(r * tile, tile), tile)
            h = toks[:, :, lanes].reshape(8 * rows, tile)
            c = cots[:, :, lanes].reshape(8 * rows, tile)
            wg[lanes, :] = rows_dot(h, ggrad[...].reshape(8 * rows, wide)).astype(wg.dtype)
            wu[lanes, :] = rows_dot(h, ugrad[...].reshape(8 * rows, wide)).astype(wu.dtype)
            wd[lanes, :] = rows_dot(c, act[...].reshape(8 * rows, wide)).astype(wd.dtype)

        def hstep(i, _):
            hchain.step(i // PIECES, lax.rem(i, PIECES))
            pl.when(i < width // tile)(lambda: grads(i))
            return 0

        lax.fori_loop(0, 3 * PIECES, hstep, 0)
        hchain.finish()
        stores = [pltpu.make_async_copy(src, dst, sems.at[i]) for i, (src, dst) in enumerate(((wg, outs[2]), (wu, outs[3]), (wd, outs[4])))]
        for store in stores:
            store.start()
        hchain.sent()
        relay.sent()
        for store in stores + [out]:
            store.wait()
        yield


class Relay:
    def __init__(self, at, x, o, sems):
        self.at, self.x, self.o = at, x, o
        self.own_sem, self.recv, self.ups, self.downs, self.sides = sems
        self.rows = x.shape[0] // PIECES

    def cut(self, p):
        return pl.ds(p * self.rows, self.rows)

    def copy(self, src, block, p, sem, target):
        return Send(src, self.o.at[block, self.cut(p)], sem, self.recv.at[block, p], target)

    def own_copy(self):
        return pltpu.make_async_copy(self.x, self.o.at[self.at.s], self.own_sem.at[0])

    def begin(self):
        at = self.at
        self.own_copy().start()
        for p in range(PIECES):
            src = self.x.at[self.cut(p)]
            self.copy(src, at.s, p, self.ups.at[0, p], at.up).start()
            self.copy(src, at.s, p, self.downs.at[0, p], at.down).start()
            self.copy(src, at.s, p, self.sides.at[0, p], at.beside).start()

    def halves(self, d):
        at = self.at
        low = (at.z >= d, jnp.maximum(at.s - 2 * d, 0), self.ups, at.up, d, at.down)
        high = (at.z + d <= 3, jnp.minimum(at.s + 2 * d, 7), self.downs, at.down, 3 + d, at.up)
        return low, high

    def step(self, d, p):
        for cond, block, along, ahead, slot, source in self.halves(d):

            @pl.when(cond)
            def _():
                here = self.o.at[block, self.cut(p)]
                arrived(here, self.ups.at[0, p], self.recv.at[block, p], source)
                self.copy(here, block, p, along.at[d, p], ahead).start()
                self.copy(here, block, p, self.sides.at[slot, p], self.at.beside).start()

    def begin_rising(self):
        at = self.at
        self.own_copy().start()
        for p in range(PIECES):
            src = self.x.at[self.cut(p)]
            self.copy(src, at.s, p, self.ups.at[0, p], at.up).start()
            self.copy(src, at.s, p, self.sides.at[0, p], at.beside).start()

    def take(self, half, d, p):
        cond, block, along, ahead, slot, source = half

        @pl.when(cond)
        def _():
            here = self.o.at[block, self.cut(p)]
            arrived(here, self.ups.at[0, p], self.recv.at[block, p], source)
            self.copy(here, block, p, along.at[d, p], ahead).start()
            self.copy(here, block, p, self.sides.at[slot, p], self.at.beside).start()

    def step_up(self, d, p):
        self.take(self.halves(d)[0], d, p)

    def step_down(self, k, p):
        at = self.at
        d = jnp.maximum(3 - k - at.z, 0)
        high = self.halves(d)[1]
        self.take((at.z < 3 - k,) + high[1:], d, p)

    def own_down(self, top):
        at = self.at
        for p in range(PIECES):

            @pl.when(at.z == 3 if top else at.z < 3)
            def _():
                self.copy(self.x.at[self.cut(p)], at.s, p, self.downs.at[0, p], at.down).start()

    def wait_beside(self, t):
        block = 2 * t + 1 - self.at.y
        for p in range(PIECES):
            arrived(self.o.at[block, self.cut(p)], self.ups.at[0, p], self.recv.at[block, p], self.at.beside)

    def sent(self):
        at = self.at
        for p in range(PIECES):
            src = self.x.at[self.cut(p)]
            self.copy(src, at.s, p, self.ups.at[0, p], at.up).sent()
            self.copy(src, at.s, p, self.downs.at[0, p], at.down).sent()
            self.copy(src, at.s, p, self.sides.at[0, p], at.beside).sent()
            for d in range(1, 4):
                for cond, block, along, ahead, slot, source in self.halves(d):

                    @pl.when(cond)
                    def _():
                        here = self.o.at[block, self.cut(p)]
                        self.copy(here, block, p, along.at[d, p], ahead).sent()
                        self.copy(here, block, p, self.sides.at[slot, p], at.beside).sent()


def exchange(jobs, collective, name, plan=()):
    def kernel(*refs):
        at = Spot()
        refs = list(refs)
        take = lambda count: [refs.pop(0) for _ in range(count)]
        ins = [take(len(job.ins)) for job in jobs]
        outs = [take(len(job.outs)) for job in jobs]
        scratch = [take(len(job.scratch)) for job in jobs]
        at.meet({one for job in jobs for one in job.reach})
        running = [job.steps(at, i, o, s) for job, i, o, s in zip(jobs, ins, outs, scratch)]
        turns = iter(plan)
        while running:
            if plan and running[0] is not None:
                if next(running[0], plan) is plan:
                    running[0] = None
                for letter in next(turns, ""):
                    for job, one in zip(jobs, running):
                        if one is not None and job.letter == letter:
                            next(one, None)
            else:
                running = [one for one in running if one is not None and next(one, running) is not running]

    count = sum(len(job.ins) for job in jobs)
    return pl.pallas_call(
        kernel,
        out_shape=[shape for job in jobs for shape in job.outs],
        in_specs=[pl.BlockSpec(memory_space=pl.ANY)] * count,
        out_specs=[pl.BlockSpec(memory_space=pl.ANY)] * sum(len(job.outs) for job in jobs),
        scratch_shapes=[shape for job in jobs for shape in job.scratch],
        compiler_params=pltpu.CompilerParams(
            collective_id=collective, has_side_effects=True, vmem_limit_bytes=62 * 2**20
        ),
        name=name,
    )(*[x for job in jobs for x in job.ins])


class Window:
    def __init__(self, own, head, width, rows):
        self.own, self.head, self.heads, self.rows = own, head, width // head, rows
        self.size = 2 * head

    def first(self, s):
        return self.head * jnp.minimum(self.own * s // self.head, self.heads - 2)

    def offset(self, s):
        return self.own * s - self.first(s)

    def takes(self, s, slot, f):
        before = self.offset(s)
        if slot == 0:
            return self.own - before < (f + 1) * self.rows
        return f * self.rows < self.size - self.own - before


class Rows:
    letter = "o"

    def __init__(self, x, window=None):
        self.window = window
        self.slots = 1 if window is None else 3
        self.reach = ("pair",) if window is None else ("seq", "pair")
        self.ins = [x]
        self.outs = [jax.ShapeDtypeStruct((self.slots, 4) + x.shape, x.dtype)]
        dma = pltpu.SemaphoreType.DMA
        self.scratch = [dma((3,))] * 4 + [dma((3, 2))] * 2

    def steps(self, at, ins, outs, scratch):
        (x,), (o,) = ins, outs
        asend, arecv, xsend, xrecv, csend, crecv = scratch
        after = lax.rem(at.s + 1, 8)
        before = lax.rem(at.s + 7, 8)
        sends = []

        def send(src, dst, ss, rs, target, cond=None):
            one = Send(src, dst, ss, rs, (cond, target[1]))
            one.start()
            sends.append(one)

        middle = self.slots // 2
        takes = (lambda j, f: self.window.takes(at.s, j, f)) if self.window else None
        holds = lambda j, f: None if j == middle else takes(j, f)
        if self.slots == 3:
            send(x, o.at[0, at.f], asend.at[0], arecv.at[0], (None, (after, at.f)), (at.s < 7) & self.window.takes(after, 0, at.f))
            send(x, o.at[2, at.f], asend.at[2], arecv.at[2], (None, (before, at.f)), (at.s > 0) & self.window.takes(before, 2, at.f))
        own = pltpu.make_async_copy(x, o.at[middle, at.f], asend.at[1])
        own.start()
        send(x, o.at[middle, at.f], xsend.at[middle], xrecv.at[middle], at.across)
        send(x, o.at[middle, at.f], csend.at[middle, 0], crecv.at[middle, 0], at.twin)
        yield
        for j in range(self.slots):
            if j != middle:
                here = o.at[j, at.f]
                cond = holds(j, at.f)
                arrived(here, asend.at[j], arecv.at[j], at.twin, cond)
                send(here, here, xsend.at[j], xrecv.at[j], at.across, cond)
                send(here, here, csend.at[j, 0], crecv.at[j, 0], at.twin, cond)
        yield
        for j in range(self.slots):
            there = o.at[j, at.f ^ 2]
            cond = holds(j, at.f ^ 2)
            arrived(there, xsend.at[j], xrecv.at[j], at.across, cond)
            send(there, there, csend.at[j, 1], crecv.at[j, 1], at.twin, cond)
            yield
        for j in range(self.slots):
            for k in range(2):
                other = (at.f ^ 1) ^ (2 * k)
                arrived(o.at[j, other], csend.at[j, k], crecv.at[j, k], at.twin, holds(j, other))
        for one in sends:
            one.sent()
        own.wait()


def runs(starts, size):
    marks = sorted({edge for start in starts for edge in (start, start + size)})
    found = []
    for begin, end in zip(marks[:-1], marks[1:]):
        found.append((begin, end, [(at, begin - start) for at, start in enumerate(starts) if start <= begin and end <= start + size]))
    return found


def join_kernel(terms, *refs):
    half = len(refs) // 2
    for term, parts_ref, out_ref in zip(terms, refs[:half], refs[half:]):
        for begin, end, sources in term:
            value = None
            for at, first in sources:
                part = parts_ref[at, :, first : first + end - begin].astype(jnp.float32)
                value = part if value is None else value + part
            out_ref[:, begin:end] = value
    refs[-1][...] = refs[half - 1][0].astype(jnp.float32)


def join(dense, dense_starts, mixer, mixer_starts, plain):
    steps = 4
    terms, ins, outs, shapes = [], [], [], []
    for arrays, starts, period, every in ((dense, dense_starts, 2, 1), (mixer, mixer_starts, 4, 2)):
        for x in arrays:
            _, rows, size = x.shape
            term = runs(starts[:period], size)
            columns = term[-1][1]
            terms.append(term)
            ins.append(pl.BlockSpec((period, rows, size), lambda i, every=every: (i // every, 0, 0)))
            outs.append(pl.BlockSpec((rows, columns), lambda i, every=every: (0, i // every)))
            shapes.append(jax.ShapeDtypeStruct((rows, columns * steps // every), jnp.float32))
    _, rows, columns = plain.shape
    ins.append(pl.BlockSpec((1, rows, columns // steps), lambda i: (0, 0, i)))
    outs.append(pl.BlockSpec((rows, columns // steps), lambda i: (0, i)))
    shapes.append(jax.ShapeDtypeStruct((rows, columns), jnp.float32))
    return pl.pallas_call(
        functools.partial(join_kernel, terms), grid=(steps,), in_specs=ins, out_specs=outs, out_shape=shapes, name="join"
    )(*dense, *mixer, plain)


def rms_rows(values):
    mean = jnp.mean(values * values, axis=1, keepdims=True) + EPSILON
    guess = lax.rsqrt(mean)
    return guess * (1.5 - 0.5 * mean * guess * guess)


class MixerForward:
    letter = "m"
    reach = ("line",)

    def __init__(self, window_of, x_full, w_branch, w_input, w_out, igate, dgate, gain, mask, taps, soft):
        self.window_of = window_of
        _, rows, width = x_full.shape
        window, head = igate.shape
        tokens = 8 * rows
        low, full = x_full.dtype, jnp.float32
        dma = pltpu.SemaphoreType.DMA
        self.ins = [x_full, w_branch, w_input, w_out, igate, dgate, gain, mask, taps, soft]
        kinds = [low, full, low, low, full, full, full, low]
        shapes = [(8, rows, width)] + [(tokens, window)] * 7
        self.outs = [jax.ShapeDtypeStruct((rows, width), full)]
        self.outs += [jax.ShapeDtypeStruct(shape, kind) for shape, kind in zip(shapes, kinds)]
        self.kept = [pltpu.VMEM(shape, kind) for shape, kind in zip(shapes, kinds)]
        self.held = [pltpu.VMEM(x.shape, x.dtype) for x in self.ins[1:]]
        self.held[2] = pltpu.VMEM((window, width), low)
        self.local = [
            pltpu.VMEM((8, rows, width), low),
            pltpu.VMEM((8 + 2 * rows, window), full),
            pltpu.VMEM((CHUNK, head), full),
            pltpu.VMEM((CHUNK, head), full),
            pltpu.VMEM((8, window), full),
            dma((len(self.ins),)),
            dma((len(kinds),)),
        ]
        self.chain = Chain.scratch(rows, width, low)
        self.scratch = self.kept + self.held + self.local + self.chain

    def steps(self, at, ins, outs, scratch):
        take = lambda count: [scratch.pop(0) for _ in range(count)]
        scratch = list(scratch)
        kept = take(len(self.kept))
        held = take(len(self.held))
        parts, padded, coef, drive, carry, lsem, ssem = take(len(self.local))
        normed, pre, conv_in, rounded, gin, gdec, states, mixed = kept
        w_branch, w_input, w_out, igate, dgate, gain, mask, taps, soft = held
        chain = Chain(at, parts, outs[0], scratch, farthest)
        _, rows, width = normed.shape
        window, head = igate.shape
        span = 2 * rows
        w_out[...] = jnp.zeros_like(w_out)
        offset = pl.multiple_of(self.window_of.offset(at.s), 16)
        place = lambda dst: dst.at[pl.ds(offset, ins[3].shape[0])] if dst is w_out else dst
        loads = [pltpu.make_async_copy(src, place(dst), lsem.at[i]) for i, (src, dst) in enumerate(zip(ins, [normed] + held))]
        for load in loads:
            load.start()
        yield
        for load in loads:
            load.wait()
        padded[0:8, :] = jnp.zeros((8, window), jnp.float32)
        carry[...] = jnp.zeros_like(carry)
        line = lax.broadcasted_iota(jnp.int32, (8, head), 0)

        def scale(i, _):
            block, here = i // (rows // 16), pl.ds(pl.multiple_of(lax.rem(i, rows // 16) * 16, 16), 16)
            value = normed[block, here, :].astype(jnp.float32)
            normed[block, here, :] = (value * rms_rows(value) * gain[0:1, :]).astype(normed.dtype)
            return 0

        def work(t):
            lax.fori_loop(2 * t * (rows // 16), 2 * (t + 1) * (rows // 16), scale, 0)
            tokens = pl.ds(span * t, span)
            source = normed[2 * t : 2 * t + 2].reshape(span, width)
            if t:
                padded[0:8, :] = padded[span : span + 8, :]
            for h in range(window // head):
                lanes = slice(h * head, (h + 1) * head)
                pre[tokens, lanes] = jnp.dot(source, w_branch[:, lanes], preferred_element_type=jnp.float32)
                value = jnp.dot(source, w_input[:, lanes], preferred_element_type=jnp.float32).astype(conv_in.dtype)
                conv_in[tokens, lanes] = value
                padded[8:, lanes] = value.astype(jnp.float32)
            if t:
                yield
            def piece(c, _):
                for h in range(window // head):
                    lanes = slice(h * head, (h + 1) * head)
                    base = pl.multiple_of(c * CHUNK, CHUNK)
                    here = pl.ds(pl.multiple_of(t * span + base, CHUNK), CHUNK)
                    marks = mask[here, :]
                    rolls = padded[pl.ds(base, CHUNK + 8), lanes]
                    out = taps[0:1, lanes] * rolls[8:]
                    for k in range(1, TAPS):
                        out = out + taps[k : k + 1, lanes] * rolls[8 - k : 8 - k + CHUNK] * marks[:, k : k + 1]
                    small = out.astype(rounded.dtype)
                    rounded[here, lanes] = small
                    g_in = jax.nn.sigmoid(jnp.dot(small, igate[lanes, :], preferred_element_type=jnp.float32))
                    g_dec = jax.nn.sigmoid(jnp.dot(small, dgate[lanes, :], preferred_element_type=jnp.float32))
                    gin[here, lanes] = g_in
                    gdec[here, lanes] = g_dec
                    log_decay = -soft[0:1, lanes] * (1.0 + 7.0 * g_dec)
                    root = jnp.sqrt(minus_expm1(2.0 * log_decay))
                    restart = marks[:, 0:1]
                    carried = 1.0 - restart
                    coef[...] = jnp.exp(log_decay) * carried
                    drive[...] = small.astype(jnp.float32) * g_in * (restart + carried * root)

                    def tile(i, state):
                        now = pl.multiple_of(i * 8, 8)
                        a = coef[pl.ds(now, 8), :]
                        b = drive[pl.ds(now, 8), :]
                        for sh in (1, 2, 4):
                            keep = line >= sh
                            b = b + a * jnp.where(keep, pltpu.roll(b, sh, 0), 0.0)
                            a = a * jnp.where(keep, pltpu.roll(a, sh, 0), 1.0)
                        new = b + a * state
                        there = pl.ds(pl.multiple_of(t * span + base + now, 8), 8)
                        states[there, lanes] = new
                        return jnp.broadcast_to(new[7:8, :], (8, head))

                    carry[:, lanes] = lax.fori_loop(0, CHUNK // 8, tile, carry[:, lanes], unroll=True)
                    branch, _ = gelu_parts(pre[here, lanes])
                    mixed[here, lanes] = (states[here, lanes] * branch).astype(mixed.dtype)
                return 0

            lax.fori_loop(0, span // CHUNK, piece, 0)
            if t:
                yield
            values = mixed[tokens, :]

            def product(n, _):
                columns = pl.ds(pl.multiple_of(n * 256, 256), 256)
                out = jnp.dot(values, w_out[:, columns], preferred_element_type=jnp.float32)
                parts[2 * t : 2 * t + 2, :, columns] = out.astype(parts.dtype).reshape(2, rows, 256)
                return 0

            lax.fori_loop(0, width // 256, product, 0)
            chain.send_side(t)

        for t in range(4):
            yield from work(t)
            yield
        stores = [pltpu.make_async_copy(src, dst, ssem.at[i]) for i, (src, dst) in enumerate(zip(kept, outs[1:]))]
        for store in stores:
            store.start()
        for k in range(3):
            for p in range(PIECES):
                chain.step(k, p)
                yield
        chain.finish()
        yield
        chain.sent()
        for store in stores:
            store.wait()


class MixerBackward:
    letter = "b"
    reach = ("line",)

    def __init__(self, window_of, out_grad, w_out, w_branch, w_input, normed, pre, conv_in, rounded, gin, gdec, states, mixed, igate, dgate, mask, ahead, taps, soft, owned):
        self.window_of = window_of
        rows, width = out_grad.shape
        tokens, window = pre.shape
        head = igate.shape[1]
        low, full = out_grad.dtype, jnp.float32
        dma = pltpu.SemaphoreType.DMA
        self.ins = [out_grad, w_out, w_branch, w_input, normed, pre, conv_in, rounded, gin, gdec, states, mixed, igate, dgate, mask, ahead, taps, soft, owned]
        shape = jax.ShapeDtypeStruct
        self.outs = [
            shape((rows, width), full), shape((width, window - 128), low), shape((width, window - 128), low), shape((window, width), low),
            shape((window, 2 * head), low), shape((window, 128), full),
        ]
        self.held = [pltpu.VMEM(x.shape, x.dtype) for x in self.ins[1:]]
        self.held[0] = pltpu.VMEM((window, width), low)
        self.held[9] = pltpu.VMEM((8 + tokens, window), full)
        self.local = [
            pltpu.VMEM((8, rows, width), low),
            pltpu.VMEM((8, rows, width), low),
            pltpu.VMEM((2 * rows, window), full),
            pltpu.VMEM((tokens, window), low),
            pltpu.VMEM((tokens, window), low),
            pltpu.VMEM((2 * rows + 8, window), full),
            pltpu.VMEM((2 * rows + 8, window), full),
            pltpu.VMEM((CHUNK, head), full),
            pltpu.VMEM((CHUNK, head), full),
            pltpu.VMEM((16, window), full),
            pltpu.VMEM((window, head), full),
            pltpu.VMEM((window, head), full),
            pltpu.VMEM((8 * 5, window), full),
            pltpu.VMEM((window, 2 * head), low),
            pltpu.VMEM((window, 128), full),
            dma((len(self.ins),)),
            dma((8,)),
        ]
        self.gather = Gather(out_grad)
        self.chain = Chain.scratch(rows, width, low)
        self.scratch = self.held + self.local + self.gather.scratch + self.chain

    def steps(self, at, ins, outs, scratch):
        scratch = list(scratch)
        take = lambda count: [scratch.pop(0) for _ in range(count)]
        held = take(len(self.held))
        toks, parts, mgrad, pgrad, cgrad, padded, later, coef, drive, carry, igrad, dgrad, sums, gates, lines, lsem, ssem = take(len(self.local))
        gsems = take(len(self.gather.scratch))
        w_out, w_branch, w_input, normed, pre, conv_in, rounded, gin, gdec, states, mixed, igate, dgate, mask, ahead, taps, soft, owned = held
        chain = Chain(at, parts, outs[0], scratch, descending)
        relay = Relay(at, ins[0], toks, gsems)
        _, rows, width = toks.shape
        tokens, window = pre.shape
        head = igate.shape[1]
        span = 2 * rows
        heads = [slice(h * head, (h + 1) * head) for h in range(window // head)]
        relay.begin()
        loads = []
        for i, (src, dst) in enumerate(zip(ins[1:], held)):
            if dst is w_out:
                first = pl.multiple_of(self.window_of.own - self.window_of.offset(at.s), 16)
                src = src.at[pl.ds(first, window)]
            loads.append(pltpu.make_async_copy(src, dst.at[8:] if dst is states else dst, lsem.at[i]))
            loads[-1].start()
        states[0:8, :] = jnp.zeros((8, window), jnp.float32)
        for ref in (later, carry, igrad, dgrad, sums):
            ref[...] = jnp.zeros_like(ref)
        yield
        for d in range(1, 4):
            for p in range(PIECES):
                relay.step(d, p)
                yield
        for load in loads:
            load.wait()
        relay.own_copy().wait()
        for t in range(4):
            relay.wait_beside(t)
        line = lax.broadcasted_iota(jnp.int32, (8, head), 0)
        rows_dot = lambda a, b: lax.dot_general(a, b, CONTRACT_ROWS, preferred_element_type=jnp.float32)
        last_dot = lambda a, b: lax.dot_general(a, b, CONTRACT_LAST, preferred_element_type=jnp.float32)
        fold = lambda v: jnp.sum(v.reshape(v.shape[0] // 8, 8, v.shape[1]), axis=0)

        def work(t):
            source = toks[2 * t : 2 * t + 2].reshape(span, width)
            for lanes in heads:
                mgrad[:, lanes] = last_dot(source, w_out[lanes, :])
            later[span : span + 8, :] = later[0:8, :]
            if t:
                padded[0:8, :] = conv_in[span * t - 16 : span * t, :].astype(jnp.float32)[8:]
            else:
                padded[0:8, :] = jnp.zeros((8, window), jnp.float32)
            padded[8:, :] = conv_in[span * t : span * (t + 1), :].astype(jnp.float32)

            def piece(step, _):
                base = pl.multiple_of((span // CHUNK - 1 - step) * CHUNK, CHUNK)
                here = pl.ds(pl.multiple_of(t * span + base, CHUNK), CHUNK)
                inside = pl.ds(base, CHUNK)
                marks = mask[here, :]
                restart = marks[:, 0:1]
                carried = 1.0 - restart
                for lanes in heads:
                    branch, slope = gelu_parts(pre[here, lanes])
                    grad = mgrad[inside, lanes]
                    state = states[pl.ds(pl.multiple_of(t * span + base, CHUNK), CHUNK + 8), lanes]
                    pgrad[here, lanes] = (grad * state[8:] * slope * owned[0:1, lanes]).astype(pgrad.dtype)
                    g_dec = gdec[here, lanes]
                    g_in = gin[here, lanes]
                    log_decay = -soft[0:1, lanes] * (1.0 + 7.0 * g_dec)
                    decays = jnp.exp(log_decay)
                    root = jnp.sqrt(minus_expm1(2.0 * log_decay))
                    coef[...] = decays * carried
                    drive[...] = grad * branch

                    def tile(i, pair):
                        adj_next, coef_next = pair
                        now = pl.multiple_of(CHUNK - 8 - i * 8, 8)
                        first = coef[pl.ds(now, 8), :]
                        a = jnp.where(line == 7, coef_next, pltpu.roll(first, 7, 0))
                        b = drive[pl.ds(now, 8), :]
                        for sh in (1, 2, 4):
                            keep = line < 8 - sh
                            b = b + a * jnp.where(keep, pltpu.roll(b, 8 - sh, 0), 0.0)
                            a = a * jnp.where(keep, pltpu.roll(a, 8 - sh, 0), 1.0)
                        new = b + a * adj_next
                        drive[pl.ds(now, 8), :] = new
                        return jnp.broadcast_to(new[0:1, :], (8, head)), jnp.broadcast_to(first[0:1, :], (8, head))

                    adj_next, coef_next = lax.fori_loop(0, CHUNK // 8, tile, (carry[0:8, lanes], carry[8:16, lanes]), unroll=True)
                    carry[0:8, lanes] = adj_next
                    carry[8:16, lanes] = coef_next
                    adjoint = drive[...]
                    small = rounded[here, lanes]
                    value = small.astype(jnp.float32)
                    log_grad = adjoint * carried * decays * (state[7 : 7 + CHUNK] - value * g_in * decays / root)
                    sums[32:40, lanes] += fold(-log_grad * (1.0 + 7.0 * g_dec))
                    through = adjoint * g_in * (restart + carried * root)
                    ipg = (through * value * (1.0 - g_in)).astype(jnp.bfloat16)
                    dpg = (log_grad * (-7.0 * soft[0:1, lanes]) * g_dec * (1.0 - g_dec)).astype(jnp.bfloat16)
                    igrad[lanes, :] += rows_dot(small, ipg)
                    dgrad[lanes, :] += rows_dot(small, dpg)
                    through = through + last_dot(ipg, igate[lanes, :]) + last_dot(dpg, dgate[lanes, :])
                    later[inside, lanes] = through.astype(jnp.bfloat16).astype(jnp.float32)
                return 0

            lax.fori_loop(0, span // CHUNK, piece, 0)
            yield

            def after(c, _):
                base = pl.multiple_of(c * CHUNK, CHUNK)
                here = pl.ds(pl.multiple_of(t * span + base, CHUNK), CHUNK)
                marks = mask[here, :]
                ahead_marks = ahead[here, :]
                for lanes in heads:
                    follow = later[pl.ds(base, CHUNK + 8), lanes]
                    before = padded[pl.ds(base, CHUNK + 8), lanes]
                    grad = follow[:CHUNK]
                    total = taps[0:1, lanes] * grad
                    sums[0:8, lanes] += fold(grad * before[8:])
                    for k in range(1, TAPS):
                        total = total + taps[k : k + 1, lanes] * follow[k : k + CHUNK] * ahead_marks[:, k : k + 1]
                        sums[8 * k : 8 * k + 8, lanes] += fold(grad * before[8 - k : 8 - k + CHUNK] * marks[:, k : k + 1])
                    cgrad[here, lanes] = (total * owned[0:1, lanes]).astype(cgrad.dtype)
                return 0

            lax.fori_loop(0, span // CHUNK, after, 0)
            mine = slice(span * t, span * (t + 1))

            def product(n, _):
                columns = pl.ds(pl.multiple_of(n * 256, 256), 256)
                out = last_dot(pgrad[mine, :], w_branch[columns, :]) + last_dot(cgrad[mine, :], w_input[columns, :])
                parts[2 * t : 2 * t + 2, :, columns] = out.astype(parts.dtype).reshape(2, rows, 256)
                return 0

            lax.fori_loop(0, width // 256, product, 0)
            if t > 1:
                chain.send_side(t)

        for t in (3, 2, 1, 0):
            yield from work(t)
            if t == 0:
                chain.send_side(jnp.where(at.z == 0, 1, 0))
                chain.send_side(jnp.where(at.z == 0, 0, 1))
            yield
        gates[:, :head] = igrad[...].astype(gates.dtype)
        gates[:, head:] = dgrad[...].astype(gates.dtype)
        totals = [jnp.sum(sums[8 * k : 8 * k + 8, :], axis=0, keepdims=True) for k in range(5)]
        lines[...] = jnp.concatenate(totals + [jnp.zeros((123, window), jnp.float32)], axis=0).T

        def grads(r):
            lanes = pl.ds(pl.multiple_of(r * 256, 256), 256)
            value = normed[:, :, lanes].reshape(tokens, 256)
            w_branch[lanes, :] = rows_dot(value, pgrad[...]).astype(w_branch.dtype)
            w_input[lanes, :] = rows_dot(value, cgrad[...]).astype(w_input.dtype)
            w_out[:, lanes] = rows_dot(mixed[...], toks[:, :, lanes].reshape(tokens, 256)).astype(w_out.dtype)

        done = 0
        for k in range(3):

            def chain_step(p, _):
                chain.step(k, p)
                pl.when(k * PIECES + p < width // 256)(lambda: grads(k * PIECES + p))
                return 0

            lax.fori_loop(0, PIECES, chain_step, 0)
            yield
        chain.finish()
        owned_lanes = pl.ds(pl.multiple_of(self.window_of.offset(at.s) // 128 * 128, 128), window - 128)
        stores = [
            pltpu.make_async_copy(src.at[:, owned_lanes] if i < 2 else src, dst, ssem.at[i])
            for i, (src, dst) in enumerate(zip((w_branch, w_input, w_out, gates, lines), outs[1:]))
        ]
        for store in stores:
            store.start()
        yield
        chain.sent()
        relay.sent()
        for store in stores:
            store.wait()


def fast(
    inputs,
    resets,
    cotangent,
    first_gain,
    branch_weight,
    input_weight,
    conv_weight,
    input_gate,
    decay_gate,
    decay_param,
    output_weight,
    second_gain,
    gate_weight,
    up_weight,
    down_weight,
):
    low = jnp.bfloat16
    peers, groups = 8, 4
    s, f = lax.axis_index("seq"), lax.axis_index("fsdp")
    sources_low = inputs[0]
    sources = sources_low.astype(jnp.float32)
    returned = cotangent[0]
    tokens, width = sources.shape
    rows = branch_weight.shape[0]
    head = input_gate.shape[1]
    own = width // peers
    hidden_own = gate_weight.shape[1] // peers
    all_tokens = peers * tokens
    window = 2 * head
    channels = Window(own, head, width, rows)
    offset = channels.offset(s)
    owned = ((jnp.arange(window) >= offset) & (jnp.arange(window) < offset + own)).astype(jnp.float32)

    wide_row = lambda v: jnp.pad(v.astype(jnp.float32), (0, 128 - v.shape[0]))
    small = jnp.pad(jnp.stack([wide_row(first_gain), wide_row(second_gain), wide_row(resets[0])]), ((0, 5), (0, 0)))[None]
    dense_start = lambda to: 128 * (hidden_own * to // 128)
    wide = 128 * -(-hidden_own // 128)
    lanes = jnp.arange(wide) + dense_start(s) - hidden_own * s
    held = jnp.broadcast_to(((lanes >= 0) & (lanes < hidden_own)).astype(jnp.float32)[None], (8, wide))
    pad = jnp.zeros((rows, 128 - 5), low)
    row_pack = jnp.concatenate([input_gate, decay_gate, conv_weight, decay_param[:, None], pad], axis=1)
    x_full, w_branch, w_input, row_w, out_w, vectors = exchange(
        [
            Gather(sources_low),
            Spread(branch_weight, channels.first, window),
            Spread(input_weight, channels.first, window),
            Rows(row_pack, channels),
            Rows(output_weight),
            Tiny(small),
        ],
        1,
        "first_exchange",
        ["sot", "sso", "sso", "sso", "ss", "ss", "ss", "s", "s", "s", "s"],
    )
    whole = lambda w: w.reshape(width, w.shape[-1])
    w_branch, w_input = whole(w_branch), whole(w_input)
    w_output = out_w.reshape(own, width)
    near = lax.dynamic_slice_in_dim(row_w.reshape(3 * own, row_pack.shape[1]), own - offset, window, 0)
    w_igate, w_dgate = near[:, :head], near[:, head : 2 * head]
    taps = jnp.zeros((8, window), jnp.float32).at[:4].set(near[:, 2 * head : 2 * head + 4].astype(jnp.float32).T)
    w_decay = near[:, 2 * head + 4].astype(jnp.float32)
    soft = jnp.broadcast_to(jax.nn.softplus(w_decay)[None], (8, window))
    gain_first = vectors[:, 0, :rows].reshape(width)
    gain_second = vectors[:, 1, :rows].reshape(width)
    flags = lax.dynamic_index_in_dim(vectors.reshape(peers, groups, 8, 128), f, 1, False)[:, 2, :tokens].reshape(all_tokens)
    segment = jnp.cumsum(flags)
    masks, aheads = [flags], [jnp.ones_like(flags)]
    for k in range(1, 4):
        same = (segment[k:] == segment[:-k]).astype(jnp.float32)
        masks.append(jnp.concatenate([jnp.zeros((k,), jnp.float32), same]))
        aheads.append(jnp.concatenate([same, jnp.zeros((k,), jnp.float32)]))
    masks = jnp.stack(masks + [jnp.zeros_like(flags)] * 4, axis=1)
    aheads = jnp.stack(aheads + [jnp.zeros_like(flags)] * 4, axis=1)
    owned_rows = jnp.broadcast_to(owned[None], (8, window))

    gain_rows = jnp.broadcast_to(gain_first[None], (8, width))
    (
        mixer_out, normed, pre, conv_in, rounded, gate_in, gate_dec, states, mixed,
        returned_full, w_gate, w_up, w_down, w_output_near,
    ) = exchange(
        [
            MixerForward(channels, x_full, w_branch, w_input, w_output, w_igate, w_dgate, gain_rows, masks, taps, soft),
            Gather(returned),
        ]
        + [Spread(w, dense_start, wide) for w in (gate_weight, up_weight, down_weight)]
        + [Rows(output_weight, channels)],
        2,
        "mixer_forward",
        ["gso", "s", "", "", "s", "", "", "s", "", "", "ggggssggggssggggs"],
    )
    resid = sources + mixer_out
    scale_two = lax.rsqrt(jnp.mean(resid * resid, axis=1, keepdims=True) + EPSILON)
    hidden = (resid * scale_two * gain_second).astype(low)
    hidden_grad, result_part, grad_gate, grad_up, grad_down = exchange(
        [Dense(hidden, returned_full, whole(w_gate), whole(w_up), whole(w_down), held)], 3, "dense"
    )
    weighted = hidden_grad * gain_second
    resid_grad = (
        returned.astype(jnp.float32)
        + scale_two * weighted
        - resid * scale_two**3 * jnp.mean(weighted * resid, axis=1, keepdims=True)
    )
    second_term = jnp.sum(hidden_grad * resid * scale_two, axis=0)
    out_grad = resid_grad.astype(low)
    split = lambda g: g.reshape(peers, groups, rows, g.shape[-1])
    (
        normed_grad, grad_branch, grad_input, grad_output, gates, lines,
        grad_gate, grad_up, grad_down,
    ) = exchange(
        [
            MixerBackward(
                channels, out_grad, w_output_near.reshape(3 * own, width), w_branch, w_input, normed, pre, conv_in, rounded, gate_in, gate_dec, states, mixed,
                w_igate, w_dgate, masks, aheads, taps, soft, owned_rows,
            )
        ]
        + [Collect(split(g)) for g in (grad_gate, grad_up, grad_down)],
        4,
        "mixer_backward",
        ["c"] * 13 + ["c", "", "c", "", "c", "", "", "c"],
    )
    scale_one = lax.rsqrt(jnp.mean(sources * sources, axis=1, keepdims=True) + EPSILON)
    weighted = normed_grad * gain_first
    source_grad = (
        resid_grad
        + scale_one * weighted
        - sources * scale_one**3 * jnp.mean(weighted * sources, axis=1, keepdims=True)
    )
    first_term = jnp.sum(normed_grad * sources * scale_one, axis=0)
    grad_branch, grad_input = split(grad_branch), split(grad_input)
    terms = jnp.stack([first_term.reshape(peers * groups, rows), second_term.reshape(peers * groups, rows)], axis=1)
    vectors = jnp.pad(terms, ((0, 0), (0, 6), (0, 128 - rows)))
    ffn_out, grad_branch, grad_input, grad_output, gates, lines, vectors = exchange(
        [
            Reduce(result_part),
            Collect(grad_branch),
            Collect(grad_input),
            Collect(grad_output, channels),
            Collect(gates, channels),
            Collect(lines, channels),
            Tiny(vectors),
        ],
        6,
        "mixer_collect",
        ["ct"] + ["c"] * 8 + ["", "c"] * 4 + ["c"] * 4,
    )
    result = (resid + ffn_out).astype(low)
    vectors = jnp.sum(vectors, axis=0)
    gates = gates[0].astype(jnp.float32)

    dense_grads, dense_starts = (grad_gate, grad_up, grad_down), [128 * (hidden_own * at // 128) for at in range(peers)]
    mixer_starts = [own * at // 128 * 128 for at in range(peers)]
    grad_gate, grad_up, grad_down, grad_branch, grad_input, grad_output = join(
        dense_grads, dense_starts, (grad_branch, grad_input), mixer_starts, grad_output
    )
    return (
        result[None],
        source_grad.astype(low)[None],
        vectors[0, :rows],
        grad_branch,
        grad_input,
        lines[0, :, :4],
        gates[:, :head],
        gates[:, head:],
        lines[0, :, 4] * jax.nn.sigmoid(decay_param.astype(jnp.float32)),
        grad_output,
        vectors[1, :rows],
        grad_gate,
        grad_up,
        grad_down,
    )


def solution(mesh):
    in_specs = (
        P("fsdp", "seq", None),
        P("fsdp", "seq"),
        P("fsdp", "seq", None),
        P(("seq", "fsdp")),
        P(("seq", "fsdp"), None),
        P(("seq", "fsdp"), None),
        P(("seq", "fsdp"), None),
        P(("seq", "fsdp"), None),
        P(("seq", "fsdp"), None),
        P(("seq", "fsdp")),
        P(("seq", "fsdp"), None),
        P(("seq", "fsdp")),
        P(("seq", "fsdp"), None),
        P(("seq", "fsdp"), None),
        P(("seq", "fsdp"), None),
    )
    out_specs = (
        P("fsdp", "seq", None),
        P("fsdp", "seq", None),
        P(("seq", "fsdp")),
        P(("seq", "fsdp"), None),
        P(("seq", "fsdp"), None),
        P(("seq", "fsdp"), None),
        P(("seq", "fsdp"), None),
        P(("seq", "fsdp"), None),
        P(("seq", "fsdp")),
        P(("seq", "fsdp"), None),
        P(("seq", "fsdp")),
        P(("seq", "fsdp"), None),
        P(("seq", "fsdp"), None),
        P(("seq", "fsdp"), None),
    )
    program = fast if dict(mesh.shape) == {"seq": 8, "fsdp": 4} else local
    return jax.shard_map(program, mesh=mesh, in_specs=in_specs, out_specs=out_specs, check_vma=False)
```

```python
import functools

import jax
import jax.numpy as jnp
from jax import lax
from jax.experimental import pallas as pl
from jax.experimental.pallas import tpu as pltpu
from jax.sharding import PartitionSpec as P

EPSILON = 1e-06
CONTRACT_ROWS = (((0,), (0,)), ((), ()))
CONTRACT_LAST = (((1,), (1,)), ((), ()))


def shifted_2(value, axis, steps):
    count = lax.axis_size(axis)
    leading, last = (max(0, -steps), min(count, count - steps))
    return lax.ppermute(value, axis, [(source, source + steps) for source in range(leading, last)])


def entering(x, axis, combine, identity, reverse):
    peers, index = (lax.axis_size(axis), lax.axis_index(axis))
    everything = jax.tree.map(lambda part: lax.all_gather(part, axis), x)
    start = jax.tree.map(
        lambda part, zero: jnp.broadcast_to(jnp.asarray(zero, part.dtype), part.shape), x, identity
    )

    def lap(k, before):
        at = peers - 1 - k if reverse else k
        reached = at > index if reverse else at < index
        new = combine(before, jax.tree.map(lambda part: part[at], everything))
        return jax.tree.map(lambda a, b: jnp.where(reached, a, b), new, before)

    return lax.fori_loop(0, peers, lap, start)


def affine(earlier, later):
    return (earlier[0] * later[0], later[0] * earlier[1] + later[1])


def product(operand_one, operand_two):
    return jnp.dot(operand_one, operand_two, preferred_element_type=jnp.float32)


def rows_product(operand_one, operand_two):
    return lax.dot_general(
        operand_one, operand_two, CONTRACT_ROWS, preferred_element_type=jnp.float32
    )


def last_product(operand_one, operand_two):
    return lax.dot_general(
        operand_one, operand_two, CONTRACT_LAST, preferred_element_type=jnp.float32
    )


def heads_apply(values, weight, head_count):
    token_count = values.shape[0]
    head_width = weight.shape[1]
    shaped = values.reshape(token_count, head_count, head_width)
    blocks = weight.reshape(head_count, head_width, head_width)
    mixed = jnp.einsum("thi,hij->thj", shaped, blocks, preferred_element_type=jnp.float32)
    return mixed.reshape(token_count, head_count * head_width)


def heads_back(gradients, weight, head_count):
    token_count = gradients.shape[0]
    head_width = weight.shape[1]
    shaped = gradients.reshape(token_count, head_count, head_width)
    blocks = weight.reshape(head_count, head_width, head_width)
    mixed = jnp.einsum("thj,hij->thi", shaped, blocks, preferred_element_type=jnp.float32)
    return mixed.reshape(token_count, head_count * head_width)


def heads_grad(values, gradients, head_count):
    token_count = values.shape[0]
    head_width = values.shape[1] // head_count
    left_side = values.reshape(token_count, head_count, head_width)
    right_side = gradients.reshape(token_count, head_count, head_width)
    summed = jnp.einsum("thi,thj->hij", left_side, right_side, preferred_element_type=jnp.float32)
    return summed.reshape(head_count * head_width, head_width)


def slab_count():
    for candidate in (5, 4, 2):
        return candidate
    return 1


def local(
    inputs,
    resets,
    cotangent,
    first_gain,
    branch_weight,
    input_weight,
    conv_weight,
    input_gate,
    decay_gate,
    decay_param,
    output_weight,
    second_gain,
    gate_weight,
    up_weight,
    down_weight,
):
    sources = inputs[0].astype(jnp.float32)
    flags = resets[0]
    returned = cotangent[0]
    returned_float = returned.astype(jnp.float32)
    tokens = sources.shape[0]
    shared = (
        lax.all_gather(first_gain, ("seq", "fsdp"), axis=0, tiled=True),
        lax.all_gather(branch_weight, ("seq", "fsdp"), axis=0, tiled=True),
        lax.all_gather(input_weight, ("seq", "fsdp"), axis=0, tiled=True),
        lax.all_gather(conv_weight, ("seq", "fsdp"), axis=0, tiled=True),
        lax.all_gather(input_gate, ("seq", "fsdp"), axis=0, tiled=True),
        lax.all_gather(decay_gate, ("seq", "fsdp"), axis=0, tiled=True),
        lax.all_gather(decay_param, ("seq", "fsdp"), axis=0, tiled=True),
        lax.all_gather(output_weight, ("seq", "fsdp"), axis=0, tiled=True),
        lax.all_gather(second_gain, ("seq", "fsdp"), axis=0, tiled=True),
    )
    dense_parts = (
        lax.all_gather(gate_weight, ("seq", "fsdp"), axis=0, tiled=True),
        lax.all_gather(up_weight, ("seq", "fsdp"), axis=0, tiled=True),
        lax.all_gather(down_weight, ("seq", "fsdp"), axis=0, tiled=True),
    )
    gain_first = shared[0].astype(jnp.float32)
    w_branch = shared[1]
    w_input = shared[2]
    w_conv = shared[3].astype(jnp.float32)
    w_igate = shared[4]
    w_dgate = shared[5]
    w_decay = shared[6].astype(jnp.float32)
    w_output = shared[7]
    gain_second = shared[8].astype(jnp.float32)
    w_gate = dense_parts[0]
    w_up = dense_parts[1]
    w_down = dense_parts[2]
    model_width = w_branch.shape[0]
    head_width = w_igate.shape[1]
    head_count = model_width // head_width
    tap_count = w_conv.shape[1]
    scale_one = lax.rsqrt(jnp.mean(sources * sources, axis=1, keepdims=True) + EPSILON)
    normed = (sources * scale_one * gain_first).astype(jnp.bfloat16)
    branch_pre = product(normed, w_branch)
    branch, branch_pull = jax.vjp(jax.nn.gelu, branch_pre)
    conv_in = product(normed, w_input).astype(jnp.bfloat16)
    resets_seen = jnp.cumsum(flags)
    tail_keep = resets_seen[-1] - resets_seen[tokens - tap_count + 1 :] == 0
    tail_rows = conv_in[tokens - tap_count + 1 :] * tail_keep[:, None]
    before = shifted_2(tail_rows, "seq", 1)
    padded = jnp.concatenate([before, conv_in], axis=0)
    seen_before = jnp.concatenate([jnp.zeros((tap_count - 1,), jnp.int32), resets_seen])
    conv_out = jnp.zeros((tokens, model_width), jnp.float32)
    usable_list = []
    for offset in range(tap_count):
        first_row = tap_count - 1 - offset
        shifted = padded[first_row : first_row + tokens].astype(jnp.float32)
        usable = (resets_seen - seen_before[first_row : first_row + tokens] == 0).astype(
            jnp.float32
        )[:, None]
        usable_list.append(usable)
        conv_out = conv_out + w_conv[:, offset] * shifted * usable
    rounded = conv_out.astype(jnp.bfloat16)
    rounded_float = rounded.astype(jnp.float32)
    gate_input = jax.nn.sigmoid(heads_apply(rounded, w_igate, head_count))
    gate_decay = jax.nn.sigmoid(heads_apply(rounded, w_dgate, head_count))
    softened = jax.nn.softplus(w_decay)
    log_decay = -softened * (1.0 + 7.0 * gate_decay)
    decays = jnp.exp(log_decay)
    root_term = jnp.sqrt(-jnp.expm1(2.0 * log_decay))
    restart = flags.astype(jnp.float32)[:, None]
    carried = 1.0 - restart
    scaling = restart + carried * root_term
    driven = rounded_float * gate_input * scaling
    coefficient = decays * carried
    running, local_state = lax.associative_scan(affine, (coefficient, driven), axis=0)
    unit_ones = jnp.ones((model_width,), jnp.float32)
    unit_zeros = jnp.zeros((model_width,), jnp.float32)
    incoming = entering(
        (running[-1], local_state[-1]), "seq", affine, (unit_ones, unit_zeros), False
    )
    state_in = incoming[1]
    states = local_state + running * state_in
    mixed = (states * branch).astype(jnp.bfloat16)
    resid = sources + product(mixed, w_output)
    scale_two = lax.rsqrt(jnp.mean(resid * resid, axis=1, keepdims=True) + EPSILON)
    hidden = (resid * scale_two * gain_second).astype(jnp.bfloat16)
    gate_pre = product(hidden, w_gate)
    up_values = product(hidden, w_up)
    gate_act, gate_pull = jax.vjp(jax.nn.gelu, gate_pre)
    active = (gate_act * up_values).astype(jnp.bfloat16)
    result = (resid + last_product(active, w_down)).astype(jnp.bfloat16)
    act_grad = product(returned, w_down)
    gate_grad = gate_pull(act_grad * up_values)[0].astype(jnp.bfloat16)
    up_grad = (act_grad * gate_act).astype(jnp.bfloat16)
    hidden_grad = last_product(gate_grad, w_gate) + last_product(up_grad, w_up)
    weighted_two = hidden_grad * gain_second
    resid_grad = (
        returned_float
        + scale_two * weighted_two
        - resid * scale_two**3 * jnp.mean(weighted_two * resid, axis=1, keepdims=True)
    )
    second_term = jnp.sum(hidden_grad * resid * scale_two, axis=0)
    branch_out_grad = resid_grad.astype(jnp.bfloat16)
    mixed_grad = last_product(branch_out_grad, w_output)
    state_grad = mixed_grad * branch
    branch_grad = mixed_grad * states
    branch_pre_grad = branch_pull(branch_grad)[0].astype(jnp.bfloat16)
    next_coef = jnp.concatenate([coefficient[1:], jnp.ones((1, model_width), jnp.float32)], axis=0)
    reaches, adjoint_local = lax.associative_scan(
        affine, (next_coef, state_grad), reverse=True, axis=0
    )
    carry_back = entering(
        (coefficient[0] * reaches[0], coefficient[0] * adjoint_local[0]),
        "seq",
        affine,
        (unit_ones, unit_zeros),
        True,
    )
    adjoint = adjoint_local + reaches * carry_back[1]
    earlier_state = jnp.concatenate([state_in[None], states[:-1]], axis=0)
    log_grad = (
        adjoint * earlier_state * carried * decays
        - adjoint * rounded_float * gate_input * carried * decays * decays / root_term
    )
    decay_term = jnp.sum(-log_grad * (1.0 + 7.0 * gate_decay), axis=0) * jax.nn.sigmoid(w_decay)
    input_pre_grad = (adjoint * rounded_float * scaling * gate_input * (1.0 - gate_input)).astype(
        jnp.bfloat16
    )
    decay_pre_grad = (log_grad * (-7.0 * softened) * gate_decay * (1.0 - gate_decay)).astype(
        jnp.bfloat16
    )
    conv_out_grad = (
        adjoint * gate_input * scaling
        + heads_back(input_pre_grad, w_igate, head_count)
        + heads_back(decay_pre_grad, w_dgate, head_count)
    )
    conv_grad = conv_out_grad.astype(jnp.bfloat16)
    igate_term = heads_grad(rounded, input_pre_grad, head_count)
    dgate_term = heads_grad(rounded, decay_pre_grad, head_count)
    head_keep = resets_seen[: tap_count - 1] == 0
    head_rows = conv_grad[: tap_count - 1] * head_keep[:, None]
    following = shifted_2(head_rows, "seq", -1)
    padded_back = jnp.concatenate([conv_grad, following], axis=0)
    seen_after = jnp.concatenate(
        [resets_seen, jnp.full((tap_count - 1,), resets_seen[-1], jnp.int32)]
    )
    conv_grad_float = conv_grad.astype(jnp.float32)
    conv_in_grad = jnp.zeros((tokens, model_width), jnp.float32)
    tap_terms = []
    for offset in range(tap_count):
        first_row = tap_count - 1 - offset
        shifted = padded[first_row : first_row + tokens].astype(jnp.float32)
        tap_terms.append(jnp.sum(conv_grad_float * shifted * usable_list[offset], axis=0))
        ahead_usable = (seen_after[offset : offset + tokens] - resets_seen == 0).astype(
            jnp.float32
        )[:, None]
        conv_in_grad = (
            conv_in_grad
            + w_conv[:, offset]
            * padded_back[offset : offset + tokens].astype(jnp.float32)
            * ahead_usable
        )
    tap_grad = jnp.stack(tap_terms, axis=1)
    conv_in_low = conv_in_grad.astype(jnp.bfloat16)
    normed_grad = last_product(branch_pre_grad, w_branch) + last_product(conv_in_low, w_input)
    weighted_one = normed_grad * gain_first
    source_grad = (
        resid_grad
        + scale_one * weighted_one
        - sources * scale_one**3 * jnp.mean(weighted_one * sources, axis=1, keepdims=True)
    )
    first_term = jnp.sum(normed_grad * sources * scale_one, axis=0)
    grad_inputs = source_grad.astype(jnp.bfloat16)[None]
    vector_part = jnp.concatenate(
        [
            igate_term,
            dgate_term,
            tap_grad,
            decay_term[:, None],
            first_term[:, None],
            second_term[:, None],
        ],
        axis=1,
    )
    owned_rows = gate_weight.shape[0]
    owner_count = lax.axis_size(("seq", "fsdp"))
    slab_total = slab_count()
    slab_rows = owned_rows // slab_total
    vector_shaped = vector_part.reshape(owner_count, owned_rows, vector_part.shape[1])

    def pick_rows(values, portion):
        shaped = values.reshape(values.shape[0], owner_count, owned_rows)
        taken = shaped[:, :, portion * slab_rows : (portion + 1) * slab_rows]
        return taken.reshape(values.shape[0], owner_count * slab_rows)

    gate_pieces = []
    up_pieces = []
    down_pieces = []
    branch_pieces = []
    input_pieces = []
    output_pieces = []
    vector_pieces = []
    for portion in range(slab_total):
        hidden_rows = pick_rows(hidden, portion)
        return_rows = pick_rows(returned, portion)
        dense_sums = (
            lax.psum_scatter(
                rows_product(hidden_rows, gate_grad),
                ("seq", "fsdp"),
                scatter_dimension=0,
                tiled=True,
            ),
            lax.psum_scatter(
                rows_product(hidden_rows, up_grad), ("seq", "fsdp"), scatter_dimension=0, tiled=True
            ),
            lax.psum_scatter(
                rows_product(return_rows, active), ("seq", "fsdp"), scatter_dimension=0, tiled=True
            ),
        )
        gate_pieces.append(dense_sums[0])
        up_pieces.append(dense_sums[1])
        down_pieces.append(dense_sums[2])
        normed_rows = pick_rows(normed, portion)
        mixed_rows = pick_rows(mixed, portion)
        vector_rows = vector_shaped[:, portion * slab_rows : (portion + 1) * slab_rows].reshape(
            owner_count * slab_rows, vector_part.shape[1]
        )
        mixer_sums = (
            lax.psum_scatter(
                rows_product(normed_rows, branch_pre_grad),
                ("seq", "fsdp"),
                scatter_dimension=0,
                tiled=True,
            ),
            lax.psum_scatter(
                rows_product(normed_rows, conv_in_low),
                ("seq", "fsdp"),
                scatter_dimension=0,
                tiled=True,
            ),
            lax.psum_scatter(
                rows_product(mixed_rows, branch_out_grad),
                ("seq", "fsdp"),
                scatter_dimension=0,
                tiled=True,
            ),
            lax.psum_scatter(vector_rows, ("seq", "fsdp"), scatter_dimension=0, tiled=True),
        )
        branch_pieces.append(mixer_sums[0])
        input_pieces.append(mixer_sums[1])
        output_pieces.append(mixer_sums[2])
        vector_pieces.append(mixer_sums[3])
    grad_gate = jnp.concatenate(gate_pieces, axis=0)
    grad_up = jnp.concatenate(up_pieces, axis=0)
    grad_down = jnp.concatenate(down_pieces, axis=0)
    grad_branch = jnp.concatenate(branch_pieces, axis=0)
    grad_input = jnp.concatenate(input_pieces, axis=0)
    grad_output = jnp.concatenate(output_pieces, axis=0)
    vector_sums = jnp.concatenate(vector_pieces, axis=0)
    edge_five = 2 * head_width
    edge_six = edge_five + tap_count
    grad_igate = vector_sums[:, :head_width]
    grad_dgate = vector_sums[:, head_width:edge_five]
    grad_conv = vector_sums[:, edge_five:edge_six]
    grad_decay = vector_sums[:, edge_six]
    grad_gain_first = vector_sums[:, edge_six + 1]
    grad_gain_second = vector_sums[:, edge_six + 2]
    return (
        result[None],
        grad_inputs,
        grad_gain_first,
        grad_branch,
        grad_input,
        grad_conv,
        grad_igate,
        grad_dgate,
        grad_decay,
        grad_output,
        grad_gain_second,
        grad_gate,
        grad_up,
        grad_down,
    )


CHUNK = 128
TAPS = 4


def gelu_parts(x):
    inner = 0.7978845608028654 * (x + 0.044715 * x * x * x)
    bent = jnp.tanh(inner)
    value = 0.5 * x * (1.0 + bent)
    slope = 0.5 * (1.0 + bent) + 0.5 * x * (1.0 - bent * bent) * 0.7978845608028654 * (
        1.0 + 3.0 * 0.044715 * x * x
    )
    return value, slope


def minus_expm1(x):
    series = x / 8.0 + 1.0
    for step in (7.0, 6.0, 5.0, 4.0, 3.0, 2.0):
        series = series * x / step + 1.0
    return jnp.where(x > -0.5, -x * series, 1.0 - jnp.exp(x))


def mixer_forward_kernel(
    conv_in_ref, pre_ref, mask_ref, taps_ref, igate_ref, dgate_ref, soft_ref,
    rounded_ref, gin_ref, gdec_ref, states_ref, earlier_ref, mixed_ref,
    padded, coef, drive,
):
    tokens, width = conv_in_ref.shape
    chunk = min(CHUNK, tokens)
    padded[0:8, :] = jnp.zeros((8, width), jnp.float32)
    soft = soft_ref[0:1, :]
    igate = igate_ref[...]
    dgate = dgate_ref[...]

    def fill(c, _):
        base = pl.multiple_of(c * chunk, chunk)
        padded[pl.ds(pl.multiple_of(base + 8, 8), chunk), :] = conv_in_ref[pl.ds(base, chunk), :].astype(jnp.float32)
        return 0

    lax.fori_loop(0, tokens // chunk, fill, 0)
    row = lax.broadcasted_iota(jnp.int32, (8, width), 0)

    def body(c, carry):
        base = pl.multiple_of(c * chunk, chunk)
        mask = mask_ref[pl.ds(base, chunk), :]
        span = padded[pl.ds(base, chunk + 8), :]
        out = taps_ref[0:1, :] * span[8:]
        for k in range(1, TAPS):
            out = out + taps_ref[k : k + 1, :] * span[8 - k : 8 - k + chunk] * mask[:, k : k + 1]
        rounded = out.astype(jnp.bfloat16)
        rounded_ref[pl.ds(base, chunk), :] = rounded
        gin = jax.nn.sigmoid(jnp.dot(rounded, igate, preferred_element_type=jnp.float32))
        gdec = jax.nn.sigmoid(jnp.dot(rounded, dgate, preferred_element_type=jnp.float32))
        gin_ref[pl.ds(base, chunk), :] = gin
        gdec_ref[pl.ds(base, chunk), :] = gdec
        log_decay = -soft * (1.0 + 7.0 * gdec)
        root = jnp.sqrt(minus_expm1(2.0 * log_decay))
        restart = mask[:, 0:1]
        carried = 1.0 - restart
        coef[...] = jnp.exp(log_decay) * carried
        drive[...] = rounded.astype(jnp.float32) * gin * (restart + carried * root)

        def tile(i, state):
            at = pl.multiple_of(i * 8, 8)
            a = coef[pl.ds(at, 8), :]
            b = drive[pl.ds(at, 8), :]
            for sh in (1, 2, 4):
                keep = row >= sh
                b = b + a * jnp.where(keep, pltpu.roll(b, sh, 0), 0.0)
                a = a * jnp.where(keep, pltpu.roll(a, sh, 0), 1.0)
            new = b + a * state
            states_ref[pl.ds(pl.multiple_of(base + at, 8), 8), :] = new
            earlier_ref[pl.ds(pl.multiple_of(base + at, 8), 8), :] = jnp.where(row == 0, state, pltpu.roll(new, 1, 0))
            return jnp.broadcast_to(new[7:8, :], (8, width))

        carry = lax.fori_loop(0, chunk // 8, tile, carry, unroll=True)
        branch, _ = gelu_parts(pre_ref[pl.ds(base, chunk), :])
        mixed_ref[pl.ds(base, chunk), :] = (states_ref[pl.ds(base, chunk), :] * branch).astype(jnp.bfloat16)
        return carry

    lax.fori_loop(0, tokens // chunk, body, jnp.zeros((8, width), jnp.float32))


def mixer_forward(conv_in, pre, mask, taps, igate, dgate, soft, width):
    tokens, total = conv_in.shape
    heads = total // width
    column = lambda h: (0, h)
    row = lambda h: (h, 0)
    whole = lambda h: (0, 0)
    big = pl.BlockSpec((tokens, width), column)
    shape = lambda kind: jax.ShapeDtypeStruct((tokens, total), kind)
    return pl.pallas_call(
        mixer_forward_kernel,
        grid=(heads,),
        in_specs=[
            big, big, pl.BlockSpec(mask.shape, whole), pl.BlockSpec((8, width), column),
            pl.BlockSpec((width, width), row), pl.BlockSpec((width, width), row),
            pl.BlockSpec((8, width), column),
        ],
        out_specs=[big] * 6,
        out_shape=[shape(jnp.bfloat16), shape(jnp.float32), shape(jnp.float32), shape(jnp.float32), shape(jnp.float32), shape(jnp.bfloat16)],
        scratch_shapes=[
            pltpu.VMEM((tokens + 8, width), jnp.float32),
            pltpu.VMEM((min(CHUNK, tokens), width), jnp.float32),
            pltpu.VMEM((min(CHUNK, tokens), width), jnp.float32),
        ],
        compiler_params=pltpu.CompilerParams(vmem_limit_bytes=48 * 2**20),
        name="mixer_forward",
    )(conv_in, pre, mask, taps, igate, dgate, soft)


def mixer_backward_kernel(
    grad_ref, pre_ref, states_ref, earlier_ref, rounded_ref, gin_ref, gdec_ref, conv_in_ref, mask_ref, ahead_ref,
    taps_ref, igate_ref, dgate_ref, soft_ref, own_ref,
    bpg_ref, cig_ref, igrad_ref, dgrad_ref, tapgrad_ref,
    padded, ahead_pad, coef, drive, decay_sum, tap_sum,
):
    tokens, width = grad_ref.shape
    chunk = min(CHUNK, tokens)
    count = tokens // chunk
    padded[0:8, :] = jnp.zeros((8, width), jnp.float32)
    ahead_pad[tokens : tokens + 8, :] = jnp.zeros((8, width), jnp.float32)
    soft = soft_ref[0:1, :]
    own = own_ref[0:1, :]
    igate = igate_ref[...]
    dgate = dgate_ref[...]
    igrad_ref[...] = jnp.zeros_like(igrad_ref)
    dgrad_ref[...] = jnp.zeros_like(dgrad_ref)
    decay_sum[...] = jnp.zeros_like(decay_sum)
    tap_sum[...] = jnp.zeros_like(tap_sum)
    row = lax.broadcasted_iota(jnp.int32, (8, width), 0)
    rows_dot = lambda a, b: lax.dot_general(a, b, (((0,), (0,)), ((), ())), preferred_element_type=jnp.float32)
    last_dot = lambda a, b: lax.dot_general(a, b, (((1,), (1,)), ((), ())), preferred_element_type=jnp.float32)

    def body(step, carry):
        c = count - 1 - step
        base = pl.multiple_of(c * chunk, chunk)
        here = pl.ds(base, chunk)
        padded[pl.ds(pl.multiple_of(base + 8, 8), chunk), :] = conv_in_ref[here, :].astype(jnp.float32)
        mask = mask_ref[here, :]
        restart = mask[:, 0:1]
        carried = 1.0 - restart
        branch, slope = gelu_parts(pre_ref[here, :])
        grad = grad_ref[here, :]
        bpg_ref[here, :] = (grad * states_ref[here, :] * slope * own).astype(jnp.bfloat16)
        gdec = gdec_ref[here, :]
        gin = gin_ref[here, :]
        log_decay = -soft * (1.0 + 7.0 * gdec)
        decays = jnp.exp(log_decay)
        root = jnp.sqrt(minus_expm1(2.0 * log_decay))
        coef[...] = decays * carried
        drive[...] = grad * branch

        def tile(i, pair):
            adj_next, coef_next = pair
            at = pl.multiple_of(chunk - 8 - i * 8, 8)
            first = coef[pl.ds(at, 8), :]
            a = jnp.where(row == 7, coef_next, pltpu.roll(first, 7, 0))
            b = drive[pl.ds(at, 8), :]
            for sh in (1, 2, 4):
                keep = row < 8 - sh
                b = b + a * jnp.where(keep, pltpu.roll(b, 8 - sh, 0), 0.0)
                a = a * jnp.where(keep, pltpu.roll(a, 8 - sh, 0), 1.0)
            new = b + a * adj_next
            drive[pl.ds(at, 8), :] = new
            return jnp.broadcast_to(new[0:1, :], (8, width)), jnp.broadcast_to(first[0:1, :], (8, width))

        carry = lax.fori_loop(0, chunk // 8, tile, carry, unroll=True)
        adjoint = drive[...]
        rounded = rounded_ref[here, :]
        rounded_float = rounded.astype(jnp.float32)
        pull = adjoint * carried * decays
        log_grad = pull * (earlier_ref[here, :] - rounded_float * gin * decays / root)
        decay_sum[...] += jnp.sum((-log_grad * (1.0 + 7.0 * gdec)).reshape(chunk // 8, 8, width), axis=0)
        through = adjoint * gin * (restart + carried * root)
        ipg = (through * rounded_float * (1.0 - gin)).astype(jnp.bfloat16)
        dpg = (log_grad * (-7.0 * soft) * gdec * (1.0 - gdec)).astype(jnp.bfloat16)
        igrad_ref[...] += rows_dot(rounded, ipg)
        dgrad_ref[...] += rows_dot(rounded, dpg)
        through = through + last_dot(ipg, igate) + last_dot(dpg, dgate)
        ahead_pad[here, :] = through.astype(jnp.bfloat16).astype(jnp.float32)
        return carry

    zero = jnp.zeros((8, width), jnp.float32)
    lax.fori_loop(0, count, body, (zero, zero))

    def after(c, _):
        base = pl.multiple_of(c * chunk, chunk)
        here = pl.ds(base, chunk)
        mask = mask_ref[here, :]
        ahead = ahead_ref[here, :]
        later = ahead_pad[pl.ds(base, chunk + 8), :]
        span = padded[pl.ds(base, chunk + 8), :]
        grad = later[:chunk]
        total = taps_ref[0:1, :] * grad
        tap_sum[0:8, :] += jnp.sum((grad * span[8:]).reshape(chunk // 8, 8, width), axis=0)
        for k in range(1, TAPS):
            total = total + taps_ref[k : k + 1, :] * later[k : k + chunk] * ahead[:, k : k + 1]
            shifted = span[8 - k : 8 - k + chunk]
            tap_sum[8 * k : 8 * k + 8, :] += jnp.sum((grad * shifted * mask[:, k : k + 1]).reshape(chunk // 8, 8, width), axis=0)
        cig_ref[here, :] = (total * own).astype(jnp.bfloat16)
        return 0

    lax.fori_loop(0, count, after, 0)
    for k in range(TAPS):
        tapgrad_ref[k : k + 1, :] = jnp.sum(tap_sum[8 * k : 8 * k + 8, :], axis=0, keepdims=True)
    tapgrad_ref[4:5, :] = jnp.sum(decay_sum[...], axis=0, keepdims=True)
    tapgrad_ref[5:8, :] = jnp.zeros((3, width), jnp.float32)


def mixer_backward(grad, pre, states, earlier, rounded, gin, gdec, conv_in, mask, ahead, taps, igate, dgate, soft, own, width):
    tokens, total = grad.shape
    heads = total // width
    column = lambda h: (0, h)
    row = lambda h: (h, 0)
    whole = lambda h: (0, 0)
    big = pl.BlockSpec((tokens, width), column)
    line = pl.BlockSpec((8, width), column)
    square = pl.BlockSpec((width, width), row)
    shape = lambda kind: jax.ShapeDtypeStruct((tokens, total), kind)
    chunk = min(CHUNK, tokens)
    return pl.pallas_call(
        mixer_backward_kernel,
        grid=(heads,),
        in_specs=[big] * 8 + [pl.BlockSpec(mask.shape, whole)] * 2 + [line, square, square, line, line],
        out_specs=[big, big, square, square, line],
        out_shape=[
            shape(jnp.bfloat16), shape(jnp.bfloat16),
            jax.ShapeDtypeStruct((total, width), jnp.float32), jax.ShapeDtypeStruct((total, width), jnp.float32),
            jax.ShapeDtypeStruct((8, total), jnp.float32),
        ],
        scratch_shapes=[
            pltpu.VMEM((tokens + 8, width), jnp.float32),
            pltpu.VMEM((tokens + 8, width), jnp.float32),
            pltpu.VMEM((chunk, width), jnp.float32),
            pltpu.VMEM((chunk, width), jnp.float32),
            pltpu.VMEM((8, width), jnp.float32),
            pltpu.VMEM((8 * TAPS, width), jnp.float32),
        ],
        compiler_params=pltpu.CompilerParams(vmem_limit_bytes=56 * 2**20),
        name="mixer_backward",
    )(grad, pre, states, earlier, rounded, gin, gdec, conv_in, mask, ahead, taps, igate, dgate, soft, own)


MESH_ID = pl.DeviceIdType.MESH
PIECES = 4


class Spot:
    def __init__(self):
        self.s = lax.axis_index("seq")
        self.f = lax.axis_index("fsdp")
        self.z = self.s // 2
        self.y = self.s % 2
        self.up = (self.z < 3, (jnp.minimum(self.s + 2, 7), self.f))
        self.down = (self.z > 0, (jnp.maximum(self.s - 2, 0), self.f))
        self.beside = (None, (self.s ^ 1, self.f))
        self.across = (None, (self.s, self.f ^ 2))
        self.twin = (None, (self.s, self.f ^ 1))

    def peer(self, j):
        return (None, (self.s ^ j, self.f))

    def other(self, j):
        return (None, (self.s ^ (j // 4), self.f ^ (j % 4)))

    def meet(self, reach):
        barrier = pltpu.get_barrier_semaphore()
        if "all" in reach:
            peers = [self.other(j) for j in range(1, 32)]
        else:
            peers = [self.peer(j) for j in range(1, 8)] if "seq" in reach else []
            if "line" in reach and not peers:
                peers = [self.up, self.down, self.beside]
            if "pair" in reach:
                peers += [self.across, self.twin]
        count = 0
        for cond, where in peers:
            count = count + (1 if cond is None else cond.astype(jnp.int32))
            guarded(cond, lambda: pl.semaphore_signal(barrier, 1, device_id=where, device_id_type=MESH_ID))
        pl.semaphore_wait(barrier, count)


def guarded(cond, action):
    if cond is None:
        action()
    else:
        pl.when(cond)(action)


class Send:
    def __init__(self, src, dst, send_sem, recv_sem, target):
        self.cond, where = target
        self.copy = pltpu.make_async_remote_copy(
            src_ref=src, dst_ref=dst, send_sem=send_sem, recv_sem=recv_sem, device_id=where, device_id_type=MESH_ID
        )

    def start(self):
        guarded(self.cond, self.copy.start)

    def sent(self):
        guarded(self.cond, self.copy.wait_send)


def arrived(dst, send_sem, recv_sem, target, cond=None):
    copy = pltpu.make_async_remote_copy(
        src_ref=dst, dst_ref=dst, send_sem=send_sem, recv_sem=recv_sem, device_id=target[1], device_id_type=MESH_ID
    )
    guarded(cond, copy.wait_recv)


class Gather:
    letter = "g"
    def __init__(self, x):
        self.ins = [x]
        self.outs = [jax.ShapeDtypeStruct((8,) + x.shape, x.dtype)]
        dma = pltpu.SemaphoreType.DMA
        self.scratch = [dma((1,)), dma((8, PIECES)), dma((4, PIECES)), dma((4, PIECES)), dma((7, PIECES))]

    reach = ("line",)

    def steps(self, at, ins, outs, scratch):
        (x,), (o,) = ins, outs
        own_sem, recv, ups, downs, sides = scratch
        rows = x.shape[0] // PIECES
        cut = lambda p: pl.ds(p * rows, rows)
        sends = []

        def send(src, block, p, sem, target):
            one = Send(src, o.at[block, cut(p)], sem, recv.at[block, p], target)
            one.start()
            sends.append(one)

        own = pltpu.make_async_copy(x, o.at[at.s], own_sem.at[0])
        own.start()
        for p in range(PIECES):
            send(x.at[cut(p)], at.s, p, ups.at[0, p], at.up)
            send(x.at[cut(p)], at.s, p, downs.at[0, p], at.down)
            send(x.at[cut(p)], at.s, p, sides.at[0, p], at.beside)
        yield
        for d in range(1, 4):
            for p in range(PIECES):
                low, high = at.z >= d, at.z + d <= 3
                block = jnp.maximum(at.s - 2 * d, 0)
                arrived(o.at[block, cut(p)], ups.at[0, p], recv.at[block, p], at.down, low)
                if d < 3:
                    send(o.at[block, cut(p)], block, p, ups.at[d, p], (low & (at.z < 3), at.up[1]))
                send(o.at[block, cut(p)], block, p, sides.at[d, p], (low, at.beside[1]))
                block = jnp.minimum(at.s + 2 * d, 7)
                arrived(o.at[block, cut(p)], ups.at[0, p], recv.at[block, p], at.up, high)
                if d < 3:
                    send(o.at[block, cut(p)], block, p, downs.at[d, p], (high & (at.z > 0), at.down[1]))
                send(o.at[block, cut(p)], block, p, sides.at[3 + d, p], (high, at.beside[1]))
                yield
        for z in range(4):
            for p in range(PIECES):
                block = 2 * z + 1 - at.y
                arrived(o.at[block, cut(p)], ups.at[0, p], recv.at[block, p], at.beside)
        yield
        for one in sends:
            one.sent()
        own.wait()


class Reduce:
    letter = "r"
    def __init__(self, x):
        _, rows, width = x.shape
        self.ins = [x]
        self.outs = [jax.ShapeDtypeStruct((rows, width), jnp.float32)]
        dma = pltpu.SemaphoreType.DMA
        hold = pltpu.VMEM((4, rows, width), x.dtype)
        self.scratch = [hold, hold, hold, hold, pltpu.VMEM((rows, width), jnp.float32)]
        self.scratch += [dma((4, PIECES)) for _ in range(6)] + [dma((1,))]

    reach = ("line",)

    def steps(self, at, ins, outs, scratch):
        (x,), (o,) = ins, outs
        mine, side, below, above, total, load, ysend, yrecv, zsend, urecv, drecv, osem = scratch
        rows = x.shape[1] // PIECES
        cut = lambda p: pl.ds(p * rows, rows)
        group = 16
        sends = []
        order = []
        for k in range(3):
            order.append((3 - k, at.z < 3 - k, True))
            order.append((k, at.z > k, False))
        order.append((at.z, None, None))

        loads = []
        for t, cond, _ in order:
            for p in range(PIECES):
                one = Send(x.at[2 * t + 1 - at.y, cut(p)], side.at[t, cut(p)], ysend.at[t, p], yrecv.at[t, p], (cond, at.beside[1]))
                one.start()
                sends.append(one)
                copy = pltpu.make_async_copy(x.at[2 * t + at.y, cut(p)], mine.at[t, cut(p)], load.at[t, p])
                guarded(cond, copy.start)
        yield
        for t, cond, rising in order:
            for p in range(PIECES):
                copy = pltpu.make_async_copy(x.at[2 * t + at.y, cut(p)], mine.at[t, cut(p)], load.at[t, p])
                guarded(cond, copy.wait)
                arrived(side.at[t, cut(p)], ysend.at[t, p], yrecv.at[t, p], at.beside, cond)
                if rising is None:
                    arrived(below.at[t, cut(p)], zsend.at[t, p], urecv.at[t, p], at.down, at.z > 0)
                    arrived(above.at[t, cut(p)], zsend.at[t, p], drecv.at[t, p], at.up, at.z < 3)

                    def final(i, _):
                        here = pl.ds(pl.multiple_of(p * rows + i * group, group), group)
                        value = mine[t, here, :].astype(jnp.float32) + side[t, here, :].astype(jnp.float32)
                        total[here, :] = value

                        @pl.when(at.z > 0)
                        def _():
                            total[here, :] += below[t, here, :].astype(jnp.float32)

                        @pl.when(at.z < 3)
                        def _():
                            total[here, :] += above[t, here, :].astype(jnp.float32)

                        return 0

                    lax.fori_loop(0, rows // group, final, 0)
                else:
                    source = below if rising else above
                    inner = (cond & (at.z > 0)) if rising else (cond & (at.z < 3))
                    outer = (cond & (at.z == 0)) if rising else (cond & (at.z == 3))
                    rsem = urecv if rising else drecv
                    arrived(source.at[t, cut(p)], zsend.at[t, p], rsem.at[t, p], at.down if rising else at.up, inner)

                    def add(with_source):
                        def one(i, _):
                            here = pl.ds(pl.multiple_of(p * rows + i * group, group), group)
                            value = mine[t, here, :].astype(jnp.float32) + side[t, here, :].astype(jnp.float32)
                            if with_source:
                                value = value + source[t, here, :].astype(jnp.float32)
                            mine[t, here, :] = value.astype(mine.dtype)
                            return 0

                        lax.fori_loop(0, rows // group, one, 0)

                    pl.when(inner)(lambda: add(True))
                    pl.when(outer)(lambda: add(False))
                    one = Send(mine.at[t, cut(p)], source.at[t, cut(p)], zsend.at[t, p], rsem.at[t, p], (cond, (at.up if rising else at.down)[1]))
                    one.start()
                    sends.append(one)
                yield
        out = pltpu.make_async_copy(total, o, osem.at[0])
        out.start()
        for one in sends:
            one.sent()
        out.wait()


class Spread:
    letter = "s"
    reach = ("seq", "pair")

    def __init__(self, x, starts, wide, letter="s"):
        self.ins = [x]
        self.starts, self.wide, self.letter = starts, wide, letter
        self.outs = [jax.ShapeDtypeStruct((8, 4, x.shape[0], wide), x.dtype)]
        dma = pltpu.SemaphoreType.DMA
        self.scratch = [dma((8,)), dma((8,)), dma((8,)), dma((8,)), dma((8, 2)), dma((8, 2))]

    def steps(self, at, ins, outs, scratch):
        (x,), (o,) = ins, outs
        asend, arecv, xsend, xrecv, csend, crecv = scratch
        sends = []
        part = lambda to: x.at[:, pl.ds(pl.multiple_of(self.starts(to), 128), self.wide)]

        def send(src, dst, ss, rs, target):
            one = Send(src, dst, ss, rs, target)
            one.start()
            sends.append(one)

        for j in range(1, 8):
            send(part(at.s ^ j), o.at[at.s, at.f], asend.at[j], arecv.at[j], at.peer(j))
        own = pltpu.make_async_copy(part(at.s), o.at[at.s, at.f], asend.at[0])
        own.start()
        yield
        for j in range(8):
            block = at.s ^ j
            here = o.at[block, at.f]
            if j == 0:
                own.wait()
            else:
                arrived(here, asend.at[j], arecv.at[j], at.peer(j))
            send(here, here, xsend.at[j], xrecv.at[j], at.across)
            send(here, here, csend.at[j, 0], crecv.at[j, 0], at.twin)
            yield
        for j in range(8):
            there = o.at[at.s ^ j, at.f ^ 2]
            arrived(there, xsend.at[j], xrecv.at[j], at.across)
            send(there, there, csend.at[j, 1], crecv.at[j, 1], at.twin)
            yield
        for j in range(8):
            for k in range(2):
                arrived(o.at[at.s ^ j, (at.f ^ 1) ^ (2 * k)], csend.at[j, k], crecv.at[j, k], at.twin)
        for one in sends:
            one.sent()


def add_rows(dst, terms, rows):
    group = 16

    def one(i, _):
        here = pl.ds(pl.multiple_of(i * group, group), group)
        value = terms[0][here, :].astype(jnp.float32)
        for term in terms[1:]:
            value = value + term[here, :].astype(jnp.float32)
        dst[here, :] = value.astype(dst.dtype)
        return 0

    lax.fori_loop(0, rows // group, one, 0)


class Collect:
    letter = "c"
    def __init__(self, x, window=None):
        self.window = window
        blocks, rows, width = (1, window.rows, x.shape[1]) if window else (x.shape[0],) + x.shape[2:]
        self.shape = (blocks, rows, width)
        self.ins = [x]
        self.blocks = blocks
        self.reach = ("seq", "pair") if blocks > 1 else ("pair",)
        self.outs = [jax.ShapeDtypeStruct((blocks, rows, width), x.dtype)]
        dma = pltpu.SemaphoreType.DMA
        hold = pltpu.VMEM((blocks, rows, width), x.dtype)
        self.scratch = [pltpu.VMEM((2, rows, width), x.dtype)] + [hold] * 3 + [dma((2,))] + [dma((blocks, 2))] * 2 + [dma((blocks,))] * 4

    def steps(self, at, ins, outs, scratch):
        (x,), (o,) = ins, outs
        stage, tnear, tfar, xin, lsem, csend, crecv, xsend, xrecv, asend, arecv = scratch
        rows = self.shape[1]
        many = self.blocks > 1
        spot = (lambda j: at.s ^ j) if many else (lambda j: j)
        sends = []

        def part(j, whose):
            if self.window is None:
                return x.at[spot(j), whose]
            return x.at[pl.ds(pl.multiple_of(self.window.offset(at.s) + rows * whose, 16), rows)]

        def send(src, dst, ss, rs, target):
            one = Send(src, dst, ss, rs, target)
            one.start()
            sends.append(one)

        order = [j for j in range(1, 8)] + [0] if many else [0]
        pieces = [(j, at.f ^ 2) for j in order] + [(j, at.f) for j in order]

        def load(i):
            j, whose = pieces[i]
            return pltpu.make_async_copy(part(j, whose), stage.at[i % 2], lsem.at[i % 2])

        for j in order:
            send(part(j, at.f ^ 3), tfar.at[j], csend.at[j, 0], crecv.at[j, 0], at.twin)
            send(part(j, at.f ^ 1), tnear.at[j], csend.at[j, 1], crecv.at[j, 1], at.twin)
        load(0).start()
        yield
        outs_done = []
        for i, (j, _) in enumerate(pieces):
            far = i < len(order)
            if i + 1 < len(pieces):
                load(i + 1).start()
            load(i).wait()
            if far:
                arrived(tfar.at[j], csend.at[j, 0], crecv.at[j, 0], at.twin)
                add_rows(tfar.at[j], (tfar.at[j], stage.at[i % 2]), rows)
                send(tfar.at[j], xin.at[j], xsend.at[j], xrecv.at[j], at.across)
            else:
                arrived(tnear.at[j], csend.at[j, 1], crecv.at[j, 1], at.twin)
                arrived(xin.at[j], xsend.at[j], xrecv.at[j], at.across)
                add_rows(tnear.at[j], (tnear.at[j], stage.at[i % 2], xin.at[j]), rows)
                if j:
                    send(tnear.at[j], o.at[at.s], asend.at[j], arecv.at[j], at.peer(j))
                else:
                    outs_done.append(pltpu.make_async_copy(tnear.at[0], o.at[at.s if many else 0], asend.at[0]))
                    outs_done[-1].start()
            yield
        for j in order:
            if j:
                arrived(o.at[at.s ^ j], asend.at[j], arecv.at[j], at.peer(j))
        for one in sends:
            one.sent()
        for one in outs_done:
            one.wait()


class Tiny:
    letter = "t"
    def __init__(self, x):
        self.ins = [x]
        self.outs = [jax.ShapeDtypeStruct((32,) + x.shape[1:], x.dtype)]
        self.same = x.shape[0] == 1
        dma = pltpu.SemaphoreType.DMA
        self.scratch = [dma((32,)), dma((32,))]

    reach = ("all",)

    def steps(self, at, ins, outs, scratch):
        (x,), (o,) = ins, outs
        ss, rs = scratch
        me = at.s * 4 + at.f
        part = lambda to: x.at[0] if self.same else x.at[to]
        sends = []
        for j in range(1, 32):
            one = Send(part(me ^ j), o.at[me], ss.at[j], rs.at[j], at.other(j))
            one.start()
            sends.append(one)
        own = pltpu.make_async_copy(part(me), o.at[me], ss.at[0])
        own.start()
        for _ in range(40):
            yield
        for j in range(1, 32):
            arrived(o.at[me ^ j], ss.at[j], rs.at[j], at.other(j))
        for one in sends:
            one.sent()
        own.wait()


class Chain:
    @staticmethod
    def scratch(rows, width, kind):
        dma = pltpu.SemaphoreType.DMA
        return [
            pltpu.VMEM((4, rows, width), kind),
            pltpu.VMEM((5, rows, width), kind),
            pltpu.VMEM((rows, width), jnp.float32),
            dma((4, PIECES)),
            dma((4, PIECES)),
            dma((4, PIECES)),
            dma((5, PIECES)),
            dma((1,)),
        ]

    def __init__(self, at, parts, out, scratch, order):
        self.at, self.parts, self.out, self.order = at, parts, out, order
        self.side, self.inflow, self.total, self.ysend, self.yrecv, self.zsend, self.zrecv, self.osem = scratch
        self.rows = parts.shape[1] // PIECES

    def cut(self, p):
        return pl.ds(pl.multiple_of(p * self.rows, self.rows), self.rows)

    def side_copy(self, t, p):
        at = self.at
        return Send(
            self.parts.at[2 * t + 1 - at.y, self.cut(p)], self.side.at[t, self.cut(p)], self.ysend.at[t, p], self.yrecv.at[t, p], at.beside
        )

    def send_side(self, t):
        for p in range(PIECES):
            self.side_copy(t, p).start()

    def z_copy(self, t, p, rising):
        at = self.at
        slot = t if rising else jnp.where(t == at.z - 1, 4, t)
        mine = self.parts.at[2 * t + at.y, self.cut(p)]
        target = (None, (at.up if rising else at.down)[1])
        return Send(mine, self.inflow.at[slot, self.cut(p)], self.zsend.at[t, p], self.zrecv.at[slot, p], target)

    def wait_side(self, t, p):
        arrived(self.side.at[t, self.cut(p)], self.ysend.at[t, p], self.yrecv.at[t, p], self.at.beside)

    def wait_inflow(self, slot, p):
        arrived(self.inflow.at[slot, self.cut(p)], self.zsend.at[0, p], self.zrecv.at[slot, p], self.at.down)

    def step(self, k, p):
        at = self.at
        group = 16
        rises, falls = self.order(k)
        for t, cond, rising in ((rises, at.z < rises, True), (falls, at.z > falls, False)):

            @pl.when(cond)
            def _():
                self.wait_side(t, p)
                first = at.z == (0 if rising else 3)

                def add(inner):
                    def one(i, _):
                        here = pl.ds(pl.multiple_of(p * self.rows + i * group, group), group)
                        value = self.parts[2 * t + at.y, here, :].astype(jnp.float32) + self.side[t, here, :].astype(jnp.float32)
                        if inner:
                            value = value + self.inflow[t, here, :].astype(jnp.float32)
                        self.parts[2 * t + at.y, here, :] = value.astype(self.parts.dtype)
                        return 0

                    lax.fori_loop(0, self.rows // group, one, 0)

                pl.when(first)(lambda: add(False))

                @pl.when(jnp.logical_not(first))
                def _():
                    self.wait_inflow(t, p)
                    add(True)

                self.z_copy(t, p, rising).start()

    def last(self, p):
        at = self.at
        group = 16
        self.wait_side(at.z, p)
        pl.when(at.z > 0)(lambda: self.wait_inflow(at.z, p))
        pl.when(at.z < 3)(lambda: self.wait_inflow(4, p))

        def one(i, _):
            here = pl.ds(pl.multiple_of(p * self.rows + i * group, group), group)
            self.total[here, :] = self.parts[at.s, here, :].astype(jnp.float32) + self.side[at.z, here, :].astype(jnp.float32)

            @pl.when(at.z > 0)
            def _():
                self.total[here, :] += self.inflow[at.z, here, :].astype(jnp.float32)

            @pl.when(at.z < 3)
            def _():
                self.total[here, :] += self.inflow[4, here, :].astype(jnp.float32)

            return 0

        lax.fori_loop(0, self.rows // group, one, 0)

    def finish(self):
        def one(p, _):
            self.last(p)
            return 0

        lax.fori_loop(0, PIECES, one, 0)
        self.out_copy().start()

    def out_copy(self):
        return pltpu.make_async_copy(self.total, self.out, self.osem.at[0])

    def sent(self):
        def one(i, _):
            t, p = i // PIECES, lax.rem(i, PIECES)
            self.side_copy(t, p).sent()

            @pl.when(t != self.at.z)
            def _():
                self.z_copy(t, p, True).sent()

            return 0

        lax.fori_loop(0, 4 * PIECES, one, 0)
        self.out_copy().wait()


def outward(k):
    rises = jnp.where(k == 0, 1, jnp.where(k == 1, 3, 2))
    return rises, 3 - rises


def farthest(k):
    return 3 - k, k


def descending(k):
    return 3 - k, (2, 0, 1)[k]


class Dense:
    letter = "d"
    reach = ("line",)

    def __init__(self, hidden, returned, w_gate, w_up, w_down, held):
        rows, width = hidden.shape
        wide = w_gate.shape[1]
        low = hidden.dtype
        dma = pltpu.SemaphoreType.DMA
        self.ins = [hidden, returned, w_gate, w_up, w_down, held]
        sums = jax.ShapeDtypeStruct((rows, width), jnp.float32)
        grad = jax.ShapeDtypeStruct((width, wide), low)
        self.outs = [sums, jax.ShapeDtypeStruct((8, rows, width), low), grad, grad, grad]
        tokens = pltpu.VMEM((8, rows, width), low)
        weight = pltpu.VMEM((width, wide), low)
        inner = pltpu.VMEM((8, rows, wide), low)
        self.own = [tokens, tokens, weight, weight, weight, inner, inner, inner, tokens, tokens, pltpu.VMEM(held.shape, held.dtype), pltpu.VMEM((8 * rows, wide), jnp.float32), dma((8,))]
        self.gather = Gather(hidden)
        self.chain = Chain.scratch(rows, width, low)
        self.scratch = self.own + self.gather.scratch + self.chain

    def steps(self, at, ins, outs, scratch):
        hidden, returned, w_gate, w_up, w_down, held = ins
        count = len(self.own)
        toks, cots, wg, wu, wd, act, ggrad, ugrad, hpart, rpart, mask, agrad, sems = scratch[:count]
        scratch = scratch[count:]
        gsems, scratch = scratch[: len(self.gather.scratch)], scratch[len(self.gather.scratch) :]
        hchain = Chain(at, hpart, outs[0], scratch, outward)
        rows, width = hidden.shape
        wide = w_gate.shape[1]
        tile = 256
        loads = [
            pltpu.make_async_copy(src, dst, sems.at[i])
            for i, (src, dst) in enumerate(((w_down, wd), (returned, cots), (w_gate, wg), (w_up, wu), (held, mask)))
        ]
        relay = Relay(at, hidden, toks, gsems)
        relay.begin()
        for load in loads:
            load.start()
        yield
        for load in loads[:2]:
            load.wait()

        def early(p, _):
            source = cots[pl.ds(2 * p, 2)].reshape(2 * rows, width)
            here = pl.ds(pl.multiple_of(2 * rows * p, 2 * rows), 2 * rows)

            def one(n, _):
                lanes = pl.ds(pl.multiple_of(n * tile, tile), tile)
                agrad[here, lanes] = jnp.dot(source, wd[:, lanes], preferred_element_type=jnp.float32)
                return 0

            lax.fori_loop(0, wide // tile, one, 0)
            return 0

        for p in range(PIECES):
            early(p, 0)
            relay.step(1, p)
        for load in loads[2:]:
            load.wait()
        relay.own_copy().wait()
        last_dot = lambda a, b: lax.dot_general(a, b, CONTRACT_LAST, preferred_element_type=jnp.float32)
        rows_dot = lambda a, b: lax.dot_general(a, b, CONTRACT_ROWS, preferred_element_type=jnp.float32)

        def pair(i, _):
            far = at.z < 2
            t = jnp.where(
                i == 0, at.z, jnp.where(i == 1, at.z ^ 1, jnp.where(i == 2, jnp.where(far, 2, 1), jnp.where(far, 3, 0)))
            )
            relay.wait_beside(t)

            @pl.when(i == 3)
            def _():
                hchain.send_side(at.z ^ 1)

            both = pl.ds(2 * t, 2)

            def first(n, _):
                lanes = pl.ds(pl.multiple_of(n * tile, tile), tile)
                h = toks[both].reshape(2 * rows, width)
                pre = jnp.dot(h, wg[:, lanes], preferred_element_type=jnp.float32)
                up = jnp.dot(h, wu[:, lanes], preferred_element_type=jnp.float32)
                grad = agrad[pl.ds(pl.multiple_of(2 * rows * t, 2 * rows), 2 * rows), lanes]
                value, slope = gelu_parts(pre)
                keep = mask[0:1, lanes]
                put = lambda ref, v: ref.__setitem__((both, slice(None), lanes), v.astype(ref.dtype).reshape(2, rows, tile))
                put(act, value * up * keep)
                put(ggrad, grad * up * slope * keep)
                put(ugrad, grad * value * keep)
                for p in range(PIECES // 2):
                    pl.when(n == (p + 1) * wide // tile // (PIECES // 2) - 1)(lambda: relay.step(i + 2, p))
                return 0

            lax.fori_loop(0, wide // tile, first, 0)

            def second(n, _):
                lanes = pl.ds(pl.multiple_of(n * tile, tile), tile)
                a = act[both].reshape(2 * rows, wide)
                g = ggrad[both].reshape(2 * rows, wide)
                u = ugrad[both].reshape(2 * rows, wide)
                put = lambda ref, v: ref.__setitem__((both, slice(None), lanes), v.astype(ref.dtype).reshape(2, rows, tile))
                put(hpart, last_dot(g, wg[lanes, :]) + last_dot(u, wu[lanes, :]))
                put(rpart, last_dot(a, wd[lanes, :]))
                for p in range(PIECES // 2):
                    pl.when(n == 2 + p * (8 // PIECES + 1 if PIECES > 4 else 4))(lambda: relay.step(i + 2, PIECES // 2 + p))
                return 0

            lax.fori_loop(0, width // tile, second, 0)
            return 0

        lax.fori_loop(0, 4, pair, 0)
        hchain.send_side(jnp.where(at.z < 2, 3, 0))
        hchain.send_side(jnp.where(at.z < 2, 2, 1))
        hchain.send_side(at.z)
        out = pltpu.make_async_copy(rpart, outs[1], sems.at[7])
        out.start()

        def grads(r):
            lanes = pl.ds(pl.multiple_of(r * tile, tile), tile)
            h = toks[:, :, lanes].reshape(8 * rows, tile)
            c = cots[:, :, lanes].reshape(8 * rows, tile)
            wg[lanes, :] = rows_dot(h, ggrad[...].reshape(8 * rows, wide)).astype(wg.dtype)
            wu[lanes, :] = rows_dot(h, ugrad[...].reshape(8 * rows, wide)).astype(wu.dtype)
            wd[lanes, :] = rows_dot(c, act[...].reshape(8 * rows, wide)).astype(wd.dtype)

        def hstep(i, _):
            hchain.step(i // PIECES, lax.rem(i, PIECES))
            pl.when(i < width // tile)(lambda: grads(i))
            return 0

        lax.fori_loop(0, 3 * PIECES, hstep, 0)
        hchain.finish()
        stores = [pltpu.make_async_copy(src, dst, sems.at[i]) for i, (src, dst) in enumerate(((wg, outs[2]), (wu, outs[3]), (wd, outs[4])))]
        for store in stores:
            store.start()
        hchain.sent()
        relay.sent()
        for store in stores + [out]:
            store.wait()
        yield


class Relay:
    def __init__(self, at, x, o, sems):
        self.at, self.x, self.o = at, x, o
        self.own_sem, self.recv, self.ups, self.downs, self.sides = sems
        self.rows = x.shape[0] // PIECES

    def cut(self, p):
        return pl.ds(p * self.rows, self.rows)

    def copy(self, src, block, p, sem, target):
        return Send(src, self.o.at[block, self.cut(p)], sem, self.recv.at[block, p], target)

    def own_copy(self):
        return pltpu.make_async_copy(self.x, self.o.at[self.at.s], self.own_sem.at[0])

    def begin(self):
        at = self.at
        self.own_copy().start()
        for p in range(PIECES):
            src = self.x.at[self.cut(p)]
            self.copy(src, at.s, p, self.ups.at[0, p], at.up).start()
            self.copy(src, at.s, p, self.downs.at[0, p], at.down).start()
            self.copy(src, at.s, p, self.sides.at[0, p], at.beside).start()

    def halves(self, d):
        at = self.at
        low = (at.z >= d, jnp.maximum(at.s - 2 * d, 0), self.ups, at.up, d, at.down)
        high = (at.z + d <= 3, jnp.minimum(at.s + 2 * d, 7), self.downs, at.down, 3 + d, at.up)
        return low, high

    def step(self, d, p):
        for cond, block, along, ahead, slot, source in self.halves(d):

            @pl.when(cond)
            def _():
                here = self.o.at[block, self.cut(p)]
                arrived(here, self.ups.at[0, p], self.recv.at[block, p], source)
                self.copy(here, block, p, along.at[d, p], ahead).start()
                self.copy(here, block, p, self.sides.at[slot, p], self.at.beside).start()

    def begin_rising(self):
        at = self.at
        self.own_copy().start()
        for p in range(PIECES):
            src = self.x.at[self.cut(p)]
            self.copy(src, at.s, p, self.ups.at[0, p], at.up).start()
            self.copy(src, at.s, p, self.sides.at[0, p], at.beside).start()

    def take(self, half, d, p):
        cond, block, along, ahead, slot, source = half

        @pl.when(cond)
        def _():
            here = self.o.at[block, self.cut(p)]
            arrived(here, self.ups.at[0, p], self.recv.at[block, p], source)
            self.copy(here, block, p, along.at[d, p], ahead).start()
            self.copy(here, block, p, self.sides.at[slot, p], self.at.beside).start()

    def step_up(self, d, p):
        self.take(self.halves(d)[0], d, p)

    def step_down(self, k, p):
        at = self.at
        d = jnp.maximum(3 - k - at.z, 0)
        high = self.halves(d)[1]
        self.take((at.z < 3 - k,) + high[1:], d, p)

    def own_down(self, top):
        at = self.at
        for p in range(PIECES):

            @pl.when(at.z == 3 if top else at.z < 3)
            def _():
                self.copy(self.x.at[self.cut(p)], at.s, p, self.downs.at[0, p], at.down).start()

    def wait_beside(self, t):
        block = 2 * t + 1 - self.at.y
        for p in range(PIECES):
            arrived(self.o.at[block, self.cut(p)], self.ups.at[0, p], self.recv.at[block, p], self.at.beside)

    def sent(self):
        at = self.at
        for p in range(PIECES):
            src = self.x.at[self.cut(p)]
            self.copy(src, at.s, p, self.ups.at[0, p], at.up).sent()
            self.copy(src, at.s, p, self.downs.at[0, p], at.down).sent()
            self.copy(src, at.s, p, self.sides.at[0, p], at.beside).sent()
            for d in range(1, 4):
                for cond, block, along, ahead, slot, source in self.halves(d):

                    @pl.when(cond)
                    def _():
                        here = self.o.at[block, self.cut(p)]
                        self.copy(here, block, p, along.at[d, p], ahead).sent()
                        self.copy(here, block, p, self.sides.at[slot, p], at.beside).sent()


def exchange(jobs, collective, name, plan=()):
    def kernel(*refs):
        at = Spot()
        refs = list(refs)
        take = lambda count: [refs.pop(0) for _ in range(count)]
        ins = [take(len(job.ins)) for job in jobs]
        outs = [take(len(job.outs)) for job in jobs]
        scratch = [take(len(job.scratch)) for job in jobs]
        at.meet({one for job in jobs for one in job.reach})
        running = [job.steps(at, i, o, s) for job, i, o, s in zip(jobs, ins, outs, scratch)]
        turns = iter(plan)
        while running:
            if plan and running[0] is not None:
                if next(running[0], plan) is plan:
                    running[0] = None
                for letter in next(turns, ""):
                    for job, one in zip(jobs, running):
                        if one is not None and job.letter == letter:
                            next(one, None)
            else:
                running = [one for one in running if one is not None and next(one, running) is not running]

    count = sum(len(job.ins) for job in jobs)
    return pl.pallas_call(
        kernel,
        out_shape=[shape for job in jobs for shape in job.outs],
        in_specs=[pl.BlockSpec(memory_space=pl.ANY)] * count,
        out_specs=[pl.BlockSpec(memory_space=pl.ANY)] * sum(len(job.outs) for job in jobs),
        scratch_shapes=[shape for job in jobs for shape in job.scratch],
        compiler_params=pltpu.CompilerParams(
            collective_id=collective, has_side_effects=True, vmem_limit_bytes=62 * 2**20
        ),
        name=name,
    )(*[x for job in jobs for x in job.ins])


class Window:
    def __init__(self, own, head, width, rows):
        self.own, self.head, self.heads, self.rows = own, head, width // head, rows
        self.size = 2 * head

    def first(self, s):
        return self.head * jnp.minimum(self.own * s // self.head, self.heads - 2)

    def offset(self, s):
        return self.own * s - self.first(s)

    def takes(self, s, slot, f):
        before = self.offset(s)
        if slot == 0:
            return self.own - before < (f + 1) * self.rows
        return f * self.rows < self.size - self.own - before


class Rows:
    letter = "o"

    def __init__(self, x, window=None):
        self.window = window
        self.slots = 1 if window is None else 3
        self.reach = ("pair",) if window is None else ("seq", "pair")
        self.ins = [x]
        self.outs = [jax.ShapeDtypeStruct((self.slots, 4) + x.shape, x.dtype)]
        dma = pltpu.SemaphoreType.DMA
        self.scratch = [dma((3,))] * 4 + [dma((3, 2))] * 2

    def steps(self, at, ins, outs, scratch):
        (x,), (o,) = ins, outs
        asend, arecv, xsend, xrecv, csend, crecv = scratch
        after = lax.rem(at.s + 1, 8)
        before = lax.rem(at.s + 7, 8)
        sends = []

        def send(src, dst, ss, rs, target, cond=None):
            one = Send(src, dst, ss, rs, (cond, target[1]))
            one.start()
            sends.append(one)

        middle = self.slots // 2
        takes = (lambda j, f: self.window.takes(at.s, j, f)) if self.window else None
        holds = lambda j, f: None if j == middle else takes(j, f)
        if self.slots == 3:
            send(x, o.at[0, at.f], asend.at[0], arecv.at[0], (None, (after, at.f)), (at.s < 7) & self.window.takes(after, 0, at.f))
            send(x, o.at[2, at.f], asend.at[2], arecv.at[2], (None, (before, at.f)), (at.s > 0) & self.window.takes(before, 2, at.f))
        own = pltpu.make_async_copy(x, o.at[middle, at.f], asend.at[1])
        own.start()
        send(x, o.at[middle, at.f], xsend.at[middle], xrecv.at[middle], at.across)
        send(x, o.at[middle, at.f], csend.at[middle, 0], crecv.at[middle, 0], at.twin)
        yield
        for j in range(self.slots):
            if j != middle:
                here = o.at[j, at.f]
                cond = holds(j, at.f)
                arrived(here, asend.at[j], arecv.at[j], at.twin, cond)
                send(here, here, xsend.at[j], xrecv.at[j], at.across, cond)
                send(here, here, csend.at[j, 0], crecv.at[j, 0], at.twin, cond)
        yield
        for j in range(self.slots):
            there = o.at[j, at.f ^ 2]
            cond = holds(j, at.f ^ 2)
            arrived(there, xsend.at[j], xrecv.at[j], at.across, cond)
            send(there, there, csend.at[j, 1], crecv.at[j, 1], at.twin, cond)
            yield
        for j in range(self.slots):
            for k in range(2):
                other = (at.f ^ 1) ^ (2 * k)
                arrived(o.at[j, other], csend.at[j, k], crecv.at[j, k], at.twin, holds(j, other))
        for one in sends:
            one.sent()
        own.wait()


def runs(starts, size):
    marks = sorted({edge for start in starts for edge in (start, start + size)})
    found = []
    for begin, end in zip(marks[:-1], marks[1:]):
        found.append((begin, end, [(at, begin - start) for at, start in enumerate(starts) if start <= begin and end <= start + size]))
    return found


def join_kernel(terms, *refs):
    half = len(refs) // 2
    for term, parts_ref, out_ref in zip(terms, refs[:half], refs[half:]):
        for begin, end, sources in term:
            value = None
            for at, first in sources:
                part = parts_ref[at, :, first : first + end - begin].astype(jnp.float32)
                value = part if value is None else value + part
            out_ref[:, begin:end] = value
    refs[-1][...] = refs[half - 1][0].astype(jnp.float32)


def join(dense, dense_starts, mixer, mixer_starts, plain):
    steps = 4
    terms, ins, outs, shapes = [], [], [], []
    for arrays, starts, period, every in ((dense, dense_starts, 2, 1), (mixer, mixer_starts, 4, 2)):
        for x in arrays:
            _, rows, size = x.shape
            term = runs(starts[:period], size)
            columns = term[-1][1]
            terms.append(term)
            ins.append(pl.BlockSpec((period, rows, size), lambda i, every=every: (i // every, 0, 0)))
            outs.append(pl.BlockSpec((rows, columns), lambda i, every=every: (0, i // every)))
            shapes.append(jax.ShapeDtypeStruct((rows, columns * steps // every), jnp.float32))
    _, rows, columns = plain.shape
    ins.append(pl.BlockSpec((1, rows, columns // steps), lambda i: (0, 0, i)))
    outs.append(pl.BlockSpec((rows, columns // steps), lambda i: (0, i)))
    shapes.append(jax.ShapeDtypeStruct((rows, columns), jnp.float32))
    return pl.pallas_call(
        functools.partial(join_kernel, terms), grid=(steps,), in_specs=ins, out_specs=outs, out_shape=shapes, name="join"
    )(*dense, *mixer, plain)


def rms_rows(values):
    mean = jnp.mean(values * values, axis=1, keepdims=True) + EPSILON
    guess = lax.rsqrt(mean)
    return guess * (1.5 - 0.5 * mean * guess * guess)


class MixerForward:
    letter = "m"
    reach = ("line",)

    def __init__(self, window_of, x_full, w_branch, w_input, w_out, igate, dgate, gain, mask, taps, soft):
        self.window_of = window_of
        _, rows, width = x_full.shape
        window, head = igate.shape
        tokens = 8 * rows
        low, full = x_full.dtype, jnp.float32
        dma = pltpu.SemaphoreType.DMA
        self.ins = [x_full, w_branch, w_input, w_out, igate, dgate, gain, mask, taps, soft]
        kinds = [low, full, low, low, full, full, full, low]
        shapes = [(8, rows, width)] + [(tokens, window)] * 7
        self.outs = [jax.ShapeDtypeStruct((rows, width), full)]
        self.outs += [jax.ShapeDtypeStruct(shape, kind) for shape, kind in zip(shapes, kinds)]
        self.kept = [pltpu.VMEM(shape, kind) for shape, kind in zip(shapes, kinds)]
        self.held = [pltpu.VMEM(x.shape, x.dtype) for x in self.ins[1:]]
        self.held[2] = pltpu.VMEM((window, width), low)
        self.local = [
            pltpu.VMEM((8, rows, width), low),
            pltpu.VMEM((8 + 2 * rows, window), full),
            pltpu.VMEM((CHUNK, head), full),
            pltpu.VMEM((CHUNK, head), full),
            pltpu.VMEM((8, window), full),
            dma((len(self.ins),)),
            dma((len(kinds),)),
        ]
        self.chain = Chain.scratch(rows, width, low)
        self.scratch = self.kept + self.held + self.local + self.chain

    def steps(self, at, ins, outs, scratch):
        take = lambda count: [scratch.pop(0) for _ in range(count)]
        scratch = list(scratch)
        kept = take(len(self.kept))
        held = take(len(self.held))
        parts, padded, coef, drive, carry, lsem, ssem = take(len(self.local))
        normed, pre, conv_in, rounded, gin, gdec, states, mixed = kept
        w_branch, w_input, w_out, igate, dgate, gain, mask, taps, soft = held
        chain = Chain(at, parts, outs[0], scratch, farthest)
        _, rows, width = normed.shape
        window, head = igate.shape
        span = 2 * rows
        w_out[...] = jnp.zeros_like(w_out)
        offset = pl.multiple_of(self.window_of.offset(at.s), 16)
        place = lambda dst: dst.at[pl.ds(offset, ins[3].shape[0])] if dst is w_out else dst
        loads = [pltpu.make_async_copy(src, place(dst), lsem.at[i]) for i, (src, dst) in enumerate(zip(ins, [normed] + held))]
        for load in loads:
            load.start()
        yield
        for load in loads:
            load.wait()
        padded[0:8, :] = jnp.zeros((8, window), jnp.float32)
        carry[...] = jnp.zeros_like(carry)
        line = lax.broadcasted_iota(jnp.int32, (8, head), 0)

        def scale(i, _):
            block, here = i // (rows // 16), pl.ds(pl.multiple_of(lax.rem(i, rows // 16) * 16, 16), 16)
            value = normed[block, here, :].astype(jnp.float32)
            normed[block, here, :] = (value * rms_rows(value) * gain[0:1, :]).astype(normed.dtype)
            return 0

        def work(t):
            lax.fori_loop(2 * t * (rows // 16), 2 * (t + 1) * (rows // 16), scale, 0)
            tokens = pl.ds(span * t, span)
            source = normed[2 * t : 2 * t + 2].reshape(span, width)
            if t:
                padded[0:8, :] = padded[span : span + 8, :]
            for h in range(window // head):
                lanes = slice(h * head, (h + 1) * head)
                pre[tokens, lanes] = jnp.dot(source, w_branch[:, lanes], preferred_element_type=jnp.float32)
                value = jnp.dot(source, w_input[:, lanes], preferred_element_type=jnp.float32).astype(conv_in.dtype)
                conv_in[tokens, lanes] = value
                padded[8:, lanes] = value.astype(jnp.float32)
            if t:
                yield
            def piece(c, _):
                for h in range(window // head):
                    lanes = slice(h * head, (h + 1) * head)
                    base = pl.multiple_of(c * CHUNK, CHUNK)
                    here = pl.ds(pl.multiple_of(t * span + base, CHUNK), CHUNK)
                    marks = mask[here, :]
                    rolls = padded[pl.ds(base, CHUNK + 8), lanes]
                    out = taps[0:1, lanes] * rolls[8:]
                    for k in range(1, TAPS):
                        out = out + taps[k : k + 1, lanes] * rolls[8 - k : 8 - k + CHUNK] * marks[:, k : k + 1]
                    small = out.astype(rounded.dtype)
                    rounded[here, lanes] = small
                    g_in = jax.nn.sigmoid(jnp.dot(small, igate[lanes, :], preferred_element_type=jnp.float32))
                    g_dec = jax.nn.sigmoid(jnp.dot(small, dgate[lanes, :], preferred_element_type=jnp.float32))
                    gin[here, lanes] = g_in
                    gdec[here, lanes] = g_dec
                    log_decay = -soft[0:1, lanes] * (1.0 + 7.0 * g_dec)
                    root = jnp.sqrt(minus_expm1(2.0 * log_decay))
                    restart = marks[:, 0:1]
                    carried = 1.0 - restart
                    coef[...] = jnp.exp(log_decay) * carried
                    drive[...] = small.astype(jnp.float32) * g_in * (restart + carried * root)

                    def tile(i, state):
                        now = pl.multiple_of(i * 8, 8)
                        a = coef[pl.ds(now, 8), :]
                        b = drive[pl.ds(now, 8), :]
                        for sh in (1, 2, 4):
                            keep = line >= sh
                            b = b + a * jnp.where(keep, pltpu.roll(b, sh, 0), 0.0)
                            a = a * jnp.where(keep, pltpu.roll(a, sh, 0), 1.0)
                        new = b + a * state
                        there = pl.ds(pl.multiple_of(t * span + base + now, 8), 8)
                        states[there, lanes] = new
                        return jnp.broadcast_to(new[7:8, :], (8, head))

                    carry[:, lanes] = lax.fori_loop(0, CHUNK // 8, tile, carry[:, lanes], unroll=True)
                    branch, _ = gelu_parts(pre[here, lanes])
                    mixed[here, lanes] = (states[here, lanes] * branch).astype(mixed.dtype)
                return 0

            lax.fori_loop(0, span // CHUNK, piece, 0)
            if t:
                yield
            values = mixed[tokens, :]

            def product(n, _):
                columns = pl.ds(pl.multiple_of(n * 256, 256), 256)
                out = jnp.dot(values, w_out[:, columns], preferred_element_type=jnp.float32)
                parts[2 * t : 2 * t + 2, :, columns] = out.astype(parts.dtype).reshape(2, rows, 256)
                return 0

            lax.fori_loop(0, width // 256, product, 0)
            chain.send_side(t)

        for t in range(4):
            yield from work(t)
            yield
        stores = [pltpu.make_async_copy(src, dst, ssem.at[i]) for i, (src, dst) in enumerate(zip(kept, outs[1:]))]
        for store in stores:
            store.start()
        for k in range(3):
            for p in range(PIECES):
                chain.step(k, p)
                yield
        chain.finish()
        yield
        chain.sent()
        for store in stores:
            store.wait()


class MixerBackward:
    letter = "b"
    reach = ("line",)

    def __init__(self, window_of, out_grad, w_out, w_branch, w_input, normed, pre, conv_in, rounded, gin, gdec, states, mixed, igate, dgate, mask, ahead, taps, soft, owned):
        self.window_of = window_of
        rows, width = out_grad.shape
        tokens, window = pre.shape
        head = igate.shape[1]
        low, full = out_grad.dtype, jnp.float32
        dma = pltpu.SemaphoreType.DMA
        self.ins = [out_grad, w_out, w_branch, w_input, normed, pre, conv_in, rounded, gin, gdec, states, mixed, igate, dgate, mask, ahead, taps, soft, owned]
        shape = jax.ShapeDtypeStruct
        self.outs = [
            shape((rows, width), full), shape((width, window - 128), low), shape((width, window - 128), low), shape((window, width), low),
            shape((window, 2 * head), low), shape((window, 128), full),
        ]
        self.held = [pltpu.VMEM(x.shape, x.dtype) for x in self.ins[1:]]
        self.held[0] = pltpu.VMEM((window, width), low)
        self.held[9] = pltpu.VMEM((8 + tokens, window), full)
        self.held[3] = pltpu.VMEM((2, 8, rows, 256), low)
        self.local = [
            pltpu.VMEM((8, rows, width), low),
            pltpu.VMEM((8, rows, width), low),
            pltpu.VMEM((tokens, window), full),
            pltpu.VMEM((tokens, window), low),
            pltpu.VMEM((tokens, window), low),
            pltpu.VMEM((2 * rows + 8, window), full),
            pltpu.VMEM((2 * rows + 8, window), full),
            pltpu.VMEM((CHUNK, head), full),
            pltpu.VMEM((CHUNK, head), full),
            pltpu.VMEM((16, window), full),
            pltpu.VMEM((window, head), full),
            pltpu.VMEM((window, head), full),
            pltpu.VMEM((8 * 5, window), full),
            pltpu.VMEM((window, 2 * head), low),
            pltpu.VMEM((window, 128), full),
            dma((len(self.ins),)),
            dma((8,)),
        ]
        self.gather = Gather(out_grad)
        self.chain = Chain.scratch(rows, width, low)
        self.scratch = self.held + self.local + self.gather.scratch + self.chain

    def steps(self, at, ins, outs, scratch):
        scratch = list(scratch)
        take = lambda count: [scratch.pop(0) for _ in range(count)]
        held = take(len(self.held))
        toks, parts, mgrad, pgrad, cgrad, padded, later, coef, drive, carry, igrad, dgrad, sums, gates, lines, lsem, ssem = take(len(self.local))
        gsems = take(len(self.gather.scratch))
        w_out, w_branch, w_input, normed, pre, conv_in, rounded, gin, gdec, states, mixed, igate, dgate, mask, ahead, taps, soft, owned = held
        chain = Chain(at, parts, outs[0], scratch, descending)
        relay = Relay(at, ins[0], toks, gsems)
        _, rows, width = toks.shape
        tokens, window = pre.shape
        head = igate.shape[1]
        span = 2 * rows
        heads = [slice(h * head, (h + 1) * head) for h in range(window // head)]
        relay.begin()
        loads = []
        for i, (src, dst) in enumerate(zip(ins[1:], held)):
            if dst is normed:
                continue
            if dst is w_out:
                first = pl.multiple_of(self.window_of.own - self.window_of.offset(at.s), 16)
                src = src.at[pl.ds(first, window)]
            loads.append(pltpu.make_async_copy(src, dst.at[8:] if dst is states else dst, lsem.at[i]))
            loads[-1].start()
        states[0:8, :] = jnp.zeros((8, window), jnp.float32)
        for ref in (later, carry, igrad, dgrad, sums):
            ref[...] = jnp.zeros_like(ref)
        yield
        last_dot = lambda a, b: lax.dot_general(a, b, CONTRACT_LAST, preferred_element_type=jnp.float32)
        far = at.z < 2
        order = (at.z, at.z ^ 1, jnp.where(far, 2, 1), jnp.where(far, 3, 0))

        def pull(t):
            relay.wait_beside(t)
            source = toks[pl.ds(2 * t, 2)].reshape(span, width)
            for lanes in heads:
                mgrad[pl.ds(pl.multiple_of(span * t, span), span), lanes] = last_dot(source, w_out[lanes, :])

        for d in range(1, 4):
            for p in range(PIECES):
                relay.step(d, p)
                yield
            if d == 1:
                for load in loads:
                    load.wait()
                relay.own_copy().wait()
            pull(order[d - 1])
        pull(order[3])
        line = lax.broadcasted_iota(jnp.int32, (8, head), 0)
        rows_dot = lambda a, b: lax.dot_general(a, b, CONTRACT_ROWS, preferred_element_type=jnp.float32)
        fold = lambda v: jnp.sum(v.reshape(v.shape[0] // 8, 8, v.shape[1]), axis=0)

        def work(t):
            later[span : span + 8, :] = later[0:8, :]
            if t:
                padded[0:8, :] = conv_in[span * t - 16 : span * t, :].astype(jnp.float32)[8:]
            else:
                padded[0:8, :] = jnp.zeros((8, window), jnp.float32)
            padded[8:, :] = conv_in[span * t : span * (t + 1), :].astype(jnp.float32)

            def piece(step, _):
                base = pl.multiple_of((span // CHUNK - 1 - step) * CHUNK, CHUNK)
                here = pl.ds(pl.multiple_of(t * span + base, CHUNK), CHUNK)
                inside = pl.ds(base, CHUNK)
                marks = mask[here, :]
                restart = marks[:, 0:1]
                carried = 1.0 - restart
                for lanes in heads:
                    branch, slope = gelu_parts(pre[here, lanes])
                    grad = mgrad[here, lanes]
                    state = states[pl.ds(pl.multiple_of(t * span + base, CHUNK), CHUNK + 8), lanes]
                    pgrad[here, lanes] = (grad * state[8:] * slope * owned[0:1, lanes]).astype(pgrad.dtype)
                    g_dec = gdec[here, lanes]
                    g_in = gin[here, lanes]
                    log_decay = -soft[0:1, lanes] * (1.0 + 7.0 * g_dec)
                    decays = jnp.exp(log_decay)
                    root = jnp.sqrt(minus_expm1(2.0 * log_decay))
                    coef[...] = decays * carried
                    drive[...] = grad * branch

                    def tile(i, pair):
                        adj_next, coef_next = pair
                        now = pl.multiple_of(CHUNK - 8 - i * 8, 8)
                        first = coef[pl.ds(now, 8), :]
                        a = jnp.where(line == 7, coef_next, pltpu.roll(first, 7, 0))
                        b = drive[pl.ds(now, 8), :]
                        for sh in (1, 2, 4):
                            keep = line < 8 - sh
                            b = b + a * jnp.where(keep, pltpu.roll(b, 8 - sh, 0), 0.0)
                            a = a * jnp.where(keep, pltpu.roll(a, 8 - sh, 0), 1.0)
                        new = b + a * adj_next
                        drive[pl.ds(now, 8), :] = new
                        return jnp.broadcast_to(new[0:1, :], (8, head)), jnp.broadcast_to(first[0:1, :], (8, head))

                    adj_next, coef_next = lax.fori_loop(0, CHUNK // 8, tile, (carry[0:8, lanes], carry[8:16, lanes]), unroll=True)
                    carry[0:8, lanes] = adj_next
                    carry[8:16, lanes] = coef_next
                    adjoint = drive[...]
                    small = rounded[here, lanes]
                    value = small.astype(jnp.float32)
                    log_grad = adjoint * carried * decays * (state[7 : 7 + CHUNK] - value * g_in * decays / root)
                    sums[32:40, lanes] += fold(-log_grad * (1.0 + 7.0 * g_dec))
                    through = adjoint * g_in * (restart + carried * root)
                    ipg = (through * value * (1.0 - g_in)).astype(jnp.bfloat16)
                    dpg = (log_grad * (-7.0 * soft[0:1, lanes]) * g_dec * (1.0 - g_dec)).astype(jnp.bfloat16)
                    igrad[lanes, :] += rows_dot(small, ipg)
                    dgrad[lanes, :] += rows_dot(small, dpg)
                    through = through + last_dot(ipg, igate[lanes, :]) + last_dot(dpg, dgate[lanes, :])
                    later[inside, lanes] = through.astype(jnp.bfloat16).astype(jnp.float32)
                return 0

            lax.fori_loop(0, span // CHUNK, piece, 0)
            yield

            def after(c, _):
                base = pl.multiple_of(c * CHUNK, CHUNK)
                here = pl.ds(pl.multiple_of(t * span + base, CHUNK), CHUNK)
                marks = mask[here, :]
                ahead_marks = ahead[here, :]
                for lanes in heads:
                    follow = later[pl.ds(base, CHUNK + 8), lanes]
                    before = padded[pl.ds(base, CHUNK + 8), lanes]
                    grad = follow[:CHUNK]
                    total = taps[0:1, lanes] * grad
                    sums[0:8, lanes] += fold(grad * before[8:])
                    for k in range(1, TAPS):
                        total = total + taps[k : k + 1, lanes] * follow[k : k + CHUNK] * ahead_marks[:, k : k + 1]
                        sums[8 * k : 8 * k + 8, lanes] += fold(grad * before[8 - k : 8 - k + CHUNK] * marks[:, k : k + 1])
                    cgrad[here, lanes] = (total * owned[0:1, lanes]).astype(cgrad.dtype)
                return 0

            lax.fori_loop(0, span // CHUNK, after, 0)
            mine = slice(span * t, span * (t + 1))

            def product(n, _):
                columns = pl.ds(pl.multiple_of(n * 256, 256), 256)
                out = last_dot(pgrad[mine, :], w_branch[columns, :]) + last_dot(cgrad[mine, :], w_input[columns, :])
                parts[2 * t : 2 * t + 2, :, columns] = out.astype(parts.dtype).reshape(2, rows, 256)
                return 0

            lax.fori_loop(0, width // 256, product, 0)
            if t > 1:
                chain.send_side(t)

        for t in (3, 2, 1, 0):
            yield from work(t)
            if t == 0:
                chain.send_side(jnp.where(at.z == 0, 1, 0))
                chain.send_side(jnp.where(at.z == 0, 0, 1))
            yield
        gates[:, :head] = igrad[...].astype(gates.dtype)
        gates[:, head:] = dgrad[...].astype(gates.dtype)
        totals = [jnp.sum(sums[8 * k : 8 * k + 8, :], axis=0, keepdims=True) for k in range(5)]
        lines[...] = jnp.concatenate(totals + [jnp.zeros((123, window), jnp.float32)], axis=0).T

        def fetch(r):
            lanes = pl.ds(pl.multiple_of(r * 256, 256), 256)
            return pltpu.make_async_copy(ins[4].at[:, :, lanes], normed.at[lax.rem(r, 2)], ssem.at[6 + lax.rem(r, 2)])

        def grads(r):
            lanes = pl.ds(pl.multiple_of(r * 256, 256), 256)
            pl.when(r + 1 < width // 256)(lambda: fetch(r + 1).start())
            fetch(r).wait()
            value = normed[lax.rem(r, 2)].reshape(tokens, 256)
            w_branch[lanes, :] = rows_dot(value, pgrad[...]).astype(w_branch.dtype)
            w_input[lanes, :] = rows_dot(value, cgrad[...]).astype(w_input.dtype)
            w_out[:, lanes] = rows_dot(mixed[...], toks[:, :, lanes].reshape(tokens, 256)).astype(w_out.dtype)

        fetch(0).start()
        for k in range(3):

            def chain_step(p, _):
                chain.step(k, p)
                pl.when(k * PIECES + p < width // 256)(lambda: grads(k * PIECES + p))
                return 0

            lax.fori_loop(0, PIECES, chain_step, 0)
            yield
        chain.finish()
        owned_lanes = pl.ds(pl.multiple_of(self.window_of.offset(at.s) // 128 * 128, 128), window - 128)
        stores = [
            pltpu.make_async_copy(src.at[:, owned_lanes] if i < 2 else src, dst, ssem.at[i])
            for i, (src, dst) in enumerate(zip((w_branch, w_input, w_out, gates, lines), outs[1:]))
        ]
        for store in stores:
            store.start()
        yield
        chain.sent()
        relay.sent()
        for store in stores:
            store.wait()


def fast(
    inputs,
    resets,
    cotangent,
    first_gain,
    branch_weight,
    input_weight,
    conv_weight,
    input_gate,
    decay_gate,
    decay_param,
    output_weight,
    second_gain,
    gate_weight,
    up_weight,
    down_weight,
):
    low = jnp.bfloat16
    peers, groups = 8, 4
    s, f = lax.axis_index("seq"), lax.axis_index("fsdp")
    sources_low = inputs[0]
    sources = sources_low.astype(jnp.float32)
    returned = cotangent[0]
    tokens, width = sources.shape
    rows = branch_weight.shape[0]
    head = input_gate.shape[1]
    own = width // peers
    hidden_own = gate_weight.shape[1] // peers
    all_tokens = peers * tokens
    window = 2 * head
    channels = Window(own, head, width, rows)
    offset = channels.offset(s)
    owned = ((jnp.arange(window) >= offset) & (jnp.arange(window) < offset + own)).astype(jnp.float32)

    wide_row = lambda v: jnp.pad(v.astype(jnp.float32), (0, 128 - v.shape[0]))
    small = jnp.pad(jnp.stack([wide_row(first_gain), wide_row(second_gain), wide_row(resets[0])]), ((0, 5), (0, 0)))[None]
    dense_start = lambda to: 128 * (hidden_own * to // 128)
    wide = 128 * -(-hidden_own // 128)
    lanes = jnp.arange(wide) + dense_start(s) - hidden_own * s
    held = jnp.broadcast_to(((lanes >= 0) & (lanes < hidden_own)).astype(jnp.float32)[None], (8, wide))
    pad = jnp.zeros((rows, 128 - 5), low)
    row_pack = jnp.concatenate([input_gate, decay_gate, conv_weight, decay_param[:, None], pad], axis=1)
    x_full, w_branch, w_input, row_w, out_w, vectors = exchange(
        [
            Gather(sources_low),
            Spread(branch_weight, channels.first, window),
            Spread(input_weight, channels.first, window),
            Rows(row_pack, channels),
            Rows(output_weight),
            Tiny(small),
        ],
        1,
        "first_exchange",
        ["sot", "sso", "sso", "sso", "ss", "ss", "ss", "s", "s", "s", "s"],
    )
    whole = lambda w: w.reshape(width, w.shape[-1])
    w_branch, w_input = whole(w_branch), whole(w_input)
    w_output = out_w.reshape(own, width)
    near = lax.dynamic_slice_in_dim(row_w.reshape(3 * own, row_pack.shape[1]), own - offset, window, 0)
    w_igate, w_dgate = near[:, :head], near[:, head : 2 * head]
    taps = jnp.zeros((8, window), jnp.float32).at[:4].set(near[:, 2 * head : 2 * head + 4].astype(jnp.float32).T)
    w_decay = near[:, 2 * head + 4].astype(jnp.float32)
    soft = jnp.broadcast_to(jax.nn.softplus(w_decay)[None], (8, window))
    gain_first = vectors[:, 0, :rows].reshape(width)
    gain_second = vectors[:, 1, :rows].reshape(width)
    flags = lax.dynamic_index_in_dim(vectors.reshape(peers, groups, 8, 128), f, 1, False)[:, 2, :tokens].reshape(all_tokens)
    segment = jnp.cumsum(flags)
    masks, aheads = [flags], [jnp.ones_like(flags)]
    for k in range(1, 4):
        same = (segment[k:] == segment[:-k]).astype(jnp.float32)
        masks.append(jnp.concatenate([jnp.zeros((k,), jnp.float32), same]))
        aheads.append(jnp.concatenate([same, jnp.zeros((k,), jnp.float32)]))
    masks = jnp.stack(masks + [jnp.zeros_like(flags)] * 4, axis=1)
    aheads = jnp.stack(aheads + [jnp.zeros_like(flags)] * 4, axis=1)
    owned_rows = jnp.broadcast_to(owned[None], (8, window))

    gain_rows = jnp.broadcast_to(gain_first[None], (8, width))
    (
        mixer_out, normed, pre, conv_in, rounded, gate_in, gate_dec, states, mixed,
        returned_full, w_gate, w_up, w_down, w_output_near,
    ) = exchange(
        [
            MixerForward(channels, x_full, w_branch, w_input, w_output, w_igate, w_dgate, gain_rows, masks, taps, soft),
            Gather(returned),
        ]
        + [Spread(w, dense_start, wide) for w in (gate_weight, up_weight, down_weight)]
        + [Rows(output_weight, channels)],
        2,
        "mixer_forward",
        ["gso", "s", "", "", "s", "", "", "s", "", "", "ggggssggggssggggs"],
    )
    resid = sources + mixer_out
    scale_two = lax.rsqrt(jnp.mean(resid * resid, axis=1, keepdims=True) + EPSILON)
    hidden = (resid * scale_two * gain_second).astype(low)
    hidden_grad, result_part, grad_gate, grad_up, grad_down = exchange(
        [Dense(hidden, returned_full, whole(w_gate), whole(w_up), whole(w_down), held)], 3, "dense"
    )
    weighted = hidden_grad * gain_second
    resid_grad = (
        returned.astype(jnp.float32)
        + scale_two * weighted
        - resid * scale_two**3 * jnp.mean(weighted * resid, axis=1, keepdims=True)
    )
    second_term = jnp.sum(hidden_grad * resid * scale_two, axis=0)
    out_grad = resid_grad.astype(low)
    split = lambda g: g.reshape(peers, groups, rows, g.shape[-1])
    (
        normed_grad, grad_branch, grad_input, grad_output, gates, lines,
        grad_gate, grad_up, grad_down,
    ) = exchange(
        [
            MixerBackward(
                channels, out_grad, w_output_near.reshape(3 * own, width), w_branch, w_input, normed, pre, conv_in, rounded, gate_in, gate_dec, states, mixed,
                w_igate, w_dgate, masks, aheads, taps, soft, owned_rows,
            )
        ]
        + [Collect(split(g)) for g in (grad_gate, grad_up, grad_down)],
        4,
        "mixer_backward",
        ["c"] * 13 + ["c", "", "c", "", "c", "", "", "c"],
    )
    scale_one = lax.rsqrt(jnp.mean(sources * sources, axis=1, keepdims=True) + EPSILON)
    weighted = normed_grad * gain_first
    source_grad = (
        resid_grad
        + scale_one * weighted
        - sources * scale_one**3 * jnp.mean(weighted * sources, axis=1, keepdims=True)
    )
    first_term = jnp.sum(normed_grad * sources * scale_one, axis=0)
    grad_branch, grad_input = split(grad_branch), split(grad_input)
    terms = jnp.stack([first_term.reshape(peers * groups, rows), second_term.reshape(peers * groups, rows)], axis=1)
    vectors = jnp.pad(terms, ((0, 0), (0, 6), (0, 128 - rows)))
    ffn_out, grad_branch, grad_input, grad_output, gates, lines, vectors = exchange(
        [
            Reduce(result_part),
            Collect(grad_branch),
            Collect(grad_input),
            Collect(grad_output, channels),
            Collect(gates, channels),
            Collect(lines, channels),
            Tiny(vectors),
        ],
        6,
        "mixer_collect",
        ["ct"] + ["c"] * 8 + ["", "c"] * 4 + ["c"] * 4,
    )
    result = (resid + ffn_out).astype(low)
    vectors = jnp.sum(vectors, axis=0)
    gates = gates[0].astype(jnp.float32)

    dense_grads, dense_starts = (grad_gate, grad_up, grad_down), [128 * (hidden_own * at // 128) for at in range(peers)]
    mixer_starts = [own * at // 128 * 128 for at in range(peers)]
    grad_gate, grad_up, grad_down, grad_branch, grad_input, grad_output = join(
        dense_grads, dense_starts, (grad_branch, grad_input), mixer_starts, grad_output
    )
    return (
        result[None],
        source_grad.astype(low)[None],
        vectors[0, :rows],
        grad_branch,
        grad_input,
        lines[0, :, :4],
        gates[:, :head],
        gates[:, head:],
        lines[0, :, 4] * jax.nn.sigmoid(decay_param.astype(jnp.float32)),
        grad_output,
        vectors[1, :rows],
        grad_gate,
        grad_up,
        grad_down,
    )


def solution(mesh):
    in_specs = (
        P("fsdp", "seq", None),
        P("fsdp", "seq"),
        P("fsdp", "seq", None),
        P(("seq", "fsdp")),
        P(("seq", "fsdp"), None),
        P(("seq", "fsdp"), None),
        P(("seq", "fsdp"), None),
        P(("seq", "fsdp"), None),
        P(("seq", "fsdp"), None),
        P(("seq", "fsdp")),
        P(("seq", "fsdp"), None),
        P(("seq", "fsdp")),
        P(("seq", "fsdp"), None),
        P(("seq", "fsdp"), None),
        P(("seq", "fsdp"), None),
    )
    out_specs = (
        P("fsdp", "seq", None),
        P("fsdp", "seq", None),
        P(("seq", "fsdp")),
        P(("seq", "fsdp"), None),
        P(("seq", "fsdp"), None),
        P(("seq", "fsdp"), None),
        P(("seq", "fsdp"), None),
        P(("seq", "fsdp"), None),
        P(("seq", "fsdp")),
        P(("seq", "fsdp"), None),
        P(("seq", "fsdp")),
        P(("seq", "fsdp"), None),
        P(("seq", "fsdp"), None),
        P(("seq", "fsdp"), None),
    )
    program = fast if dict(mesh.shape) == {"seq": 8, "fsdp": 4} else local
    return jax.shard_map(program, mesh=mesh, in_specs=in_specs, out_specs=out_specs, check_vma=False)
```
